32 devices in a mesh: wide: 32 (over z, y, x, core).
Axes of the slice: x: 2, y: 2, z: 4, core: 2. Of those that a mesh axis runs over, the one named last changes fastest.
Arguments:
- tokens: bfloat16 [16384, 768], P('wide'), may hold values from -6 to 6
- cotangent: bfloat16 [16384, 768], P('wide'), may hold values from -6 to 6
- cond: bfloat16 [96, 768], replicated, may hold values from -6 to 6
- kept: int32 [96, 128], replicated, may hold values from 0 to 255, as said below
- counts: int32 [32], replicated, may hold values from 256 to 512, as said below
- ada_w: bfloat16 [768, 4608], P('wide'), may hold values from -0.21875 to 0.21875
- ada_bias: bfloat16 [4608], P('wide'), may hold values from -3 to 3
- qkv_w: bfloat16 [768, 2304], P('wide'), may hold values from -0.21875 to 0.21875
- q_bias: bfloat16 [768], P('wide'), may hold values from -3 to 3
- v_bias: bfloat16 [768], P('wide'), may hold values from -3 to 3
- proj_w: bfloat16 [768, 768], P('wide'), may hold values from -0.875 to 0.875
- proj_bias: bfloat16 [768], P('wide'), may hold values from -3 to 3
- fc1_w: bfloat16 [768, 3072], P('wide'), may hold values from -0.21875 to 0.21875
- fc1_bias: bfloat16 [3072], P('wide'), may hold values from -3 to 3
- fc2_w: bfloat16 [3072, 768], P('wide'), may hold values from -0.109375 to 0.109375
- fc2_bias: bfloat16 [768], P('wide'), may hold values from -3 to 3
Outputs:
- out: bfloat16 [16384, 768], P('wide')
- tokens_grad: float32 [16384, 768], P('wide')
- cond_grad: float32 [96, 768], replicated
- ada_w_grad: float32 [768, 4608], P('wide')
- ada_bias_grad: float32 [4608], P('wide')
- qkv_w_grad: float32 [768, 2304], P('wide')
- q_bias_grad: float32 [768], P('wide')
- v_bias_grad: float32 [768], P('wide')
- proj_w_grad: float32 [768, 768], P('wide')
- proj_bias_grad: float32 [768], P('wide')
- fc1_w_grad: float32 [768, 3072], P('wide')
- fc1_bias_grad: float32 [3072], P('wide')
- fc2_w_grad: float32 [3072, 768], P('wide')
- fc2_bias_grad: float32 [768], P('wide')
The draws below stay inside these ranges and needn't reach their ends.
Inputs may be any that keep to these rules, and one draw needn't show every extreme that they name: Each image's kept positions are distinct and increasing. The counts sum to 12288; in every draw some device has all its rows used and some device has 256 used rows.
All inputs are finite; a program needn't handle non-finite values.
Results may differ from the reference program's by a relative error of at most 0.013.
The reference program's roundings to bfloat16 on the way count: a program that leaves them out, or rounds other values in their place, can miss the bound.
Values may be sent and summed in bfloat16 or wider, within the bound.
No kernel may reach another device: no remote copies, remote signals or barrier semaphores. Data moves between devices by JAX's collectives and lax.ppermute only.
A program may use at most 192 MiB of HBM per device.

```python
import math
import jax
import jax.numpy as jnp
from jax import lax

D = 768
HEADS = 12
HD = 64
F = 3072
GRID = 16
LEN = 128
IMG_DEV = 3
PATCHES = 256
TOK_DEV = 512
IMAGES = 96
N_WIDE = 32


def draw_counts(key, part):
    key = jax.random.fold_in(key, 11)
    pair_key, order_key = jax.random.split(key)
    half_pads = jax.random.randint(pair_key, (N_WIDE // 2,), 0, 2 * LEN + 1)
    half_pads = half_pads.at[0].set(0)
    pad_rows = jnp.concatenate([half_pads, 2 * LEN - half_pads])
    pad_rows = jax.random.permutation(order_key, pad_rows)
    return (TOK_DEV - pad_rows).astype(jnp.int32)


def draw_kept(key, part):
    key = jax.random.fold_in(key, 23)
    image_keys = jax.random.split(key, IMAGES)

    def one_image(image_key):
        return jnp.sort(jax.random.permutation(image_key, PATCHES)[:LEN])
    return jax.vmap(one_image)(image_keys).astype(jnp.int32)


def steps_of(rng, extent, cuts, smallest, largest):
    level = 1.0
    for axis_at, shards_of in cuts:
        heights = jax.random.uniform(jax.random.fold_in(jax.random.fold_in(rng, 6), axis_at), (shards_of,), jnp.float32, smallest / len(cuts), largest / len(cuts))
        level = level * jnp.repeat(jnp.exp(heights), extent[axis_at] // shards_of).reshape((-1,) + (1,) * (len(extent) - 1 - axis_at))
    return level


def noise(own_key, dims, deviation, most, cuts=(), held_as=jnp.bfloat16):
    loudness = steps_of(own_key, dims, cuts, -0.22, 0.18) if cuts else 1.0
    array = jax.random.normal(own_key, dims, jnp.float32) * deviation * loudness
    return jnp.minimum(jnp.maximum(array, -most), most).astype(held_as)


def setup_inputs(seed: int = 0) -> dict:
    arg_keys = jax.random.split(jax.random.key(seed), 17)
    tokens = noise(arg_keys[0], (N_WIDE * TOK_DEV, D), 1.0, 6.0, ((0, 32),))
    cotangent = noise(arg_keys[1], (N_WIDE * TOK_DEV, D), 1.0, 6.0, ((0, 32),))
    cond = noise(arg_keys[2], (IMAGES, D), 1.0, 6.0)
    kept = draw_kept(jax.random.fold_in(arg_keys[16], 71), 0)
    counts = draw_counts(jax.random.fold_in(arg_keys[16], 71), 0)
    ada_w = noise(arg_keys[5], (D, 6 * D), D ** -0.5, 0.21875, ((0, 32),))
    ada_bias = noise(arg_keys[6], (6 * D,), 0.5, 3.0, ((0, 32),))
    qkv_w = noise(arg_keys[7], (D, 3 * D), D ** -0.5, 0.21875, ((0, 32),))
    q_bias = noise(arg_keys[8], (D,), 0.5, 3.0, ((0, 32),))
    v_bias = noise(arg_keys[9], (D,), 0.5, 3.0, ((0, 32),))
    proj_w = noise(arg_keys[10], (D, D), (D // 16) ** -0.5, 0.875, ((0, 32),))
    proj_bias = noise(arg_keys[11], (D,), 0.5, 3.0, ((0, 32),))
    fc1_w = noise(arg_keys[12], (D, F), D ** -0.5, 0.21875, ((0, 32),))
    fc1_bias = noise(arg_keys[13], (F,), 0.5, 3.0, ((0, 32),))
    fc2_w = noise(arg_keys[14], (F, D), F ** -0.5, 0.109375, ((0, 32),))
    fc2_bias = noise(arg_keys[15], (D,), 0.5, 3.0, ((0, 32),))
    return {"tokens": tokens, "cotangent": cotangent, "cond": cond, "kept": kept, "counts": counts, "ada_w": ada_w, "ada_bias": ada_bias, "qkv_w": qkv_w, "q_bias": q_bias, "v_bias": v_bias, "proj_w": proj_w, "proj_bias": proj_bias, "fc1_w": fc1_w, "fc1_bias": fc1_bias, "fc2_w": fc2_w, "fc2_bias": fc2_bias}


NORM_EPS = 1e-06
GELU_COEF = 0.7978845608028654

@jax.custom_vjp
def low(v):
    return lax.optimization_barrier(v.astype(jnp.bfloat16)).astype(jnp.float32)

@jax.custom_vjp
def low_back(v):
    return v

def low_keep(v):
    return (low(v), None)

def low_pass(kept, grad):
    return (grad,)

def back_keep(v):
    return (v, None)

def back_low(kept, grad):
    return (low(grad),)
low.defvjp(low_keep, low_pass)
low_back.defvjp(back_keep, back_low)

def matmul_high(left, right):
    return jnp.dot(left, right, precision=lax.Precision.HIGHEST)

def layer_norm(values):
    row_mean = lax.optimization_barrier(jnp.mean(values, axis=-1, keepdims=True))
    centred = values - row_mean
    spread = lax.optimization_barrier(jnp.mean(centred * centred, axis=-1, keepdims=True))
    return centred * lax.rsqrt(spread + NORM_EPS)

def modulate(values, scale_part, shift_part):
    return layer_norm(values) * (1.0 + scale_part) + shift_part

def gelu_tanh(values):
    return 0.5 * values * (1.0 + jnp.tanh(GELU_COEF * (values + 0.044715 * values * values * values)))

def silu(values):
    return values / (1.0 + jnp.exp(-values))

def position_table(patch_index):
    quarter = D // 4
    frequency = jnp.exp(-math.log(10000.0) * jnp.arange(quarter).astype(jnp.float32) / quarter)
    row_angle = (patch_index // GRID).astype(jnp.float32)[:, None] * frequency[None, :]
    col_angle = (patch_index % GRID).astype(jnp.float32)[:, None] * frequency[None, :]
    return jnp.concatenate([jnp.sin(row_angle), jnp.cos(row_angle), jnp.sin(col_angle), jnp.cos(col_angle)], axis=1)

def block_layer(x_block, mod_block, qkv_w, q_b, v_b, proj_w, proj_b, fc1_w, fc1_b, fc2_w, fc2_b):
    row_mod = jnp.repeat(mod_block, LEN, axis=0)
    shift_one, scale_one, gate_one, shift_two, scale_two, gate_two = jnp.split(row_mod, 6, axis=1)
    attn_in = low(modulate(x_block, scale_one, shift_one))
    qkv_bias = jnp.concatenate([q_b, jnp.zeros_like(q_b), v_b])
    qkv = low(low_back(matmul_high(attn_in, qkv_w) + qkv_bias))
    split_qkv = qkv.reshape(IMG_DEV, LEN, 3, HEADS, HD)
    query_part = split_qkv[:, :, 0]
    key_part = split_qkv[:, :, 1]
    value_part = split_qkv[:, :, 2]
    scores = low_back(jnp.einsum('bqhd,bkhd->bhqk', query_part, key_part, precision=lax.Precision.HIGHEST) * (1.0 / math.sqrt(HD)))
    row_max = lax.optimization_barrier(jnp.max(scores, axis=-1, keepdims=True))
    exp_terms = jnp.exp(scores - row_max)
    attn_prob = exp_terms / lax.optimization_barrier(jnp.sum(exp_terms, axis=-1, keepdims=True))
    attended = jnp.einsum('bhqk,bkhd->bqhd', low(attn_prob), value_part, precision=lax.Precision.HIGHEST)
    attended = low(low_back(attended.reshape(IMG_DEV * LEN, D)))
    branch = low_back(matmul_high(attended, proj_w) + proj_b)
    middle = x_block + gate_one * branch
    mlp_in = low(modulate(middle, scale_two, shift_two))
    hidden = low_back(matmul_high(mlp_in, fc1_w) + fc1_b)
    mlp_out = low_back(matmul_high(low(gelu_tanh(hidden)), fc2_w) + fc2_b)
    return middle + gate_two * mlp_out

def reference(tokens, cotangent, cond, kept, counts, ada_w, ada_bias, qkv_w, q_bias, v_bias, proj_w, proj_bias, fc1_w, fc1_bias, fc2_w, fc2_bias):
    first_rows = (jnp.cumsum(counts) - counts).astype(jnp.int32)
    global_rows = jnp.arange(IMAGES * LEN, dtype=jnp.int32)
    owner_dev = (lax.optimization_barrier(jnp.sum((first_rows[None, :] <= global_rows[:, None]).astype(jnp.int32), axis=1)) - 1).astype(jnp.int32)
    physical = (owner_dev * TOK_DEV + global_rows - first_rows[owner_dev]).astype(jnp.int32)
    position = position_table(kept.reshape(-1).astype(jnp.int32))

    def forward(tok_f, cond_f, ada_wf, ada_bf, qkv_wf, q_bf, v_bf, proj_wf, proj_bf, fc1_wf, fc1_bf, fc2_wf, fc2_bf):
        cond_act = low(silu(cond_f))
        modulation = matmul_high(cond_act, ada_wf) + ada_bf
        residual = tok_f[physical] + position

        def one_block(pair):
            return block_layer(pair[0], pair[1], qkv_wf, q_bf, v_bf, proj_wf, proj_bf, fc1_wf, fc1_bf, fc2_wf, fc2_bf)
        blocks = lax.map(jax.checkpoint(one_block), (residual.reshape(N_WIDE, IMG_DEV * LEN, D), modulation.reshape(N_WIDE, IMG_DEV, 6 * D)))
        return tok_f.at[physical].set(blocks.reshape(IMAGES * LEN, D))
    floats = [tokens, cond, ada_w, ada_bias, qkv_w, q_bias, v_bias, proj_w, proj_bias, fc1_w, fc1_bias, fc2_w, fc2_bias]
    floats = [item.astype(jnp.float32) for item in floats]
    output, pull_back = jax.vjp(forward, floats[0], floats[1], floats[2], floats[3], floats[4], floats[5], floats[6], floats[7], floats[8], floats[9], floats[10], floats[11], floats[12])
    grad_list = pull_back(cotangent.astype(jnp.float32))
    return (output.astype(jnp.bfloat16), grad_list[0], grad_list[1], grad_list[2], grad_list[3], grad_list[4], grad_list[5], grad_list[6], grad_list[7], grad_list[8], grad_list[9], grad_list[10], grad_list[11], grad_list[12])
```

```python
import functools
import math

import jax
import jax.numpy as jnp
from jax import lax
from jax.experimental import pallas as pl
from jax.experimental.pallas import tpu as pltpu
from jax.sharding import PartitionSpec as P

D = 768
HEADS = 12
HD = 64
GRID = 16
LEN = 128
TOK_DEV = 512
SLOTS = TOK_DEV // LEN
F = 3072
BLOCKS = 16

NORM_EPS = 1e-06
GELU_COEF = 0.7978845608028654

f32 = jnp.float32
bf16 = jnp.bfloat16

VM = pl.BlockSpec(memory_space=pltpu.VMEM)
SM = pl.BlockSpec(memory_space=pltpu.SMEM)
ANY = pl.BlockSpec(memory_space=pl.ANY)


def params(mib):
    return pltpu.CompilerParams(vmem_limit_bytes=mib * 1024 * 1024)


def cost(flops, size):
    return pl.CostEstimate(flops=int(flops), bytes_accessed=int(size), transcendentals=0)


def dot(left, right):
    return jnp.dot(left, right, preferred_element_type=f32)


def dot_nt(left, right):
    return lax.dot_general(left, right, (((1,), (1,)), ((), ())), preferred_element_type=f32)


def dot_tn(left, right):
    return lax.dot_general(left, right, (((0,), (0,)), ((), ())), preferred_element_type=f32)


def silu(values):
    return values / (1.0 + jnp.exp(-values))


def norm_parts(values):
    centred = values - jnp.mean(values, axis=-1, keepdims=True)
    spread = jnp.mean(centred * centred, axis=-1, keepdims=True)
    inverse = lax.rsqrt(spread + NORM_EPS)
    return centred * inverse, inverse


def norm_back(normed, inverse, scale_part, grad):
    t = grad * (1.0 + scale_part)
    mean_t = jnp.mean(t, axis=-1, keepdims=True)
    mean_tn = jnp.mean(t * normed, axis=-1, keepdims=True)
    return (t - mean_t - normed * mean_tn) * inverse


def rows_from(ref, start):
    base = pl.multiple_of(start // 8 * 8, 8)
    shift = start - base
    tall = LEN + 8
    turned = pltpu.roll(ref[pl.ds(base, tall), :], jnp.where(shift == 0, 0, tall - shift), 0)
    return turned[:LEN]


def slot_rows(slot):
    return slice(slot * LEN, (slot + 1) * LEN)


def mod_part(mod_ref, slot, part):
    return mod_ref[slot : slot + 1, part * D : (part + 1) * D]


def weight_copies(where_ref, pieces, rows, targets, sems, split_rows=False):
    chip, core = where_ref[0], where_ref[1]
    copies = []
    for side in range(2):
        near, over_x, over_y, diag_low, diag_high = pieces[side * 5 : side * 5 + 5]
        half = core if side == 0 else 1 - core
        for turn in range(4):
            for z in range(4):
                if turn < 3:
                    ref, place = (near, over_x, over_y)[turn], z
                else:
                    ref, place = (diag_low, diag_high)[z // 2], z % 2
                block = jnp.bitwise_xor(z * 4 + turn, chip)
                for target, first, width in targets:
                    if split_rows:
                        to_row, to_col = block * (2 * rows) + half * rows, 0
                    else:
                        to_row, to_col = block * rows, half * width
                        to_col = pl.multiple_of(to_col, 128)
                    to_row = pl.multiple_of(to_row, 16)
                    copies.append(
                        pltpu.make_async_copy(
                            ref.at[pl.ds(place * rows, rows), pl.ds(first, width)],
                            target.at[pl.ds(to_row, rows), pl.ds(to_col, width)],
                            sems.at[len(copies)],
                        )
                    )
    for copy in copies:
        copy.start()
    return copies


def wait_all(copies):
    for copy in copies:
        copy.wait()


def align_kernel(place_ref, tok_ref, cot_ref, halo_ref, kept_ref, table_ref, res_ref, gc_ref):
    lead, count, slots = place_ref[0], place_ref[1], place_ref[2]
    table = table_ref[...]
    high = table.astype(bf16)
    rest = table - high.astype(f32)
    middle = rest.astype(bf16)
    low = (rest - middle.astype(f32)).astype(bf16)
    for slot in range(SLOTS):
        row = lax.broadcasted_iota(jnp.int32, (LEN, TOK_DEV), 0) + slot * LEN
        source = row + lead
        live = slot < slots
        column = lax.broadcasted_iota(jnp.int32, (LEN, TOK_DEV), 1)
        own = jnp.where((column == source) & (source < count) & live, 1.0, 0.0).astype(bf16)
        far = source[:, :LEN] - count
        halo = jnp.where((column[:, :LEN] == far) & live, 1.0, 0.0).astype(bf16)
        taken = dot(own, tok_ref[...]) + dot(halo, halo_ref[0:LEN, :])
        grad = dot(own, cot_ref[...]) + dot(halo, halo_ref[LEN : 2 * LEN, :])
        gc_ref[slot_rows(slot), :] = grad.astype(bf16)
        patch = kept_ref[slot : slot + 1, :]
        index = lax.broadcasted_iota(jnp.int32, (GRID, LEN), 0)
        line = jnp.where((index == patch // GRID) & live, 1.0, 0.0).astype(bf16)
        across = jnp.where((index == patch % GRID) & live, 1.0, 0.0).astype(bf16)
        half = D // 2
        for start, picked in ((0, line), (half, across)):
            spot = dot_tn(picked, high) + (dot_tn(picked, middle) + dot_tn(picked, low))
            res_ref[slot_rows(slot), start : start + half] = taken[:, start : start + half] + spot


def head_masks():
    lane = lax.broadcasted_iota(jnp.int32, (1, 2 * HD), 1)
    first = jnp.where(lane < HD, 1.0, 0.0).astype(bf16)
    return first, (1.0 - first.astype(f32)).astype(bf16)


def both_heads(pair, masks):
    return jnp.concatenate([pair * masks[0], pair * masks[1]], axis=0)


def side_by_side(stacked):
    return jnp.concatenate([stacked[:LEN], stacked[LEN:]], axis=1)


def pair_probs(queries, keys):
    scores = dot_nt(queries, keys) * (1.0 / math.sqrt(HD))
    exp_terms = jnp.exp(scores - jnp.max(scores, axis=1, keepdims=True))
    return exp_terms * (1.0 / jnp.sum(exp_terms, axis=1, keepdims=True))


def attend_kernel(where_ref, res_ref, mod_ref, bias_ref, *rest):
    pieces, (ain_ref, qkv_ref, att_ref, weight, sems) = rest[:10], rest[10:]
    copies = weight_copies(where_ref, pieces, D // BLOCKS, [(weight, 0, 3 * D // 2)], sems)
    for slot in range(SLOTS):
        normed, _ = norm_parts(res_ref[slot_rows(slot), :])
        ain_ref[slot_rows(slot), :] = (
            normed * (1.0 + mod_part(mod_ref, slot, 1)) + mod_part(mod_ref, slot, 0)
        ).astype(bf16)
    wait_all(copies)

    @pl.loop(0, 3 * D // 256)
    def _(j):
        cols = pl.ds(pl.multiple_of(j * 256, 256), 256)
        qkv_ref[:, cols] = (dot(ain_ref[...], weight[:, cols]) + bias_ref[:, cols]).astype(bf16)

    masks = head_masks()

    @pl.loop(0, SLOTS)
    def _(slot):
        rows = pl.ds(pl.multiple_of(slot * LEN, LEN), LEN)
        for pair in range(HEADS // 2):
            at = pair * 2 * HD
            probs = pair_probs(
                both_heads(qkv_ref[rows, at : at + 2 * HD], masks),
                qkv_ref[rows, D + at : D + at + 2 * HD],
            )
            values = both_heads(qkv_ref[rows, 2 * D + at : 2 * D + at + 2 * HD], masks)
            att_ref[rows, at : at + 2 * HD] = dot(
                side_by_side(probs.astype(bf16)), values
            ).astype(bf16)


def hidden_kernel(
    where_ref, res_ref, att_ref, mod_ref, gc_ref, proj_bias_ref, bias_ref, *rest
):
    pieces = rest[:10]
    branch_ref, mid_ref, min_ref, act_ref, slope_ref, gmo_ref, colsum_ref = rest[10:17]
    proj, weight, sems = rest[17:]
    copies = weight_copies(
        where_ref, pieces, D // BLOCKS, [(proj, 0, D // 2), (weight, D // 2, F // 2)], sems
    )
    total = jnp.zeros((1, D), f32)
    for slot in range(SLOTS):
        rows = slot_rows(slot)
        grad = (mod_part(mod_ref, slot, 5) * gc_ref[rows, :].astype(f32)).astype(bf16)
        gmo_ref[rows, :] = grad
        total += jnp.sum(grad.astype(f32), axis=0, keepdims=True)
    colsum_ref[...] = total
    wait_all(copies)
    for j in range(D // 256):
        cols = slice(j * 256, (j + 1) * 256)
        branch_ref[:, cols] = dot(att_ref[...], proj[:, cols]) + proj_bias_ref[:, cols]
    for slot in range(SLOTS):
        rows = slot_rows(slot)
        mid = res_ref[rows, :] + mod_part(mod_ref, slot, 2) * branch_ref[rows, :]
        mid_ref[rows, :] = mid
        normed, _ = norm_parts(mid)
        min_ref[rows, :] = (
            normed * (1.0 + mod_part(mod_ref, slot, 4)) + mod_part(mod_ref, slot, 3)
        ).astype(bf16)

    @pl.loop(0, F // 256)
    def _(j):
        cols = pl.ds(pl.multiple_of(j * 256, 256), 256)
        u = dot(min_ref[...], weight[:, cols]) + bias_ref[:, cols]
        square = u * u
        bend = jnp.tanh(GELU_COEF * (u + 0.044715 * square * u))
        left = 0.5 * (1.0 + bend)
        act_ref[:, cols] = (u * left).astype(bf16)
        slope_ref[:, cols] = (
            left
            + 0.5 * u * (1.0 - bend * bend) * (GELU_COEF * (1.0 + 3.0 * 0.044715 * square))
        ).astype(bf16)


def wgrad_kernel(split_rows, where_ref, lhs_ref, rhs_ref, send_ref, keep_ref, flipped, ordered):
    chip, core = where_ref[0], where_ref[1]
    depth = flipped.shape[0]
    block = depth // BLOCKS
    for m in range(depth // 128):
        flipped[m * 128 : (m + 1) * 128, :] = lhs_ref[:, m * 128 : (m + 1) * 128].T
    width = send_ref.shape[1]
    size = block // 2 if split_rows else block
    for b in range(BLOCKS):
        rel = jnp.bitwise_xor(b, chip)
        spot = jnp.bitwise_and(rel, 3) * 4 + lax.shift_right_logical(rel, 2)
        if split_rows:
            for side in range(2):
                to = jnp.where(side == core, BLOCKS * size, 0) + spot * size
                ordered[pl.ds(pl.multiple_of(to, 16), size), :] = flipped[
                    b * block + side * size : b * block + (side + 1) * size, :
                ]
        else:
            ordered[pl.ds(pl.multiple_of(spot * size, 16), size), :] = flipped[
                b * block : (b + 1) * block, :
            ]
    if split_rows:
        step = 512
        for ref, first in ((send_ref, 0), (keep_ref, BLOCKS * size)):

            @pl.loop(0, BLOCKS * size // step)
            def _(j):
                rows = pl.ds(pl.multiple_of(j * step, step), step)
                left = ordered[pl.ds(pl.multiple_of(first + j * step, step), step), :]
                ref[rows, :] = dot(left, rhs_ref[...]).astype(bf16)
    else:
        step = 256
        for ref, half in ((send_ref, 1 - core), (keep_ref, core)):
            cols = pl.ds(pl.multiple_of(half * width, 128), width)

            @pl.loop(0, depth // step)
            def _(j):
                rows = pl.ds(pl.multiple_of(j * step, step), step)
                ref[rows, :] = dot(ordered[rows, :], rhs_ref[:, cols]).astype(bf16)


def fc2_back_kernel(where_ref, gmo_ref, slope_ref, *rest):
    pieces, (gh_ref, colsum_ref, weight, sems) = rest[:10], rest[10:]
    copies = weight_copies(
        where_ref, pieces, F // (2 * BLOCKS), [(weight, 0, D)], sems, split_rows=True
    )
    wait_all(copies)

    @pl.loop(0, F // 256)
    def _(j):
        cols = pl.ds(pl.multiple_of(j * 256, 256), 256)
        grad = dot_nt(gmo_ref[...], weight[cols, :])
        low = (slope_ref[:, cols].astype(f32) * grad).astype(bf16)
        gh_ref[:, cols] = low
        colsum_ref[:, cols] = jnp.sum(low.astype(f32), axis=0, keepdims=True)


def fc2_out_kernel(where_ref, place_ref, act_ref, mid_ref, mod_ref, gc_ref, bias_ref, *rest):
    pieces, (out_ref, tail_ref, gate_ref, weight, mlp, sems) = rest[:10], rest[10:]
    copies = weight_copies(
        where_ref, pieces, F // (2 * BLOCKS), [(weight, 0, D)], sems, split_rows=True
    )
    wait_all(copies)
    for j in range(D // 256):
        cols = slice(j * 256, (j + 1) * 256)
        mlp[0:TOK_DEV, cols] = dot(act_ref[...], weight[:, cols]) + bias_ref[:, cols]
    for slot in range(SLOTS):
        rows = slot_rows(slot)
        value = mlp[rows, :]
        gate_ref[slot : slot + 1, :] = jnp.sum(
            value * gc_ref[rows, :].astype(f32), axis=0, keepdims=True
        )
        value = mid_ref[rows, :] + mod_part(mod_ref, slot, 5) * value
        mlp[rows, :] = value
        out_ref[rows, :] = value.astype(bf16)
    mlp[TOK_DEV:, :] = jnp.zeros((LEN + 8, D), f32)
    tail_ref[...] = rows_from(mlp, place_ref[3]).astype(bf16)


def mid_back_kernel(where_ref, gh_ref, mid_ref, branch_ref, mod_ref, gc_ref, *rest):
    pieces = rest[:10]
    gm_ref, gb_ref, ga_ref, sums_ref, colsum_ref = rest[10:15]
    proj, weight, grads, sems = rest[15:]
    copies = weight_copies(
        where_ref, pieces, D // BLOCKS, [(proj, 0, D // 2), (weight, D // 2, F // 2)], sems
    )
    wait_all(copies)
    for j in range(D // 256):
        cols = slice(j * 256, (j + 1) * 256)
        grads[:, cols] = dot_nt(gh_ref[...], weight[cols, :])
    total = jnp.zeros((1, D), f32)
    for slot in range(SLOTS):
        rows = slot_rows(slot)
        normed, inverse = norm_parts(mid_ref[rows, :])
        e = grads[rows, :]
        one = slice(slot, slot + 1)
        sums_ref[one, D : 2 * D] = jnp.sum(e, axis=0, keepdims=True)
        sums_ref[one, 2 * D : 3 * D] = jnp.sum(e * normed, axis=0, keepdims=True)
        grad_mid = gc_ref[rows, :].astype(f32) + norm_back(
            normed, inverse, mod_part(mod_ref, slot, 4), e
        )
        gm_ref[rows, :] = grad_mid
        sums_ref[one, 0:D] = jnp.sum(branch_ref[rows, :] * grad_mid, axis=0, keepdims=True)
        low = (mod_part(mod_ref, slot, 2) * grad_mid).astype(bf16)
        gb_ref[rows, :] = low
        total += jnp.sum(low.astype(f32), axis=0, keepdims=True)
    colsum_ref[...] = total
    for j in range(D // 256):
        cols = slice(j * 256, (j + 1) * 256)
        ga_ref[:, cols] = dot_nt(gb_ref[...], proj[cols, :]).astype(bf16)


def attend_back_kernel(qkv_ref, ga_ref, gqkv_ref, colsum_ref):
    masks = head_masks()
    scale = 1.0 / math.sqrt(HD)

    @pl.loop(0, SLOTS)
    def _(slot):
        rows = pl.ds(pl.multiple_of(slot * LEN, LEN), LEN)
        for pair in range(HEADS // 2):
            at = pair * 2 * HD
            q_cols, k_cols, v_cols = (
                slice(part * D + at, part * D + at + 2 * HD) for part in range(3)
            )
            queries = both_heads(qkv_ref[rows, q_cols], masks)
            keys = qkv_ref[rows, k_cols]
            probs = pair_probs(queries, keys)
            grads = both_heads(ga_ref[rows, q_cols], masks)
            grad_probs = dot_nt(grads, qkv_ref[rows, v_cols])
            weighed = probs * grad_probs
            inner = jnp.sum(weighed, axis=1, keepdims=True)
            grad_scores = (weighed - probs * inner).astype(bf16)
            gqkv_ref[rows, q_cols] = (
                dot(side_by_side(grad_scores), both_heads(keys, masks)) * scale
            ).astype(bf16)
            gqkv_ref[rows, k_cols] = (dot_tn(grad_scores, queries) * scale).astype(bf16)
            gqkv_ref[rows, v_cols] = dot_tn(probs.astype(bf16), grads).astype(bf16)

    for j in range(3 * D // 256):
        cols = slice(j * 256, (j + 1) * 256)
        colsum_ref[:, cols] = jnp.sum(gqkv_ref[:, cols].astype(f32), axis=0, keepdims=True)


def start_back_kernel(where_ref, place_ref, gqkv_ref, res_ref, gm_ref, mod_ref, *rest):
    pieces, (tg_ref, tail_ref, sums_ref, weight, grads, sems) = rest[:10], rest[10:]
    copies = weight_copies(where_ref, pieces, D // BLOCKS, [(weight, 0, 3 * D // 2)], sems)
    wait_all(copies)
    for j in range(D // 256):
        cols = slice(j * 256, (j + 1) * 256)
        grads[0:TOK_DEV, cols] = dot_nt(gqkv_ref[...], weight[cols, :])
    for slot in range(SLOTS):
        rows = slot_rows(slot)
        normed, inverse = norm_parts(res_ref[rows, :])
        e = grads[rows, :]
        one = slice(slot, slot + 1)
        sums_ref[one, 0:D] = jnp.sum(e, axis=0, keepdims=True)
        sums_ref[one, D : 2 * D] = jnp.sum(e * normed, axis=0, keepdims=True)
        value = gm_ref[rows, :] + norm_back(normed, inverse, mod_part(mod_ref, slot, 1), e)
        tg_ref[rows, :] = value
        grads[rows, :] = value
    grads[TOK_DEV:, :] = jnp.zeros((LEN + 8, D), f32)
    tail_ref[...] = rows_from(grads, place_ref[3])


def place_kernel(
    place_ref, tok_ref, cot_ref, out_ref, tg_ref, out_tail_ref, tg_tail_ref,
    final_out_ref, final_tg_ref, spread,
):
    lead, count = place_ref[0], place_ref[1]
    for got_ref, tail_ref, pad_ref, final_ref in (
        (out_ref, out_tail_ref, tok_ref, final_out_ref),
        (tg_ref, tg_tail_ref, cot_ref, final_tg_ref),
    ):
        spread[0:LEN, :] = jnp.zeros((LEN, D), f32)
        spread[LEN : LEN + TOK_DEV, :] = got_ref[...].astype(f32)
        spread[LEN + TOK_DEV :, :] = jnp.zeros((8, D), f32)
        for slot in range(SLOTS):
            rows = slot_rows(slot)
            row = lax.broadcasted_iota(jnp.int32, (LEN, 1), 0) + slot * LEN
            value = rows_from(spread, LEN - lead + slot * LEN)
            if slot == 0:
                value = jnp.where(row < lead, tail_ref[...].astype(f32), value)
            value = jnp.where(row < count, value, pad_ref[rows, :].astype(f32))
            final_ref[rows, :] = value.astype(final_ref.dtype)


def shape(*dims, dtype=f32):
    return jax.ShapeDtypeStruct(dims, dtype)


def call(kernel, outs, scratch, mib, work, *args, spaces):
    size = sum(math.prod(o.shape) * o.dtype.itemsize for o in outs)
    size += sum(math.prod(a.shape) * a.dtype.itemsize for a in args)
    return pl.pallas_call(
        kernel,
        out_shape=outs,
        in_specs=spaces,
        out_specs=[VM] * len(outs),
        scratch_shapes=scratch,
        compiler_params=params(mib),
        cost_estimate=cost(work, size),
    )(*args)


def swap(array, bits, devices):
    return lax.ppermute(array, "wide", [(i, i ^ bits) for i in range(devices)])


class Links:
    def __init__(self, devices):
        self.devices = devices
        self.cube = devices == 32
        self.me = lax.axis_index("wide")
        self.core = self.me % 2 if self.cube else 0
        self.chip = self.me // 2 if self.cube else 0
        self.where = jnp.stack([jnp.int32(self.chip), jnp.int32(self.core)]).astype(jnp.int32)

    def swap(self, array, bits):
        return swap(array, bits, self.devices)

    def by_core(self, first, second):
        return jnp.where(self.core == 0, first, second)

    def gather(self, local, split_rows):
        if not self.cube:
            pieces = []
            wholes = [lax.all_gather(item, "wide", axis=0, tiled=True) for item in local]
            for half in range(2):
                parts = []
                for whole in wholes:
                    cube = whole.reshape(4, 4, 2, -1, whole.shape[1])
                    if split_rows:
                        parts.append(cube[:, :, half])
                    else:
                        width = whole.shape[1] // 2
                        cube = cube.reshape(4, 4, -1, whole.shape[1])
                        parts.append(cube[..., half * width : (half + 1) * width])
                part = jnp.concatenate(parts, axis=-1)
                turns = [part[:, t].reshape(-1, part.shape[-1]) for t in range(4)]
                rows = turns[3].shape[0] // 2
                pieces += [turns[0], turns[1], turns[2], turns[3][:rows], turns[3][rows:]]
            return pieces
        if split_rows:
            pair = local[0]
        else:
            firsts = jnp.concatenate([item[:, : item.shape[1] // 2] for item in local], axis=1)
            seconds = jnp.concatenate([item[:, item.shape[1] // 2 :] for item in local], axis=1)
            mine = self.by_core(firsts, seconds)
            got = self.swap(self.by_core(seconds, firsts), 1)
            pair = self.by_core(
                jnp.concatenate([mine, got], axis=0), jnp.concatenate([got, mine], axis=0)
            )
        near = jnp.concatenate(
            [pair, self.swap(pair, 8), self.swap(pair, 16), self.swap(pair, 24)], axis=0
        )
        over_x = self.swap(near, 2)
        over_y = self.swap(near, 4)
        rows = near.shape[0] // 2
        diag_low = self.swap(over_y[:rows], 2)
        diag_high = self.swap(over_x[rows:], 4)
        pieces = [near, over_x, over_y, diag_low, diag_high]
        return pieces + [self.swap(piece, 1) for piece in pieces]

    def scatter(self, send, keep, split_rows):
        if not self.cube:
            both = [
                part.reshape(4, 4, -1, part.shape[1]).transpose(1, 0, 2, 3)
                for part in (keep, send)
            ]
            if split_rows:
                whole = jnp.stack(both, axis=2).reshape(-1, keep.shape[1])
            else:
                whole = jnp.concatenate(both, axis=-1).reshape(-1, 2 * keep.shape[1])
            return lax.psum_scatter(whole.astype(f32), "wide", scatter_dimension=0, tiled=True)
        got = self.swap(send, 1)
        size = keep.shape[0] // 8

        def part(first, last):
            rows = slice(first * size, last * size)
            return keep[rows].astype(f32) + got[rows].astype(f32)

        def low(value):
            return value.astype(bf16)

        x_first = self.swap(low(part(6, 7)), 2).astype(f32)
        y_first = self.swap(low(part(7, 8)), 4).astype(f32)
        x_near = self.swap(low(part(2, 3)), 2).astype(f32)
        y_near = self.swap(low(part(5, 6)), 4).astype(f32)
        y_second = self.swap(low(part(4, 5) + x_first), 4).astype(f32)
        x_second = self.swap(low(part(3, 4) + y_first), 2).astype(f32)
        lower = part(0, 1) + x_near + y_second
        upper = part(1, 2) + y_near + x_second
        half = size // 2
        own = lower[:half]
        own = own + self.swap(low(lower[half:]), 8).astype(f32)
        own = own + self.swap(low(upper[:half]), 16).astype(f32)
        own = own + self.swap(low(upper[half:]), 24).astype(f32)
        if split_rows:
            return own
        rows = own.shape[0] // 2
        mine = self.by_core(own[:rows], own[rows:])
        got = self.swap(self.by_core(own[rows:], own[:rows]), 1)
        return mine, got

    def join(self, mine, got):
        return self.by_core(
            jnp.concatenate([mine, got], axis=1), jnp.concatenate([got, mine], axis=1)
        )

    def gather_rows(self, local):
        if not self.cube:
            return lax.all_gather(local, "wide", axis=0, tiled=True)
        pair = jnp.concatenate([local, self.swap(local, 1)], axis=0)
        near = jnp.concatenate(
            [pair, self.swap(pair, 8), self.swap(pair, 16), self.swap(pair, 24)], axis=0
        )
        return jnp.concatenate(
            [near, self.swap(near, 2), self.swap(near, 4), self.swap(near, 6)], axis=0
        )

    def others(self):
        places = jnp.arange(self.devices, dtype=jnp.int32)
        if not self.cube:
            return places
        bits = (places // 8) * 2 + ((places // 2) % 4) * 8 + places % 2
        return jnp.bitwise_xor(bits, self.me)


def on_device(
    tokens,
    cotangent,
    cond,
    kept,
    counts,
    ada_w,
    ada_bias,
    qkv_w,
    q_bias,
    v_bias,
    proj_w,
    proj_bias,
    fc1_w,
    fc1_bias,
    fc2_w,
    fc2_bias,
):
    devices = lax.axis_size("wide")
    images = cond.shape[0]
    links = Links(devices)
    me = links.me
    where = links.where

    first_rows = jnp.cumsum(counts) - counts
    first_images = (first_rows + LEN - 1) // LEN
    last_images = (first_rows + counts + LEN - 1) // LEN
    count = counts[me]
    lead = first_images[me] * LEN - first_rows[me]
    slots = last_images[me] - first_images[me]
    place = jnp.stack([lead, count, slots, count - lead]).astype(jnp.int32)

    halo = lax.ppermute(
        jnp.concatenate([tokens[:LEN], cotangent[:LEN]], axis=0),
        "wide",
        [(i + 1, i) for i in range(devices - 1)],
    )

    cond_float = cond.astype(f32)
    cond_low = silu(cond_float).astype(bf16)
    slot_steps = jnp.arange(SLOTS, dtype=jnp.int32)

    def slot_picker(starts):
        wanted = (starts[:, None] + slot_steps[None, :]).reshape(-1)
        return (wanted[:, None] == jnp.arange(images, dtype=jnp.int32)[None, :]).astype(bf16)

    span = ada_bias.shape[0]
    rows_own = ada_w.shape[0]
    ada_cols = lax.all_to_all(
        ada_w.reshape(rows_own, devices, span).transpose(1, 0, 2).reshape(devices, -1),
        "wide", 0, 0, tiled=True,
    ).reshape(D, span)
    cond_slots = dot(slot_picker(first_images), cond_low).astype(bf16)
    mod_cols = dot(cond_slots, ada_cols) + ada_bias.astype(f32)[None, :]
    small = jnp.concatenate([q_bias, v_bias, proj_bias, fc2_bias, fc1_bias]).astype(f32)
    mixed = jnp.concatenate(
        [
            mod_cols.reshape(devices, SLOTS * span),
            jnp.broadcast_to(small[None, :], (devices, small.shape[0])),
        ],
        axis=1,
    )
    mixed = lax.all_to_all(mixed, "wide", 0, 0, tiled=True)
    mod = mixed[:, : SLOTS * span].reshape(devices, SLOTS, span)
    mod = mod.transpose(1, 0, 2).reshape(SLOTS, 6 * D)
    biases = mixed[:, SLOTS * span :]

    def bias_at(start, stop):
        return biases[:, start * rows_own : stop * rows_own].reshape(1, -1)

    qkv_bias = jnp.concatenate([bias_at(0, 1), jnp.zeros((1, D), f32), bias_at(1, 2)], axis=1)
    proj_bias_all, fc2_bias_all, fc1_bias_all = bias_at(2, 3), bias_at(3, 4), bias_at(4, 8)

    qkv_pieces = links.gather([qkv_w], False)
    mid_pieces = links.gather([proj_w, fc1_w], False)
    fc2_pieces = links.gather([fc2_w], True)

    quarter = D // 4
    frequency = jnp.exp(-math.log(10000.0) * jnp.arange(quarter).astype(f32) / quarter)
    angle = jnp.arange(GRID).astype(f32)[:, None] * frequency[None, :]
    table = jnp.concatenate([jnp.sin(angle), jnp.cos(angle)], axis=1)
    kept_own = lax.dynamic_slice_in_dim(
        jnp.pad(kept, ((0, SLOTS), (0, 0))), first_images[me], SLOTS, 0
    )
    rows = TOK_DEV
    residual, grad_out = call(
        align_kernel,
        [shape(rows, D), shape(rows, D, dtype=bf16)],
        [],
        32,
        4 * rows * 640 * D,
        place, tokens, cotangent, halo, kept_own, table,
        spaces=[SM] + [VM] * 5,
    )

    attn_in, qkv, attended = call(
        attend_kernel,
        [
            shape(rows, D, dtype=bf16),
            shape(rows, 3 * D, dtype=bf16),
            shape(rows, D, dtype=bf16),
        ],
        [pltpu.VMEM((D, 3 * D), bf16), pltpu.SemaphoreType.DMA((32,))],
        40,
        6 * rows * D * D + 24e8,
        where, residual, mod, qkv_bias, *qkv_pieces,
        spaces=[SM] + [VM] * 3 + [ANY] * 10,
    )

    branch, middle, mlp_in, activated, slope, grad_mlp_out, fc2_bias_sum = call(
        hidden_kernel,
        [
            shape(rows, D),
            shape(rows, D),
            shape(rows, D, dtype=bf16),
            shape(rows, F, dtype=bf16),
            shape(rows, F, dtype=bf16),
            shape(rows, D, dtype=bf16),
            shape(1, D),
        ],
        [
            pltpu.VMEM((D, D), bf16),
            pltpu.VMEM((D, F), bf16),
            pltpu.SemaphoreType.DMA((64,)),
        ],
        48,
        2 * rows * D * (D + F) + 24e8,
        where, residual, attended, mod, grad_out, proj_bias_all, fc1_bias_all, *mid_pieces,
        spaces=[SM] + [VM] * 6 + [ANY] * 10,
    )

    def weight_grad(lhs, rhs, split_rows):
        deep, wide = lhs.shape[1], rhs.shape[1]
        half = (deep // 2, wide) if split_rows else (deep, wide // 2)
        return call(
            functools.partial(wgrad_kernel, split_rows),
            [shape(*half, dtype=bf16)] * 2,
            [pltpu.VMEM((deep, rows), bf16)] * 2,
            48,
            2 * rows * deep * wide,
            where, lhs, rhs,
            spaces=[SM, VM, VM],
        )

    fc2_send, fc2_keep = weight_grad(activated, grad_mlp_out, True)
    fc2_grad = links.scatter(fc2_send, fc2_keep, True)

    grad_hidden, fc1_bias_sum = call(
        fc2_back_kernel,
        [shape(rows, F, dtype=bf16), shape(1, F)],
        [pltpu.VMEM((F, D), bf16), pltpu.SemaphoreType.DMA((32,))],
        40,
        2 * rows * D * F,
        where, grad_mlp_out, slope, *fc2_pieces,
        spaces=[SM] + [VM] * 2 + [ANY] * 10,
    )
    result, out_tail, gate_two_sum = call(
        fc2_out_kernel,
        [shape(rows, D, dtype=bf16), shape(LEN, D, dtype=bf16), shape(SLOTS, D)],
        [
            pltpu.VMEM((F, D), bf16),
            pltpu.VMEM((rows + LEN + 8, D), f32),
            pltpu.SemaphoreType.DMA((32,)),
        ],
        40,
        2 * rows * D * F,
        where, place, activated, middle, mod, grad_out, fc2_bias_all, *fc2_pieces,
        spaces=[SM] * 2 + [VM] * 5 + [ANY] * 10,
    )

    grad_middle, grad_branch, grad_attended, mid_sums, proj_bias_sum = call(
        mid_back_kernel,
        [
            shape(rows, D),
            shape(rows, D, dtype=bf16),
            shape(rows, D, dtype=bf16),
            shape(SLOTS, 3 * D),
            shape(1, D),
        ],
        [
            pltpu.VMEM((D, D), bf16),
            pltpu.VMEM((D, F), bf16),
            pltpu.VMEM((rows, D), f32),
            pltpu.SemaphoreType.DMA((64,)),
        ],
        48,
        2 * rows * D * (D + F),
        where, grad_hidden, middle, branch, mod, grad_out, *mid_pieces,
        spaces=[SM] + [VM] * 5 + [ANY] * 10,
    )
    fc1_send, fc1_keep = weight_grad(mlp_in, grad_hidden, False)
    proj_send, proj_keep = weight_grad(attended, grad_branch, False)

    grad_qkv, qkv_bias_sum = call(
        attend_back_kernel,
        [shape(rows, 3 * D, dtype=bf16), shape(1, 3 * D)],
        [],
        32,
        50e8,
        qkv, grad_attended,
        spaces=[VM] * 2,
    )
    qkv_send, qkv_keep = weight_grad(attn_in, grad_qkv, False)

    tokens_back, tokens_tail, start_sums = call(
        start_back_kernel,
        [shape(rows, D), shape(LEN, D), shape(SLOTS, 2 * D)],
        [
            pltpu.VMEM((D, 3 * D), bf16),
            pltpu.VMEM((rows + LEN + 8, D), f32),
            pltpu.SemaphoreType.DMA((32,)),
        ],
        40,
        6 * rows * D * D,
        where, place, grad_qkv, residual, grad_middle, mod, *qkv_pieces,
        spaces=[SM] * 2 + [VM] * 4 + [ANY] * 10,
    )

    if links.cube:
        fc1_grad = links.join(*links.scatter(fc1_send, fc1_keep, False))
        proj_grad = links.join(*links.scatter(proj_send, proj_keep, False))
        qkv_grad = links.join(*links.scatter(qkv_send, qkv_keep, False))
    else:
        fc1_grad = links.scatter(fc1_send, fc1_keep, False)
        proj_grad = links.scatter(proj_send, proj_keep, False)
        qkv_grad = links.scatter(qkv_send, qkv_keep, False)

    onward = [(i, i + 1) for i in range(devices - 1)]
    out_got = lax.ppermute(out_tail, "wide", onward)
    tokens_got = lax.ppermute(tokens_tail, "wide", onward)
    out, tokens_grad = call(
        place_kernel,
        [shape(rows, D, dtype=bf16), shape(rows, D)],
        [pltpu.VMEM((rows + LEN + 8, D), f32)],
        32,
        1e6,
        place, tokens, cotangent, result, tokens_back, out_got, tokens_got,
        spaces=[SM] + [VM] * 6,
    )

    late = links.gather_rows(start_sums.astype(bf16))
    early = links.gather_rows(jnp.concatenate([mid_sums, gate_two_sum], axis=1).astype(bf16))
    grad_mod = jnp.concatenate([late, early], axis=1)
    picker = slot_picker(first_images[links.others()])
    own_at = me * rows_own
    own_act = dot(picker, lax.dynamic_slice_in_dim(cond_low, own_at, rows_own, 1)).astype(bf16)
    ada_grad = dot_tn(own_act, grad_mod)
    ada_bias_grad = lax.dynamic_slice_in_dim(
        jnp.sum(grad_mod.astype(f32), axis=0), me * span, span, 0
    )
    grad_act = dot_nt(grad_mod, ada_w)
    grad_act = lax.dot_general(
        picker.astype(f32), grad_act, (((0,), (0,)), ((), ())), precision=lax.Precision.HIGHEST
    )
    own_cond = lax.dynamic_slice_in_dim(cond_float, own_at, rows_own, 1)
    gate = 1.0 / (1.0 + jnp.exp(-own_cond))
    cond_part = grad_act * (gate * (1.0 + own_cond * (1.0 - gate)))

    bias_sums = jnp.concatenate(
        [
            item.reshape(devices, -1)
            for item in (
                qkv_bias_sum[:, :D],
                qkv_bias_sum[:, 2 * D :],
                proj_bias_sum,
                fc2_bias_sum,
                fc1_bias_sum,
            )
        ],
        axis=1,
    )
    last = jnp.concatenate(
        [jnp.broadcast_to(cond_part.reshape(1, -1), (devices, images * rows_own)), bias_sums],
        axis=1,
    )
    last = lax.all_to_all(last, "wide", 0, 0, tiled=True)
    cond_grad = last[:, : images * rows_own].reshape(devices, images, rows_own)
    cond_grad = cond_grad.transpose(1, 0, 2).reshape(images, D)
    bias_grads = jnp.sum(last[:, images * rows_own :], axis=0)
    q_grad, v_grad, proj_bias_grad, fc2_bias_grad, fc1_bias_grad = (
        bias_grads[a * rows_own : b * rows_own] for a, b in ((0, 1), (1, 2), (2, 3), (3, 4), (4, 8))
    )
    return (
        out,
        tokens_grad,
        cond_grad,
        ada_grad,
        ada_bias_grad,
        qkv_grad,
        q_grad,
        v_grad,
        proj_grad,
        proj_bias_grad,
        fc1_grad,
        fc1_bias_grad,
        fc2_grad,
        fc2_bias_grad,
    )


def solution(mesh):
    row, flat = P("wide", None), P("wide")
    return jax.shard_map(
        on_device,
        mesh=mesh,
        in_specs=(row, row, P(), P(), P(), row, flat, row, flat, flat, row, flat, row, flat, row, flat),
        out_specs=(row, row, P(), row, flat, row, flat, flat, row, flat, row, flat, row, flat),
        check_vma=False,
    )
```

```python
import functools
import math

import jax
import jax.numpy as jnp
from jax import lax
from jax.experimental import pallas as pl
from jax.experimental.pallas import tpu as pltpu
from jax.sharding import PartitionSpec as P

D = 768
HEADS = 12
HD = 64
GRID = 16
LEN = 128
TOK_DEV = 512
SLOTS = TOK_DEV // LEN
F = 3072
BLOCKS = 16

NORM_EPS = 1e-06
GELU_COEF = 0.7978845608028654

f32 = jnp.float32
bf16 = jnp.bfloat16

VM = pl.BlockSpec(memory_space=pltpu.VMEM)
SM = pl.BlockSpec(memory_space=pltpu.SMEM)
ANY = pl.BlockSpec(memory_space=pl.ANY)
HBM = pl.BlockSpec(memory_space=pltpu.HBM)


def params(mib):
    return pltpu.CompilerParams(vmem_limit_bytes=mib * 1024 * 1024)


def cost(us):
    return pl.CostEstimate(flops=max(1, int(us * 1e9)), bytes_accessed=1, transcendentals=0)


def dot(left, right):
    return jnp.dot(left, right, preferred_element_type=f32)


def dot_nt(left, right):
    return lax.dot_general(left, right, (((1,), (1,)), ((), ())), preferred_element_type=f32)


def dot_tn(left, right):
    return lax.dot_general(left, right, (((0,), (0,)), ((), ())), preferred_element_type=f32)


def silu(values):
    return values / (1.0 + jnp.exp(-values))


def norm_parts(values):
    centred = values - jnp.mean(values, axis=-1, keepdims=True)
    spread = jnp.mean(centred * centred, axis=-1, keepdims=True)
    inverse = lax.rsqrt(spread + NORM_EPS)
    return centred * inverse, inverse


def norm_back(normed, inverse, scale_part, grad):
    t = grad * (1.0 + scale_part)
    mean_t = jnp.mean(t, axis=-1, keepdims=True)
    mean_tn = jnp.mean(t * normed, axis=-1, keepdims=True)
    return (t - mean_t - normed * mean_tn) * inverse


def rows_from(ref, start):
    base = pl.multiple_of(start // 8 * 8, 8)
    shift = start - base
    tall = LEN + 8
    turned = pltpu.roll(ref[pl.ds(base, tall), :], jnp.where(shift == 0, 0, tall - shift), 0)
    return turned[:LEN]


def slot_rows(slot):
    return slice(slot * LEN, (slot + 1) * LEN)


def mod_part(mod_ref, slot, part):
    return mod_ref[slot : slot + 1, part * D : (part + 1) * D]


def place_of(block, chip):
    rel = jnp.bitwise_xor(block, chip)
    return jnp.bitwise_and(rel, 3) * 4 + lax.shift_right_logical(rel, 2)


def weight_copies(where_ref, halves, rows, targets, sems, split_rows=False):
    chip, core = where_ref[0], where_ref[1]
    copies = []
    for side in range(2):
        half = core if side == 0 else 1 - core
        place = 0
        for ref in halves[side]:
            for spot in range(ref.shape[0] // rows):
                block = jnp.bitwise_xor(place % 4 * 4 + place // 4, chip)
                place += 1
                for target, first, width in targets:
                    if split_rows:
                        to_row, to_col = (2 * block + half) * rows, 0
                    else:
                        to_row, to_col = block * rows, pl.multiple_of(half * width, 128)
                    to_row = pl.multiple_of(to_row, 16)
                    copies.append(
                        pltpu.make_async_copy(
                            ref.at[pl.ds(spot * rows, rows), pl.ds(first, width)],
                            target.at[pl.ds(to_row, rows), pl.ds(to_col, width)],
                            sems.at[len(copies)],
                        )
                    )
    return start_all(copies)


def start_all(copies):
    for copy in copies:
        copy.start()
    return copies


def fetch(pairs, sems, first=0):
    return start_all(
        [pltpu.make_async_copy(a, b, sems.at[first + i]) for i, (a, b) in enumerate(pairs)]
    )


def wait_all(copies):
    for copy in copies:
        copy.wait()


def begin_kernel(
    where_ref, counts_ref, cond_in, ada_in, tok_in, cot_in, qkv_in, proj_in, fc1_in,
    mine_ref, send_ref, edge_ref, place_ref, starts_ref, slots_ref, parts_ref,
    wide, cond, ada, sems,
):
    devices = counts_ref.shape[0]
    images = cond.shape[0]
    core, me = where_ref[1], where_ref[2]
    copies = []
    first = 0
    for ref in (qkv_in, proj_in, fc1_in):
        half = ref.shape[1] // 2
        for out, at in ((send_ref, 1 - core), (mine_ref, core)):
            copies.append(
                (
                    ref.at[:, pl.ds(pl.multiple_of(at * half, 128), half)],
                    out.at[:, pl.ds(first, half)],
                )
            )
        first += half
    copies.append((tok_in.at[pl.ds(0, LEN), :], edge_ref.at[pl.ds(0, LEN), :]))
    copies.append((cot_in.at[pl.ds(0, LEN), :], edge_ref.at[pl.ds(LEN, LEN), :]))
    copies = fetch([*copies, (cond_in, cond), (ada_in, ada)], sems)

    def step(d, first_row):
        count = counts_ref[d]
        begin = (first_row + LEN - 1) // LEN
        starts_ref[d] = begin

        @pl.when(d == me)
        def _():
            lead = begin * LEN - first_row
            place_ref[0] = lead
            place_ref[1] = count
            place_ref[2] = (first_row + count + LEN - 1) // LEN - begin
            place_ref[3] = count - lead
            place_ref[4] = begin

        return first_row + count

    lax.fori_loop(0, devices, step, jnp.int32(0))
    sub = lax.broadcasted_iota(jnp.int32, (8, images), 0)
    lane = lax.broadcasted_iota(jnp.int32, (8, images), 1)

    @pl.loop(0, devices)
    def _(d):
        hit = (lane == starts_ref[d] + sub) & (sub < SLOTS)
        wide[pl.ds(pl.multiple_of(d * 8, 8), 8), :] = jnp.where(hit, 1.0, 0.0)

    wait_all(copies)
    span = parts_ref.shape[2]
    for d in range(devices):
        parts_ref[d] = ada[:, d * span : (d + 1) * span]
    act = silu(cond[...].astype(f32)).astype(bf16)
    slots_ref[...] = dot(wide[...].astype(bf16), act).astype(bf16)


def ada_kernel(
    where_ref, starts_ref, early_ref, late_ref, ada_ref, cond_ref,
    qkv_sum_ref, proj_sum_ref, fc2_sum_ref, fc1_sum_ref,
    grad_ref, colsum_ref, last_ref, wide, packed,
):
    devices = early_ref.shape[0]
    images, own = cond_ref.shape[0], ada_ref.shape[0]
    me = where_ref[2]
    row = lax.broadcasted_iota(jnp.int32, (own, D), 0)
    lane = lax.broadcasted_iota(jnp.int32, (own, D), 1)
    chosen = jnp.where(lane == me * own + row, 1.0, 0.0).astype(bf16)
    act = silu(cond_ref[...].astype(f32)).astype(bf16)
    act_own = dot_nt(act, chosen).astype(bf16)
    cond_own = dot_nt(chosen, cond_ref[...])
    total = jnp.zeros((own, images), f32)
    for ref, parts in ((early_ref, (2, 3, 4)), (late_ref, (0, 1, 5))):
        tall = 4 * SLOTS
        sums = ref[...].reshape(devices * tall, D)
        sub = lax.broadcasted_iota(jnp.int32, (tall, images), 0)
        lane = lax.broadcasted_iota(jnp.int32, (tall, images), 1)
        for i, part in enumerate(parts):

            @pl.loop(0, devices)
            def _(d):
                slot = sub - SLOTS * i
                hit = (lane == starts_ref[d] + slot) & (slot >= 0) & (slot < SLOTS)
                wide[pl.ds(pl.multiple_of(d * tall, tall), tall), :] = jnp.where(hit, 1.0, 0.0)

            picked = wide[0 : devices * tall, :]
            act_rows = dot(picked.astype(bf16), act_own).astype(bf16)
            ours = lax.broadcasted_iota(jnp.int32, (8, devices * tall), 1) % tall // SLOTS == i
            ours = jnp.where(ours, 1.0, 0.0).astype(bf16)
            cols = slice(part * D, (part + 1) * D)
            grad_ref[:, cols] = dot_tn(act_rows, sums)
            colsum_ref[:, cols] = dot(ours, sums)[0:1]
            total += jnp.dot(
                dot_nt(ada_ref[:, cols], sums), picked, precision=lax.Precision.HIGHEST
            )
    gate = 1.0 / (1.0 + jnp.exp(-cond_own))
    total = total * (gate * (1.0 + cond_own * (1.0 - gate)))
    lanes = last_ref.shape[2]
    fc1_sum = fc1_sum_ref[...]
    both = qkv_sum_ref[...]
    vectors = [both[:, :D], both[:, 2 * D :], proj_sum_ref[...], fc2_sum_ref[...]]
    for d in range(devices):
        packed[...] = jnp.zeros(packed.shape, f32)
        packed[0:own, 0:images] = total
        for j in range(8):
            if j < 4:
                value = vectors[j][:, d * own : (d + 1) * own]
            else:
                at = (4 * d + j - 4) * own
                value = fc1_sum[:, at : at + own]
            packed[own + j : own + j + 1, 0:own] = value
        last_ref[d] = packed[...].astype(bf16)


def finish_kernel(got_ref, cond_ref, bias_ref, tall):
    devices, rows, _ = got_ref.shape
    own = rows - 8
    total = None
    for d in range(devices):
        got = got_ref[d].astype(f32)
        tall[d * own : (d + 1) * own, :] = got[0:own]
        total = got[own:rows] if total is None else total + got[own:rows]
    cond_ref[...] = tall[...].T[0 : cond_ref.shape[0], :]
    bias_ref[...] = total


def mod_kernel(slots_ref, cols_ref, addend_ref, out_ref):
    value = dot(slots_ref[...], cols_ref[...])
    for d in range(out_ref.shape[0]):
        out_ref[d] = value[d * 8 : (d + 1) * 8, :] + addend_ref[...]


def prep_kernel(
    place_ref, got_ref, tok_in, cot_in, halo_in, kept_in, table_in,
    res_ref, gc_ref, mod_ref, qkv_bias_ref, proj_bias_ref, fc2_bias_ref, fc1_bias_ref,
    tok, cot, halo, kept, table, sems,
):
    copies = fetch(
        [(table_in, table), (kept_in, kept), (halo_in, halo), (tok_in, tok), (cot_in, cot)], sems
    )
    devices, _, span = got_ref.shape
    width = D // devices
    qkv_bias_ref[:, D : 2 * D] = jnp.zeros((1, D), f32)
    for d in range(devices):
        got = got_ref[d]
        mod_ref[:, d * span : (d + 1) * span] = got[0:SLOTS]
        cols = slice(d * width, (d + 1) * width)
        qkv_bias_ref[:, cols] = got[4:5, 0:width]
        qkv_bias_ref[:, 2 * D + d * width : 2 * D + (d + 1) * width] = got[4:5, width : 2 * width]
        proj_bias_ref[:, cols] = got[4:5, 2 * width : 3 * width]
        fc2_bias_ref[:, cols] = got[4:5, 3 * width : 4 * width]
        fc1_bias_ref[:, d * 4 * width : (d + 1) * 4 * width] = got[5:6, 0 : 4 * width]
    lead, count, slots, begin = place_ref[0], place_ref[1], place_ref[2], place_ref[4]
    wait_all(copies)
    angles = table[...]
    high = angles.astype(bf16)
    rest = angles - high.astype(f32)
    middle = rest.astype(bf16)
    lowest = (rest - middle.astype(f32)).astype(bf16)
    images = kept.shape[0]
    sub = lax.broadcasted_iota(jnp.int32, (8, images), 0)
    lane = lax.broadcasted_iota(jnp.int32, (8, images), 1)
    picker = jnp.where(lane == begin + sub, 1.0, 0.0).astype(bf16)
    patches = dot(picker, kept[...].astype(f32).astype(bf16)).astype(jnp.int32)
    for slot in range(SLOTS):
        row = lax.broadcasted_iota(jnp.int32, (LEN, TOK_DEV), 0) + slot * LEN
        source = row + lead
        live = slot < slots
        column = lax.broadcasted_iota(jnp.int32, (LEN, TOK_DEV), 1)
        own = jnp.where((column == source) & (source < count) & live, 1.0, 0.0).astype(bf16)
        far = source[:, :LEN] - count
        spill = jnp.where((column[:, :LEN] == far) & live, 1.0, 0.0).astype(bf16)
        taken = dot(own, tok[...]) + dot(spill, halo[0:LEN, :])
        grad = dot(own, cot[...]) + dot(spill, halo[LEN : 2 * LEN, :])
        gc_ref[slot_rows(slot), :] = grad.astype(bf16)
        patch = patches[slot : slot + 1, :]
        index = lax.broadcasted_iota(jnp.int32, (GRID, LEN), 0)
        line = jnp.where((index == patch // GRID) & live, 1.0, 0.0).astype(bf16)
        across = jnp.where((index == patch % GRID) & live, 1.0, 0.0).astype(bf16)
        half = D // 2
        for start, picked in ((0, line), (half, across)):
            spot = dot_tn(picked, high) + (dot_tn(picked, middle) + dot_tn(picked, lowest))
            res_ref[slot_rows(slot), start : start + half] = taken[:, start : start + half] + spot


def head_masks():
    lane = lax.broadcasted_iota(jnp.int32, (1, 2 * HD), 1)
    first = jnp.where(lane < HD, 1.0, 0.0).astype(bf16)
    return first, (1.0 - first.astype(f32)).astype(bf16)


def both_heads(pair, masks):
    return jnp.concatenate([pair * masks[0], pair * masks[1]], axis=0)


def side_by_side(stacked):
    return jnp.concatenate([stacked[:LEN], stacked[LEN:]], axis=1)


def pair_probs(queries, keys):
    scores = dot_nt(queries, keys) * (1.0 / math.sqrt(HD))
    exp_terms = jnp.exp(scores - jnp.max(scores, axis=1, keepdims=True))
    return exp_terms * (1.0 / jnp.sum(exp_terms, axis=1, keepdims=True))


def qkv_kernel(
    where_ref, res_ref, mod_ref, bias_ref, near_ref, far_ref, ain_out, qkv_ref, ain_ref, weight, sems, out_sems
):
    copies = weight_copies(
        where_ref, ([near_ref], [far_ref]), D // BLOCKS, [(weight, 0, 3 * D // 2)], sems
    )
    for slot in range(SLOTS):
        normed, _ = norm_parts(res_ref[slot_rows(slot), :])
        ain_ref[slot_rows(slot), :] = (
            normed * (1.0 + mod_part(mod_ref, slot, 1)) + mod_part(mod_ref, slot, 0)
        ).astype(bf16)
    out = fetch([(ain_ref, ain_out)], out_sems)
    wait_all(copies)

    @pl.loop(0, 3 * D // 256)
    def _(j):
        cols = pl.ds(pl.multiple_of(j * 256, 256), 256)
        qkv_ref[:, cols] = (dot(ain_ref[...], weight[:, cols]) + bias_ref[:, cols]).astype(bf16)

    wait_all(out)


def attend_kernel(qkv_ref, att_ref, att_out, sems):
    masks = head_masks()

    @pl.loop(0, SLOTS)
    def _(slot):
        rows = pl.ds(pl.multiple_of(slot * LEN, LEN), LEN)
        for pair in range(HEADS // 2):
            at = pair * 2 * HD
            probs = pair_probs(
                both_heads(qkv_ref[rows, at : at + 2 * HD], masks),
                qkv_ref[rows, D + at : D + at + 2 * HD],
            )
            values = both_heads(qkv_ref[rows, 2 * D + at : 2 * D + at + 2 * HD], masks)
            att_ref[rows, at : at + 2 * HD] = dot(
                side_by_side(probs.astype(bf16)), values
            ).astype(bf16)

    wait_all(fetch([(att_ref, att_out)], sems))


def join_kernel(*refs):
    *parts, both, sems = refs
    pairs, first = [], 0
    for ref in parts:
        rows = ref.shape[0]
        pairs.append((ref, both.at[pl.ds(first, rows), :]))
        first += rows
    wait_all(fetch(pairs, sems))


def flip(where_ref, lhs_ref, ordered, split_rows):
    chip, core = where_ref[0], where_ref[1]
    depth = ordered.shape[0]
    size = depth // BLOCKS
    if split_rows:
        size //= 2
    step = 384
    for m in range(depth // step):
        turned = lhs_ref[:, m * step : (m + 1) * step].T
        for i in range(step // size):
            block = m * (step // size) + i
            side = block % 2
            to = place_of(block // 2 if split_rows else block, chip) * size
            if split_rows:
                to = to + jnp.where(core == side, depth // 2, 0)
            ordered[pl.ds(pl.multiple_of(to, 16), size), :] = turned[i * size : (i + 1) * size, :]


def hidden_kernel(
    where_ref, res_ref, att_ref, mod_ref, gc_ref, proj_bias_ref, bias_ref, *rest
):
    mine, more, theirs, rest_far = rest[:4]
    branch_ref, mid_ref, min_ref, gmo_ref, colsum_ref, act_out, slope_out, send_out, keep_out, mid_out = rest[4:14]
    proj, weight, act, slope, ordered, made, sems, out_sems = rest[14:]
    copies = weight_copies(
        where_ref,
        ([mine, more], [theirs, rest_far]),
        D // BLOCKS,
        [(proj, 0, D // 2), (weight, D // 2, F // 2)],
        sems,
    )
    total = jnp.zeros((1, D), f32)
    for slot in range(SLOTS):
        rows = slot_rows(slot)
        grad = (mod_part(mod_ref, slot, 5) * gc_ref[rows, :].astype(f32)).astype(bf16)
        gmo_ref[rows, :] = grad
        total += jnp.sum(grad.astype(f32), axis=0, keepdims=True)
    colsum_ref[...] = total
    wait_all(copies)
    for j in range(D // 256):
        cols = slice(j * 256, (j + 1) * 256)
        branch_ref[:, cols] = dot(att_ref[...], proj[:, cols]) + proj_bias_ref[:, cols]
    for slot in range(SLOTS):
        rows = slot_rows(slot)
        mid = res_ref[rows, :] + mod_part(mod_ref, slot, 2) * branch_ref[rows, :]
        mid_ref[rows, :] = mid
        normed, _ = norm_parts(mid)
        min_ref[rows, :] = (
            normed * (1.0 + mod_part(mod_ref, slot, 4)) + mod_part(mod_ref, slot, 3)
        ).astype(bf16)

    @pl.loop(0, F // 256)
    def _(j):
        cols = pl.ds(pl.multiple_of(j * 256, 256), 256)
        u = dot(min_ref[...], weight[:, cols]) + bias_ref[:, cols]
        square = u * u
        bend = jnp.tanh(GELU_COEF * (u + 0.044715 * square * u))
        left = 0.5 * (1.0 + bend)
        act[:, cols] = (u * left).astype(bf16)
        slope[:, cols] = (
            left
            + 0.5 * u * (1.0 - bend * bend) * (GELU_COEF * (1.0 + 3.0 * 0.044715 * square))
        ).astype(bf16)

    out = fetch([(act, act_out), (slope, slope_out)], out_sems)
    out += fetch([(mid_ref, mid_out)], out_sems, 8)
    flip(where_ref, act, ordered, True)
    step = 512
    for j in range(F // step):
        made[j * step : (j + 1) * step, :] = dot(
            ordered[j * step : (j + 1) * step, :], gmo_ref[...]
        ).astype(bf16)
        to, at = (send_out, j) if j < F // step // 2 else (keep_out, j - F // step // 2)
        out += fetch(
            [(made.at[pl.ds(j * step, step), :], to.at[pl.ds(at * step, step), :])],
            out_sems,
            2 + j,
        )
    wait_all(out)


def wgrad_kernel(count, where_ref, *rest):
    lhs, rhs = rest[:count], rest[count : 2 * count]
    send_out, keep_out, ordered, send, keep, sems, *late = rest[2 * count :]
    core = where_ref[1]
    if late:
        *bufs, in_sems = late
        ins = fetch([(lhs[0], bufs[0]), (rhs[0], bufs[1]), (lhs[1], bufs[2])], in_sems)
        wait_all(ins)
        lhs, rhs = (bufs[0], bufs[2]), (bufs[1], rhs[1])
    depth = ordered.shape[0]
    step = 384
    first = 0
    out = []
    for lhs_ref, rhs_ref in zip(lhs, rhs):
        flip(where_ref, lhs_ref, ordered, False)
        width = rhs_ref.shape[1] // 2
        for buf, to, half in ((send, send_out, 1 - core), (keep, keep_out, core)):
            cols = pl.ds(pl.multiple_of(half * width, 128), width)
            for j in range(depth // step):
                rows = slice(j * step, (j + 1) * step)
                buf[rows, first : first + width] = dot(
                    ordered[rows, :], rhs_ref[:, cols]
                ).astype(bf16)
                here = (pl.ds(j * step, step), pl.ds(first, width))
                out += fetch([(buf.at[here], to.at[here])], sems, len(out))
        first += width
    wait_all(out)


def turns_kernel(keep_in, got_in, x_ref, y_ref, both_ref, keep, got, sems):
    rows = x_ref.shape[0]
    copies = []
    for i in range(3):
        here, there = pl.ds(i * rows, rows), pl.ds((i + 1) * rows, rows)
        copies += fetch(
            [(keep_in.at[there, :], keep.at[here, :]), (got_in.at[there, :], got.at[here, :])],
            sems,
            2 * i,
        )
    for i, ref in enumerate((x_ref, y_ref, both_ref)):
        wait_all(copies[2 * i : 2 * i + 2])
        here = slice(i * rows, (i + 1) * rows)
        ref[...] = (keep[here, :].astype(f32) + got[here, :].astype(f32)).astype(bf16)


def near_kernel(direct, keep_in, got_in, x_in, y_in, both_in, *rest):
    outs, (parts, sems) = rest[:-2], rest[-2:]
    tall = x_in.shape[0]
    wait_all(
        fetch(
            [
                (ref.at[pl.ds(0, tall), :], parts.at[i])
                for i, ref in enumerate((keep_in, got_in, x_in, y_in, both_in))
            ],
            sems,
        )
    )
    rows = tall // 4
    for z in range(4):
        here = slice(z * rows, (z + 1) * rows)
        total = parts[0, here, :].astype(f32)
        for i in range(1, 5):
            total += parts[i, here, :].astype(f32)
        if direct:
            outs[z][...] = total.astype(outs[z].dtype)
        elif z % 2:
            outs[0][z // 2 * rows : (z // 2 + 1) * rows, :] = total.astype(bf16)
        else:
            outs[1 + z // 2][...] = total


def beyond_kernel(own_ref, beyond_ref, got_ref, send_ref, total_ref):
    rows = own_ref.shape[0]
    send_ref[...] = (beyond_ref[...] + got_ref[rows:, :].astype(f32)).astype(bf16)
    total_ref[...] = own_ref[...] + got_ref[0:rows, :].astype(f32)


def fc2_copies(where_ref, near_ref, far_ref, fc2, sems):
    rows = F // (2 * BLOCKS)
    return weight_copies(where_ref, ([near_ref], [far_ref]), rows, [(fc2, 0, D)], sems, True)


def fc2_back_kernel(
    where_ref, gmo_ref, slope_in, near_ref, far_ref, gh_ref, colsum_ref, fc2, slope, sems, in_sems
):
    step = 512
    copies = fc2_copies(where_ref, near_ref, far_ref, fc2, sems)
    parts = [pl.ds(j * step, step) for j in range(F // step)]
    late = fetch([(slope_in.at[:, part], slope.at[:, part]) for part in parts], in_sems)
    wait_all(copies)
    for j in range(F // step):
        wait_all([late[j]])
        for half in range(2):
            cols = slice(j * step + half * 256, j * step + (half + 1) * 256)
            grad = dot_nt(gmo_ref[...], fc2[cols, :])
            value = (slope[:, cols].astype(f32) * grad).astype(bf16)
            gh_ref[:, cols] = value
            colsum_ref[:, cols] = jnp.sum(value.astype(f32), axis=0, keepdims=True)


def fc2_out_kernel(
    where_ref, place_ref, mod_ref, gc_ref, bias_ref, mid_in, act_in, near_ref, far_ref,
    tail_ref, gate_ref, out_out, mid_ref, act, fc2, mlp, made, sems, in_sems,
):
    last = fetch([(act_in, act), (mid_in, mid_ref)], in_sems)
    wait_all(fc2_copies(where_ref, near_ref, far_ref, fc2, sems))
    wait_all(last)
    for j in range(D // 256):
        cols = slice(j * 256, (j + 1) * 256)
        mlp[0:TOK_DEV, cols] = dot(act[...], fc2[:, cols]) + bias_ref[:, cols]
    for slot in range(SLOTS):
        rows = slot_rows(slot)
        value = mlp[rows, :]
        gate_ref[slot : slot + 1, :] = jnp.sum(
            value * gc_ref[rows, :].astype(f32), axis=0, keepdims=True
        )
        value = mid_ref[rows, :] + mod_part(mod_ref, slot, 5) * value
        mlp[rows, :] = value
        made[rows, :] = value.astype(bf16)
    out = fetch([(made, out_out)], in_sems, 2)
    mlp[TOK_DEV:, :] = jnp.zeros((LEN + 8, D), f32)
    tail_ref[...] = rows_from(mlp, place_ref[3]).astype(bf16)
    wait_all(out)


def keep_sum(sums, part, slot, values):
    at = part * SLOTS + slot
    sums[at : at + 1, :] = jnp.sum(values, axis=0, keepdims=True)


def spread_sums(sums, spread_ref):
    sums[3 * SLOTS :, :] = jnp.zeros((SLOTS, D), f32)
    value = sums[...].astype(bf16)
    for d in range(spread_ref.shape[0]):
        spread_ref[d] = value


def mid_back_kernel(
    where_ref, gh_ref, mid_ref, branch_ref, mod_ref, gc_ref, mine, more, theirs, rest_far,
    ga_ref, proj_sum_ref, gm_out, gb_out, spread_out,
    gm_ref, gb_ref, spread_ref, proj, weight, grads, sums, sems, out_sems,
):
    copies = weight_copies(
        where_ref,
        ([mine, more], [theirs, rest_far]),
        D // BLOCKS,
        [(proj, 0, D // 2), (weight, D // 2, F // 2)],
        sems,
    )
    wait_all(copies)
    for j in range(D // 256):
        cols = slice(j * 256, (j + 1) * 256)
        grads[:, cols] = dot_nt(gh_ref[...], weight[cols, :])
    total = jnp.zeros((1, D), f32)
    for slot in range(SLOTS):
        rows = slot_rows(slot)
        normed, inverse = norm_parts(mid_ref[rows, :])
        e = grads[rows, :]
        keep_sum(sums, 1, slot, e)
        keep_sum(sums, 2, slot, e * normed)
        grad_mid = gc_ref[rows, :].astype(f32) + norm_back(
            normed, inverse, mod_part(mod_ref, slot, 4), e
        )
        gm_ref[rows, :] = grad_mid
        keep_sum(sums, 0, slot, branch_ref[rows, :] * grad_mid)
        value = (mod_part(mod_ref, slot, 2) * grad_mid).astype(bf16)
        gb_ref[rows, :] = value
        total += jnp.sum(value.astype(f32), axis=0, keepdims=True)
    proj_sum_ref[...] = total
    spread_sums(sums, spread_ref)
    out = fetch([(gm_ref, gm_out), (gb_ref, gb_out), (spread_ref, spread_out)], out_sems)
    for j in range(D // 256):
        cols = slice(j * 256, (j + 1) * 256)
        ga_ref[:, cols] = dot_nt(gb_ref[...], proj[cols, :]).astype(bf16)
    wait_all(out)


def attend_back_kernel(qkv_in, ga_ref, gqkv_ref, colsum_ref, qkv, sems):
    masks = head_masks()
    scale = 1.0 / math.sqrt(HD)
    copies = fetch(
        [
            (qkv_in.at[pl.ds(slot * LEN, LEN), :], qkv.at[pl.ds(slot * LEN, LEN), :])
            for slot in range(SLOTS)
        ],
        sems,
    )
    for first in range(0, SLOTS, 2):
        wait_all(copies[first : first + 2])

        @pl.loop(first, first + 2)
        def _(slot):
            rows = pl.ds(pl.multiple_of(slot * LEN, LEN), LEN)
            for pair in range(HEADS // 2):
                at = pair * 2 * HD
                q_cols, k_cols, v_cols = (
                    slice(part * D + at, part * D + at + 2 * HD) for part in range(3)
                )
                queries = both_heads(qkv[rows, q_cols], masks)
                keys = qkv[rows, k_cols]
                probs = pair_probs(queries, keys)
                grads = both_heads(ga_ref[rows, q_cols], masks)
                grad_probs = dot_nt(grads, qkv[rows, v_cols])
                weighed = probs * grad_probs
                inner = jnp.sum(weighed, axis=1, keepdims=True)
                grad_scores = (weighed - probs * inner).astype(bf16)
                gqkv_ref[rows, q_cols] = (
                    dot(side_by_side(grad_scores), both_heads(keys, masks)) * scale
                ).astype(bf16)
                gqkv_ref[rows, k_cols] = (dot_tn(grad_scores, queries) * scale).astype(bf16)
                gqkv_ref[rows, v_cols] = dot_tn(probs.astype(bf16), grads).astype(bf16)

    for j in range(3 * D // 256):
        cols = slice(j * 256, (j + 1) * 256)
        colsum_ref[:, cols] = jnp.sum(gqkv_ref[:, cols].astype(f32), axis=0, keepdims=True)


def start_back_kernel(
    where_ref, place_ref, gqkv_ref, mod_ref, gate_ref, out_tail_ref, res_in, gm_in, near_ref, far_ref,
    tg_ref, tail_ref, spread_ref, weight, grads, res, gm, sums, sems, in_sems,
):
    copies = weight_copies(
        where_ref, ([near_ref], [far_ref]), D // BLOCKS, [(weight, 0, 3 * D // 2)], sems
    )
    late = fetch([(res_in, res), (gm_in, gm)], in_sems)
    wait_all(copies)
    for j in range(D // 256):
        cols = slice(j * 256, (j + 1) * 256)
        grads[0:TOK_DEV, cols] = dot_nt(gqkv_ref[...], weight[cols, :])
    wait_all(late)
    for slot in range(SLOTS):
        rows = slot_rows(slot)
        normed, inverse = norm_parts(res[rows, :])
        e = grads[rows, :]
        keep_sum(sums, 0, slot, e)
        keep_sum(sums, 1, slot, e * normed)
        value = gm[rows, :] + norm_back(normed, inverse, mod_part(mod_ref, slot, 1), e)
        tg_ref[rows, :] = value
        grads[rows, :] = value
    sums[2 * SLOTS : 3 * SLOTS, :] = gate_ref[...]
    spread_sums(sums, spread_ref)
    grads[TOK_DEV:, :] = jnp.zeros((LEN + 8, D), f32)
    tail = rows_from(grads, place_ref[3])
    high = tail.astype(bf16)
    tail_ref[0:LEN, :] = out_tail_ref[...]
    tail_ref[LEN : 2 * LEN, :] = high
    tail_ref[2 * LEN :, :] = (tail - high.astype(f32)).astype(bf16)


def place_kernel(
    place_ref, tail_ref, tok_in, cot_in, out_in, tg_in,
    final_out, final_tg, out_rows, tg_rows, tok, cot, out, made_out, made_tg, sems,
):
    lead, count = place_ref[0], place_ref[1]
    copies = fetch(
        [(out_in, out), (tok_in, tok), (tg_in, tg_rows.at[pl.ds(LEN, TOK_DEV), :]), (cot_in, cot)],
        sems,
    )
    for rows in (out_rows, tg_rows):
        rows[0:LEN, :] = jnp.zeros((LEN, D), f32)
        rows[LEN + TOK_DEV :, :] = jnp.zeros((8, D), f32)
    wait_all(copies[:2])
    out_rows[LEN : LEN + TOK_DEV, :] = out[...].astype(f32)
    last = []
    out_tail = tail_ref[0:LEN, :].astype(f32)
    tg_tail = tail_ref[LEN : 2 * LEN, :].astype(f32) + tail_ref[2 * LEN :, :].astype(f32)
    for k, (rows, tail, pad, made, final) in enumerate(
        ((out_rows, out_tail, tok, made_out, final_out), (tg_rows, tg_tail, cot, made_tg, final_tg))
    ):
        if k:
            wait_all(copies[2:])
        for slot in range(SLOTS):
            here = slot_rows(slot)
            row = lax.broadcasted_iota(jnp.int32, (LEN, 1), 0) + slot * LEN
            value = rows_from(rows, LEN - lead + slot * LEN)
            if slot == 0:
                value = jnp.where(row < lead, tail, value)
            value = jnp.where(row < count, value, pad[here, :].astype(f32))
            made[here, :] = value.astype(made.dtype)
        last += fetch([(made, final)], sems, 4 + k)
    wait_all(last)


def shape(*dims, dtype=f32):
    return jax.ShapeDtypeStruct(dims, dtype)


def call(kernel, outs, scratch, mib, ins, spaces, after=(), out_specs=None, us=0):
    taken, held, made = len(ins), len(after), len(outs)
    out_specs = out_specs or [VM] * made

    def body(*refs):
        first = taken + held
        kernel(*refs[:taken], *refs[first : first + made], *refs[first + made + 1 :])
        refs[first + made][...] = jnp.zeros((8, 128), f32)

    def placed(item, spec):
        return pltpu.with_memory_space_constraint(item, pltpu.HBM) if spec is HBM else item

    out_shape = [
        pltpu.HBM(item.shape, item.dtype) if spec is HBM else item
        for item, spec in zip(outs, out_specs)
    ]
    *results, token = pl.pallas_call(
        body,
        out_shape=[*out_shape, shape(8, 128)],
        in_specs=list(spaces) + [ANY] * held,
        out_specs=[*out_specs, VM],
        scratch_shapes=scratch,
        compiler_params=params(mib),
        cost_estimate=cost(us),
        name=getattr(kernel, "func", kernel).__name__,
    )(*[placed(item, spec) for item, spec in zip(ins, spaces)], *after)
    return results, token


def join(parts, after=(), us=0):
    rows = sum(part.shape[0] for part in parts)
    (both,), token = call(
        join_kernel,
        [shape(rows, parts[0].shape[1], dtype=parts[0].dtype)],
        [pltpu.SemaphoreType.DMA((len(parts),))],
        8,
        parts,
        [ANY] * len(parts),
        after=after,
        out_specs=[ANY],
        us=us,
    )
    return both, token


def tie(value, token):
    return jnp.where(token[0, 0] == 0.0, value, jnp.zeros_like(value))


def low(value):
    return value.astype(bf16)


class Links:
    def __init__(self, devices):
        self.devices = devices
        self.cube = devices == 32
        self.me = lax.axis_index("wide").astype(jnp.int32)
        self.core = self.me % 2 if self.cube else jnp.int32(0)
        self.chip = self.me // 2 if self.cube else jnp.int32(0)
        self.where = jnp.stack([self.chip, self.core, self.me])

    def swap(self, array, bits):
        return lax.ppermute(array, "wide", [(i, i ^ bits) for i in range(self.devices)])

    def by_core(self, first, second):
        return jnp.where(self.core == 0, first, second)

    def pair(self, mine, got):
        return self.by_core(
            jnp.concatenate([mine, got], axis=0), jnp.concatenate([got, mine], axis=0)
        )

    def along_z(self, pair):
        return jnp.concatenate(
            [pair, self.swap(pair, 8), self.swap(pair, 16), self.swap(pair, 24)], axis=0
        )

    def doubled_z(self, pair):
        two = jnp.concatenate([pair, self.swap(pair, 8)], axis=0)
        return jnp.concatenate([two, self.swap(two, 16)], axis=0)

    def gathered(self, shards):
        halves = [[], []]
        for shard in shards:
            whole = lax.all_gather(shard, "wide", axis=0, tiled=True)
            rows, width = whole.shape[0], whole.shape[1] // 2
            whole = whole.reshape(4, 4, rows // BLOCKS, -1).transpose(1, 0, 2, 3)
            whole = whole.reshape(rows, -1)
            halves[0].append(whole[:, :width])
            halves[1].append(whole[:, width:])
        return [jnp.concatenate(half, axis=1) for half in halves]

    def scattered(self, send, keep, widths):
        outs, first = [], 0
        rows = keep.shape[0]
        for width in widths:
            cols = slice(first, first + width)
            whole = jnp.concatenate([keep[:, cols], send[:, cols]], axis=1)
            whole = whole.reshape(4, 4, rows // BLOCKS, -1).transpose(1, 0, 2, 3)
            whole = whole.reshape(rows, -1).astype(f32)
            outs.append(lax.psum_scatter(whole, "wide", scatter_dimension=0, tiled=True))
            first += width
        return outs

    def scattered_rows(self, send, keep):
        whole = jnp.stack([keep, send]).reshape(2, 4, 4, -1, D)
        whole = whole.transpose(2, 1, 0, 3, 4).reshape(-1, D)
        return lax.psum_scatter(whole.astype(f32), "wide", scatter_dimension=0, tiled=True)

    def gathered_rows(self, shard):
        whole = lax.all_gather(shard, "wide", axis=0, tiled=True).reshape(4, 4, 2, -1, D)
        return [whole[:, :, half].transpose(1, 0, 2, 3).reshape(-1, D) for half in range(2)]

    def turns(self, keep, got, after):
        rows, width = keep.shape[0] // 4, keep.shape[1]
        parts, token = call(
            turns_kernel,
            [shape(rows, width, dtype=bf16)] * 3,
            [pltpu.VMEM((3 * rows, width), bf16)] * 2 + [pltpu.SemaphoreType.DMA((6,))],
            16,
            [keep, got],
            [HBM, ANY],
            after=after,
        )
        return [self.swap(part, bits) for part, bits in zip(parts, (2, 4, 6))], token

    def near_sum(self, keep, got, parts, direct, after):
        tall, width = keep.shape[0] // 4, keep.shape[1]
        rows = tall // 4
        if direct:
            outs = [shape(rows, width)] + [shape(rows, width, dtype=bf16)] * 3
        else:
            outs = [shape(2 * rows, width, dtype=bf16)] + [shape(rows, width)] * 2
        return call(
            functools.partial(near_kernel, direct),
            outs,
            [pltpu.VMEM((5, tall, width), bf16), pltpu.SemaphoreType.DMA((5,))],
            16,
            [keep, got, *parts],
            [HBM] + [ANY] * 4,
            after=after,
            us=100,
        )

    def z_sum(self, token, own, *parts):
        own = tie(own, token)
        for part, bits in zip(parts, (8, 16, 24)):
            own = own + self.swap(part, bits).astype(f32)
        return own

    def halved_z(self, send, own, beyond, after):
        (send, total), token = call(
            beyond_kernel,
            [shape(*own.shape, dtype=bf16), shape(*own.shape)],
            [],
            8,
            [own, beyond, self.swap(send, 8)],
            [VM] * 3,
            after=after,
        )
        return total, self.swap(send, 16), token

    def own_rows(self, own, widths):
        rows = own.shape[0] // 2
        mine = self.by_core(own[:rows], own[rows:])
        got = self.swap(self.by_core(own[rows:], own[:rows]), 1)
        outs, first = [], 0
        for width in widths:
            a, b = mine[:, first : first + width], got[:, first : first + width]
            outs.append(
                self.by_core(jnp.concatenate([a, b], axis=1), jnp.concatenate([b, a], axis=1))
            )
            first += width
        return outs


def on_device(
    tokens,
    cotangent,
    cond,
    kept,
    counts,
    ada_w,
    ada_bias,
    qkv_w,
    q_bias,
    v_bias,
    proj_w,
    proj_bias,
    fc1_w,
    fc1_bias,
    fc2_w,
    fc2_bias,
):
    devices = lax.axis_size("wide")
    images = cond.shape[0]
    span = ada_bias.shape[0]
    own_dim = ada_w.shape[0]
    links = Links(devices)
    me, where, cube = links.me, links.where, links.cube
    rows = TOK_DEV
    dma = pltpu.SemaphoreType.DMA
    half_sum = (qkv_w.shape[1] + proj_w.shape[1] + fc1_w.shape[1]) // 2

    (mine, send, edge, place, starts, cond_slots, ada_parts), _ = call(
        begin_kernel,
        [
            shape(own_dim, half_sum, dtype=bf16),
            shape(own_dim, half_sum, dtype=bf16),
            shape(2 * LEN, D, dtype=bf16),
            shape(8, dtype=jnp.int32),
            shape(devices, dtype=jnp.int32),
            shape(devices * 8, D, dtype=bf16),
            shape(devices, own_dim, span, dtype=bf16),
        ],
        [
            pltpu.VMEM((devices * 8, images), f32),
            pltpu.VMEM(cond.shape, bf16),
            pltpu.VMEM(ada_w.shape, bf16),
            dma((10,)),
        ],
        16,
        [where, counts, cond, ada_w, tokens, cotangent, qkv_w, proj_w, fc1_w],
        [SM, SM] + [HBM] * 7,
        out_specs=[VM, VM, VM, SM, SM, VM, VM],
    )
    if cube:
        pair = links.pair(mine, links.swap(send, 1))
        near_one = links.along_z(pair[:, : 3 * D // 2])
        before_mod = [pair]
    else:
        before_mod = []
    halo = lax.ppermute(edge, "wide", [(i + 1, i) for i in range(devices - 1)])

    ada_cols = lax.all_to_all(ada_parts, "wide", 0, 0, tiled=True)
    ada_cols = ada_cols.reshape(D, span)
    lanes = lambda items: jnp.pad(
        jnp.concatenate(items), (0, span - sum(i.shape[0] for i in items))
    ).reshape(1, span)
    addend = jnp.concatenate(
        [
            jnp.broadcast_to(ada_bias.reshape(1, span), (SLOTS, span)),
            lanes([q_bias, v_bias, proj_bias, fc2_bias]),
            lanes([fc1_bias]),
            jnp.zeros((2, span), bf16),
        ],
        axis=0,
    ).astype(f32)
    (mod_cols,), mod_ran = call(
        mod_kernel,
        [shape(devices, 8, span)],
        [],
        16,
        [cond_slots, ada_cols, addend],
        [VM] * 3,
        after=before_mod,
    )
    mixed = lax.all_to_all(mod_cols, "wide", 0, 0, tiled=True)

    quarter = D // 4
    frequency = jnp.exp(-math.log(10000.0) * jnp.arange(quarter).astype(f32) / quarter)
    angle = jnp.arange(GRID).astype(f32)[:, None] * frequency[None, :]
    table = jnp.concatenate([jnp.sin(angle), jnp.cos(angle)], axis=1)
    if cube:
        near_one = tie(near_one, mod_ran)
        over = [links.swap(near_one, bits) for bits in (2, 4, 6)]
        pair_two = tie(pair[:, 3 * D // 2 :], mod_ran)
        two = jnp.concatenate([pair_two, links.swap(pair_two, 8)], axis=0)
        before_prep = [near_one, two]
    else:
        before_prep = []
    (residual, grad_out, mod, qkv_bias, proj_bias_all, fc2_bias_all, fc1_bias_all), prepared = call(
        prep_kernel,
        [
            shape(rows, D),
            shape(rows, D, dtype=bf16),
            shape(SLOTS, 6 * D),
            shape(1, 3 * D),
            shape(1, D),
            shape(1, D),
            shape(1, F),
        ],
        [
            pltpu.VMEM((rows, D), bf16),
            pltpu.VMEM((rows, D), bf16),
            pltpu.VMEM((2 * LEN, D), bf16),
            pltpu.VMEM(kept.shape, jnp.int32),
            pltpu.VMEM(table.shape, f32),
            dma((5,)),
        ],
        16,
        [place, mixed, tokens, cotangent, halo, kept, table],
        [SM, VM, HBM, HBM, ANY, HBM, ANY],
        after=before_prep,
        us=10,
    )

    if cube:
        near_two = jnp.concatenate([two, links.swap(two, 16)], axis=0)
        qkv_near, joined = join([near_one, *over], [prepared, near_two])
        qkv_far = links.swap(qkv_near, 1)
        over_x, over_y = links.swap(near_two, 2), links.swap(near_two, 4)
        before_qkv = []
    else:
        qkv_near, qkv_far = links.gathered([qkv_w])
        before_qkv = []

    (attn_in, qkv), qkv_ran = call(
        qkv_kernel,
        [shape(rows, D, dtype=bf16), shape(rows, 3 * D, dtype=bf16)],
        [pltpu.VMEM((rows, D), bf16), pltpu.VMEM((D, 3 * D), bf16), dma((32,)), dma((1,))],
        16,
        [where, residual, mod, qkv_bias, qkv_near, qkv_far],
        [SM] + [VM] * 3 + [ANY] * 2,
        after=before_qkv,
        out_specs=[HBM, VM],
    )
    before_attend = [qkv_ran]
    if cube:
        two = tie(jnp.concatenate([fc2_w, links.swap(fc2_w, 8)], axis=0), qkv_ran)
        before_attend.append(two)
        near_three = jnp.concatenate([two, links.swap(two, 16)], axis=0)
    (attended, attended_kept), attend_ran = call(
        attend_kernel,
        [shape(rows, D, dtype=bf16)] * 2,
        [dma((1,))],
        16,
        [qkv],
        [VM],
        after=before_attend,
        out_specs=[VM, HBM],
    )
    if cube:
        half = near_two.shape[0] // 2
        most, _ = join([near_two, over_x, over_y], [attend_ran, near_three])
        most_far = links.swap(most, 1)
        diag_low = links.swap(tie(over_y[:half], attend_ran), 2)
        diag_high = links.swap(tie(over_x[half:], attend_ran), 4)
        diag, joined = join([diag_low, diag_high])
        mid_halves = [most, diag, most_far, links.swap(diag, 1)]
        near_three = tie(near_three, joined)
        over = [links.swap(near_three, bits) for bits in (2, 4, 6)]
    else:
        mid_near, mid_far = links.gathered([proj_w, fc1_w])
        cut = 3 * D // 4
        mid_halves = [mid_near[:cut], mid_near[cut:], mid_far[:cut], mid_far[cut:]]
        fc2_near, fc2_far = links.gathered_rows(fc2_w)

    (
        branch, middle, mlp_in, grad_mlp_out, fc2_bias_sum, activated, slope, fc2_send, fc2_keep,
        middle_kept,
    ), hidden_ran = call(
        hidden_kernel,
        [
            shape(rows, D),
            shape(rows, D),
            shape(rows, D, dtype=bf16),
            shape(rows, D, dtype=bf16),
            shape(1, D),
            shape(rows, F, dtype=bf16),
            shape(rows, F, dtype=bf16),
            shape(F // 2, D, dtype=bf16),
            shape(F // 2, D, dtype=bf16),
            shape(rows, D),
        ],
        [
            pltpu.VMEM((D, D), bf16),
            pltpu.VMEM((D, F), bf16),
            pltpu.VMEM((rows, F), bf16),
            pltpu.VMEM((rows, F), bf16),
            pltpu.VMEM((F, rows), bf16),
            pltpu.VMEM((F, D), bf16),
            dma((64,)),
            dma((9,)),
        ],
        32,
        [where, residual, attended, mod, grad_out, proj_bias_all, fc1_bias_all, *mid_halves],
        [SM] + [VM] * 6 + [ANY] * 4,
        out_specs=[VM] * 5 + [HBM] * 5,
    )
    def weight_grad(*pairs, after=()):
        half = sum(right.shape[1] for _, right in pairs) // 2
        scratch = [
            pltpu.VMEM((D, rows), bf16),
            pltpu.VMEM((D, half), bf16),
            pltpu.VMEM((D, half), bf16),
            dma((8,)),
        ]
        spaces = [VM, VM]
        if len(pairs) == 2:
            scratch += [pltpu.VMEM((rows, D), bf16)] * 3 + [dma((3,))]
            spaces = [HBM, HBM, HBM, VM]
        return call(
            functools.partial(wgrad_kernel, len(pairs)),
            [shape(D, half, dtype=bf16)] * 2,
            scratch,
            20,
            [where, *[left for left, _ in pairs], *[right for _, right in pairs]],
            [SM, *spaces],
            after=after,
            out_specs=[HBM] * 2,
        )

    if cube:
        fc2_got = links.swap(fc2_send, 1)
        fc2_near, gathered = join([near_three, *over], [hidden_ran], us=100)
        fc2_far = links.swap(fc2_near, 1)
        fc2_parts, fc2_turned = links.turns(fc2_keep, fc2_got, [gathered])
        before_fc2 = [fc2_turned]
    else:
        before_fc2 = []
    (grad_hidden, fc1_bias_sum), _ = call(
        fc2_back_kernel,
        [shape(rows, F, dtype=bf16), shape(1, F)],
        [pltpu.VMEM((F, D), bf16), pltpu.VMEM((rows, F), bf16), dma((32,)), dma((6,))],
        20,
        [where, grad_mlp_out, slope, fc2_near, fc2_far],
        [SM, VM, HBM, ANY, ANY],
        after=before_fc2,
    )
    (fc1_send, fc1_keep), fc1_ran = weight_grad((mlp_in, grad_hidden))
    if cube:
        fc1_got = links.swap(fc1_send, 1)
    (grad_attended, proj_bias_sum, grad_middle, grad_branch, early), mid_ran = call(
        mid_back_kernel,
        [
            shape(rows, D, dtype=bf16),
            shape(1, D),
            shape(rows, D),
            shape(rows, D, dtype=bf16),
            shape(devices, 16, D, dtype=bf16),
        ],
        [
            pltpu.VMEM((rows, D), f32),
            pltpu.VMEM((rows, D), bf16),
            pltpu.VMEM((devices, 16, D), bf16),
            pltpu.VMEM((D, D), bf16),
            pltpu.VMEM((D, F), bf16),
            pltpu.VMEM((rows, D), f32),
            pltpu.VMEM((16, D), f32),
            dma((64,)),
            dma((3,)),
        ],
        20,
        [where, grad_hidden, middle, branch, mod, grad_out, *mid_halves],
        [SM] + [VM] * 5 + [ANY] * 4,
        out_specs=[VM] * 2 + [HBM] * 3,
        after=[fc1_ran],
    )
    early = lax.all_to_all(early, "wide", 0, 0, tiled=True)
    if cube:
        fc2_near_sum, fc2_summed = links.near_sum(fc2_keep, fc2_got, fc2_parts, False, [mid_ran])
        fc1_parts, fc1_turned = links.turns(fc1_keep, fc1_got, [fc2_summed])
        before_back = [fc1_turned]
    else:
        before_back = []
    (grad_qkv, qkv_bias_sum), _ = call(
        attend_back_kernel,
        [shape(rows, 3 * D, dtype=bf16), shape(1, 3 * D)],
        [pltpu.VMEM((rows, 3 * D), bf16), dma((SLOTS,))],
        16,
        [qkv, grad_attended],
        [HBM, VM],
        after=before_back,
    )
    (qkv_send, qkv_keep), qkv_grad_ran = weight_grad(
        (attended_kept, grad_branch), (attn_in, grad_qkv), after=[early]
    )
    if cube:
        qkv_got = links.swap(qkv_send, 1)
        fc2_own, fc2_beyond, fc2_halved = links.halved_z(*fc2_near_sum, [qkv_grad_ran])
        fc1_near_sum, fc1_summed = links.near_sum(
            fc1_keep, fc1_got, fc1_parts, False, [qkv_grad_ran, fc2_halved]
        )
        qkv_parts, qkv_turned = links.turns(qkv_keep, qkv_got, [fc1_summed])
        before_out = [qkv_turned]
    else:
        before_out = [qkv_grad_ran]
    (out_tail, gate_two_sum, result), out_ran = call(
        fc2_out_kernel,
        [shape(LEN, D, dtype=bf16), shape(SLOTS, D), shape(rows, D, dtype=bf16)],
        [
            pltpu.VMEM((rows, D), f32),
            pltpu.VMEM((rows, F), bf16),
            pltpu.VMEM((F, D), bf16),
            pltpu.VMEM((rows + LEN + 8, D), f32),
            pltpu.VMEM((rows, D), bf16),
            dma((32,)),
            dma((3,)),
        ],
        20,
        [where, place, mod, grad_out, fc2_bias_all, middle_kept, activated, fc2_near, fc2_far],
        [SM] * 2 + [VM] * 3 + [HBM] * 2 + [ANY] * 2,
        after=before_out,
        out_specs=[VM] * 2 + [HBM],
    )
    if cube:
        fc1_own, fc1_beyond, fc1_halved = links.halved_z(*fc1_near_sum, [out_ran])
        fc2_grad = fc2_own + fc2_beyond.astype(f32)
        before_start = [fc1_halved, fc2_grad]
    else:
        before_start = [out_ran]
    (tokens_back, tail, late), start_ran = call(
        start_back_kernel,
        [shape(rows, D), shape(3 * LEN, D, dtype=bf16), shape(devices, 16, D, dtype=bf16)],
        [
            pltpu.VMEM((D, 3 * D), bf16),
            pltpu.VMEM((rows + LEN + 8, D), f32),
            pltpu.VMEM((rows, D), f32),
            pltpu.VMEM((rows, D), f32),
            pltpu.VMEM((16, D), f32),
            dma((32,)),
            dma((2,)),
        ],
        20,
        [where, place, grad_qkv, mod, gate_two_sum, out_tail, residual, grad_middle, qkv_near, qkv_far],
        [SM] * 2 + [VM] * 4 + [HBM] * 2 + [ANY] * 2,
        after=before_start,
    )
    late = lax.all_to_all(late, "wide", 0, 0, tiled=True)

    if cube:
        qkv_near_sum, qkv_summed = links.near_sum(
            qkv_keep, qkv_got, qkv_parts, True, [start_ran]
        )
        before_ada = [qkv_summed]
    else:
        before_ada = [start_ran]

    onward = [(i, i + 1) for i in range(devices - 1)]
    tail = lax.ppermute(tail, "wide", onward)
    wide_images = -(-images // 128) * 128
    (ada_grad, ada_bias_sum, last), ada_ran = call(
        ada_kernel,
        [
            shape(own_dim, 6 * D),
            shape(1, 6 * D),
            shape(devices, own_dim + 8, wide_images, dtype=bf16),
        ],
        [pltpu.VMEM((devices * 16, images), f32), pltpu.VMEM((own_dim + 8, wide_images), f32)],
        24,
        [where, starts, early, late, ada_w, cond, qkv_bias_sum, proj_bias_sum, fc2_bias_sum, fc1_bias_sum],
        [SM] * 2 + [VM] * 8,
        after=before_ada,
    )
    last = lax.all_to_all(last, "wide", 0, 0, tiled=True)
    (out, tokens_grad), placed = call(
        place_kernel,
        [shape(rows, D, dtype=bf16), shape(rows, D)],
        [
            pltpu.VMEM((rows + LEN + 8, D), f32),
            pltpu.VMEM((rows + LEN + 8, D), f32),
            pltpu.VMEM((rows, D), bf16),
            pltpu.VMEM((rows, D), bf16),
            pltpu.VMEM((rows, D), bf16),
            pltpu.VMEM((rows, D), bf16),
            pltpu.VMEM((rows, D), f32),
            dma((6,)),
        ],
        16,
        [place, tail, tokens, cotangent, result, tokens_back],
        [SM, VM] + [HBM] * 4,
        after=[ada_ran],
        out_specs=[HBM] * 2,
    )


    fc1_widths, qkv_widths = [F // 2], [D // 2, 3 * D // 2]
    if cube:
        (fc1_grad,) = links.own_rows(fc1_own + fc1_beyond.astype(f32), fc1_widths)
        proj_grad, qkv_grad = links.own_rows(links.z_sum(ada_ran, *qkv_near_sum), qkv_widths)
        before_finish = [placed]
    else:
        fc2_grad = links.scattered_rows(fc2_send, fc2_keep)
        (fc1_grad,) = links.scattered(fc1_send, fc1_keep, fc1_widths)
        proj_grad, qkv_grad = links.scattered(qkv_send, qkv_keep, qkv_widths)
        before_finish = []
    (cond_grad, bias_grads), _ = call(
        finish_kernel,
        [shape(images, D), shape(8, wide_images)],
        [pltpu.VMEM((D, wide_images), f32)],
        16,
        [last],
        [VM],
        after=before_finish,
    )
    bias_grads = bias_grads[:, :own_dim]
    ada_bias_grad = lax.dynamic_slice_in_dim(ada_bias_sum[0], me * span, span, 0)
    return (
        out,
        tokens_grad,
        cond_grad,
        ada_grad,
        ada_bias_grad,
        qkv_grad,
        bias_grads[0],
        bias_grads[1],
        proj_grad,
        bias_grads[2],
        fc1_grad,
        bias_grads[4:].reshape(-1),
        fc2_grad,
        bias_grads[3],
    )


def solution(mesh):
    row, flat = P("wide", None), P("wide")
    return jax.shard_map(
        on_device,
        mesh=mesh,
        in_specs=(row, row, P(), P(), P(), row, flat, row, flat, flat, row, flat, row, flat, row, flat),
        out_specs=(row, row, P(), row, flat, row, flat, flat, row, flat, row, flat, row, flat),
        check_vma=False,
    )
```

```python
import functools
import math

import jax
import jax.numpy as jnp
from jax import lax
from jax.experimental import pallas as pl
from jax.experimental.pallas import tpu as pltpu
from jax.sharding import PartitionSpec as P

D = 768
HEADS = 12
HD = 64
GRID = 16
LEN = 128
TOK_DEV = 512
SLOTS = TOK_DEV // LEN
F = 3072
BLOCKS = 16

NORM_EPS = 1e-06
GELU_COEF = 0.7978845608028654

f32 = jnp.float32
bf16 = jnp.bfloat16

VM = pl.BlockSpec(memory_space=pltpu.VMEM)
SM = pl.BlockSpec(memory_space=pltpu.SMEM)
ANY = pl.BlockSpec(memory_space=pl.ANY)
HBM = pl.BlockSpec(memory_space=pltpu.HBM)


def params(mib):
    return pltpu.CompilerParams(vmem_limit_bytes=mib * 1024 * 1024)


def cost(us):
    return pl.CostEstimate(flops=max(1, int(us * 1e9)), bytes_accessed=1, transcendentals=0)


def dot(left, right):
    return jnp.dot(left, right, preferred_element_type=f32)


def dot_nt(left, right):
    return lax.dot_general(left, right, (((1,), (1,)), ((), ())), preferred_element_type=f32)


def dot_tn(left, right):
    return lax.dot_general(left, right, (((0,), (0,)), ((), ())), preferred_element_type=f32)


def silu(values):
    return values / (1.0 + jnp.exp(-values))


def norm_parts(values):
    centred = values - jnp.mean(values, axis=-1, keepdims=True)
    spread = jnp.mean(centred * centred, axis=-1, keepdims=True)
    inverse = lax.rsqrt(spread + NORM_EPS)
    return centred * inverse, inverse


def norm_back(normed, inverse, scale_part, grad):
    t = grad * (1.0 + scale_part)
    mean_t = jnp.mean(t, axis=-1, keepdims=True)
    mean_tn = jnp.mean(t * normed, axis=-1, keepdims=True)
    return (t - mean_t - normed * mean_tn) * inverse


def rows_from(ref, start):
    base = pl.multiple_of(start // 8 * 8, 8)
    shift = start - base
    tall = LEN + 8
    turned = pltpu.roll(ref[pl.ds(base, tall), :], jnp.where(shift == 0, 0, tall - shift), 0)
    return turned[:LEN]


def slot_rows(slot):
    return slice(slot * LEN, (slot + 1) * LEN)


def mod_part(mod_ref, slot, part):
    return mod_ref[slot : slot + 1, part * D : (part + 1) * D]


def place_of(block, chip):
    rel = jnp.bitwise_xor(block, chip)
    return jnp.bitwise_and(rel, 3) * 4 + lax.shift_right_logical(rel, 2)


def lay_out(where_ref, halves, rows, targets, split_rows=False):
    chip, core = where_ref[0], where_ref[1]
    for side in range(2):
        half = core if side == 0 else 1 - core
        place = 0
        for ref in halves[side]:
            for spot in range(ref.shape[0] // rows):
                block = jnp.bitwise_xor(place % 4 * 4 + place // 4, chip)
                place += 1
                for target, first, width in targets:
                    if split_rows:
                        to_row, to_col = (2 * block + half) * rows, 0
                    else:
                        to_row, to_col = block * rows, pl.multiple_of(half * width, 128)
                    to_row = pl.multiple_of(to_row, 16)
                    target[pl.ds(to_row, rows), pl.ds(to_col, width)] = ref[
                        spot * rows : (spot + 1) * rows, first : first + width
                    ]


def start_all(copies):
    for copy in copies:
        copy.start()
    return copies


def fetch(pairs, sems, first=0):
    return start_all(
        [pltpu.make_async_copy(a, b, sems.at[first + i]) for i, (a, b) in enumerate(pairs)]
    )


def wait_all(copies):
    for copy in copies:
        copy.wait()


def begin_kernel(
    where_ref, counts_ref, cond_in, ada_in, tok_in, cot_in, qkv_in, proj_in, fc1_in,
    mine_ref, send_ref, edge_ref, place_ref, starts_ref, slots_ref, parts_ref,
    wide, cond, ada, sems,
):
    devices = counts_ref.shape[0]
    images = cond.shape[0]
    core, me = where_ref[1], where_ref[2]
    copies = []
    first = 0
    for ref in (qkv_in, proj_in, fc1_in):
        half = ref.shape[1] // 2
        for out, at in ((send_ref, 1 - core), (mine_ref, core)):
            copies.append(
                (
                    ref.at[:, pl.ds(pl.multiple_of(at * half, 128), half)],
                    out.at[:, pl.ds(first, half)],
                )
            )
        first += half
    copies.append((tok_in.at[pl.ds(0, LEN), :], edge_ref.at[pl.ds(0, LEN), :]))
    copies.append((cot_in.at[pl.ds(0, LEN), :], edge_ref.at[pl.ds(LEN, LEN), :]))
    copies = fetch([*copies, (cond_in, cond), (ada_in, ada)], sems)

    def step(d, first_row):
        count = counts_ref[d]
        begin = (first_row + LEN - 1) // LEN
        starts_ref[d] = begin

        @pl.when(d == me)
        def _():
            lead = begin * LEN - first_row
            place_ref[0] = lead
            place_ref[1] = count
            place_ref[2] = (first_row + count + LEN - 1) // LEN - begin
            place_ref[3] = count - lead
            place_ref[4] = begin

        return first_row + count

    lax.fori_loop(0, devices, step, jnp.int32(0))
    sub = lax.broadcasted_iota(jnp.int32, (8, images), 0)
    lane = lax.broadcasted_iota(jnp.int32, (8, images), 1)

    @pl.loop(0, devices)
    def _(d):
        hit = (lane == starts_ref[d] + sub) & (sub < SLOTS)
        wide[pl.ds(pl.multiple_of(d * 8, 8), 8), :] = jnp.where(hit, 1.0, 0.0)

    wait_all(copies)
    span = parts_ref.shape[2]
    for d in range(devices):
        parts_ref[d] = ada[:, d * span : (d + 1) * span]
    act = silu(cond[...].astype(f32)).astype(bf16)
    slots_ref[...] = dot(wide[...].astype(bf16), act).astype(bf16)


def ada_kernel(
    where_ref, starts_ref, early_ref, late_ref, ada_ref, cond_ref,
    qkv_sum_ref, proj_sum_ref, fc2_sum_ref, fc1_sum_ref,
    grad_ref, colsum_ref, last_ref, wide, packed,
):
    devices = early_ref.shape[0]
    images, own = cond_ref.shape[0], ada_ref.shape[0]
    me = where_ref[2]
    row = lax.broadcasted_iota(jnp.int32, (own, D), 0)
    lane = lax.broadcasted_iota(jnp.int32, (own, D), 1)
    chosen = jnp.where(lane == me * own + row, 1.0, 0.0).astype(bf16)
    act = silu(cond_ref[...].astype(f32)).astype(bf16)
    act_own = dot_nt(act, chosen).astype(bf16)
    cond_own = dot_nt(chosen, cond_ref[...])
    total = jnp.zeros((own, images), f32)
    for ref, parts in ((early_ref, (2, 3, 4, 5)), (late_ref, (0, 1))):
        many = len(parts)
        high = many * SLOTS
        tall = devices * high
        sub = lax.broadcasted_iota(jnp.int32, (high, images), 0)
        lane = lax.broadcasted_iota(jnp.int32, (high, images), 1)

        @pl.loop(0, devices)
        def _(d):
            hit = lane == starts_ref[d] + sub % SLOTS
            wide[pl.ds(pl.multiple_of(d * high, high), high), :] = jnp.where(hit, 1.0, 0.0)

        picker = wide[0:tall, :]
        act_rows = dot(picker.astype(bf16), act_own)
        part_down = lax.broadcasted_iota(jnp.int32, (tall, 1), 0) % high // SLOTS
        part_across = lax.broadcasted_iota(jnp.int32, (1, tall), 1) % high // SLOTS
        act_parts = jnp.concatenate(
            [jnp.where(part_down == i, act_rows, 0.0) for i in range(many)], axis=1
        ).astype(bf16)
        ours = lax.broadcasted_iota(jnp.int32, (8, tall), 0) == part_across
        ours = jnp.where(ours, 1.0, 0.0).astype(bf16)
        sums = ref[...].reshape(tall, D)
        grads = dot_tn(act_parts, sums)
        colsums = dot(ours, sums)
        back = jnp.zeros((own, tall), f32)
        for i, part in enumerate(parts):
            cols = slice(part * D, (part + 1) * D)
            grad_ref[:, cols] = grads[i * own : (i + 1) * own]
            colsum_ref[:, cols] = colsums[i : i + 1]
            back += jnp.where(part_across == i, dot_nt(ada_ref[:, cols], sums), 0.0)
        total += jnp.dot(back, picker, precision=lax.Precision.HIGHEST)
    gate = 1.0 / (1.0 + jnp.exp(-cond_own))
    total = total * (gate * (1.0 + cond_own * (1.0 - gate)))
    lanes = last_ref.shape[2]
    fc1_sum = fc1_sum_ref[...]
    both = qkv_sum_ref[...]
    vectors = [both[:, :D], both[:, 2 * D :], proj_sum_ref[...], fc2_sum_ref[...]]
    for d in range(devices):
        packed[...] = jnp.zeros(packed.shape, f32)
        packed[0:own, 0:images] = total
        for j in range(8):
            if j < 4:
                value = vectors[j][:, d * own : (d + 1) * own]
            else:
                at = (4 * d + j - 4) * own
                value = fc1_sum[:, at : at + own]
            packed[own + j : own + j + 1, 0:own] = value
        last_ref[d] = packed[...].astype(bf16)


def finish_kernel(got_ref, cond_ref, bias_ref, tall):
    devices, rows, _ = got_ref.shape
    own = rows - 8
    total = None
    for d in range(devices):
        got = got_ref[d].astype(f32)
        tall[d * own : (d + 1) * own, :] = got[0:own]
        total = got[own:rows] if total is None else total + got[own:rows]
    cond_ref[...] = tall[...].T[0 : cond_ref.shape[0], :]
    bias_ref[...] = total


def mod_kernel(slots_ref, cols_ref, addend_ref, out_ref):
    value = dot(slots_ref[...], cols_ref[...])
    for d in range(out_ref.shape[0]):
        out_ref[d] = value[d * 8 : (d + 1) * 8, :] + addend_ref[...]


def prep_kernel(
    place_ref, got_ref, tok_in, cot_in, halo_in, kept_in, table_in,
    res_ref, gc_ref, mod_ref, qkv_bias_ref, proj_bias_ref, fc2_bias_ref, fc1_bias_ref,
    tok, cot, halo, kept, table, sems,
):
    copies = fetch(
        [(table_in, table), (kept_in, kept), (halo_in, halo), (tok_in, tok), (cot_in, cot)], sems
    )
    devices, _, span = got_ref.shape
    width = D // devices
    qkv_bias_ref[:, D : 2 * D] = jnp.zeros((1, D), f32)
    for d in range(devices):
        got = got_ref[d]
        mod_ref[:, d * span : (d + 1) * span] = got[0:SLOTS]
        cols = slice(d * width, (d + 1) * width)
        qkv_bias_ref[:, cols] = got[4:5, 0:width]
        qkv_bias_ref[:, 2 * D + d * width : 2 * D + (d + 1) * width] = got[4:5, width : 2 * width]
        proj_bias_ref[:, cols] = got[4:5, 2 * width : 3 * width]
        fc2_bias_ref[:, cols] = got[4:5, 3 * width : 4 * width]
        fc1_bias_ref[:, d * 4 * width : (d + 1) * 4 * width] = got[5:6, 0 : 4 * width]
    lead, count, slots, begin = place_ref[0], place_ref[1], place_ref[2], place_ref[4]
    wait_all(copies)
    angles = table[...]
    high = angles.astype(bf16)
    rest = angles - high.astype(f32)
    middle = rest.astype(bf16)
    lowest = (rest - middle.astype(f32)).astype(bf16)
    images = kept.shape[0]
    sub = lax.broadcasted_iota(jnp.int32, (8, images), 0)
    lane = lax.broadcasted_iota(jnp.int32, (8, images), 1)
    picker = jnp.where(lane == begin + sub, 1.0, 0.0).astype(bf16)
    patches = dot(picker, kept[...].astype(f32).astype(bf16)).astype(jnp.int32)
    for slot in range(SLOTS):
        row = lax.broadcasted_iota(jnp.int32, (LEN, TOK_DEV), 0) + slot * LEN
        source = row + lead
        live = slot < slots
        column = lax.broadcasted_iota(jnp.int32, (LEN, TOK_DEV), 1)
        own = jnp.where((column == source) & (source < count) & live, 1.0, 0.0).astype(bf16)
        far = source[:, :LEN] - count
        spill = jnp.where((column[:, :LEN] == far) & live, 1.0, 0.0).astype(bf16)
        taken = dot(own, tok[...]) + dot(spill, halo[0:LEN, :])
        grad = dot(own, cot[...]) + dot(spill, halo[LEN : 2 * LEN, :])
        gc_ref[slot_rows(slot), :] = grad.astype(bf16)
        patch = patches[slot : slot + 1, :]
        index = lax.broadcasted_iota(jnp.int32, (GRID, LEN), 0)
        line = jnp.where((index == patch // GRID) & live, 1.0, 0.0).astype(bf16)
        across = jnp.where((index == patch % GRID) & live, 1.0, 0.0).astype(bf16)
        half = D // 2
        for start, picked in ((0, line), (half, across)):
            spot = dot_tn(picked, high) + (dot_tn(picked, middle) + dot_tn(picked, lowest))
            res_ref[slot_rows(slot), start : start + half] = taken[:, start : start + half] + spot


def head_masks():
    lane = lax.broadcasted_iota(jnp.int32, (1, 2 * HD), 1)
    first = jnp.where(lane < HD, 1.0, 0.0).astype(bf16)
    return first, (1.0 - first.astype(f32)).astype(bf16)


def both_heads(pair, masks):
    return jnp.concatenate([pair * masks[0], pair * masks[1]], axis=0)


def side_by_side(stacked):
    return jnp.concatenate([stacked[:LEN], stacked[LEN:]], axis=1)


def pair_probs(queries, keys):
    scores = dot_nt(queries, keys) * (1.0 / math.sqrt(HD))
    exp_terms = jnp.exp(scores - jnp.max(scores, axis=1, keepdims=True))
    return exp_terms * (1.0 / jnp.sum(exp_terms, axis=1, keepdims=True))


def qkv_kernel(
    where_ref, res_ref, mod_ref, bias_ref, near_ref, far_ref, ain_out, qkv_ref, weight_out, ain_ref, weight, sems
):
    for slot in range(SLOTS):
        normed, _ = norm_parts(res_ref[slot_rows(slot), :])
        ain_ref[slot_rows(slot), :] = (
            normed * (1.0 + mod_part(mod_ref, slot, 1)) + mod_part(mod_ref, slot, 0)
        ).astype(bf16)
    out = fetch([(ain_ref, ain_out)], sems)
    lay_out(where_ref, ([near_ref], [far_ref]), D // BLOCKS, [(weight, 0, 3 * D // 2)])
    out += fetch([(weight, weight_out)], sems, 1)

    @pl.loop(0, 3 * D // 256)
    def _(j):
        cols = pl.ds(pl.multiple_of(j * 256, 256), 256)
        qkv_ref[:, cols] = (dot(ain_ref[...], weight[:, cols]) + bias_ref[:, cols]).astype(bf16)

    wait_all(out)


def attend_kernel(qkv_ref, att_ref, att_out, sems):
    masks = head_masks()

    @pl.loop(0, SLOTS)
    def _(slot):
        rows = pl.ds(pl.multiple_of(slot * LEN, LEN), LEN)
        for pair in range(HEADS // 2):
            at = pair * 2 * HD
            probs = pair_probs(
                both_heads(qkv_ref[rows, at : at + 2 * HD], masks),
                qkv_ref[rows, D + at : D + at + 2 * HD],
            )
            values = both_heads(qkv_ref[rows, 2 * D + at : 2 * D + at + 2 * HD], masks)
            att_ref[rows, at : at + 2 * HD] = dot(
                side_by_side(probs.astype(bf16)), values
            ).astype(bf16)

    wait_all(fetch([(att_ref, att_out)], sems))


def join_kernel(*refs):
    *parts, both, sems = refs
    pairs, first = [], 0
    for ref in parts:
        rows = ref.shape[0]
        pairs.append((ref, both.at[pl.ds(first, rows), :]))
        first += rows
    wait_all(fetch(pairs, sems))


def flip(where_ref, lhs_ref, ordered, split_rows):
    chip, core = where_ref[0], where_ref[1]
    depth = ordered.shape[0]
    size = depth // BLOCKS
    if split_rows:
        size //= 2
    step = 384
    for m in range(depth // step):
        turned = lhs_ref[:, m * step : (m + 1) * step].T
        for i in range(step // size):
            block = m * (step // size) + i
            side = block % 2
            to = place_of(block // 2 if split_rows else block, chip) * size
            if split_rows:
                to = to + jnp.where(core == side, depth // 2, 0)
            ordered[pl.ds(pl.multiple_of(to, 16), size), :] = turned[i * size : (i + 1) * size, :]


def hidden_kernel(
    where_ref, res_ref, att_ref, mod_ref, gc_ref, proj_bias_ref, bias_ref, *rest
):
    mine, more, theirs, rest_far = rest[:4]
    branch_ref, mid_ref, min_ref, gmo_ref, colsum_ref, act_out, slope_out, send_out, keep_out, mid_out = rest[4:14]
    proj, weight, act, slope, ordered, made, out_sems = rest[14:]
    total = jnp.zeros((1, D), f32)
    for slot in range(SLOTS):
        rows = slot_rows(slot)
        grad = (mod_part(mod_ref, slot, 5) * gc_ref[rows, :].astype(f32)).astype(bf16)
        gmo_ref[rows, :] = grad
        total += jnp.sum(grad.astype(f32), axis=0, keepdims=True)
    colsum_ref[...] = total
    lay_out(
        where_ref,
        ([mine, more], [theirs, rest_far]),
        D // BLOCKS,
        [(proj, 0, D // 2), (weight, D // 2, F // 2)],
    )
    for j in range(D // 256):
        cols = slice(j * 256, (j + 1) * 256)
        branch_ref[:, cols] = dot(att_ref[...], proj[:, cols]) + proj_bias_ref[:, cols]
    for slot in range(SLOTS):
        rows = slot_rows(slot)
        mid = res_ref[rows, :] + mod_part(mod_ref, slot, 2) * branch_ref[rows, :]
        mid_ref[rows, :] = mid
        normed, _ = norm_parts(mid)
        min_ref[rows, :] = (
            normed * (1.0 + mod_part(mod_ref, slot, 4)) + mod_part(mod_ref, slot, 3)
        ).astype(bf16)

    @pl.loop(0, F // 256)
    def _(j):
        cols = pl.ds(pl.multiple_of(j * 256, 256), 256)
        u = dot(min_ref[...], weight[:, cols]) + bias_ref[:, cols]
        square = u * u
        bend = jnp.tanh(GELU_COEF * (u + 0.044715 * square * u))
        left = 0.5 * (1.0 + bend)
        act[:, cols] = (u * left).astype(bf16)
        slope[:, cols] = (
            left
            + 0.5 * u * (1.0 - bend * bend) * (GELU_COEF * (1.0 + 3.0 * 0.044715 * square))
        ).astype(bf16)

    out = fetch([(act, act_out), (slope, slope_out)], out_sems)
    out += fetch([(mid_ref, mid_out)], out_sems, 8)
    flip(where_ref, act, ordered, True)
    step = 512
    for j in range(F // step):
        made[j * step : (j + 1) * step, :] = dot(
            ordered[j * step : (j + 1) * step, :], gmo_ref[...]
        ).astype(bf16)
        to, at = (send_out, j) if j < F // step // 2 else (keep_out, j - F // step // 2)
        out += fetch(
            [(made.at[pl.ds(j * step, step), :], to.at[pl.ds(at * step, step), :])],
            out_sems,
            2 + j,
        )
    wait_all(out)


def wgrad_kernel(count, where_ref, *rest):
    lhs, rhs = rest[:count], rest[count : 2 * count]
    send_out, keep_out, ordered, send, keep, sems, *late = rest[2 * count :]
    core = where_ref[1]
    if late:
        *bufs, in_sems = late
        ins = fetch([(lhs[0], bufs[0]), (rhs[0], bufs[1]), (lhs[1], bufs[2])], in_sems)
        lhs, rhs = (bufs[0], bufs[2]), (bufs[1], rhs[1])
    depth = ordered.shape[0]
    step = 384
    first = 0
    out = []
    for lhs_ref, rhs_ref in zip(lhs, rhs):
        if late:
            wait_all(ins[2:] if first else ins[:2])
        flip(where_ref, lhs_ref, ordered, False)
        width = rhs_ref.shape[1] // 2
        for buf, to, half in ((send, send_out, 1 - core), (keep, keep_out, core)):
            cols = pl.ds(pl.multiple_of(half * width, 128), width)
            for j in range(depth // step):
                rows = slice(j * step, (j + 1) * step)
                buf[rows, first : first + width] = dot(
                    ordered[rows, :], rhs_ref[:, cols]
                ).astype(bf16)
                here = (pl.ds(j * step, step), pl.ds(first, width))
                out += fetch([(buf.at[here], to.at[here])], sems, len(out))
        first += width
    wait_all(out)


def pair_sums(keep_in, got_in, rows, spans, keep, got, sems):
    copies = []
    for i, first in enumerate(spans):
        here, there = pl.ds(i * rows, rows), pl.ds(first, rows)
        copies += fetch(
            [(keep_in.at[there, :], keep.at[here, :]), (got_in.at[there, :], got.at[here, :])],
            sems,
            2 * i,
        )

    def total(i):
        wait_all(copies[2 * i : 2 * i + 2])
        here = slice(i * rows, (i + 1) * rows)
        return keep[here, :].astype(f32) + got[here, :].astype(f32)

    return total


def first_kernel(keep_in, got_in, x_ref, y_ref, keep, got, sems):
    rows = x_ref.shape[0] // 2
    total = pair_sums(
        keep_in, got_in, rows, [2 * rows, 6 * rows, 5 * rows, 7 * rows], keep, got, sems
    )
    for i in range(4):
        ref = (x_ref, y_ref)[i // 2]
        ref[i % 2 * rows : (i % 2 + 1) * rows, :] = total(i).astype(bf16)


def second_kernel(keep_in, got_in, x_got_ref, y_got_ref, x_ref, y_ref, keep, got, sems):
    rows = x_ref.shape[0]
    total = pair_sums(keep_in, got_in, rows, [3 * rows, 4 * rows], keep, got, sems)
    x_ref[...] = (total(0) + y_got_ref[rows:, :].astype(f32)).astype(bf16)
    y_ref[...] = (total(1) + x_got_ref[rows:, :].astype(f32)).astype(bf16)


def near_kernel(direct, keep_in, got_in, x_one_ref, y_one_ref, x_two_ref, y_two_ref, *rest):
    if direct:
        outs, (keep, got, sems) = rest[:4], rest[4:]
    else:
        send_ref, own_out, beyond_out, keep, got, sems, own, beyond, out_sems = rest
        outs = (send_ref, own, beyond)
    half = x_two_ref.shape[0]
    rows = half // 2
    total = pair_sums(keep_in, got_in, half, [0, half], keep, got, sems)
    for i, (one_ref, two_ref) in enumerate(((x_one_ref, y_two_ref), (y_one_ref, x_two_ref))):
        both = total(i) + one_ref[0:half, :].astype(f32) + two_ref[...].astype(f32)
        for j in range(2):
            z = 2 * i + j
            value = both[j * rows : (j + 1) * rows]
            if direct:
                outs[z][...] = value.astype(outs[z].dtype)
            elif j:
                outs[0][i * rows : (i + 1) * rows, :] = value.astype(bf16)
            else:
                outs[1 + i][...] = value
    if not direct:
        wait_all(fetch([(own, own_out), (beyond, beyond_out)], out_sems))


def beyond_kernel(got_ref, own_in, beyond_in, send_ref, total_out, own, beyond, sems):
    wait_all(fetch([(own_in, own), (beyond_in, beyond)], sems))
    rows = own.shape[0]
    send_ref[...] = (beyond[...] + got_ref[rows:, :].astype(f32)).astype(bf16)
    own[...] = own[...] + got_ref[0:rows, :].astype(f32)
    wait_all(fetch([(own, total_out)], sems, 2))


def lay_out_fc2(where_ref, near_ref, far_ref, fc2):
    lay_out(where_ref, ([near_ref], [far_ref]), F // (2 * BLOCKS), [(fc2, 0, D)], True)


def fc2_back_kernel(
    where_ref, gmo_ref, slope_in, near_ref, far_ref, gh_ref, colsum_ref, fc2, slope, in_sems
):
    step = 512
    parts = [pl.ds(j * step, step) for j in range(F // step)]
    late = fetch([(slope_in.at[:, part], slope.at[:, part]) for part in parts], in_sems)
    lay_out_fc2(where_ref, near_ref, far_ref, fc2)
    for j in range(F // step):
        wait_all([late[j]])
        for half in range(2):
            cols = slice(j * step + half * 256, j * step + (half + 1) * 256)
            grad = dot_nt(gmo_ref[...], fc2[cols, :])
            value = (slope[:, cols].astype(f32) * grad).astype(bf16)
            gh_ref[:, cols] = value
            colsum_ref[:, cols] = jnp.sum(value.astype(f32), axis=0, keepdims=True)


def fc2_out_kernel(
    where_ref, place_ref, mod_ref, gc_ref, bias_ref, mid_in, act_in, near_ref, far_ref,
    tail_ref, gate_ref, out_out, mid_ref, act, fc2, mlp, made, in_sems,
):
    last = fetch([(act_in, act), (mid_in, mid_ref)], in_sems)
    lay_out_fc2(where_ref, near_ref, far_ref, fc2)
    wait_all(last)
    for j in range(D // 256):
        cols = slice(j * 256, (j + 1) * 256)
        mlp[0:TOK_DEV, cols] = dot(act[...], fc2[:, cols]) + bias_ref[:, cols]
    for slot in range(SLOTS):
        rows = slot_rows(slot)
        value = mlp[rows, :]
        gate_ref[slot : slot + 1, :] = jnp.sum(
            value * gc_ref[rows, :].astype(f32), axis=0, keepdims=True
        )
        value = mid_ref[rows, :] + mod_part(mod_ref, slot, 5) * value
        mlp[rows, :] = value
        made[rows, :] = value.astype(bf16)
    out = fetch([(made, out_out)], in_sems, 2)
    mlp[TOK_DEV:, :] = jnp.zeros((LEN + 8, D), f32)
    tail_ref[...] = rows_from(mlp, place_ref[3]).astype(bf16)
    wait_all(out)


def keep_sum(sums, part, slot, values):
    at = part * SLOTS + slot
    sums[at : at + 1, :] = jnp.sum(values, axis=0, keepdims=True)


def spread_sums(sums, spread_ref):
    value = sums[...].astype(bf16)
    for d in range(spread_ref.shape[0]):
        spread_ref[d] = value


def mid_back_kernel(
    where_ref, gh_ref, mid_ref, branch_ref, mod_ref, gc_ref, gate_ref, mine, more, theirs, rest_far,
    ga_ref, proj_sum_ref, gm_out, gb_out, spread_out,
    gm_ref, gb_ref, spread_ref, proj, weight, grads, sums, out_sems,
):
    lay_out(
        where_ref,
        ([mine, more], [theirs, rest_far]),
        D // BLOCKS,
        [(proj, 0, D // 2), (weight, D // 2, F // 2)],
    )
    for j in range(D // 256):
        cols = slice(j * 256, (j + 1) * 256)
        grads[:, cols] = dot_nt(gh_ref[...], weight[cols, :])
    total = jnp.zeros((1, D), f32)
    for slot in range(SLOTS):
        rows = slot_rows(slot)
        normed, inverse = norm_parts(mid_ref[rows, :])
        e = grads[rows, :]
        keep_sum(sums, 1, slot, e)
        keep_sum(sums, 2, slot, e * normed)
        grad_mid = gc_ref[rows, :].astype(f32) + norm_back(
            normed, inverse, mod_part(mod_ref, slot, 4), e
        )
        gm_ref[rows, :] = grad_mid
        keep_sum(sums, 0, slot, branch_ref[rows, :] * grad_mid)
        value = (mod_part(mod_ref, slot, 2) * grad_mid).astype(bf16)
        gb_ref[rows, :] = value
        total += jnp.sum(value.astype(f32), axis=0, keepdims=True)
    proj_sum_ref[...] = total
    sums[3 * SLOTS :, :] = gate_ref[...]
    spread_sums(sums, spread_ref)
    out = fetch([(gm_ref, gm_out), (gb_ref, gb_out), (spread_ref, spread_out)], out_sems)
    for j in range(D // 256):
        cols = slice(j * 256, (j + 1) * 256)
        ga_ref[:, cols] = dot_nt(gb_ref[...], proj[cols, :]).astype(bf16)
    wait_all(out)


def attend_back_kernel(qkv_in, ga_ref, gqkv_ref, colsum_ref, qkv, sems):
    masks = head_masks()
    first_head = lax.broadcasted_iota(jnp.int32, (1, 2 * HD), 1) < HD
    scale = 1.0 / math.sqrt(HD)
    copies = fetch(
        [
            (qkv_in.at[pl.ds(slot * LEN, LEN), :], qkv.at[pl.ds(slot * LEN, LEN), :])
            for slot in range(SLOTS)
        ],
        sems,
    )
    for first in range(0, SLOTS, 2):
        wait_all(copies[first : first + 2])

        @pl.loop(first, first + 2)
        def _(slot):
            rows = pl.ds(pl.multiple_of(slot * LEN, LEN), LEN)
            for pair in range(HEADS // 2):
                at = pair * 2 * HD
                q_cols, k_cols, v_cols = (
                    slice(part * D + at, part * D + at + 2 * HD) for part in range(3)
                )
                queries = both_heads(qkv[rows, q_cols], masks)
                keys = qkv[rows, k_cols]
                scores = dot_nt(keys, queries) * scale
                exp_terms = jnp.exp(scores - jnp.max(scores, axis=0, keepdims=True))
                probs = exp_terms * (1.0 / jnp.sum(exp_terms, axis=0, keepdims=True))
                grads = both_heads(ga_ref[rows, q_cols], masks)
                weighed = probs * dot_nt(qkv[rows, v_cols], grads)
                inner = jnp.sum(weighed, axis=0, keepdims=True)
                grad_scores = (weighed - probs * inner).astype(bf16)
                grad_queries = dot_tn(grad_scores, keys) * scale
                gqkv_ref[rows, q_cols] = jnp.where(
                    first_head, grad_queries[:LEN], grad_queries[LEN:]
                ).astype(bf16)
                gqkv_ref[rows, k_cols] = (dot(grad_scores, queries) * scale).astype(bf16)
                gqkv_ref[rows, v_cols] = dot(probs.astype(bf16), grads).astype(bf16)

    for j in range(3 * D // 256):
        cols = slice(j * 256, (j + 1) * 256)
        colsum_ref[:, cols] = jnp.sum(gqkv_ref[:, cols].astype(f32), axis=0, keepdims=True)


def start_back_kernel(
    place_ref, gqkv_ref, mod_ref, out_tail_ref, res_in, gm_in, weight_in,
    tg_out, tail_out, spread_out, weight, grads, res, gm, sums, tail_ref, spread_ref, in_sems, out_sems,
):
    step = 256
    parts = [pl.ds(j * step, step) for j in range(D // step)]
    copies = fetch([(weight_in.at[part, :], weight.at[part, :]) for part in parts], in_sems)
    late = fetch([(res_in, res), (gm_in, gm)], in_sems, len(parts))
    for j in range(D // step):
        wait_all([copies[j]])
        cols = slice(j * step, (j + 1) * step)
        grads[0:TOK_DEV, cols] = dot_nt(gqkv_ref[...], weight[cols, :])
    wait_all(late)
    for slot in range(SLOTS):
        rows = slot_rows(slot)
        normed, inverse = norm_parts(res[rows, :])
        e = grads[rows, :]
        keep_sum(sums, 0, slot, e)
        keep_sum(sums, 1, slot, e * normed)
        grads[rows, :] = gm[rows, :] + norm_back(normed, inverse, mod_part(mod_ref, slot, 1), e)
    out = fetch([(grads.at[pl.ds(0, TOK_DEV), :], tg_out)], out_sems)
    spread_sums(sums, spread_ref)
    out += fetch([(spread_ref, spread_out)], out_sems, 1)
    grads[TOK_DEV:, :] = jnp.zeros((LEN + 8, D), f32)
    tail = rows_from(grads, place_ref[3])
    high = tail.astype(bf16)
    tail_ref[0:LEN, :] = out_tail_ref[...]
    tail_ref[LEN : 2 * LEN, :] = high
    tail_ref[2 * LEN :, :] = (tail - high.astype(f32)).astype(bf16)
    wait_all(out + fetch([(tail_ref, tail_out)], out_sems, 2))


def place_kernel(
    place_ref, tail_ref, tok_in, cot_in, out_in, tg_in,
    final_out, final_tg, out_rows, tg_rows, tok, cot, out, made_out, made_tg, sems,
):
    lead, count = place_ref[0], place_ref[1]
    copies = fetch(
        [(out_in, out), (tok_in, tok), (tg_in, tg_rows.at[pl.ds(LEN, TOK_DEV), :]), (cot_in, cot)],
        sems,
    )
    for rows in (out_rows, tg_rows):
        rows[0:LEN, :] = jnp.zeros((LEN, D), f32)
        rows[LEN + TOK_DEV :, :] = jnp.zeros((8, D), f32)
    wait_all(copies[:2])
    out_rows[LEN : LEN + TOK_DEV, :] = out[...].astype(f32)
    last = []
    out_tail = tail_ref[0:LEN, :].astype(f32)
    tg_tail = tail_ref[LEN : 2 * LEN, :].astype(f32) + tail_ref[2 * LEN :, :].astype(f32)
    for k, (rows, tail, pad, made, final) in enumerate(
        ((out_rows, out_tail, tok, made_out, final_out), (tg_rows, tg_tail, cot, made_tg, final_tg))
    ):
        if k:
            wait_all(copies[2:])
        for slot in range(SLOTS):
            here = slot_rows(slot)
            row = lax.broadcasted_iota(jnp.int32, (LEN, 1), 0) + slot * LEN
            value = rows_from(rows, LEN - lead + slot * LEN)
            if slot == 0:
                value = jnp.where(row < lead, tail, value)
            value = jnp.where(row < count, value, pad[here, :].astype(f32))
            made[here, :] = value.astype(made.dtype)
        last += fetch([(made, final)], sems, 4 + k)
    wait_all(last)


def shape(*dims, dtype=f32):
    return jax.ShapeDtypeStruct(dims, dtype)


def call(kernel, outs, scratch, mib, ins, spaces, after=(), out_specs=None, us=0, zeros=False):
    taken, held, made = len(ins), len(after), len(outs)
    out_specs = out_specs or [VM] * made

    def body(*refs):
        first = taken + held
        kernel(*refs[:taken], *refs[first : first + made], *refs[first + made + 1 :])
        if zeros:
            refs[first + made][...] = jnp.zeros((8, 128), f32)

    def settled(item):
        is_token = item.shape == (8, 128) and item.dtype == f32
        return pltpu.with_memory_space_constraint(item, pltpu.HBM) if is_token else item

    def placed(item, spec):
        return pltpu.with_memory_space_constraint(item, pltpu.HBM) if spec is HBM else item

    out_specs = [*out_specs, VM if zeros else HBM]
    out_shape = [
        pltpu.HBM(item.shape, item.dtype) if spec is HBM else item
        for item, spec in zip([*outs, shape(8, 128)], out_specs)
    ]
    *results, token = pl.pallas_call(
        body,
        out_shape=out_shape,
        in_specs=list(spaces) + [ANY] * held,
        out_specs=out_specs,
        scratch_shapes=scratch,
        compiler_params=params(mib),
        cost_estimate=cost(us),
        name=getattr(kernel, "func", kernel).__name__,
    )(*[placed(item, spec) for item, spec in zip(ins, spaces)], *[settled(item) for item in after])
    return results, token


def tie(value, token):
    return jnp.where(token[0, 0] == 0.0, value, jnp.zeros_like(value))


def join(parts, after=(), us=0, zeros=False):
    rows = sum(part.shape[0] for part in parts)
    (both,), token = call(
        join_kernel,
        [shape(rows, parts[0].shape[1], dtype=parts[0].dtype)],
        [pltpu.SemaphoreType.DMA((len(parts),))],
        8,
        parts,
        [ANY] * len(parts),
        after=after,
        out_specs=[ANY],
        us=us,
        zeros=zeros,
    )
    return both, token


def tie(value, token):
    return jnp.where(token[0, 0] == 0.0, value, jnp.zeros_like(value))


def low(value):
    return value.astype(bf16)


class Links:
    def __init__(self, devices):
        self.devices = devices
        self.cube = devices == 32
        self.me = lax.axis_index("wide").astype(jnp.int32)
        self.core = self.me % 2 if self.cube else jnp.int32(0)
        self.chip = self.me // 2 if self.cube else jnp.int32(0)
        self.where = jnp.stack([self.chip, self.core, self.me])

    def swap(self, array, bits):
        return lax.ppermute(array, "wide", [(i, i ^ bits) for i in range(self.devices)])

    def by_core(self, first, second):
        return jnp.where(self.core == 0, first, second)

    def pair(self, mine, got):
        return self.by_core(
            jnp.concatenate([mine, got], axis=0), jnp.concatenate([got, mine], axis=0)
        )

    def along_z(self, pair):
        return jnp.concatenate(
            [pair, self.swap(pair, 8), self.swap(pair, 16), self.swap(pair, 24)], axis=0
        )

    def doubled_z(self, pair):
        two = jnp.concatenate([pair, self.swap(pair, 8)], axis=0)
        return jnp.concatenate([two, self.swap(two, 16)], axis=0)

    def gathered(self, shards):
        halves = [[], []]
        for shard in shards:
            whole = lax.all_gather(shard, "wide", axis=0, tiled=True)
            rows, width = whole.shape[0], whole.shape[1] // 2
            whole = whole.reshape(4, 4, rows // BLOCKS, -1).transpose(1, 0, 2, 3)
            whole = whole.reshape(rows, -1)
            halves[0].append(whole[:, :width])
            halves[1].append(whole[:, width:])
        return [jnp.concatenate(half, axis=1) for half in halves]

    def scattered(self, send, keep, widths):
        outs, first = [], 0
        rows = keep.shape[0]
        for width in widths:
            cols = slice(first, first + width)
            whole = jnp.concatenate([keep[:, cols], send[:, cols]], axis=1)
            whole = whole.reshape(4, 4, rows // BLOCKS, -1).transpose(1, 0, 2, 3)
            whole = whole.reshape(rows, -1).astype(f32)
            outs.append(lax.psum_scatter(whole, "wide", scatter_dimension=0, tiled=True))
            first += width
        return outs

    def scattered_rows(self, send, keep):
        whole = jnp.stack([keep, send]).reshape(2, 4, 4, -1, D)
        whole = whole.transpose(2, 1, 0, 3, 4).reshape(-1, D)
        return lax.psum_scatter(whole.astype(f32), "wide", scatter_dimension=0, tiled=True)

    def gathered_rows(self, shard):
        whole = lax.all_gather(shard, "wide", axis=0, tiled=True).reshape(4, 4, 2, -1, D)
        return [whole[:, :, half].transpose(1, 0, 2, 3).reshape(-1, D) for half in range(2)]

    def first(self, keep, got, after):
        rows, width = keep.shape[0] // 4, keep.shape[1]
        (x, y), token = call(
            first_kernel,
            [shape(rows, width, dtype=bf16)] * 2,
            [pltpu.VMEM((2 * rows, width), bf16)] * 2 + [pltpu.SemaphoreType.DMA((8,))],
            16,
            [keep, got],
            [HBM, HBM],
            after=after,
        )
        return [self.swap(x, 2), self.swap(y, 4)], token

    def second(self, keep, got, ones, after):
        rows, width = keep.shape[0] // 8, keep.shape[1]
        (x, y), token = call(
            second_kernel,
            [shape(rows, width, dtype=bf16)] * 2,
            [pltpu.VMEM((2 * rows, width), bf16)] * 2 + [pltpu.SemaphoreType.DMA((4,))],
            16,
            [keep, got, *ones],
            [HBM, HBM, VM, VM],
            after=after,
            us=100,
            zeros=True,
        )
        return [self.swap(x, 2), self.swap(y, 4)], token

    def near_sum(self, keep, got, ones, twos, direct, after):
        tall, width = keep.shape[0] // 4, keep.shape[1]
        rows = tall // 4
        if direct:
            outs = [shape(rows, width)] + [shape(rows, width, dtype=bf16)] * 3
        else:
            outs = [shape(2 * rows, width, dtype=bf16)] + [shape(rows, width)] * 2
        scratch = [pltpu.VMEM((tall, width), bf16)] * 2 + [pltpu.SemaphoreType.DMA((4,))]
        if not direct:
            scratch += [pltpu.VMEM((rows, width), f32)] * 2 + [pltpu.SemaphoreType.DMA((2,))]
        return call(
            functools.partial(near_kernel, direct),
            outs,
            scratch,
            16,
            [keep, got, *ones, *twos],
            [HBM, HBM] + [VM] * 4,
            after=after,
            out_specs=[VM] * 4 if direct else [VM, HBM, HBM],
            us=100,
        )

    def z_sum(self, token, own, *parts):
        own = tie(own, token)
        for part, bits in zip(parts, (8, 16, 24)):
            own = own + self.swap(part, bits).astype(f32)
        return own

    def halved_z(self, send, own, beyond, after):
        (send, total), token = call(
            beyond_kernel,
            [shape(*own.shape, dtype=bf16), shape(*own.shape)],
            [pltpu.VMEM(own.shape, f32)] * 2 + [pltpu.SemaphoreType.DMA((3,))],
            8,
            [self.swap(send, 8), own, beyond],
            [VM, HBM, HBM],
            after=after,
            out_specs=[VM, HBM],
        )
        return total, self.swap(send, 16), token

    def own_rows(self, own, widths):
        rows = own.shape[0] // 2
        mine = self.by_core(own[:rows], own[rows:])
        got = self.swap(self.by_core(own[rows:], own[:rows]), 1)
        outs, first = [], 0
        for width in widths:
            a, b = mine[:, first : first + width], got[:, first : first + width]
            outs.append(
                self.by_core(jnp.concatenate([a, b], axis=1), jnp.concatenate([b, a], axis=1))
            )
            first += width
        return outs


def on_device(
    tokens,
    cotangent,
    cond,
    kept,
    counts,
    ada_w,
    ada_bias,
    qkv_w,
    q_bias,
    v_bias,
    proj_w,
    proj_bias,
    fc1_w,
    fc1_bias,
    fc2_w,
    fc2_bias,
):
    devices = lax.axis_size("wide")
    images = cond.shape[0]
    span = ada_bias.shape[0]
    own_dim = ada_w.shape[0]
    links = Links(devices)
    me, where, cube = links.me, links.where, links.cube
    rows = TOK_DEV
    dma = pltpu.SemaphoreType.DMA
    half_sum = (qkv_w.shape[1] + proj_w.shape[1] + fc1_w.shape[1]) // 2

    (mine, send, edge, place, starts, cond_slots, ada_parts), _ = call(
        begin_kernel,
        [
            shape(own_dim, half_sum, dtype=bf16),
            shape(own_dim, half_sum, dtype=bf16),
            shape(2 * LEN, D, dtype=bf16),
            shape(8, dtype=jnp.int32),
            shape(devices, dtype=jnp.int32),
            shape(devices * 8, D, dtype=bf16),
            shape(devices, own_dim, span, dtype=bf16),
        ],
        [
            pltpu.VMEM((devices * 8, images), f32),
            pltpu.VMEM(cond.shape, bf16),
            pltpu.VMEM(ada_w.shape, bf16),
            dma((10,)),
        ],
        16,
        [where, counts, cond, ada_w, tokens, cotangent, qkv_w, proj_w, fc1_w],
        [SM, SM] + [HBM] * 7,
        out_specs=[VM, VM, VM, SM, SM, VM, VM],
    )
    if cube:
        pair = links.pair(mine, links.swap(send, 1))
        near_one = links.along_z(pair[:, : 3 * D // 2])
        before_mod = [pair]
    else:
        before_mod = []
    halo = lax.ppermute(edge, "wide", [(i + 1, i) for i in range(devices - 1)])

    ada_cols = lax.all_to_all(ada_parts, "wide", 0, 0, tiled=True)
    ada_cols = ada_cols.reshape(D, span)
    lanes = lambda items: jnp.pad(
        jnp.concatenate(items), (0, span - sum(i.shape[0] for i in items))
    ).reshape(1, span)
    addend = jnp.concatenate(
        [
            jnp.broadcast_to(ada_bias.reshape(1, span), (SLOTS, span)),
            lanes([q_bias, v_bias, proj_bias, fc2_bias]),
            lanes([fc1_bias]),
            jnp.zeros((2, span), bf16),
        ],
        axis=0,
    ).astype(f32)
    (mod_cols,), mod_ran = call(
        mod_kernel,
        [shape(devices, 8, span)],
        [],
        16,
        [cond_slots, ada_cols, addend],
        [VM] * 3,
        after=before_mod,
        zeros=True,
    )
    mixed = lax.all_to_all(mod_cols, "wide", 0, 0, tiled=True)

    quarter = D // 4
    frequency = jnp.exp(-math.log(10000.0) * jnp.arange(quarter).astype(f32) / quarter)
    angle = jnp.arange(GRID).astype(f32)[:, None] * frequency[None, :]
    table = jnp.concatenate([jnp.sin(angle), jnp.cos(angle)], axis=1)
    if cube:
        near_one = tie(near_one, mod_ran)
        over = [links.swap(near_one, bits) for bits in (2, 4, 6)]
        pair_two = tie(pair[:, 3 * D // 2 :], mod_ran)
        two = jnp.concatenate([pair_two, links.swap(pair_two, 8)], axis=0)
        before_prep = [near_one, two]
    else:
        before_prep = []
    (residual, grad_out, mod, qkv_bias, proj_bias_all, fc2_bias_all, fc1_bias_all), prepared = call(
        prep_kernel,
        [
            shape(rows, D),
            shape(rows, D, dtype=bf16),
            shape(SLOTS, 6 * D),
            shape(1, 3 * D),
            shape(1, D),
            shape(1, D),
            shape(1, F),
        ],
        [
            pltpu.VMEM((rows, D), bf16),
            pltpu.VMEM((rows, D), bf16),
            pltpu.VMEM((2 * LEN, D), bf16),
            pltpu.VMEM(kept.shape, jnp.int32),
            pltpu.VMEM(table.shape, f32),
            dma((5,)),
        ],
        16,
        [place, mixed, tokens, cotangent, halo, kept, table],
        [SM, VM, HBM, HBM, ANY, HBM, ANY],
        after=before_prep,
        us=10,
    )

    if cube:
        near_two = jnp.concatenate([two, links.swap(two, 16)], axis=0)
        qkv_near, joined = join([near_one, *over], [prepared, near_two])
        qkv_far = links.swap(qkv_near, 1)
        over_x, over_y = links.swap(near_two, 2), links.swap(near_two, 4)
        before_qkv = []
    else:
        qkv_near, qkv_far = links.gathered([qkv_w])
        before_qkv = []

    (attn_in, qkv, qkv_laid), qkv_ran = call(
        qkv_kernel,
        [
            shape(rows, D, dtype=bf16),
            shape(rows, 3 * D, dtype=bf16),
            shape(D, 3 * D, dtype=bf16),
        ],
        [pltpu.VMEM((rows, D), bf16), pltpu.VMEM((D, 3 * D), bf16), dma((2,))],
        16,
        [where, residual, mod, qkv_bias, qkv_near, qkv_far],
        [SM] + [VM] * 5,
        after=before_qkv,
        out_specs=[HBM, VM, HBM],
        zeros=True,
    )
    before_attend = [qkv_ran]
    if cube:
        two = tie(jnp.concatenate([fc2_w, links.swap(fc2_w, 8)], axis=0), qkv_ran)
        before_attend.append(two)
        near_three = jnp.concatenate([two, links.swap(two, 16)], axis=0)
    (attended, attended_kept), attend_ran = call(
        attend_kernel,
        [shape(rows, D, dtype=bf16)] * 2,
        [dma((1,))],
        16,
        [qkv],
        [VM],
        after=before_attend,
        out_specs=[VM, HBM],
        zeros=True,
    )
    if cube:
        half = near_two.shape[0] // 2
        most, _ = join([near_two, over_x, over_y], [attend_ran, near_three])
        most_far = links.swap(most, 1)
        cuts = [slice(i * half // 2, (i + 1) * half // 2) for i in range(4)]
        diag = [links.swap(tie(over_y[cut], attend_ran), 2) for cut in cuts[:2]]
        diag += [links.swap(tie(over_x[cut], attend_ran), 4) for cut in cuts[2:]]
        diag, joined = join(diag, zeros=True)
        mid_halves = [most, diag, most_far, links.swap(diag, 1)]
        near_three = tie(near_three, joined)
        over = [links.swap(near_three, bits) for bits in (2, 4, 6)]
    else:
        mid_near, mid_far = links.gathered([proj_w, fc1_w])
        cut = 3 * D // 4
        mid_halves = [mid_near[:cut], mid_near[cut:], mid_far[:cut], mid_far[cut:]]
        fc2_near, fc2_far = links.gathered_rows(fc2_w)

    (
        branch, middle, mlp_in, grad_mlp_out, fc2_bias_sum, activated, slope, fc2_send, fc2_keep,
        middle_kept,
    ), hidden_ran = call(
        hidden_kernel,
        [
            shape(rows, D),
            shape(rows, D),
            shape(rows, D, dtype=bf16),
            shape(rows, D, dtype=bf16),
            shape(1, D),
            shape(rows, F, dtype=bf16),
            shape(rows, F, dtype=bf16),
            shape(F // 2, D, dtype=bf16),
            shape(F // 2, D, dtype=bf16),
            shape(rows, D),
        ],
        [
            pltpu.VMEM((D, D), bf16),
            pltpu.VMEM((D, F), bf16),
            pltpu.VMEM((rows, F), bf16),
            pltpu.VMEM((rows, F), bf16),
            pltpu.VMEM((F, rows), bf16),
            pltpu.VMEM((F, D), bf16),
            dma((9,)),
        ],
        32,
        [where, residual, attended, mod, grad_out, proj_bias_all, fc1_bias_all, *mid_halves],
        [SM] + [VM] * 10,
        out_specs=[VM] * 5 + [HBM] * 5,
    )
    def weight_grad(*pairs, after=()):
        half = sum(right.shape[1] for _, right in pairs) // 2
        scratch = [
            pltpu.VMEM((D, rows), bf16),
            pltpu.VMEM((D, half), bf16),
            pltpu.VMEM((D, half), bf16),
            dma((8,)),
        ]
        spaces = [VM, VM]
        if len(pairs) == 2:
            scratch += [pltpu.VMEM((rows, D), bf16)] * 3 + [dma((3,))]
            spaces = [HBM, HBM, HBM, VM]
        return call(
            functools.partial(wgrad_kernel, len(pairs)),
            [shape(D, half, dtype=bf16)] * 2,
            scratch,
            20,
            [where, *[left for left, _ in pairs], *[right for _, right in pairs]],
            [SM, *spaces],
            after=after,
            out_specs=[HBM] * 2,
        )

    if cube:
        fc2_got = links.swap(fc2_send, 1)
        fc2_near, gathered = join([near_three, *over], [hidden_ran], us=100)
        fc2_far = links.swap(fc2_near, 1)
        fc2_ones, fc2_first = links.first(fc2_keep, fc2_got, [gathered])
        before_fc2 = [fc2_first]
    else:
        before_fc2 = []
    (grad_hidden, fc1_bias_sum), _ = call(
        fc2_back_kernel,
        [shape(rows, F, dtype=bf16), shape(1, F)],
        [pltpu.VMEM((F, D), bf16), pltpu.VMEM((rows, F), bf16), dma((6,))],
        20,
        [where, grad_mlp_out, slope, fc2_near, fc2_far],
        [SM, VM, HBM, VM, VM],
        after=before_fc2,
    )
    (fc1_send, fc1_keep), fc1_ran = weight_grad((mlp_in, grad_hidden))
    (out_tail, gate_two_sum, result), out_ran = call(
        fc2_out_kernel,
        [shape(LEN, D, dtype=bf16), shape(SLOTS, D), shape(rows, D, dtype=bf16)],
        [
            pltpu.VMEM((rows, D), f32),
            pltpu.VMEM((rows, F), bf16),
            pltpu.VMEM((F, D), bf16),
            pltpu.VMEM((rows + LEN + 8, D), f32),
            pltpu.VMEM((rows, D), bf16),
            dma((3,)),
        ],
        20,
        [where, place, mod, grad_out, fc2_bias_all, middle_kept, activated, fc2_near, fc2_far],
        [SM] * 2 + [VM] * 3 + [HBM] * 2 + [VM] * 2,
        after=[fc1_ran],
        out_specs=[VM] * 2 + [HBM],
    )
    if cube:
        fc1_got = links.swap(fc1_send, 1)
        fc2_twos, fc2_second = links.second(fc2_keep, fc2_got, fc2_ones, [out_ran])
        before_mid = [fc2_second]
    else:
        before_mid = [out_ran]
    (grad_attended, proj_bias_sum, grad_middle, grad_branch, early), mid_ran = call(
        mid_back_kernel,
        [
            shape(rows, D, dtype=bf16),
            shape(1, D),
            shape(rows, D),
            shape(rows, D, dtype=bf16),
            shape(devices, 16, D, dtype=bf16),
        ],
        [
            pltpu.VMEM((rows, D), f32),
            pltpu.VMEM((rows, D), bf16),
            pltpu.VMEM((devices, 16, D), bf16),
            pltpu.VMEM((D, D), bf16),
            pltpu.VMEM((D, F), bf16),
            pltpu.VMEM((rows, D), f32),
            pltpu.VMEM((16, D), f32),
            dma((3,)),
        ],
        20,
        [where, grad_hidden, middle, branch, mod, grad_out, gate_two_sum, *mid_halves],
        [SM] + [VM] * 10,
        out_specs=[VM] * 2 + [HBM] * 3,
        after=before_mid,
    )
    early = lax.all_to_all(early, "wide", 0, 0, tiled=True)
    if cube:
        fc1_ones, fc1_first = links.first(fc1_keep, fc1_got, [mid_ran])
        fc2_near_sum, fc2_summed = links.near_sum(
            fc2_keep, fc2_got, fc2_ones, fc2_twos, False, [fc1_first]
        )
        before_back = [fc2_summed]
    else:
        before_back = []
    (grad_qkv, qkv_bias_sum), back_ran = call(
        attend_back_kernel,
        [shape(rows, 3 * D, dtype=bf16), shape(1, 3 * D)],
        [pltpu.VMEM((rows, 3 * D), bf16), dma((SLOTS,))],
        16,
        [qkv, grad_attended],
        [HBM, VM],
        after=before_back,
    )
    before_qkv = [early]
    if cube:
        fc2_own, fc2_beyond, fc2_halved = links.halved_z(*fc2_near_sum, [back_ran])
        fc1_twos, fc1_second = links.second(fc1_keep, fc1_got, fc1_ones, [fc2_halved])
        before_qkv.append(fc1_second)
    (qkv_send, qkv_keep), qkv_grad_ran = weight_grad(
        (attended_kept, grad_branch), (attn_in, grad_qkv), after=before_qkv
    )
    if cube:
        qkv_got = links.swap(qkv_send, 1)
    (tokens_back, tail, late), start_ran = call(
        start_back_kernel,
        [shape(rows, D), shape(3 * LEN, D, dtype=bf16), shape(devices, 2 * SLOTS, D, dtype=bf16)],
        [
            pltpu.VMEM((D, 3 * D), bf16),
            pltpu.VMEM((rows + LEN + 8, D), f32),
            pltpu.VMEM((rows, D), f32),
            pltpu.VMEM((rows, D), f32),
            pltpu.VMEM((2 * SLOTS, D), f32),
            pltpu.VMEM((3 * LEN, D), bf16),
            pltpu.VMEM((devices, 2 * SLOTS, D), bf16),
            dma((5,)),
            dma((3,)),
        ],
        24,
        [place, grad_qkv, mod, out_tail, residual, grad_middle, qkv_laid],
        [SM] + [VM] * 3 + [HBM] * 3,
        after=[qkv_grad_ran],
        out_specs=[HBM] * 3,
    )
    late = lax.all_to_all(late, "wide", 0, 0, tiled=True)

    if cube:
        fc1_near_sum, fc1_summed = links.near_sum(
            fc1_keep, fc1_got, fc1_ones, fc1_twos, False, [start_ran]
        )
        qkv_ones, qkv_first = links.first(qkv_keep, qkv_got, [fc1_summed])
        before_ada = [qkv_first]
    else:
        before_ada = [start_ran]

    onward = [(i, i + 1) for i in range(devices - 1)]
    tail = lax.ppermute(tail, "wide", onward)
    wide_images = -(-images // 128) * 128
    (ada_grad, ada_bias_sum, last), ada_ran = call(
        ada_kernel,
        [
            shape(own_dim, 6 * D),
            shape(1, 6 * D),
            shape(devices, own_dim + 8, wide_images, dtype=bf16),
        ],
        [pltpu.VMEM((devices * 16, images), f32), pltpu.VMEM((own_dim + 8, wide_images), f32)],
        24,
        [where, starts, early, late, ada_w, cond, qkv_bias_sum, proj_bias_sum, fc2_bias_sum, fc1_bias_sum],
        [SM] * 2 + [VM] * 8,
        after=before_ada,
        zeros=True,
    )
    last = lax.all_to_all(last, "wide", 0, 0, tiled=True)
    if cube:
        fc1_own, fc1_beyond, fc1_halved = links.halved_z(*fc1_near_sum, [ada_ran])
        qkv_twos, qkv_second = links.second(qkv_keep, qkv_got, qkv_ones, [fc1_halved])
        qkv_near_sum, qkv_summed = links.near_sum(
            qkv_keep, qkv_got, qkv_ones, qkv_twos, True, [qkv_second]
        )
        before_place = [qkv_summed]
    else:
        before_place = [ada_ran]
    (out, tokens_grad), placed = call(
        place_kernel,
        [shape(rows, D, dtype=bf16), shape(rows, D)],
        [
            pltpu.VMEM((rows + LEN + 8, D), f32),
            pltpu.VMEM((rows + LEN + 8, D), f32),
            pltpu.VMEM((rows, D), bf16),
            pltpu.VMEM((rows, D), bf16),
            pltpu.VMEM((rows, D), bf16),
            pltpu.VMEM((rows, D), bf16),
            pltpu.VMEM((rows, D), f32),
            dma((6,)),
        ],
        16,
        [place, tail, tokens, cotangent, result, tokens_back],
        [SM, VM] + [HBM] * 4,
        after=before_place,
        out_specs=[HBM] * 2,
    )


    fc1_widths, qkv_widths = [F // 2], [D // 2, 3 * D // 2]
    if cube:
        fc2_grad = tie(fc2_own, qkv_second) + fc2_beyond.astype(f32)
        (fc1_grad,) = links.own_rows(
            tie(fc1_own, qkv_second) + fc1_beyond.astype(f32), fc1_widths
        )
        proj_grad, qkv_grad = links.own_rows(links.z_sum(ada_ran, *qkv_near_sum), qkv_widths)
        before_finish = [placed]
    else:
        fc2_grad = links.scattered_rows(fc2_send, fc2_keep)
        (fc1_grad,) = links.scattered(fc1_send, fc1_keep, fc1_widths)
        proj_grad, qkv_grad = links.scattered(qkv_send, qkv_keep, qkv_widths)
        before_finish = []
    (cond_grad, bias_grads), _ = call(
        finish_kernel,
        [shape(images, D), shape(8, wide_images)],
        [pltpu.VMEM((D, wide_images), f32)],
        16,
        [last],
        [VM],
        after=before_finish,
    )
    bias_grads = bias_grads[:, :own_dim]
    ada_bias_grad = lax.dynamic_slice_in_dim(ada_bias_sum[0], me * span, span, 0)
    return (
        out,
        tokens_grad,
        cond_grad,
        ada_grad,
        ada_bias_grad,
        qkv_grad,
        bias_grads[0],
        bias_grads[1],
        proj_grad,
        bias_grads[2],
        fc1_grad,
        bias_grads[4:].reshape(-1),
        fc2_grad,
        bias_grads[3],
    )


def solution(mesh):
    row, flat = P("wide", None), P("wide")
    return jax.shard_map(
        on_device,
        mesh=mesh,
        in_specs=(row, row, P(), P(), P(), row, flat, row, flat, flat, row, flat, row, flat, row, flat),
        out_specs=(row, row, P(), row, flat, row, flat, flat, row, flat, row, flat, row, flat),
        check_vma=False,
    )
```

```python
import functools
import math

import jax
import jax.numpy as jnp
from jax import lax
from jax.experimental import pallas as pl
from jax.experimental.pallas import tpu as pltpu
from jax.sharding import PartitionSpec as P

D = 768
HEADS = 12
HD = 64
GRID = 16
LEN = 128
TOK_DEV = 512
SLOTS = TOK_DEV // LEN
F = 3072
BLOCKS = 16

NORM_EPS = 1e-06
GELU_COEF = 0.7978845608028654

f32 = jnp.float32
bf16 = jnp.bfloat16

VM = pl.BlockSpec(memory_space=pltpu.VMEM)
SM = pl.BlockSpec(memory_space=pltpu.SMEM)
ANY = pl.BlockSpec(memory_space=pl.ANY)
HBM = pl.BlockSpec(memory_space=pltpu.HBM)


def params(mib):
    return pltpu.CompilerParams(vmem_limit_bytes=mib * 1024 * 1024)


def cost(us):
    return pl.CostEstimate(flops=max(1, int(us * 1e9)), bytes_accessed=1, transcendentals=0)


def dot(left, right):
    return jnp.dot(left, right, preferred_element_type=f32)


def dot_nt(left, right):
    return lax.dot_general(left, right, (((1,), (1,)), ((), ())), preferred_element_type=f32)


def dot_tn(left, right):
    return lax.dot_general(left, right, (((0,), (0,)), ((), ())), preferred_element_type=f32)


def silu(values):
    return values / (1.0 + jnp.exp(-values))


def norm_parts(values):
    centred = values - jnp.mean(values, axis=-1, keepdims=True)
    spread = jnp.mean(centred * centred, axis=-1, keepdims=True)
    inverse = lax.rsqrt(spread + NORM_EPS)
    return centred * inverse, inverse


def norm_back(normed, inverse, scale_part, grad):
    t = grad * (1.0 + scale_part)
    mean_t = jnp.mean(t, axis=-1, keepdims=True)
    mean_tn = jnp.mean(t * normed, axis=-1, keepdims=True)
    return (t - mean_t - normed * mean_tn) * inverse


def rows_from(ref, start):
    base = pl.multiple_of(start // 8 * 8, 8)
    shift = start - base
    tall = LEN + 8
    turned = pltpu.roll(ref[pl.ds(base, tall), :], jnp.where(shift == 0, 0, tall - shift), 0)
    return turned[:LEN]


def slot_rows(slot):
    return slice(slot * LEN, (slot + 1) * LEN)


def mod_part(mod_ref, slot, part):
    return mod_ref[slot : slot + 1, part * D : (part + 1) * D]


def place_of(block, chip):
    rel = jnp.bitwise_xor(block, chip)
    return jnp.bitwise_and(rel, 3) * 4 + lax.shift_right_logical(rel, 2)


def lay_out(where_ref, halves, rows, targets, split_rows=False):
    chip, core = where_ref[0], where_ref[1]
    for side in range(2):
        half = core if side == 0 else 1 - core
        place = 0
        for ref in halves[side]:
            for spot in range(ref.shape[0] // rows):
                block = jnp.bitwise_xor(place % 4 * 4 + place // 4, chip)
                place += 1
                for target, first, width in targets:
                    if split_rows:
                        to_row, to_col = (2 * block + half) * rows, 0
                    else:
                        to_row, to_col = block * rows, pl.multiple_of(half * width, 128)
                    to_row = pl.multiple_of(to_row, 16)
                    target[pl.ds(to_row, rows), pl.ds(to_col, width)] = ref[
                        spot * rows : (spot + 1) * rows, first : first + width
                    ]


def start_all(copies):
    for copy in copies:
        copy.start()
    return copies


def fetch(pairs, sems, first=0):
    return start_all(
        [pltpu.make_async_copy(a, b, sems.at[first + i]) for i, (a, b) in enumerate(pairs)]
    )


def wait_all(copies):
    for copy in copies:
        copy.wait()


def begin_kernel(
    where_ref, counts_ref, cond_in, ada_in, tok_in, cot_in, qkv_in, proj_in, fc1_in,
    mine_ref, send_ref, edge_ref, place_ref, starts_ref, slots_ref, parts_ref,
    wide, cond, ada, sems,
):
    devices = counts_ref.shape[0]
    images = cond.shape[0]
    core, me = where_ref[1], where_ref[2]
    copies = []
    first = 0
    for ref in (qkv_in, proj_in, fc1_in):
        half = ref.shape[1] // 2
        for out, at in ((send_ref, 1 - core), (mine_ref, core)):
            copies.append(
                (
                    ref.at[:, pl.ds(pl.multiple_of(at * half, 128), half)],
                    out.at[:, pl.ds(first, half)],
                )
            )
        first += half
    copies.append((tok_in.at[pl.ds(0, LEN), :], edge_ref.at[pl.ds(0, LEN), :]))
    copies.append((cot_in.at[pl.ds(0, LEN), :], edge_ref.at[pl.ds(LEN, LEN), :]))
    copies = fetch([*copies, (cond_in, cond), (ada_in, ada)], sems)

    def step(d, first_row):
        count = counts_ref[d]
        begin = (first_row + LEN - 1) // LEN
        starts_ref[d] = begin

        @pl.when(d == me)
        def _():
            lead = begin * LEN - first_row
            place_ref[0] = lead
            place_ref[1] = count
            place_ref[2] = (first_row + count + LEN - 1) // LEN - begin
            place_ref[3] = count - lead
            place_ref[4] = begin

        return first_row + count

    lax.fori_loop(0, devices, step, jnp.int32(0))
    sub = lax.broadcasted_iota(jnp.int32, (8, images), 0)
    lane = lax.broadcasted_iota(jnp.int32, (8, images), 1)

    @pl.loop(0, devices)
    def _(d):
        hit = (lane == starts_ref[d] + sub) & (sub < SLOTS)
        wide[pl.ds(pl.multiple_of(d * 8, 8), 8), :] = jnp.where(hit, 1.0, 0.0)

    wait_all(copies)
    span = parts_ref.shape[2]
    for d in range(devices):
        parts_ref[d] = ada[:, d * span : (d + 1) * span]
    act = silu(cond[...].astype(f32)).astype(bf16)
    slots_ref[...] = dot(wide[...].astype(bf16), act).astype(bf16)


def ada_kernel(
    where_ref, starts_ref, early_ref, late_ref, ada_ref, cond_ref,
    qkv_sum_ref, proj_sum_ref, fc2_sum_ref, fc1_sum_ref,
    grad_ref, colsum_ref, last_ref, wide, packed,
):
    devices = early_ref.shape[0]
    images, own = cond_ref.shape[0], ada_ref.shape[0]
    me = where_ref[2]
    row = lax.broadcasted_iota(jnp.int32, (own, D), 0)
    lane = lax.broadcasted_iota(jnp.int32, (own, D), 1)
    chosen = jnp.where(lane == me * own + row, 1.0, 0.0).astype(bf16)
    act = silu(cond_ref[...].astype(f32)).astype(bf16)
    act_own = dot_nt(act, chosen).astype(bf16)
    cond_own = dot_nt(chosen, cond_ref[...])
    total = jnp.zeros((own, images), f32)
    for ref, parts in ((early_ref, (2, 3, 4, 5)), (late_ref, (0, 1))):
        many = len(parts)
        high = many * SLOTS
        tall = devices * high
        sub = lax.broadcasted_iota(jnp.int32, (high, images), 0)
        lane = lax.broadcasted_iota(jnp.int32, (high, images), 1)

        @pl.loop(0, devices)
        def _(d):
            hit = lane == starts_ref[d] + sub % SLOTS
            wide[pl.ds(pl.multiple_of(d * high, high), high), :] = jnp.where(hit, 1.0, 0.0)

        picker = wide[0:tall, :]
        act_rows = dot(picker.astype(bf16), act_own)
        part_down = lax.broadcasted_iota(jnp.int32, (tall, 1), 0) % high // SLOTS
        part_across = lax.broadcasted_iota(jnp.int32, (1, tall), 1) % high // SLOTS
        act_parts = jnp.concatenate(
            [jnp.where(part_down == i, act_rows, 0.0) for i in range(many)], axis=1
        ).astype(bf16)
        ours = lax.broadcasted_iota(jnp.int32, (8, tall), 0) == part_across
        ours = jnp.where(ours, 1.0, 0.0).astype(bf16)
        sums = ref[...].reshape(tall, D)
        grads = dot_tn(act_parts, sums)
        colsums = dot(ours, sums)
        back = jnp.zeros((own, tall), f32)
        for i, part in enumerate(parts):
            cols = slice(part * D, (part + 1) * D)
            grad_ref[:, cols] = grads[i * own : (i + 1) * own]
            colsum_ref[:, cols] = colsums[i : i + 1]
            back += jnp.where(part_across == i, dot_nt(ada_ref[:, cols], sums), 0.0)
        total += jnp.dot(back, picker, precision=lax.Precision.HIGHEST)
    gate = 1.0 / (1.0 + jnp.exp(-cond_own))
    total = total * (gate * (1.0 + cond_own * (1.0 - gate)))
    lanes = last_ref.shape[2]
    fc1_sum = fc1_sum_ref[...]
    both = qkv_sum_ref[...]
    vectors = [both[:, :D], both[:, 2 * D :], proj_sum_ref[...], fc2_sum_ref[...]]
    for d in range(devices):
        packed[...] = jnp.zeros(packed.shape, f32)
        packed[0:own, 0:images] = total
        for j in range(8):
            if j < 4:
                value = vectors[j][:, d * own : (d + 1) * own]
            else:
                at = (4 * d + j - 4) * own
                value = fc1_sum[:, at : at + own]
            packed[own + j : own + j + 1, 0:own] = value
        last_ref[d] = packed[...].astype(bf16)


def finish_kernel(got_ref, cond_ref, bias_ref, tall):
    devices, rows, _ = got_ref.shape
    own = rows - 8
    total = None
    for d in range(devices):
        got = got_ref[d].astype(f32)
        tall[d * own : (d + 1) * own, :] = got[0:own]
        total = got[own:rows] if total is None else total + got[own:rows]
    cond_ref[...] = tall[...].T[0 : cond_ref.shape[0], :]
    bias_ref[...] = total


def mod_kernel(slots_ref, cols_ref, addend_ref, out_ref):
    value = dot(slots_ref[...], cols_ref[...])
    for d in range(out_ref.shape[0]):
        out_ref[d] = value[d * 8 : (d + 1) * 8, :] + addend_ref[...]


def prep_kernel(
    place_ref, got_ref, tok_in, cot_in, halo_in, kept_in, table_in,
    res_ref, gc_ref, mod_ref, qkv_bias_ref, proj_bias_ref, fc2_bias_ref, fc1_bias_ref,
    tok, cot, halo, kept, table, sems,
):
    copies = fetch(
        [(table_in, table), (kept_in, kept), (halo_in, halo), (tok_in, tok), (cot_in, cot)], sems
    )
    devices, _, span = got_ref.shape
    width = D // devices
    qkv_bias_ref[:, D : 2 * D] = jnp.zeros((1, D), f32)
    for d in range(devices):
        got = got_ref[d]
        mod_ref[:, d * span : (d + 1) * span] = got[0:SLOTS]
        cols = slice(d * width, (d + 1) * width)
        qkv_bias_ref[:, cols] = got[4:5, 0:width]
        qkv_bias_ref[:, 2 * D + d * width : 2 * D + (d + 1) * width] = got[4:5, width : 2 * width]
        proj_bias_ref[:, cols] = got[4:5, 2 * width : 3 * width]
        fc2_bias_ref[:, cols] = got[4:5, 3 * width : 4 * width]
        fc1_bias_ref[:, d * 4 * width : (d + 1) * 4 * width] = got[5:6, 0 : 4 * width]
    lead, count, slots, begin = place_ref[0], place_ref[1], place_ref[2], place_ref[4]
    wait_all(copies)
    angles = table[...]
    high = angles.astype(bf16)
    rest = angles - high.astype(f32)
    middle = rest.astype(bf16)
    lowest = (rest - middle.astype(f32)).astype(bf16)
    images = kept.shape[0]
    sub = lax.broadcasted_iota(jnp.int32, (8, images), 0)
    lane = lax.broadcasted_iota(jnp.int32, (8, images), 1)
    picker = jnp.where(lane == begin + sub, 1.0, 0.0).astype(bf16)
    patches = dot(picker, kept[...].astype(f32).astype(bf16)).astype(jnp.int32)
    for slot in range(SLOTS):
        row = lax.broadcasted_iota(jnp.int32, (LEN, TOK_DEV), 0) + slot * LEN
        source = row + lead
        live = slot < slots
        column = lax.broadcasted_iota(jnp.int32, (LEN, TOK_DEV), 1)
        own = jnp.where((column == source) & (source < count) & live, 1.0, 0.0).astype(bf16)
        far = source[:, :LEN] - count
        spill = jnp.where((column[:, :LEN] == far) & live, 1.0, 0.0).astype(bf16)
        taken = dot(own, tok[...]) + dot(spill, halo[0:LEN, :])
        grad = dot(own, cot[...]) + dot(spill, halo[LEN : 2 * LEN, :])
        gc_ref[slot_rows(slot), :] = grad.astype(bf16)
        patch = patches[slot : slot + 1, :]
        index = lax.broadcasted_iota(jnp.int32, (GRID, LEN), 0)
        line = jnp.where((index == patch // GRID) & live, 1.0, 0.0).astype(bf16)
        across = jnp.where((index == patch % GRID) & live, 1.0, 0.0).astype(bf16)
        half = D // 2
        for start, picked in ((0, line), (half, across)):
            spot = dot_tn(picked, high) + (dot_tn(picked, middle) + dot_tn(picked, lowest))
            res_ref[slot_rows(slot), start : start + half] = taken[:, start : start + half] + spot


def head_masks():
    lane = lax.broadcasted_iota(jnp.int32, (1, 2 * HD), 1)
    first = jnp.where(lane < HD, 1.0, 0.0).astype(bf16)
    return first, (1.0 - first.astype(f32)).astype(bf16)


def both_heads(pair, masks):
    return jnp.concatenate([pair * masks[0], pair * masks[1]], axis=0)


def side_by_side(stacked):
    return jnp.concatenate([stacked[:LEN], stacked[LEN:]], axis=1)


def pair_probs(queries, keys):
    scores = dot_nt(queries, keys) * (1.0 / math.sqrt(HD))
    exp_terms = jnp.exp(scores - jnp.max(scores, axis=1, keepdims=True))
    return exp_terms * (1.0 / jnp.sum(exp_terms, axis=1, keepdims=True))


def qkv_kernel(
    where_ref, res_ref, mod_ref, bias_ref, near_ref, far_ref, ain_out, qkv_ref, weight_out, ain_ref, weight, sems
):
    for slot in range(SLOTS):
        normed, _ = norm_parts(res_ref[slot_rows(slot), :])
        ain_ref[slot_rows(slot), :] = (
            normed * (1.0 + mod_part(mod_ref, slot, 1)) + mod_part(mod_ref, slot, 0)
        ).astype(bf16)
    out = fetch([(ain_ref, ain_out)], sems)
    lay_out(where_ref, ([near_ref], [far_ref]), D // BLOCKS, [(weight, 0, 3 * D // 2)])
    out += fetch([(weight, weight_out)], sems, 1)

    @pl.loop(0, 3 * D // 256)
    def _(j):
        cols = pl.ds(pl.multiple_of(j * 256, 256), 256)
        qkv_ref[:, cols] = (dot(ain_ref[...], weight[:, cols]) + bias_ref[:, cols]).astype(bf16)

    wait_all(out)


def attend_kernel(qkv_ref, att_ref, att_out, sems):
    masks = head_masks()

    @pl.loop(0, SLOTS)
    def _(slot):
        rows = pl.ds(pl.multiple_of(slot * LEN, LEN), LEN)
        for pair in range(HEADS // 2):
            at = pair * 2 * HD
            probs = pair_probs(
                both_heads(qkv_ref[rows, at : at + 2 * HD], masks),
                qkv_ref[rows, D + at : D + at + 2 * HD],
            )
            values = both_heads(qkv_ref[rows, 2 * D + at : 2 * D + at + 2 * HD], masks)
            att_ref[rows, at : at + 2 * HD] = dot(
                side_by_side(probs.astype(bf16)), values
            ).astype(bf16)

    wait_all(fetch([(att_ref, att_out)], sems))


def join_kernel(*refs):
    *parts, both, sems = refs
    pairs, first = [], 0
    for ref in parts:
        rows = ref.shape[0]
        pairs.append((ref, both.at[pl.ds(first, rows), :]))
        first += rows
    wait_all(fetch(pairs, sems))


def flip(where_ref, lhs_ref, ordered, split_rows):
    chip, core = where_ref[0], where_ref[1]
    depth = ordered.shape[0]
    size = depth // BLOCKS
    if split_rows:
        size //= 2
    step = 384
    for m in range(depth // step):
        turned = lhs_ref[:, m * step : (m + 1) * step].T
        for i in range(step // size):
            block = m * (step // size) + i
            side = block % 2
            to = place_of(block // 2 if split_rows else block, chip) * size
            if split_rows:
                to = to + jnp.where(core == side, depth // 2, 0)
            ordered[pl.ds(pl.multiple_of(to, 16), size), :] = turned[i * size : (i + 1) * size, :]


def hidden_kernel(
    where_ref, res_ref, att_ref, mod_ref, gc_ref, proj_bias_ref, bias_ref, *rest
):
    mine, more, theirs, rest_far = rest[:4]
    branch_ref, mid_ref, min_ref, gmo_ref, colsum_ref, act_out, slope_out, send_out, keep_out, mid_out = rest[4:14]
    proj, weight, act, slope, ordered, made, out_sems = rest[14:]
    total = jnp.zeros((1, D), f32)
    for slot in range(SLOTS):
        rows = slot_rows(slot)
        grad = (mod_part(mod_ref, slot, 5) * gc_ref[rows, :].astype(f32)).astype(bf16)
        gmo_ref[rows, :] = grad
        total += jnp.sum(grad.astype(f32), axis=0, keepdims=True)
    colsum_ref[...] = total
    lay_out(
        where_ref,
        ([mine, more], [theirs, rest_far]),
        D // BLOCKS,
        [(proj, 0, D // 2), (weight, D // 2, F // 2)],
    )
    for j in range(D // 256):
        cols = slice(j * 256, (j + 1) * 256)
        branch_ref[:, cols] = dot(att_ref[...], proj[:, cols]) + proj_bias_ref[:, cols]
    for slot in range(SLOTS):
        rows = slot_rows(slot)
        mid = res_ref[rows, :] + mod_part(mod_ref, slot, 2) * branch_ref[rows, :]
        mid_ref[rows, :] = mid
        normed, _ = norm_parts(mid)
        min_ref[rows, :] = (
            normed * (1.0 + mod_part(mod_ref, slot, 4)) + mod_part(mod_ref, slot, 3)
        ).astype(bf16)

    @pl.loop(0, F // 256)
    def _(j):
        cols = pl.ds(pl.multiple_of(j * 256, 256), 256)
        u = dot(min_ref[...], weight[:, cols]) + bias_ref[:, cols]
        square = u * u
        bend = jnp.tanh(GELU_COEF * (u + 0.044715 * square * u))
        left = 0.5 * (1.0 + bend)
        act[:, cols] = (u * left).astype(bf16)
        slope[:, cols] = (
            left
            + 0.5 * u * (1.0 - bend * bend) * (GELU_COEF * (1.0 + 3.0 * 0.044715 * square))
        ).astype(bf16)

    out = fetch([(act, act_out), (slope, slope_out)], out_sems)
    out += fetch([(mid_ref, mid_out)], out_sems, 8)
    flip(where_ref, act, ordered, True)
    step = 512
    for j in range(F // step):
        made[j * step : (j + 1) * step, :] = dot(
            ordered[j * step : (j + 1) * step, :], gmo_ref[...]
        ).astype(bf16)
        to, at = (send_out, j) if j < F // step // 2 else (keep_out, j - F // step // 2)
        out += fetch(
            [(made.at[pl.ds(j * step, step), :], to.at[pl.ds(at * step, step), :])],
            out_sems,
            2 + j,
        )
    wait_all(out)


def wgrad_kernel(count, where_ref, *rest):
    lhs, rhs = rest[:count], rest[count : 2 * count]
    send_out, keep_out, ordered, send, keep, sems, *late = rest[2 * count :]
    core = where_ref[1]
    if late:
        *bufs, in_sems = late
        ins = fetch([(lhs[0], bufs[0]), (rhs[0], bufs[1]), (lhs[1], bufs[2])], in_sems)
        lhs, rhs = (bufs[0], bufs[2]), (bufs[1], rhs[1])
    depth = ordered.shape[0]
    step = 384
    first = 0
    out = []
    for lhs_ref, rhs_ref in zip(lhs, rhs):
        if late:
            wait_all(ins[2:] if first else ins[:2])
        flip(where_ref, lhs_ref, ordered, False)
        width = rhs_ref.shape[1] // 2
        for buf, to, half in ((send, send_out, 1 - core), (keep, keep_out, core)):
            cols = pl.ds(pl.multiple_of(half * width, 128), width)
            for j in range(depth // step):
                rows = slice(j * step, (j + 1) * step)
                buf[rows, first : first + width] = dot(
                    ordered[rows, :], rhs_ref[:, cols]
                ).astype(bf16)
                here = (pl.ds(j * step, step), pl.ds(first, width))
                out += fetch([(buf.at[here], to.at[here])], sems, len(out))
        first += width
    wait_all(out)


def pair_sums(keep_in, got_ref, rows, spans, keep, sems, got=None):
    copies = []
    for i, first in enumerate(spans):
        here, there = pl.ds(i * rows, rows), pl.ds(first, rows)
        pairs = [(keep_in.at[there, :], keep.at[here, :])]
        if got is not None:
            pairs.append((got_ref.at[there, :], got.at[here, :]))
        copies.append(fetch(pairs, sems, 2 * i))

    def total(i):
        wait_all(copies[i])
        here = slice(i * rows, (i + 1) * rows)
        other = got_ref[spans[i] : spans[i] + rows, :] if got is None else got[here, :]
        return keep[here, :].astype(f32) + other.astype(f32)

    return total


def first_kernel(keep_in, got_ref, x_ref, y_ref, keep, sems, *got):
    rows = x_ref.shape[0] // 2
    total = pair_sums(keep_in, got_ref, rows, [2 * rows, 6 * rows, 5 * rows, 7 * rows], keep, sems, *got)
    for i in range(4):
        ref = (x_ref, y_ref)[i // 2]
        ref[i % 2 * rows : (i % 2 + 1) * rows, :] = total(i).astype(bf16)


def second_kernel(keep_in, got_ref, x_got_ref, y_got_ref, x_ref, y_ref, keep, sems, *got):
    rows = x_ref.shape[0]
    total = pair_sums(keep_in, got_ref, rows, [3 * rows, 4 * rows], keep, sems, *got)
    x_ref[...] = (total(0) + y_got_ref[rows:, :].astype(f32)).astype(bf16)
    y_ref[...] = (total(1) + x_got_ref[rows:, :].astype(f32)).astype(bf16)


def near_kernel(direct, keep_in, got_ref, x_one_ref, y_one_ref, x_two_ref, y_two_ref, *rest):
    if direct:
        outs, (keep, sems, *got) = rest[:4], rest[4:]
    else:
        send_ref, own_out, beyond_out, keep, sems, own, beyond, out_sems = rest
        got = ()
        outs = (send_ref, own, beyond)
    half = x_two_ref.shape[0]
    rows = half // 2
    total = pair_sums(keep_in, got_ref, half, [0, half], keep, sems, *got)
    for i, (one_ref, two_ref) in enumerate(((x_one_ref, y_two_ref), (y_one_ref, x_two_ref))):
        both = total(i) + one_ref[0:half, :].astype(f32) + two_ref[...].astype(f32)
        for j in range(2):
            z = 2 * i + j
            value = both[j * rows : (j + 1) * rows]
            if direct:
                outs[z][...] = value.astype(outs[z].dtype)
            elif j:
                outs[0][i * rows : (i + 1) * rows, :] = value.astype(bf16)
            else:
                outs[1 + i][...] = value
    if not direct:
        wait_all(fetch([(own, own_out), (beyond, beyond_out)], out_sems))


def beyond_kernel(got_ref, own_in, beyond_in, send_ref, total_out, own, beyond, sems):
    wait_all(fetch([(own_in, own), (beyond_in, beyond)], sems))
    rows = own.shape[0]
    send_ref[...] = (beyond[...] + got_ref[rows:, :].astype(f32)).astype(bf16)
    own[...] = own[...] + got_ref[0:rows, :].astype(f32)
    wait_all(fetch([(own, total_out)], sems, 2))


def lay_out_fc2(where_ref, near_ref, far_ref, fc2):
    lay_out(where_ref, ([near_ref], [far_ref]), F // (2 * BLOCKS), [(fc2, 0, D)], True)


def fc2_back_kernel(
    where_ref, gmo_ref, slope_in, near_ref, far_ref, gh_ref, colsum_ref, fc2, slope, in_sems
):
    step = 512
    parts = [pl.ds(j * step, step) for j in range(F // step)]
    late = fetch([(slope_in.at[:, part], slope.at[:, part]) for part in parts], in_sems)
    lay_out_fc2(where_ref, near_ref, far_ref, fc2)
    for j in range(F // step):
        wait_all([late[j]])
        for half in range(2):
            cols = slice(j * step + half * 256, j * step + (half + 1) * 256)
            grad = dot_nt(gmo_ref[...], fc2[cols, :])
            value = (slope[:, cols].astype(f32) * grad).astype(bf16)
            gh_ref[:, cols] = value
            colsum_ref[:, cols] = jnp.sum(value.astype(f32), axis=0, keepdims=True)


def fc2_out_kernel(
    where_ref, place_ref, mod_ref, gc_ref, bias_ref, mid_in, act_in, near_ref, far_ref,
    tail_ref, gate_ref, out_out, mid_ref, act, fc2, mlp, made, in_sems,
):
    last = fetch([(act_in, act), (mid_in, mid_ref)], in_sems)
    lay_out_fc2(where_ref, near_ref, far_ref, fc2)
    wait_all(last)
    for j in range(D // 256):
        cols = slice(j * 256, (j + 1) * 256)
        mlp[0:TOK_DEV, cols] = dot(act[...], fc2[:, cols]) + bias_ref[:, cols]
    for slot in range(SLOTS):
        rows = slot_rows(slot)
        value = mlp[rows, :]
        gate_ref[slot : slot + 1, :] = jnp.sum(
            value * gc_ref[rows, :].astype(f32), axis=0, keepdims=True
        )
        value = mid_ref[rows, :] + mod_part(mod_ref, slot, 5) * value
        mlp[rows, :] = value
        made[rows, :] = value.astype(bf16)
    out = fetch([(made, out_out)], in_sems, 2)
    mlp[TOK_DEV:, :] = jnp.zeros((LEN + 8, D), f32)
    tail_ref[...] = rows_from(mlp, place_ref[3]).astype(bf16)
    wait_all(out)


def keep_sum(sums, part, slot, values):
    at = part * SLOTS + slot
    sums[at : at + 1, :] = jnp.sum(values, axis=0, keepdims=True)


def spread_sums(sums, spread_ref):
    value = sums[...].astype(bf16)
    for d in range(spread_ref.shape[0]):
        spread_ref[d] = value


def mid_back_kernel(
    where_ref, gh_ref, mid_ref, branch_ref, mod_ref, gc_ref, gate_ref, mine, more, theirs, rest_far,
    ga_ref, proj_sum_ref, gm_out, gb_out, spread_out,
    gm_ref, gb_ref, spread_ref, proj, weight, grads, sums, out_sems,
):
    lay_out(
        where_ref,
        ([mine, more], [theirs, rest_far]),
        D // BLOCKS,
        [(proj, 0, D // 2), (weight, D // 2, F // 2)],
    )
    for j in range(D // 256):
        cols = slice(j * 256, (j + 1) * 256)
        grads[:, cols] = dot_nt(gh_ref[...], weight[cols, :])
    total = jnp.zeros((1, D), f32)
    for slot in range(SLOTS):
        rows = slot_rows(slot)
        normed, inverse = norm_parts(mid_ref[rows, :])
        e = grads[rows, :]
        keep_sum(sums, 1, slot, e)
        keep_sum(sums, 2, slot, e * normed)
        grad_mid = gc_ref[rows, :].astype(f32) + norm_back(
            normed, inverse, mod_part(mod_ref, slot, 4), e
        )
        gm_ref[rows, :] = grad_mid
        keep_sum(sums, 0, slot, branch_ref[rows, :] * grad_mid)
        value = (mod_part(mod_ref, slot, 2) * grad_mid).astype(bf16)
        gb_ref[rows, :] = value
        total += jnp.sum(value.astype(f32), axis=0, keepdims=True)
    proj_sum_ref[...] = total
    sums[3 * SLOTS :, :] = gate_ref[...]
    spread_sums(sums, spread_ref)
    out = fetch([(gm_ref, gm_out), (gb_ref, gb_out), (spread_ref, spread_out)], out_sems)
    for j in range(D // 256):
        cols = slice(j * 256, (j + 1) * 256)
        ga_ref[:, cols] = dot_nt(gb_ref[...], proj[cols, :]).astype(bf16)
    wait_all(out)


def attend_back_kernel(qkv_in, ga_ref, gqkv_ref, colsum_ref, qkv, sems):
    masks = head_masks()
    first_head = lax.broadcasted_iota(jnp.int32, (1, 2 * HD), 1) < HD
    scale = 1.0 / math.sqrt(HD)
    copies = fetch(
        [
            (qkv_in.at[pl.ds(slot * LEN, LEN), :], qkv.at[pl.ds(slot * LEN, LEN), :])
            for slot in range(SLOTS)
        ],
        sems,
    )
    for first in range(0, SLOTS, 2):
        wait_all(copies[first : first + 2])

        @pl.loop(first, first + 2)
        def _(slot):
            rows = pl.ds(pl.multiple_of(slot * LEN, LEN), LEN)
            for pair in range(HEADS // 2):
                at = pair * 2 * HD
                q_cols, k_cols, v_cols = (
                    slice(part * D + at, part * D + at + 2 * HD) for part in range(3)
                )
                queries = both_heads(qkv[rows, q_cols], masks)
                keys = qkv[rows, k_cols]
                scores = dot_nt(keys, queries) * scale
                exp_terms = jnp.exp(scores - jnp.max(scores, axis=0, keepdims=True))
                probs = exp_terms * (1.0 / jnp.sum(exp_terms, axis=0, keepdims=True))
                grads = both_heads(ga_ref[rows, q_cols], masks)
                weighed = probs * dot_nt(qkv[rows, v_cols], grads)
                inner = jnp.sum(weighed, axis=0, keepdims=True)
                grad_scores = (weighed - probs * inner).astype(bf16)
                grad_queries = dot_tn(grad_scores, keys) * scale
                gqkv_ref[rows, q_cols] = jnp.where(
                    first_head, grad_queries[:LEN], grad_queries[LEN:]
                ).astype(bf16)
                gqkv_ref[rows, k_cols] = (dot(grad_scores, queries) * scale).astype(bf16)
                gqkv_ref[rows, v_cols] = dot(probs.astype(bf16), grads).astype(bf16)

    for j in range(3 * D // 256):
        cols = slice(j * 256, (j + 1) * 256)
        colsum_ref[:, cols] = jnp.sum(gqkv_ref[:, cols].astype(f32), axis=0, keepdims=True)


def start_back_kernel(
    place_ref, gqkv_ref, mod_ref, out_tail_ref, res_in, gm_in, weight_in,
    tg_out, tail_out, spread_out, weight, grads, res, gm, sums, tail_ref, spread_ref, in_sems, out_sems,
):
    step = 256
    parts = [pl.ds(j * step, step) for j in range(D // step)]
    copies = fetch([(weight_in.at[part, :], weight.at[part, :]) for part in parts], in_sems)
    late = fetch([(res_in, res), (gm_in, gm)], in_sems, len(parts))
    for j in range(D // step):
        wait_all([copies[j]])
        cols = slice(j * step, (j + 1) * step)
        grads[0:TOK_DEV, cols] = dot_nt(gqkv_ref[...], weight[cols, :])
    wait_all(late)
    out = []
    for slot in range(SLOTS):
        rows = slot_rows(slot)
        normed, inverse = norm_parts(res[rows, :])
        e = grads[rows, :]
        keep_sum(sums, 0, slot, e)
        keep_sum(sums, 1, slot, e * normed)
        grads[rows, :] = gm[rows, :] + norm_back(normed, inverse, mod_part(mod_ref, slot, 1), e)
        here = pl.ds(slot * LEN, LEN)
        out += fetch([(grads.at[here, :], tg_out.at[here, :])], out_sems, slot)
    spread_sums(sums, spread_ref)
    out += fetch([(spread_ref, spread_out)], out_sems, SLOTS)
    grads[TOK_DEV:, :] = jnp.zeros((LEN + 8, D), f32)
    tail = rows_from(grads, place_ref[3])
    high = tail.astype(bf16)
    tail_ref[0:LEN, :] = out_tail_ref[...]
    tail_ref[LEN : 2 * LEN, :] = high
    tail_ref[2 * LEN :, :] = (tail - high.astype(f32)).astype(bf16)
    wait_all(out + fetch([(tail_ref, tail_out)], out_sems, SLOTS + 1))


def place_kernel(
    place_ref, tail_ref, tok_in, cot_in, out_in, tg_in,
    final_out, final_tg, out_rows, tg_rows, tok, cot, out, made_out, made_tg, sems,
):
    lead, count = place_ref[0], place_ref[1]
    copies = fetch(
        [(out_in, out), (tok_in, tok), (tg_in, tg_rows.at[pl.ds(LEN, TOK_DEV), :]), (cot_in, cot)],
        sems,
    )
    for rows in (out_rows, tg_rows):
        rows[0:LEN, :] = jnp.zeros((LEN, D), f32)
        rows[LEN + TOK_DEV :, :] = jnp.zeros((8, D), f32)
    wait_all(copies[:2])
    out_rows[LEN : LEN + TOK_DEV, :] = out[...].astype(f32)
    last = []
    out_tail = tail_ref[0:LEN, :].astype(f32)
    tg_tail = tail_ref[LEN : 2 * LEN, :].astype(f32) + tail_ref[2 * LEN :, :].astype(f32)
    for k, (rows, tail, pad, made, final) in enumerate(
        ((out_rows, out_tail, tok, made_out, final_out), (tg_rows, tg_tail, cot, made_tg, final_tg))
    ):
        if k:
            wait_all(copies[2:])
        for slot in range(SLOTS):
            here = slot_rows(slot)
            row = lax.broadcasted_iota(jnp.int32, (LEN, 1), 0) + slot * LEN
            value = rows_from(rows, LEN - lead + slot * LEN)
            if slot == 0:
                value = jnp.where(row < lead, tail, value)
            value = jnp.where(row < count, value, pad[here, :].astype(f32))
            made[here, :] = value.astype(made.dtype)
        last += fetch([(made, final)], sems, 4 + k)
    wait_all(last)


def shape(*dims, dtype=f32):
    return jax.ShapeDtypeStruct(dims, dtype)


def call(kernel, outs, scratch, mib, ins, spaces, after=(), out_specs=None, us=0, zeros=False):
    taken, held, made = len(ins), len(after), len(outs)
    out_specs = out_specs or [VM] * made

    def body(*refs):
        first = taken + held
        kernel(*refs[:taken], *refs[first : first + made], *refs[first + made + 1 :])
        if zeros:
            refs[first + made][...] = jnp.zeros((8, 128), f32)

    def settled(item):
        is_token = item.shape == (8, 128) and item.dtype == f32
        return pltpu.with_memory_space_constraint(item, pltpu.HBM) if is_token else item

    def placed(item, spec):
        return pltpu.with_memory_space_constraint(item, pltpu.HBM) if spec is HBM else item

    out_specs = [*out_specs, VM if zeros else HBM]
    out_shape = [
        pltpu.HBM(item.shape, item.dtype) if spec is HBM else item
        for item, spec in zip([*outs, shape(8, 128)], out_specs)
    ]
    *results, token = pl.pallas_call(
        body,
        out_shape=out_shape,
        in_specs=list(spaces) + [ANY] * held,
        out_specs=out_specs,
        scratch_shapes=scratch,
        compiler_params=params(mib),
        cost_estimate=cost(us),
        name=getattr(kernel, "func", kernel).__name__,
    )(*[placed(item, spec) for item, spec in zip(ins, spaces)], *[settled(item) for item in after])
    return results, token


def tie(value, token):
    return jnp.where(token[0, 0] == 0.0, value, jnp.zeros_like(value))


def join(parts, after=(), us=0, zeros=False):
    rows = sum(part.shape[0] for part in parts)
    (both,), token = call(
        join_kernel,
        [shape(rows, parts[0].shape[1], dtype=parts[0].dtype)],
        [pltpu.SemaphoreType.DMA((len(parts),))],
        8,
        parts,
        [ANY] * len(parts),
        after=after,
        out_specs=[ANY],
        us=us,
        zeros=zeros,
    )
    return both, token


def tie(value, token):
    return jnp.where(token[0, 0] == 0.0, value, jnp.zeros_like(value))


def low(value):
    return value.astype(bf16)


class Links:
    def __init__(self, devices):
        self.devices = devices
        self.cube = devices == 32
        self.me = lax.axis_index("wide").astype(jnp.int32)
        self.core = self.me % 2 if self.cube else jnp.int32(0)
        self.chip = self.me // 2 if self.cube else jnp.int32(0)
        self.where = jnp.stack([self.chip, self.core, self.me])

    def swap(self, array, bits):
        return lax.ppermute(array, "wide", [(i, i ^ bits) for i in range(self.devices)])

    def by_core(self, first, second):
        return jnp.where(self.core == 0, first, second)

    def pair(self, mine, got):
        return self.by_core(
            jnp.concatenate([mine, got], axis=0), jnp.concatenate([got, mine], axis=0)
        )

    def along_z(self, pair):
        return jnp.concatenate(
            [pair, self.swap(pair, 8), self.swap(pair, 16), self.swap(pair, 24)], axis=0
        )

    def doubled_z(self, pair):
        two = jnp.concatenate([pair, self.swap(pair, 8)], axis=0)
        return jnp.concatenate([two, self.swap(two, 16)], axis=0)

    def gathered(self, shards):
        halves = [[], []]
        for shard in shards:
            whole = lax.all_gather(shard, "wide", axis=0, tiled=True)
            rows, width = whole.shape[0], whole.shape[1] // 2
            whole = whole.reshape(4, 4, rows // BLOCKS, -1).transpose(1, 0, 2, 3)
            whole = whole.reshape(rows, -1)
            halves[0].append(whole[:, :width])
            halves[1].append(whole[:, width:])
        return [jnp.concatenate(half, axis=1) for half in halves]

    def scattered(self, send, keep, widths):
        outs, first = [], 0
        rows = keep.shape[0]
        for width in widths:
            cols = slice(first, first + width)
            whole = jnp.concatenate([keep[:, cols], send[:, cols]], axis=1)
            whole = whole.reshape(4, 4, rows // BLOCKS, -1).transpose(1, 0, 2, 3)
            whole = whole.reshape(rows, -1).astype(f32)
            outs.append(lax.psum_scatter(whole, "wide", scatter_dimension=0, tiled=True))
            first += width
        return outs

    def scattered_rows(self, send, keep):
        whole = jnp.stack([keep, send]).reshape(2, 4, 4, -1, D)
        whole = whole.transpose(2, 1, 0, 3, 4).reshape(-1, D)
        return lax.psum_scatter(whole.astype(f32), "wide", scatter_dimension=0, tiled=True)

    def gathered_rows(self, shard):
        whole = lax.all_gather(shard, "wide", axis=0, tiled=True).reshape(4, 4, 2, -1, D)
        return [whole[:, :, half].transpose(1, 0, 2, 3).reshape(-1, D) for half in range(2)]

    def first(self, keep, got, after, copied=False):
        rows, width = keep.shape[0] // 4, keep.shape[1]
        (x, y), token = call(
            first_kernel,
            [shape(rows, width, dtype=bf16)] * 2,
            [pltpu.VMEM((2 * rows, width), bf16), pltpu.SemaphoreType.DMA((8,))]
            + [pltpu.VMEM((2 * rows, width), bf16)] * copied,
            16,
            [keep, got],
            [HBM, HBM if copied else VM],
            after=after,
        )
        return [self.swap(x, 2), self.swap(y, 4)], token

    def second(self, keep, got, ones, after, copied=False):
        rows, width = keep.shape[0] // 8, keep.shape[1]
        (x, y), token = call(
            second_kernel,
            [shape(rows, width, dtype=bf16)] * 2,
            [pltpu.VMEM((2 * rows, width), bf16), pltpu.SemaphoreType.DMA((4,))]
            + [pltpu.VMEM((2 * rows, width), bf16)] * copied,
            16,
            [keep, got, *ones],
            [HBM, HBM if copied else VM, VM, VM],
            after=after,
            us=100,
        )
        return [self.swap(x, 2), self.swap(y, 4)], token

    def near_sum(self, keep, got, ones, twos, direct, after):
        tall, width = keep.shape[0] // 4, keep.shape[1]
        rows = tall // 4
        if direct:
            outs = [shape(rows, width)] + [shape(rows, width, dtype=bf16)] * 3
        else:
            outs = [shape(2 * rows, width, dtype=bf16)] + [shape(rows, width)] * 2
        scratch = [pltpu.VMEM((tall, width), bf16), pltpu.SemaphoreType.DMA((4,))]
        scratch += [pltpu.VMEM((tall, width), bf16)] * direct
        if not direct:
            scratch += [pltpu.VMEM((rows, width), f32)] * 2 + [pltpu.SemaphoreType.DMA((2,))]
        return call(
            functools.partial(near_kernel, direct),
            outs,
            scratch,
            16,
            [keep, got, *ones, *twos],
            [HBM, HBM if direct else VM] + [VM] * 4,
            after=after,
            out_specs=[VM] * 4 if direct else [VM, HBM, HBM],
            us=100,
        )

    def z_sum(self, token, own, *parts):
        own = tie(own, token)
        for part, bits in zip(parts, (8, 16, 24)):
            own = own + self.swap(part, bits).astype(f32)
        return own

    def halved_z(self, send, own, beyond, after):
        (send, total), token = call(
            beyond_kernel,
            [shape(*own.shape, dtype=bf16), shape(*own.shape)],
            [pltpu.VMEM(own.shape, f32)] * 2 + [pltpu.SemaphoreType.DMA((3,))],
            8,
            [self.swap(send, 8), own, beyond],
            [VM, HBM, HBM],
            after=after,
            out_specs=[VM, HBM],
        )
        return total, self.swap(send, 16), token

    def own_rows(self, own, widths):
        rows = own.shape[0] // 2
        mine = self.by_core(own[:rows], own[rows:])
        got = self.swap(self.by_core(own[rows:], own[:rows]), 1)
        outs, first = [], 0
        for width in widths:
            a, b = mine[:, first : first + width], got[:, first : first + width]
            outs.append(
                self.by_core(jnp.concatenate([a, b], axis=1), jnp.concatenate([b, a], axis=1))
            )
            first += width
        return outs


def on_device(
    tokens,
    cotangent,
    cond,
    kept,
    counts,
    ada_w,
    ada_bias,
    qkv_w,
    q_bias,
    v_bias,
    proj_w,
    proj_bias,
    fc1_w,
    fc1_bias,
    fc2_w,
    fc2_bias,
):
    devices = lax.axis_size("wide")
    images = cond.shape[0]
    span = ada_bias.shape[0]
    own_dim = ada_w.shape[0]
    links = Links(devices)
    me, where, cube = links.me, links.where, links.cube
    rows = TOK_DEV
    dma = pltpu.SemaphoreType.DMA
    half_sum = (qkv_w.shape[1] + proj_w.shape[1] + fc1_w.shape[1]) // 2

    (mine, send, edge, place, starts, cond_slots, ada_parts), _ = call(
        begin_kernel,
        [
            shape(own_dim, half_sum, dtype=bf16),
            shape(own_dim, half_sum, dtype=bf16),
            shape(2 * LEN, D, dtype=bf16),
            shape(8, dtype=jnp.int32),
            shape(devices, dtype=jnp.int32),
            shape(devices * 8, D, dtype=bf16),
            shape(devices, own_dim, span, dtype=bf16),
        ],
        [
            pltpu.VMEM((devices * 8, images), f32),
            pltpu.VMEM(cond.shape, bf16),
            pltpu.VMEM(ada_w.shape, bf16),
            dma((10,)),
        ],
        16,
        [where, counts, cond, ada_w, tokens, cotangent, qkv_w, proj_w, fc1_w],
        [SM, SM] + [HBM] * 7,
        out_specs=[VM, VM, VM, SM, SM, VM, VM],
    )
    if cube:
        pair = links.pair(mine, links.swap(send, 1))
        near_one = links.along_z(pair[:, : 3 * D // 2])
        before_mod = [pair]
    else:
        before_mod = []
    halo = lax.ppermute(edge, "wide", [(i + 1, i) for i in range(devices - 1)])

    ada_cols = lax.all_to_all(ada_parts, "wide", 0, 0, tiled=True)
    ada_cols = ada_cols.reshape(D, span)
    lanes = lambda items: jnp.pad(
        jnp.concatenate(items), (0, span - sum(i.shape[0] for i in items))
    ).reshape(1, span)
    addend = jnp.concatenate(
        [
            jnp.broadcast_to(ada_bias.reshape(1, span), (SLOTS, span)),
            lanes([q_bias, v_bias, proj_bias, fc2_bias]),
            lanes([fc1_bias]),
            jnp.zeros((2, span), bf16),
        ],
        axis=0,
    ).astype(f32)
    (mod_cols,), mod_ran = call(
        mod_kernel,
        [shape(devices, 8, span)],
        [],
        16,
        [cond_slots, ada_cols, addend],
        [VM] * 3,
        after=before_mod,
        zeros=True,
    )
    mixed = lax.all_to_all(mod_cols, "wide", 0, 0, tiled=True)

    quarter = D // 4
    frequency = jnp.exp(-math.log(10000.0) * jnp.arange(quarter).astype(f32) / quarter)
    angle = jnp.arange(GRID).astype(f32)[:, None] * frequency[None, :]
    table = jnp.concatenate([jnp.sin(angle), jnp.cos(angle)], axis=1)
    if cube:
        near_one = tie(near_one, mod_ran)
        over = [links.swap(near_one, bits) for bits in (2, 4, 6)]
        pair_two = tie(pair[:, 3 * D // 2 :], mod_ran)
        two = jnp.concatenate([pair_two, links.swap(pair_two, 8)], axis=0)
        before_prep = [near_one, two]
    else:
        before_prep = []
    (residual, grad_out, mod, qkv_bias, proj_bias_all, fc2_bias_all, fc1_bias_all), prepared = call(
        prep_kernel,
        [
            shape(rows, D),
            shape(rows, D, dtype=bf16),
            shape(SLOTS, 6 * D),
            shape(1, 3 * D),
            shape(1, D),
            shape(1, D),
            shape(1, F),
        ],
        [
            pltpu.VMEM((rows, D), bf16),
            pltpu.VMEM((rows, D), bf16),
            pltpu.VMEM((2 * LEN, D), bf16),
            pltpu.VMEM(kept.shape, jnp.int32),
            pltpu.VMEM(table.shape, f32),
            dma((5,)),
        ],
        16,
        [place, mixed, tokens, cotangent, halo, kept, table],
        [SM, VM, HBM, HBM, ANY, HBM, ANY],
        after=before_prep,
        us=10,
    )

    if cube:
        near_two = jnp.concatenate([two, links.swap(two, 16)], axis=0)
        qkv_near, joined = join([near_one, *over], [prepared, near_two])
        qkv_far = links.swap(qkv_near, 1)
        over_x, over_y = links.swap(near_two, 2), links.swap(near_two, 4)
        before_qkv = []
    else:
        qkv_near, qkv_far = links.gathered([qkv_w])
        before_qkv = []

    (attn_in, qkv, qkv_laid), qkv_ran = call(
        qkv_kernel,
        [
            shape(rows, D, dtype=bf16),
            shape(rows, 3 * D, dtype=bf16),
            shape(D, 3 * D, dtype=bf16),
        ],
        [pltpu.VMEM((rows, D), bf16), pltpu.VMEM((D, 3 * D), bf16), dma((2,))],
        16,
        [where, residual, mod, qkv_bias, qkv_near, qkv_far],
        [SM] + [VM] * 5,
        after=before_qkv,
        out_specs=[HBM, VM, HBM],
        zeros=True,
    )
    before_attend = [qkv_ran]
    if cube:
        two = tie(jnp.concatenate([fc2_w, links.swap(fc2_w, 8)], axis=0), qkv_ran)
        before_attend.append(two)
        near_three = jnp.concatenate([two, links.swap(two, 16)], axis=0)
    (attended, attended_kept), attend_ran = call(
        attend_kernel,
        [shape(rows, D, dtype=bf16)] * 2,
        [dma((1,))],
        16,
        [qkv],
        [VM],
        after=before_attend,
        out_specs=[VM, HBM],
        zeros=True,
    )
    if cube:
        half = near_two.shape[0] // 2
        most, _ = join([near_two, over_x, over_y], [attend_ran, near_three])
        most_far = links.swap(most, 1)
        cuts = [slice(i * half // 2, (i + 1) * half // 2) for i in range(4)]
        diag = [links.swap(tie(over_y[cut], attend_ran), 2) for cut in cuts[:2]]
        diag += [links.swap(tie(over_x[cut], attend_ran), 4) for cut in cuts[2:]]
        diag, joined = join(diag, zeros=True)
        mid_halves = [most, diag, most_far, links.swap(diag, 1)]
        near_three = tie(near_three, joined)
        over = [links.swap(near_three, bits) for bits in (2, 4, 6)]
    else:
        mid_near, mid_far = links.gathered([proj_w, fc1_w])
        cut = 3 * D // 4
        mid_halves = [mid_near[:cut], mid_near[cut:], mid_far[:cut], mid_far[cut:]]
        fc2_near, fc2_far = links.gathered_rows(fc2_w)

    (
        branch, middle, mlp_in, grad_mlp_out, fc2_bias_sum, activated, slope, fc2_send, fc2_keep,
        middle_kept,
    ), hidden_ran = call(
        hidden_kernel,
        [
            shape(rows, D),
            shape(rows, D),
            shape(rows, D, dtype=bf16),
            shape(rows, D, dtype=bf16),
            shape(1, D),
            shape(rows, F, dtype=bf16),
            shape(rows, F, dtype=bf16),
            shape(F // 2, D, dtype=bf16),
            shape(F // 2, D, dtype=bf16),
            shape(rows, D),
        ],
        [
            pltpu.VMEM((D, D), bf16),
            pltpu.VMEM((D, F), bf16),
            pltpu.VMEM((rows, F), bf16),
            pltpu.VMEM((rows, F), bf16),
            pltpu.VMEM((F, rows), bf16),
            pltpu.VMEM((F, D), bf16),
            dma((9,)),
        ],
        32,
        [where, residual, attended, mod, grad_out, proj_bias_all, fc1_bias_all, *mid_halves],
        [SM] + [VM] * 10,
        out_specs=[VM] * 5 + [HBM] * 5,
    )
    def weight_grad(*pairs, after=()):
        half = sum(right.shape[1] for _, right in pairs) // 2
        scratch = [
            pltpu.VMEM((D, rows), bf16),
            pltpu.VMEM((D, half), bf16),
            pltpu.VMEM((D, half), bf16),
            dma((8,)),
        ]
        spaces = [VM, VM]
        if len(pairs) == 2:
            scratch += [pltpu.VMEM((rows, D), bf16)] * 3 + [dma((3,))]
            spaces = [HBM, HBM, HBM, VM]
        return call(
            functools.partial(wgrad_kernel, len(pairs)),
            [shape(D, half, dtype=bf16)] * 2,
            scratch,
            20,
            [where, *[left for left, _ in pairs], *[right for _, right in pairs]],
            [SM, *spaces],
            after=after,
            out_specs=[HBM] * 2,
        )

    if cube:
        fc2_got = links.swap(fc2_send, 1)
        fc2_near, gathered = join([near_three, *over], [hidden_ran], us=100)
        fc2_far = links.swap(fc2_near, 1)
        fc2_ones, fc2_first = links.first(fc2_keep, fc2_got, [gathered])
        before_fc2 = [fc2_first]
    else:
        before_fc2 = []
    (grad_hidden, fc1_bias_sum), _ = call(
        fc2_back_kernel,
        [shape(rows, F, dtype=bf16), shape(1, F)],
        [pltpu.VMEM((F, D), bf16), pltpu.VMEM((rows, F), bf16), dma((6,))],
        20,
        [where, grad_mlp_out, slope, fc2_near, fc2_far],
        [SM, VM, HBM, VM, VM],
        after=before_fc2,
    )
    (fc1_send, fc1_keep), fc1_ran = weight_grad((mlp_in, grad_hidden))
    (out_tail, gate_two_sum, result), out_ran = call(
        fc2_out_kernel,
        [shape(LEN, D, dtype=bf16), shape(SLOTS, D), shape(rows, D, dtype=bf16)],
        [
            pltpu.VMEM((rows, D), f32),
            pltpu.VMEM((rows, F), bf16),
            pltpu.VMEM((F, D), bf16),
            pltpu.VMEM((rows + LEN + 8, D), f32),
            pltpu.VMEM((rows, D), bf16),
            dma((3,)),
        ],
        20,
        [where, place, mod, grad_out, fc2_bias_all, middle_kept, activated, fc2_near, fc2_far],
        [SM] * 2 + [VM] * 3 + [HBM] * 2 + [VM] * 2,
        after=[fc1_ran],
        out_specs=[VM] * 2 + [HBM],
    )
    if cube:
        fc1_got = links.swap(fc1_send, 1)
        fc2_twos, fc2_second = links.second(fc2_keep, fc2_got, fc2_ones, [out_ran])
        before_mid = [fc2_second]
    else:
        before_mid = [out_ran]
    (grad_attended, proj_bias_sum, grad_middle, grad_branch, early), mid_ran = call(
        mid_back_kernel,
        [
            shape(rows, D, dtype=bf16),
            shape(1, D),
            shape(rows, D),
            shape(rows, D, dtype=bf16),
            shape(devices, 16, D, dtype=bf16),
        ],
        [
            pltpu.VMEM((rows, D), f32),
            pltpu.VMEM((rows, D), bf16),
            pltpu.VMEM((devices, 16, D), bf16),
            pltpu.VMEM((D, D), bf16),
            pltpu.VMEM((D, F), bf16),
            pltpu.VMEM((rows, D), f32),
            pltpu.VMEM((16, D), f32),
            dma((3,)),
        ],
        20,
        [where, grad_hidden, middle, branch, mod, grad_out, gate_two_sum, *mid_halves],
        [SM] + [VM] * 10,
        out_specs=[VM] * 2 + [HBM] * 3,
        after=before_mid,
    )
    early = lax.all_to_all(early, "wide", 0, 0, tiled=True)
    if cube:
        fc1_ones, fc1_first = links.first(fc1_keep, fc1_got, [mid_ran])
        fc2_near_sum, fc2_summed = links.near_sum(
            fc2_keep, fc2_got, fc2_ones, fc2_twos, False, [fc1_first]
        )
        before_back = [fc2_summed]
    else:
        before_back = []
    (grad_qkv, qkv_bias_sum), back_ran = call(
        attend_back_kernel,
        [shape(rows, 3 * D, dtype=bf16), shape(1, 3 * D)],
        [pltpu.VMEM((rows, 3 * D), bf16), dma((SLOTS,))],
        16,
        [qkv, grad_attended],
        [HBM, VM],
        after=before_back,
    )
    before_qkv = []
    if cube:
        fc2_own, fc2_beyond, fc2_halved = links.halved_z(*fc2_near_sum, [back_ran])
        fc1_twos, fc1_second = links.second(fc1_keep, fc1_got, fc1_ones, [fc2_halved])
        before_qkv.append(fc1_second)
    (qkv_send, qkv_keep), qkv_grad_ran = weight_grad(
        (attended_kept, grad_branch), (attn_in, grad_qkv), after=before_qkv
    )
    if cube:
        qkv_got = links.swap(qkv_send, 1)
    if cube:
        fc1_near_sum, fc1_summed = links.near_sum(
            fc1_keep, fc1_got, fc1_ones, fc1_twos, False, [qkv_grad_ran]
        )
        qkv_ones, qkv_first = links.first(qkv_keep, qkv_got, [fc1_summed])
        before_start = [qkv_first, early]
    else:
        before_start = [qkv_grad_ran]
    (tokens_back, tail, late), start_ran = call(
        start_back_kernel,
        [shape(rows, D), shape(3 * LEN, D, dtype=bf16), shape(devices, 2 * SLOTS, D, dtype=bf16)],
        [
            pltpu.VMEM((D, 3 * D), bf16),
            pltpu.VMEM((rows + LEN + 8, D), f32),
            pltpu.VMEM((rows, D), f32),
            pltpu.VMEM((rows, D), f32),
            pltpu.VMEM((2 * SLOTS, D), f32),
            pltpu.VMEM((3 * LEN, D), bf16),
            pltpu.VMEM((devices, 2 * SLOTS, D), bf16),
            dma((5,)),
            dma((SLOTS + 2,)),
        ],
        24,
        [place, grad_qkv, mod, out_tail, residual, grad_middle, qkv_laid],
        [SM] + [VM] * 3 + [HBM] * 3,
        after=before_start,
        out_specs=[HBM] * 3,
    )
    late = lax.all_to_all(late, "wide", 0, 0, tiled=True)

    if cube:
        fc1_own, fc1_beyond, fc1_halved = links.halved_z(*fc1_near_sum, [start_ran])
        qkv_twos, qkv_second = links.second(qkv_keep, qkv_got, qkv_ones, [fc1_halved], True)
        before_ada = [qkv_second]
    else:
        before_ada = [start_ran]

    onward = [(i, i + 1) for i in range(devices - 1)]
    tail = lax.ppermute(tail, "wide", onward)
    wide_images = -(-images // 128) * 128
    (ada_grad, ada_bias_sum, last), ada_ran = call(
        ada_kernel,
        [
            shape(own_dim, 6 * D),
            shape(1, 6 * D),
            shape(devices, own_dim + 8, wide_images, dtype=bf16),
        ],
        [pltpu.VMEM((devices * 16, images), f32), pltpu.VMEM((own_dim + 8, wide_images), f32)],
        24,
        [where, starts, early, late, ada_w, cond, qkv_bias_sum, proj_bias_sum, fc2_bias_sum, fc1_bias_sum],
        [SM] * 2 + [VM] * 8,
        after=before_ada,
        zeros=True,
    )
    last = lax.all_to_all(last, "wide", 0, 0, tiled=True)
    if cube:
        qkv_near_sum, qkv_summed = links.near_sum(
            qkv_keep, qkv_got, qkv_ones, qkv_twos, True, [ada_ran]
        )
        before_place = [qkv_summed]
    else:
        before_place = [ada_ran]
    (out, tokens_grad), placed = call(
        place_kernel,
        [shape(rows, D, dtype=bf16), shape(rows, D)],
        [
            pltpu.VMEM((rows + LEN + 8, D), f32),
            pltpu.VMEM((rows + LEN + 8, D), f32),
            pltpu.VMEM((rows, D), bf16),
            pltpu.VMEM((rows, D), bf16),
            pltpu.VMEM((rows, D), bf16),
            pltpu.VMEM((rows, D), bf16),
            pltpu.VMEM((rows, D), f32),
            dma((6,)),
        ],
        16,
        [place, tail, tokens, cotangent, result, tokens_back],
        [SM, VM] + [HBM] * 4,
        after=before_place,
        out_specs=[HBM] * 2,
    )


    (cond_grad, bias_grads), finished = call(
        finish_kernel,
        [shape(images, D), shape(8, wide_images)],
        [pltpu.VMEM((D, wide_images), f32)],
        16,
        [last],
        [VM],
        after=[placed],
        zeros=True,
    )
    fc1_widths, qkv_widths = [F // 2], [D // 2, 3 * D // 2]
    if cube:
        fc2_grad = tie(fc2_own, finished) + fc2_beyond.astype(f32)
        (fc1_grad,) = links.own_rows(
            tie(fc1_own, ada_ran) + fc1_beyond.astype(f32), fc1_widths
        )
        proj_grad, qkv_grad = links.own_rows(links.z_sum(finished, *qkv_near_sum), qkv_widths)
    else:
        fc2_grad = links.scattered_rows(fc2_send, fc2_keep)
        (fc1_grad,) = links.scattered(fc1_send, fc1_keep, fc1_widths)
        proj_grad, qkv_grad = links.scattered(qkv_send, qkv_keep, qkv_widths)
    bias_grads = bias_grads[:, :own_dim]
    ada_bias_grad = lax.dynamic_slice_in_dim(ada_bias_sum[0], me * span, span, 0)
    return (
        out,
        tokens_grad,
        cond_grad,
        ada_grad,
        ada_bias_grad,
        qkv_grad,
        bias_grads[0],
        bias_grads[1],
        proj_grad,
        bias_grads[2],
        fc1_grad,
        bias_grads[4:].reshape(-1),
        fc2_grad,
        bias_grads[3],
    )


def solution(mesh):
    row, flat = P("wide", None), P("wide")
    return jax.shard_map(
        on_device,
        mesh=mesh,
        in_specs=(row, row, P(), P(), P(), row, flat, row, flat, flat, row, flat, row, flat, row, flat),
        out_specs=(row, row, P(), row, flat, row, flat, flat, row, flat, row, flat, row, flat),
        check_vma=False,
    )
```

```python
import functools
import math

import jax
import jax.numpy as jnp
from jax import lax
from jax.experimental import pallas as pl
from jax.experimental.pallas import tpu as pltpu
from jax.sharding import PartitionSpec as P

D = 768
HEADS = 12
HD = 64
GRID = 16
LEN = 128
TOK_DEV = 512
SLOTS = TOK_DEV // LEN
F = 3072
BLOCKS = 16
NEAR_FIRST, FAR_FIRST = (0, 1, 2, 3), (0, 2, 1, 3)

NORM_EPS = 1e-06
GELU_COEF = 0.7978845608028654

f32 = jnp.float32
bf16 = jnp.bfloat16

VM = pl.BlockSpec(memory_space=pltpu.VMEM)
SM = pl.BlockSpec(memory_space=pltpu.SMEM)
ANY = pl.BlockSpec(memory_space=pl.ANY)
HBM = pl.BlockSpec(memory_space=pltpu.HBM)


def params(mib):
    return pltpu.CompilerParams(vmem_limit_bytes=mib * 1024 * 1024)


def cost(us):
    return pl.CostEstimate(flops=max(1, int(us * 1e9)), bytes_accessed=1, transcendentals=0)


def dot(left, right):
    return jnp.dot(left, right, preferred_element_type=f32)


def dot_nt(left, right):
    return lax.dot_general(left, right, (((1,), (1,)), ((), ())), preferred_element_type=f32)


def dot_tn(left, right):
    return lax.dot_general(left, right, (((0,), (0,)), ((), ())), preferred_element_type=f32)


def silu(values):
    return values / (1.0 + jnp.exp(-values))


def norm_parts(values):
    centred = values - jnp.mean(values, axis=-1, keepdims=True)
    spread = jnp.mean(centred * centred, axis=-1, keepdims=True)
    inverse = lax.rsqrt(spread + NORM_EPS)
    return centred * inverse, inverse


def norm_back(normed, inverse, scale_part, grad):
    t = grad * (1.0 + scale_part)
    mean_t = jnp.mean(t, axis=-1, keepdims=True)
    mean_tn = jnp.mean(t * normed, axis=-1, keepdims=True)
    return (t - mean_t - normed * mean_tn) * inverse


def rows_from(ref, start):
    base = pl.multiple_of(start // 8 * 8, 8)
    shift = start - base
    tall = LEN + 8
    turned = pltpu.roll(ref[pl.ds(base, tall), :], jnp.where(shift == 0, 0, tall - shift), 0)
    return turned[:LEN]


def slot_rows(slot):
    return slice(slot * LEN, (slot + 1) * LEN)


def mod_part(mod_ref, slot, part):
    return mod_ref[slot : slot + 1, part * D : (part + 1) * D]


def place_of(block, chip):
    rel = jnp.bitwise_xor(block, chip)
    return jnp.bitwise_and(rel, 3) * 4 + lax.shift_right_logical(rel, 2)


def lay_out(where_ref, halves, rows, targets, z_order, split_rows=False):
    chip, core = where_ref[0], where_ref[1]
    for side in range(2):
        half = core if side == 0 else 1 - core
        place = 0
        for ref in halves[side]:
            for spot in range(ref.shape[0] // rows):
                block = jnp.bitwise_xor(z_order[place % 4] * 4 + place // 4, chip)
                place += 1
                for target, first, width in targets:
                    if split_rows:
                        to_row, to_col = (2 * block + half) * rows, 0
                    else:
                        to_row, to_col = block * rows, pl.multiple_of(half * width, 128)
                    to_row = pl.multiple_of(to_row, 16)
                    target[pl.ds(to_row, rows), pl.ds(to_col, width)] = ref[
                        spot * rows : (spot + 1) * rows, first : first + width
                    ]


def start_all(copies):
    for copy in copies:
        copy.start()
    return copies


def fetch(pairs, sems, first=0):
    return start_all(
        [pltpu.make_async_copy(a, b, sems.at[first + i]) for i, (a, b) in enumerate(pairs)]
    )


def wait_all(copies):
    for copy in copies:
        copy.wait()


def begin_kernel(
    where_ref, counts_ref, cond_in, ada_in, tok_in, cot_in, qkv_in, proj_in, fc1_in,
    mine_ref, send_ref, edge_ref, place_ref, starts_ref, slots_ref, parts_ref,
    wide, cond, ada, sems,
):
    devices = counts_ref.shape[0]
    images = cond.shape[0]
    core, me = where_ref[1], where_ref[2]
    copies = []
    first = 0
    for ref in (qkv_in, proj_in, fc1_in):
        half = ref.shape[1] // 2
        for out, at in ((send_ref, 1 - core), (mine_ref, core)):
            copies.append(
                (
                    ref.at[:, pl.ds(pl.multiple_of(at * half, 128), half)],
                    out.at[:, pl.ds(first, half)],
                )
            )
        first += half
    copies.append((tok_in.at[pl.ds(0, LEN), :], edge_ref.at[pl.ds(0, LEN), :]))
    copies.append((cot_in.at[pl.ds(0, LEN), :], edge_ref.at[pl.ds(LEN, LEN), :]))
    copies = fetch([*copies, (cond_in, cond), (ada_in, ada)], sems)

    def step(d, first_row):
        count = counts_ref[d]
        begin = (first_row + LEN - 1) // LEN
        starts_ref[d] = begin

        @pl.when(d == me)
        def _():
            lead = begin * LEN - first_row
            place_ref[0] = lead
            place_ref[1] = count
            place_ref[2] = (first_row + count + LEN - 1) // LEN - begin
            place_ref[3] = count - lead
            place_ref[4] = begin

        return first_row + count

    lax.fori_loop(0, devices, step, jnp.int32(0))
    sub = lax.broadcasted_iota(jnp.int32, (8, images), 0)
    lane = lax.broadcasted_iota(jnp.int32, (8, images), 1)

    @pl.loop(0, devices)
    def _(d):
        hit = (lane == starts_ref[d] + sub) & (sub < SLOTS)
        wide[pl.ds(pl.multiple_of(d * 8, 8), 8), :] = jnp.where(hit, 1.0, 0.0)

    wait_all(copies)
    span = parts_ref.shape[2]
    for d in range(devices):
        parts_ref[d] = ada[:, d * span : (d + 1) * span]
    act = silu(cond[...].astype(f32)).astype(bf16)
    slots_ref[...] = dot(wide[...].astype(bf16), act).astype(bf16)


def ada_kernel(
    where_ref, starts_ref, early_ref, late_ref, ada_ref, cond_ref,
    qkv_sum_ref, proj_sum_ref, fc2_sum_ref, fc1_sum_ref,
    grad_ref, colsum_ref, last_ref, wide, packed,
):
    devices = early_ref.shape[0]
    images, own = cond_ref.shape[0], ada_ref.shape[0]
    me = where_ref[2]
    row = lax.broadcasted_iota(jnp.int32, (own, D), 0)
    lane = lax.broadcasted_iota(jnp.int32, (own, D), 1)
    chosen = jnp.where(lane == me * own + row, 1.0, 0.0).astype(bf16)
    act = silu(cond_ref[...].astype(f32)).astype(bf16)
    act_own = dot_nt(act, chosen).astype(bf16)
    cond_own = dot_nt(chosen, cond_ref[...])
    total = jnp.zeros((own, images), f32)
    for ref, parts in ((early_ref, (2, 3, 4, 5)), (late_ref, (0, 1))):
        many = len(parts)
        high = many * SLOTS
        tall = devices * high
        sub = lax.broadcasted_iota(jnp.int32, (high, images), 0)
        lane = lax.broadcasted_iota(jnp.int32, (high, images), 1)

        @pl.loop(0, devices)
        def _(d):
            hit = lane == starts_ref[d] + sub % SLOTS
            wide[pl.ds(pl.multiple_of(d * high, high), high), :] = jnp.where(hit, 1.0, 0.0)

        picker = wide[0:tall, :]
        act_rows = dot(picker.astype(bf16), act_own)
        part_down = lax.broadcasted_iota(jnp.int32, (tall, 1), 0) % high // SLOTS
        part_across = lax.broadcasted_iota(jnp.int32, (1, tall), 1) % high // SLOTS
        act_parts = jnp.concatenate(
            [jnp.where(part_down == i, act_rows, 0.0) for i in range(many)], axis=1
        ).astype(bf16)
        ours = lax.broadcasted_iota(jnp.int32, (8, tall), 0) == part_across
        ours = jnp.where(ours, 1.0, 0.0).astype(bf16)
        sums = ref[...].reshape(tall, D)
        grads = dot_tn(act_parts, sums)
        colsums = dot(ours, sums)
        back = jnp.zeros((own, tall), f32)
        for i, part in enumerate(parts):
            cols = slice(part * D, (part + 1) * D)
            grad_ref[:, cols] = grads[i * own : (i + 1) * own]
            colsum_ref[:, cols] = colsums[i : i + 1]
            back += jnp.where(part_across == i, dot_nt(ada_ref[:, cols], sums), 0.0)
        total += jnp.dot(back, picker, precision=lax.Precision.HIGHEST)
    gate = 1.0 / (1.0 + jnp.exp(-cond_own))
    total = total * (gate * (1.0 + cond_own * (1.0 - gate)))
    lanes = last_ref.shape[2]
    fc1_sum = fc1_sum_ref[...]
    both = qkv_sum_ref[...]
    vectors = [both[:, :D], both[:, 2 * D :], proj_sum_ref[...], fc2_sum_ref[...]]
    for d in range(devices):
        packed[...] = jnp.zeros(packed.shape, f32)
        packed[0:own, 0:images] = total
        for j in range(8):
            if j < 4:
                value = vectors[j][:, d * own : (d + 1) * own]
            else:
                at = (4 * d + j - 4) * own
                value = fc1_sum[:, at : at + own]
            packed[own + j : own + j + 1, 0:own] = value
        last_ref[d] = packed[...].astype(bf16)


def finish_kernel(got_ref, cond_ref, bias_ref, tall):
    devices, rows, _ = got_ref.shape
    own = rows - 8
    total = None
    for d in range(devices):
        got = got_ref[d].astype(f32)
        tall[d * own : (d + 1) * own, :] = got[0:own]
        total = got[own:rows] if total is None else total + got[own:rows]
    cond_ref[...] = tall[...].T[0 : cond_ref.shape[0], :]
    bias_ref[...] = total


def mod_kernel(slots_ref, cols_ref, addend_ref, out_ref):
    value = dot(slots_ref[...], cols_ref[...])
    for d in range(out_ref.shape[0]):
        out_ref[d] = value[d * 8 : (d + 1) * 8, :] + addend_ref[...]


def prep_kernel(
    place_ref, got_ref, tok_in, cot_in, halo_in, kept_in, table_in,
    res_ref, gc_ref, mod_ref, qkv_bias_ref, proj_bias_ref, fc2_bias_ref, fc1_bias_ref,
    tok, cot, halo, kept, table, sems,
):
    copies = fetch(
        [(table_in, table), (kept_in, kept), (halo_in, halo), (tok_in, tok), (cot_in, cot)], sems
    )
    devices, _, span = got_ref.shape
    width = D // devices
    qkv_bias_ref[:, D : 2 * D] = jnp.zeros((1, D), f32)
    for d in range(devices):
        got = got_ref[d]
        mod_ref[:, d * span : (d + 1) * span] = got[0:SLOTS]
        cols = slice(d * width, (d + 1) * width)
        qkv_bias_ref[:, cols] = got[4:5, 0:width]
        qkv_bias_ref[:, 2 * D + d * width : 2 * D + (d + 1) * width] = got[4:5, width : 2 * width]
        proj_bias_ref[:, cols] = got[4:5, 2 * width : 3 * width]
        fc2_bias_ref[:, cols] = got[4:5, 3 * width : 4 * width]
        fc1_bias_ref[:, d * 4 * width : (d + 1) * 4 * width] = got[5:6, 0 : 4 * width]
    lead, count, slots, begin = place_ref[0], place_ref[1], place_ref[2], place_ref[4]
    wait_all(copies)
    angles = table[...]
    high = angles.astype(bf16)
    rest = angles - high.astype(f32)
    middle = rest.astype(bf16)
    lowest = (rest - middle.astype(f32)).astype(bf16)
    images = kept.shape[0]
    sub = lax.broadcasted_iota(jnp.int32, (8, images), 0)
    lane = lax.broadcasted_iota(jnp.int32, (8, images), 1)
    picker = jnp.where(lane == begin + sub, 1.0, 0.0).astype(bf16)
    patches = dot(picker, kept[...].astype(f32).astype(bf16)).astype(jnp.int32)
    for slot in range(SLOTS):
        row = lax.broadcasted_iota(jnp.int32, (LEN, TOK_DEV), 0) + slot * LEN
        source = row + lead
        live = slot < slots
        column = lax.broadcasted_iota(jnp.int32, (LEN, TOK_DEV), 1)
        own = jnp.where((column == source) & (source < count) & live, 1.0, 0.0).astype(bf16)
        far = source[:, :LEN] - count
        spill = jnp.where((column[:, :LEN] == far) & live, 1.0, 0.0).astype(bf16)
        taken = dot(own, tok[...]) + dot(spill, halo[0:LEN, :])
        grad = dot(own, cot[...]) + dot(spill, halo[LEN : 2 * LEN, :])
        gc_ref[slot_rows(slot), :] = grad.astype(bf16)
        patch = patches[slot : slot + 1, :]
        index = lax.broadcasted_iota(jnp.int32, (GRID, LEN), 0)
        line = jnp.where((index == patch // GRID) & live, 1.0, 0.0).astype(bf16)
        across = jnp.where((index == patch % GRID) & live, 1.0, 0.0).astype(bf16)
        half = D // 2
        for start, picked in ((0, line), (half, across)):
            spot = dot_tn(picked, high) + (dot_tn(picked, middle) + dot_tn(picked, lowest))
            res_ref[slot_rows(slot), start : start + half] = taken[:, start : start + half] + spot


def head_masks():
    lane = lax.broadcasted_iota(jnp.int32, (1, 2 * HD), 1)
    first = jnp.where(lane < HD, 1.0, 0.0).astype(bf16)
    return first, (1.0 - first.astype(f32)).astype(bf16)


def both_heads(pair, masks):
    return jnp.concatenate([pair * masks[0], pair * masks[1]], axis=0)


def side_by_side(stacked):
    return jnp.concatenate([stacked[:LEN], stacked[LEN:]], axis=1)


def pair_probs(queries, keys):
    scores = dot_nt(queries, keys) * (1.0 / math.sqrt(HD))
    exp_terms = jnp.exp(scores - jnp.max(scores, axis=1, keepdims=True))
    return exp_terms * (1.0 / jnp.sum(exp_terms, axis=1, keepdims=True))


def qkv_kernel(
    where_ref, res_ref, mod_ref, bias_ref, near_ref, far_ref, ain_out, qkv_ref, weight_out, ain_ref, weight, sems
):
    for slot in range(SLOTS):
        normed, _ = norm_parts(res_ref[slot_rows(slot), :])
        ain_ref[slot_rows(slot), :] = (
            normed * (1.0 + mod_part(mod_ref, slot, 1)) + mod_part(mod_ref, slot, 0)
        ).astype(bf16)
    out = fetch([(ain_ref, ain_out)], sems)
    lay_out(where_ref, ([near_ref], [far_ref]), D // BLOCKS, [(weight, 0, 3 * D // 2)], NEAR_FIRST)
    out += fetch([(weight, weight_out)], sems, 1)

    @pl.loop(0, 3 * D // 256)
    def _(j):
        cols = pl.ds(pl.multiple_of(j * 256, 256), 256)
        qkv_ref[:, cols] = (dot(ain_ref[...], weight[:, cols]) + bias_ref[:, cols]).astype(bf16)

    wait_all(out)


def attend_kernel(qkv_ref, att_ref, att_out, sems):
    masks = head_masks()

    @pl.loop(0, SLOTS)
    def _(slot):
        rows = pl.ds(pl.multiple_of(slot * LEN, LEN), LEN)
        for pair in range(HEADS // 2):
            at = pair * 2 * HD
            probs = pair_probs(
                both_heads(qkv_ref[rows, at : at + 2 * HD], masks),
                qkv_ref[rows, D + at : D + at + 2 * HD],
            )
            values = both_heads(qkv_ref[rows, 2 * D + at : 2 * D + at + 2 * HD], masks)
            att_ref[rows, at : at + 2 * HD] = dot(
                side_by_side(probs.astype(bf16)), values
            ).astype(bf16)

    wait_all(fetch([(att_ref, att_out)], sems))


def join_kernel(*refs):
    *parts, both, sems = refs
    pairs, first = [], 0
    for ref in parts:
        rows = ref.shape[0]
        pairs.append((ref, both.at[pl.ds(first, rows), :]))
        first += rows
    wait_all(fetch(pairs, sems))


def cut_kernel(near_ref, x_ref, y_ref, most_ref, low_ref, high_ref, sems):
    rows = near_ref.shape[0]
    half = rows // 2
    pairs = [(y_ref.at[pl.ds(0, half), :], low_ref), (x_ref.at[pl.ds(half, half), :], high_ref)]
    for i, ref in enumerate((near_ref, x_ref, y_ref)):
        pairs.append((ref, most_ref.at[pl.ds(i * rows, rows), :]))
    wait_all(fetch(pairs, sems))


def flip(where_ref, lhs_ref, ordered, split_rows):
    chip, core = where_ref[0], where_ref[1]
    depth = ordered.shape[0]
    size = depth // BLOCKS
    if split_rows:
        size //= 2
    step = 384
    for m in range(depth // step):
        turned = lhs_ref[:, m * step : (m + 1) * step].T
        for i in range(step // size):
            block = m * (step // size) + i
            side = block % 2
            to = place_of(block // 2 if split_rows else block, chip) * size
            if split_rows:
                to = to + jnp.where(core == side, depth // 2, 0)
            ordered[pl.ds(pl.multiple_of(to, 16), size), :] = turned[i * size : (i + 1) * size, :]


def hidden_kernel(
    where_ref, res_ref, att_ref, mod_ref, gc_ref, proj_bias_ref, bias_ref, *rest
):
    mine, more, theirs, rest_far = rest[:4]
    branch_ref, mid_ref, min_ref, gmo_ref, colsum_ref, act_out, slope_out, send_out, keep_out, mid_out = rest[4:14]
    proj, weight, act, slope, ordered, made, out_sems = rest[14:]
    total = jnp.zeros((1, D), f32)
    for slot in range(SLOTS):
        rows = slot_rows(slot)
        grad = (mod_part(mod_ref, slot, 5) * gc_ref[rows, :].astype(f32)).astype(bf16)
        gmo_ref[rows, :] = grad
        total += jnp.sum(grad.astype(f32), axis=0, keepdims=True)
    colsum_ref[...] = total
    lay_out(
        where_ref,
        ([mine, more], [theirs, rest_far]),
        D // BLOCKS,
        [(proj, 0, D // 2), (weight, D // 2, F // 2)],
        NEAR_FIRST,
    )
    for j in range(D // 256):
        cols = slice(j * 256, (j + 1) * 256)
        branch_ref[:, cols] = dot(att_ref[...], proj[:, cols]) + proj_bias_ref[:, cols]
    for slot in range(SLOTS):
        rows = slot_rows(slot)
        mid = res_ref[rows, :] + mod_part(mod_ref, slot, 2) * branch_ref[rows, :]
        mid_ref[rows, :] = mid
        normed, _ = norm_parts(mid)
        min_ref[rows, :] = (
            normed * (1.0 + mod_part(mod_ref, slot, 4)) + mod_part(mod_ref, slot, 3)
        ).astype(bf16)

    @pl.loop(0, F // 256)
    def _(j):
        cols = pl.ds(pl.multiple_of(j * 256, 256), 256)
        u = dot(min_ref[...], weight[:, cols]) + bias_ref[:, cols]
        square = u * u
        bend = jnp.tanh(GELU_COEF * (u + 0.044715 * square * u))
        left = 0.5 * (1.0 + bend)
        act[:, cols] = (u * left).astype(bf16)
        slope[:, cols] = (
            left
            + 0.5 * u * (1.0 - bend * bend) * (GELU_COEF * (1.0 + 3.0 * 0.044715 * square))
        ).astype(bf16)

    out = fetch([(act, act_out), (slope, slope_out)], out_sems)
    out += fetch([(mid_ref, mid_out)], out_sems, 8)
    flip(where_ref, act, ordered, True)
    step = 512
    for j in range(F // step):
        made[j * step : (j + 1) * step, :] = dot(
            ordered[j * step : (j + 1) * step, :], gmo_ref[...]
        ).astype(bf16)
        to, at = (send_out, j) if j < F // step // 2 else (keep_out, j - F // step // 2)
        out += fetch(
            [(made.at[pl.ds(j * step, step), :], to.at[pl.ds(at * step, step), :])],
            out_sems,
            2 + j,
        )
    wait_all(out)


def flips_kernel(where_ref, first_ref, second_in, third_in, flipped_ref, second_out, third_out, second, third, turned, sems):
    copies = fetch([(second_in, second), (third_in, third)], sems)
    flip(where_ref, first_ref, flipped_ref, False)
    out = []
    for i, (ref, to) in enumerate(((second, second_out), (third, third_out))):
        wait_all([copies[i]])
        flip(where_ref, ref, turned.at[i], False)
        out += fetch([(turned.at[i], to)], sems, 2 + i)
    wait_all(out)


def wgrad_kernel(count, where_ref, *rest):
    lhs, rhs = rest[:count], rest[count : 2 * count]
    send_out, keep_out, send, keep, sems, *late = rest[2 * count :]
    core = where_ref[1]
    if late:
        *bufs, in_sems = late
        ins = fetch([(lhs[0], bufs[0]), (rhs[0], bufs[1]), (lhs[1], bufs[2])], in_sems)
        lhs, rhs = (bufs[0], bufs[2]), (bufs[1], rhs[1])
    step = 384
    first = 0
    out = []
    for ordered, rhs_ref in zip(lhs, rhs):
        if late:
            wait_all(ins[2:] if first else ins[:2])
        width = rhs_ref.shape[1] // 2
        for buf, to, half in ((send, send_out, 1 - core), (keep, keep_out, core)):
            cols = pl.ds(pl.multiple_of(half * width, 128), width)
            for j in range(D // step):
                rows = slice(j * step, (j + 1) * step)
                buf[rows, first : first + width] = dot(
                    ordered[rows, :], rhs_ref[:, cols]
                ).astype(bf16)
                here = (pl.ds(j * step, step), pl.ds(first, width))
                out += fetch([(buf.at[here], to.at[here])], sems, len(out))
        first += width
    wait_all(out)


def pair_sums(keep_in, got_ref, rows, spans, keep, sems, got=None):
    copies = []
    for i, first in enumerate(spans):
        here, there = pl.ds(i * rows, rows), pl.ds(first, rows)
        pairs = [(keep_in.at[there, :], keep.at[here, :])]
        if got is not None:
            pairs.append((got_ref.at[there, :], got.at[here, :]))
        copies.append(fetch(pairs, sems, 2 * i))

    def total(i):
        wait_all(copies[i])
        here = slice(i * rows, (i + 1) * rows)
        other = got_ref[spans[i] : spans[i] + rows, :] if got is None else got[here, :]
        return keep[here, :].astype(f32) + other.astype(f32)

    return total


def first_kernel(keep_in, got_ref, x_ref, y_ref, keep, sems, *got):
    rows = x_ref.shape[0] // 2
    total = pair_sums(keep_in, got_ref, rows, [2 * rows, 6 * rows, 5 * rows, 7 * rows], keep, sems, *got)
    for i in range(4):
        ref = (x_ref, y_ref)[i // 2]
        ref[i % 2 * rows : (i % 2 + 1) * rows, :] = total(i).astype(bf16)


def second_kernel(keep_in, got_ref, x_got_ref, y_got_ref, x_ref, y_ref, keep, sems, *got):
    rows = x_ref.shape[0]
    total = pair_sums(keep_in, got_ref, rows, [3 * rows, 4 * rows], keep, sems, *got)
    x_ref[...] = (total(0) + y_got_ref[rows:, :].astype(f32)).astype(bf16)
    y_ref[...] = (total(1) + x_got_ref[rows:, :].astype(f32)).astype(bf16)


def near_kernel(direct, keep_in, got_ref, x_one_ref, y_one_ref, x_two_ref, y_two_ref, *rest):
    if direct:
        outs, (keep, sems, *got) = rest[:4], rest[4:]
    else:
        send_ref, own_out, beyond_out, keep, sems, own, beyond, out_sems = rest
        got = ()
        outs = (send_ref, own, beyond)
    half = x_two_ref.shape[0]
    rows = half // 2
    total = pair_sums(keep_in, got_ref, half, [0, half], keep, sems, *got)
    for i, (one_ref, two_ref) in enumerate(((x_one_ref, y_two_ref), (y_one_ref, x_two_ref))):
        both = total(i) + one_ref[0:half, :].astype(f32) + two_ref[...].astype(f32)
        for j in range(2):
            z = 2 * i + j
            value = both[j * rows : (j + 1) * rows]
            if direct:
                outs[z][...] = value.astype(outs[z].dtype)
            elif j:
                outs[0][i * rows : (i + 1) * rows, :] = value.astype(bf16)
            else:
                outs[1 + i][...] = value
    if not direct:
        wait_all(fetch([(own, own_out), (beyond, beyond_out)], out_sems))


def beyond_kernel(got_ref, own_in, beyond_in, send_ref, total_out, own, beyond, sems):
    wait_all(fetch([(own_in, own), (beyond_in, beyond)], sems))
    rows = own.shape[0]
    send_ref[...] = (beyond[...] + got_ref[rows:, :].astype(f32)).astype(bf16)
    own[...] = own[...] + got_ref[0:rows, :].astype(f32)
    wait_all(fetch([(own, total_out)], sems, 2))


def lay_out_fc2(where_ref, near_ref, far_ref, fc2):
    lay_out(where_ref, ([near_ref], [far_ref]), F // (2 * BLOCKS), [(fc2, 0, D)], FAR_FIRST, True)


def fc2_back_kernel(
    where_ref, gmo_ref, slope_in, near_ref, far_ref, gh_ref, colsum_ref, fc2, slope, in_sems
):
    step = 512
    parts = [pl.ds(j * step, step) for j in range(F // step)]
    late = fetch([(slope_in.at[:, part], slope.at[:, part]) for part in parts], in_sems)
    lay_out_fc2(where_ref, near_ref, far_ref, fc2)
    for j in range(F // step):
        wait_all([late[j]])
        for half in range(2):
            cols = slice(j * step + half * 256, j * step + (half + 1) * 256)
            grad = dot_nt(gmo_ref[...], fc2[cols, :])
            value = (slope[:, cols].astype(f32) * grad).astype(bf16)
            gh_ref[:, cols] = value
            colsum_ref[:, cols] = jnp.sum(value.astype(f32), axis=0, keepdims=True)


def fc2_out_kernel(
    where_ref, place_ref, mod_ref, gc_ref, bias_ref, mid_in, act_in, near_ref, far_ref,
    tail_ref, gate_ref, out_out, mid_ref, act, fc2, mlp, made, in_sems,
):
    last = fetch([(act_in, act), (mid_in, mid_ref)], in_sems)
    lay_out_fc2(where_ref, near_ref, far_ref, fc2)
    wait_all(last)
    for j in range(D // 256):
        cols = slice(j * 256, (j + 1) * 256)
        mlp[0:TOK_DEV, cols] = dot(act[...], fc2[:, cols]) + bias_ref[:, cols]
    for slot in range(SLOTS):
        rows = slot_rows(slot)
        value = mlp[rows, :]
        gate_ref[slot : slot + 1, :] = jnp.sum(
            value * gc_ref[rows, :].astype(f32), axis=0, keepdims=True
        )
        value = mid_ref[rows, :] + mod_part(mod_ref, slot, 5) * value
        mlp[rows, :] = value
        made[rows, :] = value.astype(bf16)
    out = fetch([(made, out_out)], in_sems, 2)
    mlp[TOK_DEV:, :] = jnp.zeros((LEN + 8, D), f32)
    tail_ref[...] = rows_from(mlp, place_ref[3]).astype(bf16)
    wait_all(out)


def keep_sum(sums, part, slot, values):
    at = part * SLOTS + slot
    sums[at : at + 1, :] = jnp.sum(values, axis=0, keepdims=True)


def spread_sums(sums, spread_ref):
    value = sums[...].astype(bf16)
    for d in range(spread_ref.shape[0]):
        spread_ref[d] = value


def mid_back_kernel(
    where_ref, gh_ref, mid_ref, branch_ref, mod_ref, gc_ref, gate_ref, mine, more, theirs, rest_far,
    ga_ref, proj_sum_ref, gm_out, gb_out, spread_out,
    gm_ref, gb_ref, spread_ref, proj, weight, grads, sums, out_sems,
):
    lay_out(
        where_ref,
        ([mine, more], [theirs, rest_far]),
        D // BLOCKS,
        [(proj, 0, D // 2), (weight, D // 2, F // 2)],
        NEAR_FIRST,
    )
    for j in range(D // 256):
        cols = slice(j * 256, (j + 1) * 256)
        grads[:, cols] = dot_nt(gh_ref[...], weight[cols, :])
    total = jnp.zeros((1, D), f32)
    for slot in range(SLOTS):
        rows = slot_rows(slot)
        normed, inverse = norm_parts(mid_ref[rows, :])
        e = grads[rows, :]
        keep_sum(sums, 1, slot, e)
        keep_sum(sums, 2, slot, e * normed)
        grad_mid = gc_ref[rows, :].astype(f32) + norm_back(
            normed, inverse, mod_part(mod_ref, slot, 4), e
        )
        gm_ref[rows, :] = grad_mid
        keep_sum(sums, 0, slot, branch_ref[rows, :] * grad_mid)
        value = (mod_part(mod_ref, slot, 2) * grad_mid).astype(bf16)
        gb_ref[rows, :] = value
        total += jnp.sum(value.astype(f32), axis=0, keepdims=True)
    proj_sum_ref[...] = total
    sums[3 * SLOTS :, :] = gate_ref[...]
    spread_sums(sums, spread_ref)
    out = fetch([(gm_ref, gm_out), (gb_ref, gb_out), (spread_ref, spread_out)], out_sems)
    for j in range(D // 256):
        cols = slice(j * 256, (j + 1) * 256)
        ga_ref[:, cols] = dot_nt(gb_ref[...], proj[cols, :]).astype(bf16)
    wait_all(out)


def probs_kernel(qk_in, probs_out, qk, probs, sems):
    masks = head_masks()
    copies = fetch(
        [
            (qk_in.at[pl.ds(slot * LEN, LEN), pl.ds(0, 2 * D)], qk.at[pl.ds(slot * LEN, LEN), :])
            for slot in range(SLOTS)
        ],
        sems,
    )
    out = []
    for slot in range(SLOTS):
        wait_all([copies[slot]])
        rows = slot_rows(slot)
        tall = HEADS // 2 * LEN
        for pair in range(HEADS // 2):
            at = pair * 2 * HD
            queries = both_heads(qk[rows, at : at + 2 * HD], masks)
            scores = dot_nt(qk[rows, D + at : D + at + 2 * HD], queries) * (1.0 / math.sqrt(HD))
            exp_terms = jnp.exp(scores - jnp.max(scores, axis=0, keepdims=True))
            first = slot * tall + pair * LEN
            probs[first : first + LEN, :] = exp_terms * (
                1.0 / jnp.sum(exp_terms, axis=0, keepdims=True)
            )
        here = pl.ds(slot * tall, tall)
        out += fetch([(probs.at[here, :], probs_out.at[here, :])], sems, SLOTS + slot)
    wait_all(out)


def attend_back_kernel(qkv_in, probs_in, ga_ref, gqkv_ref, colsum_ref, qkv, probs, sems):
    masks = head_masks()
    first_head = lax.broadcasted_iota(jnp.int32, (1, 2 * HD), 1) < HD
    scale = 1.0 / math.sqrt(HD)
    tall = HEADS // 2 * LEN
    copies = []
    for slot in range(SLOTS):
        here, there = pl.ds(slot * LEN, LEN), pl.ds(slot * tall, tall)
        copies += fetch(
            [
                (qkv_in.at[here, :], qkv.at[here, :]),
                (probs_in.at[there, :], probs.at[there, :]),
            ],
            sems,
            2 * slot,
        )
    for first in range(0, SLOTS, 2):
        wait_all(copies[2 * first : 2 * first + 4])

        @pl.loop(first, first + 2)
        def _(slot):
            rows = pl.ds(pl.multiple_of(slot * LEN, LEN), LEN)
            for pair in range(HEADS // 2):
                at = pair * 2 * HD
                q_cols, k_cols, v_cols = (
                    slice(part * D + at, part * D + at + 2 * HD) for part in range(3)
                )
                chances = probs[pl.ds(pl.multiple_of(slot * tall + pair * LEN, LEN), LEN), :]
                grads = both_heads(ga_ref[rows, q_cols], masks)
                weighed = chances * dot_nt(qkv[rows, v_cols], grads)
                inner = jnp.sum(weighed, axis=0, keepdims=True)
                grad_scores = (weighed - chances * inner).astype(bf16)
                grad_queries = dot_tn(grad_scores, qkv[rows, k_cols]) * scale
                gqkv_ref[rows, q_cols] = jnp.where(
                    first_head, grad_queries[:LEN], grad_queries[LEN:]
                ).astype(bf16)
                queries = both_heads(qkv[rows, q_cols], masks)
                gqkv_ref[rows, k_cols] = (dot(grad_scores, queries) * scale).astype(bf16)
                gqkv_ref[rows, v_cols] = dot(chances.astype(bf16), grads).astype(bf16)

    for j in range(3 * D // 256):
        cols = slice(j * 256, (j + 1) * 256)
        colsum_ref[:, cols] = jnp.sum(gqkv_ref[:, cols].astype(f32), axis=0, keepdims=True)


def start_back_kernel(
    place_ref, gqkv_ref, mod_ref, out_tail_ref, res_in, gm_in, weight_in,
    tg_out, tail_out, spread_out, weight, grads, res, gm, sums, tail_ref, spread_ref, in_sems, out_sems,
):
    step = 256
    parts = [pl.ds(j * step, step) for j in range(D // step)]
    copies = fetch([(weight_in.at[part, :], weight.at[part, :]) for part in parts], in_sems)
    late = fetch([(res_in, res), (gm_in, gm)], in_sems, len(parts))
    for j in range(D // step):
        wait_all([copies[j]])
        cols = slice(j * step, (j + 1) * step)
        grads[0:TOK_DEV, cols] = dot_nt(gqkv_ref[...], weight[cols, :])
    wait_all(late)
    out = []
    for slot in range(SLOTS):
        rows = slot_rows(slot)
        normed, inverse = norm_parts(res[rows, :])
        e = grads[rows, :]
        keep_sum(sums, 0, slot, e)
        keep_sum(sums, 1, slot, e * normed)
        grads[rows, :] = gm[rows, :] + norm_back(normed, inverse, mod_part(mod_ref, slot, 1), e)
        here = pl.ds(slot * LEN, LEN)
        out += fetch([(grads.at[here, :], tg_out.at[here, :])], out_sems, slot)
    spread_sums(sums, spread_ref)
    out += fetch([(spread_ref, spread_out)], out_sems, SLOTS)
    grads[TOK_DEV:, :] = jnp.zeros((LEN + 8, D), f32)
    tail = rows_from(grads, place_ref[3])
    high = tail.astype(bf16)
    tail_ref[0:LEN, :] = out_tail_ref[...]
    tail_ref[LEN : 2 * LEN, :] = high
    tail_ref[2 * LEN :, :] = (tail - high.astype(f32)).astype(bf16)
    wait_all(out + fetch([(tail_ref, tail_out)], out_sems, SLOTS + 1))


def place_kernel(
    place_ref, tail_ref, tok_in, cot_in, out_in, tg_in,
    final_out, final_tg, out_rows, tg_rows, tok, cot, out, made_out, made_tg, sems,
):
    lead, count = place_ref[0], place_ref[1]
    copies = fetch(
        [(out_in, out), (tok_in, tok), (tg_in, tg_rows.at[pl.ds(LEN, TOK_DEV), :]), (cot_in, cot)],
        sems,
    )
    for rows in (out_rows, tg_rows):
        rows[0:LEN, :] = jnp.zeros((LEN, D), f32)
        rows[LEN + TOK_DEV :, :] = jnp.zeros((8, D), f32)
    wait_all(copies[:2])
    out_rows[LEN : LEN + TOK_DEV, :] = out[...].astype(f32)
    last = []
    out_tail = tail_ref[0:LEN, :].astype(f32)
    tg_tail = tail_ref[LEN : 2 * LEN, :].astype(f32) + tail_ref[2 * LEN :, :].astype(f32)
    for k, (rows, tail, pad, made, final) in enumerate(
        ((out_rows, out_tail, tok, made_out, final_out), (tg_rows, tg_tail, cot, made_tg, final_tg))
    ):
        if k:
            wait_all(copies[2:])
        for slot in range(SLOTS):
            here = slot_rows(slot)
            row = lax.broadcasted_iota(jnp.int32, (LEN, 1), 0) + slot * LEN
            value = rows_from(rows, LEN - lead + slot * LEN)
            if slot == 0:
                value = jnp.where(row < lead, tail, value)
            value = jnp.where(row < count, value, pad[here, :].astype(f32))
            made[here, :] = value.astype(made.dtype)
        last += fetch([(made, final)], sems, 4 + k)
    wait_all(last)


def shape(*dims, dtype=f32):
    return jax.ShapeDtypeStruct(dims, dtype)


def call(kernel, outs, scratch, mib, ins, spaces, after=(), out_specs=None, us=0, zeros=False):
    taken, held, made = len(ins), len(after), len(outs)
    out_specs = out_specs or [VM] * made

    def body(*refs):
        first = taken + held
        kernel(*refs[:taken], *refs[first : first + made], *refs[first + made + 1 :])
        if zeros:
            refs[first + made][...] = jnp.zeros((8, 128), f32)

    def settled(item):
        is_token = item.shape == (8, 128) and item.dtype == f32
        return pltpu.with_memory_space_constraint(item, pltpu.HBM) if is_token else item

    def placed(item, spec):
        return pltpu.with_memory_space_constraint(item, pltpu.HBM) if spec is HBM else item

    out_specs = [*out_specs, VM if zeros else HBM]
    out_shape = [
        pltpu.HBM(item.shape, item.dtype) if spec is HBM else item
        for item, spec in zip([*outs, shape(8, 128)], out_specs)
    ]
    *results, token = pl.pallas_call(
        body,
        out_shape=out_shape,
        in_specs=list(spaces) + [ANY] * held,
        out_specs=out_specs,
        scratch_shapes=scratch,
        compiler_params=params(mib),
        cost_estimate=cost(us),
        name=getattr(kernel, "func", kernel).__name__,
    )(*[placed(item, spec) for item, spec in zip(ins, spaces)], *[settled(item) for item in after])
    return results, token


def tie(value, token):
    return jnp.where(token[0, 0] == 0.0, value, jnp.zeros_like(value))


def join(parts, after=(), us=0, zeros=False):
    rows = sum(part.shape[0] for part in parts)
    (both,), token = call(
        join_kernel,
        [shape(rows, parts[0].shape[1], dtype=parts[0].dtype)],
        [pltpu.SemaphoreType.DMA((len(parts),))],
        8,
        parts,
        [ANY] * len(parts),
        after=after,
        out_specs=[ANY],
        us=us,
        zeros=zeros,
    )
    return both, token


def tie(value, token):
    return jnp.where(token[0, 0] == 0.0, value, jnp.zeros_like(value))


def low(value):
    return value.astype(bf16)


class Links:
    def __init__(self, devices):
        self.devices = devices
        self.cube = devices == 32
        self.me = lax.axis_index("wide").astype(jnp.int32)
        self.core = self.me % 2 if self.cube else jnp.int32(0)
        self.chip = self.me // 2 if self.cube else jnp.int32(0)
        self.where = jnp.stack([self.chip, self.core, self.me])

    def swap(self, array, bits):
        return lax.ppermute(array, "wide", [(i, i ^ bits) for i in range(self.devices)])

    def by_core(self, first, second):
        return jnp.where(self.core == 0, first, second)

    def pair(self, mine, got):
        return self.by_core(
            jnp.concatenate([mine, got], axis=0), jnp.concatenate([got, mine], axis=0)
        )

    def along_z(self, pair):
        return jnp.concatenate(
            [pair, self.swap(pair, 8), self.swap(pair, 16), self.swap(pair, 24)], axis=0
        )

    def doubled_z(self, pair):
        two = jnp.concatenate([pair, self.swap(pair, 8)], axis=0)
        return jnp.concatenate([two, self.swap(two, 16)], axis=0)

    def gathered(self, shards):
        halves = [[], []]
        for shard in shards:
            whole = lax.all_gather(shard, "wide", axis=0, tiled=True)
            rows, width = whole.shape[0], whole.shape[1] // 2
            whole = whole.reshape(4, 4, rows // BLOCKS, -1).transpose(1, 0, 2, 3)
            whole = whole.reshape(rows, -1)
            halves[0].append(whole[:, :width])
            halves[1].append(whole[:, width:])
        return [jnp.concatenate(half, axis=1) for half in halves]

    def scattered(self, send, keep, widths):
        outs, first = [], 0
        rows = keep.shape[0]
        for width in widths:
            cols = slice(first, first + width)
            whole = jnp.concatenate([keep[:, cols], send[:, cols]], axis=1)
            whole = whole.reshape(4, 4, rows // BLOCKS, -1).transpose(1, 0, 2, 3)
            whole = whole.reshape(rows, -1).astype(f32)
            outs.append(lax.psum_scatter(whole, "wide", scatter_dimension=0, tiled=True))
            first += width
        return outs

    def scattered_rows(self, send, keep):
        whole = jnp.stack([keep, send]).reshape(2, 4, 4, -1, D)
        whole = whole.transpose(2, 1, 0, 3, 4).reshape(-1, D)
        return lax.psum_scatter(whole.astype(f32), "wide", scatter_dimension=0, tiled=True)

    def gathered_rows(self, shard):
        whole = lax.all_gather(shard, "wide", axis=0, tiled=True).reshape(4, 4, 2, -1, D)
        whole = jnp.stack([whole[z] for z in FAR_FIRST], axis=1)
        return [whole[:, :, half].reshape(-1, D) for half in range(2)]

    def first(self, keep, got, after, copied=False):
        rows, width = keep.shape[0] // 4, keep.shape[1]
        (x, y), token = call(
            first_kernel,
            [shape(rows, width, dtype=bf16)] * 2,
            [pltpu.VMEM((2 * rows, width), bf16), pltpu.SemaphoreType.DMA((8,))]
            + [pltpu.VMEM((2 * rows, width), bf16)] * copied,
            16,
            [keep, got],
            [HBM, HBM if copied else VM],
            after=after,
        )
        return [self.swap(x, 2), self.swap(y, 4)], token

    def second(self, keep, got, ones, after, copied=False):
        rows, width = keep.shape[0] // 8, keep.shape[1]
        (x, y), token = call(
            second_kernel,
            [shape(rows, width, dtype=bf16)] * 2,
            [pltpu.VMEM((2 * rows, width), bf16), pltpu.SemaphoreType.DMA((4,))]
            + [pltpu.VMEM((2 * rows, width), bf16)] * copied,
            16,
            [keep, got, *ones],
            [HBM, HBM if copied else VM, VM, VM],
            after=after,
            us=100,
        )
        return [self.swap(x, 2), self.swap(y, 4)], token

    def near_sum(self, keep, got, ones, twos, direct, after):
        tall, width = keep.shape[0] // 4, keep.shape[1]
        rows = tall // 4
        if direct:
            outs = [shape(rows, width)] + [shape(rows, width, dtype=bf16)] * 3
        else:
            outs = [shape(2 * rows, width, dtype=bf16)] + [shape(rows, width)] * 2
        scratch = [pltpu.VMEM((tall, width), bf16), pltpu.SemaphoreType.DMA((4,))]
        scratch += [pltpu.VMEM((tall, width), bf16)] * direct
        if not direct:
            scratch += [pltpu.VMEM((rows, width), f32)] * 2 + [pltpu.SemaphoreType.DMA((2,))]
        return call(
            functools.partial(near_kernel, direct),
            outs,
            scratch,
            16,
            [keep, got, *ones, *twos],
            [HBM, HBM if direct else VM] + [VM] * 4,
            after=after,
            out_specs=[VM] * 4 if direct else [VM, HBM, HBM],
            us=100,
        )

    def z_sum(self, token, own, *parts):
        own = tie(own, token)
        for part, bits in zip(parts, (8, 16, 24)):
            own = own + self.swap(part, bits).astype(f32)
        return own

    def halved_z(self, send, own, beyond, after):
        (send, total), token = call(
            beyond_kernel,
            [shape(*own.shape, dtype=bf16), shape(*own.shape)],
            [pltpu.VMEM(own.shape, f32)] * 2 + [pltpu.SemaphoreType.DMA((3,))],
            8,
            [self.swap(send, 8), own, beyond],
            [VM, HBM, HBM],
            after=after,
            out_specs=[VM, HBM],
        )
        return total, self.swap(send, 16), token

    def own_rows(self, own, widths):
        rows = own.shape[0] // 2
        mine = self.by_core(own[:rows], own[rows:])
        got = self.swap(self.by_core(own[rows:], own[:rows]), 1)
        outs, first = [], 0
        for width in widths:
            a, b = mine[:, first : first + width], got[:, first : first + width]
            outs.append(
                self.by_core(jnp.concatenate([a, b], axis=1), jnp.concatenate([b, a], axis=1))
            )
            first += width
        return outs


def on_device(
    tokens,
    cotangent,
    cond,
    kept,
    counts,
    ada_w,
    ada_bias,
    qkv_w,
    q_bias,
    v_bias,
    proj_w,
    proj_bias,
    fc1_w,
    fc1_bias,
    fc2_w,
    fc2_bias,
):
    devices = lax.axis_size("wide")
    images = cond.shape[0]
    span = ada_bias.shape[0]
    own_dim = ada_w.shape[0]
    links = Links(devices)
    me, where, cube = links.me, links.where, links.cube
    rows = TOK_DEV
    dma = pltpu.SemaphoreType.DMA
    half_sum = (qkv_w.shape[1] + proj_w.shape[1] + fc1_w.shape[1]) // 2

    (mine, send, edge, place, starts, cond_slots, ada_parts), _ = call(
        begin_kernel,
        [
            shape(own_dim, half_sum, dtype=bf16),
            shape(own_dim, half_sum, dtype=bf16),
            shape(2 * LEN, D, dtype=bf16),
            shape(8, dtype=jnp.int32),
            shape(devices, dtype=jnp.int32),
            shape(devices * 8, D, dtype=bf16),
            shape(devices, own_dim, span, dtype=bf16),
        ],
        [
            pltpu.VMEM((devices * 8, images), f32),
            pltpu.VMEM(cond.shape, bf16),
            pltpu.VMEM(ada_w.shape, bf16),
            dma((10,)),
        ],
        16,
        [where, counts, cond, ada_w, tokens, cotangent, qkv_w, proj_w, fc1_w],
        [SM, SM] + [HBM] * 7,
        out_specs=[VM, VM, VM, SM, SM, VM, VM],
    )
    if cube:
        pair = links.pair(mine, links.swap(send, 1))
        near_one = links.along_z(pair[:, : 3 * D // 2])
        before_mod = [pair]
    else:
        before_mod = []
    halo = lax.ppermute(edge, "wide", [(i + 1, i) for i in range(devices - 1)])

    ada_cols = lax.all_to_all(ada_parts, "wide", 0, 0, tiled=True)
    ada_cols = ada_cols.reshape(D, span)
    lanes = lambda items: jnp.pad(
        jnp.concatenate(items), (0, span - sum(i.shape[0] for i in items))
    ).reshape(1, span)
    addend = jnp.concatenate(
        [
            jnp.broadcast_to(ada_bias.reshape(1, span), (SLOTS, span)),
            lanes([q_bias, v_bias, proj_bias, fc2_bias]),
            lanes([fc1_bias]),
            jnp.zeros((2, span), bf16),
        ],
        axis=0,
    ).astype(f32)
    (mod_cols,), mod_ran = call(
        mod_kernel,
        [shape(devices, 8, span)],
        [],
        16,
        [cond_slots, ada_cols, addend],
        [VM] * 3,
        after=before_mod,
        zeros=True,
    )
    mixed = lax.all_to_all(mod_cols, "wide", 0, 0, tiled=True)

    quarter = D // 4
    frequency = jnp.exp(-math.log(10000.0) * jnp.arange(quarter).astype(f32) / quarter)
    angle = jnp.arange(GRID).astype(f32)[:, None] * frequency[None, :]
    table = jnp.concatenate([jnp.sin(angle), jnp.cos(angle)], axis=1)
    if cube:
        near_one = tie(near_one, mod_ran)
        over = [links.swap(near_one, bits) for bits in (2, 4, 6)]
        pair_two = tie(pair[:, 3 * D // 2 :], mod_ran)
        two = jnp.concatenate([pair_two, links.swap(pair_two, 8)], axis=0)
        before_prep = [near_one, two]
    else:
        before_prep = []
    (residual, grad_out, mod, qkv_bias, proj_bias_all, fc2_bias_all, fc1_bias_all), prepared = call(
        prep_kernel,
        [
            shape(rows, D),
            shape(rows, D, dtype=bf16),
            shape(SLOTS, 6 * D),
            shape(1, 3 * D),
            shape(1, D),
            shape(1, D),
            shape(1, F),
        ],
        [
            pltpu.VMEM((rows, D), bf16),
            pltpu.VMEM((rows, D), bf16),
            pltpu.VMEM((2 * LEN, D), bf16),
            pltpu.VMEM(kept.shape, jnp.int32),
            pltpu.VMEM(table.shape, f32),
            dma((5,)),
        ],
        16,
        [place, mixed, tokens, cotangent, halo, kept, table],
        [SM, VM, HBM, HBM, ANY, HBM, ANY],
        after=before_prep,
        us=10,
    )

    if cube:
        near_two = jnp.concatenate([two, links.swap(two, 16)], axis=0)
        qkv_near, joined = join([near_one, *over], [prepared, near_two])
        qkv_far = links.swap(qkv_near, 1)
        over_x, over_y = links.swap(near_two, 2), links.swap(near_two, 4)
        before_qkv = []
    else:
        qkv_near, qkv_far = links.gathered([qkv_w])
        before_qkv = []

    (attn_in, qkv, qkv_laid), qkv_ran = call(
        qkv_kernel,
        [
            shape(rows, D, dtype=bf16),
            shape(rows, 3 * D, dtype=bf16),
            shape(D, 3 * D, dtype=bf16),
        ],
        [pltpu.VMEM((rows, D), bf16), pltpu.VMEM((D, 3 * D), bf16), dma((2,))],
        16,
        [where, residual, mod, qkv_bias, qkv_near, qkv_far],
        [SM] + [VM] * 5,
        after=before_qkv,
        out_specs=[HBM, VM, HBM],
        zeros=True,
    )
    before_attend = [qkv_ran]
    if cube:
        two, _ = join([fc2_w, links.swap(fc2_w, 16)], [qkv_ran])
        before_attend.append(two)
        near_three = jnp.concatenate([two, links.swap(two, 8)], axis=0)
    (attended, attended_kept), attend_ran = call(
        attend_kernel,
        [shape(rows, D, dtype=bf16)] * 2,
        [dma((1,))],
        16,
        [qkv],
        [VM],
        after=before_attend,
        out_specs=[VM, HBM],
        zeros=True,
    )
    if cube:
        half = near_two.shape[0] // 2
        width = near_two.shape[1]
        (most, low_half, high_half), _ = call(
            cut_kernel,
            [
                shape(6 * half, width, dtype=bf16),
                shape(half, width, dtype=bf16),
                shape(half, width, dtype=bf16),
            ],
            [dma((5,))],
            8,
            [near_two, over_x, over_y],
            [ANY] * 3,
            after=[attend_ran],
            out_specs=[ANY] * 3,
        )
        most_far = links.swap(most, 1)
        diag = [links.swap(low_half, 2), links.swap(high_half, 4)]
        diag, _ = join(diag)
        mid_halves = [most, diag, most_far, links.swap(diag, 1)]
        over = [links.swap(near_three, bits) for bits in (2, 4, 6)]
    else:
        mid_near, mid_far = links.gathered([proj_w, fc1_w])
        cut = 3 * D // 4
        mid_halves = [mid_near[:cut], mid_near[cut:], mid_far[:cut], mid_far[cut:]]
        fc2_near, fc2_far = links.gathered_rows(fc2_w)

    (
        branch, middle, mlp_in, grad_mlp_out, fc2_bias_sum, activated, slope, fc2_send, fc2_keep,
        middle_kept,
    ), hidden_ran = call(
        hidden_kernel,
        [
            shape(rows, D),
            shape(rows, D),
            shape(rows, D, dtype=bf16),
            shape(rows, D, dtype=bf16),
            shape(1, D),
            shape(rows, F, dtype=bf16),
            shape(rows, F, dtype=bf16),
            shape(F // 2, D, dtype=bf16),
            shape(F // 2, D, dtype=bf16),
            shape(rows, D),
        ],
        [
            pltpu.VMEM((D, D), bf16),
            pltpu.VMEM((D, F), bf16),
            pltpu.VMEM((rows, F), bf16),
            pltpu.VMEM((rows, F), bf16),
            pltpu.VMEM((F, rows), bf16),
            pltpu.VMEM((F, D), bf16),
            dma((9,)),
        ],
        32,
        [where, residual, attended, mod, grad_out, proj_bias_all, fc1_bias_all, *mid_halves],
        [SM] + [VM] * 10,
        out_specs=[VM] * 5 + [HBM] * 5,
    )
    def weight_grad(*pairs, after=()):
        half = sum(right.shape[1] for _, right in pairs) // 2
        scratch = [pltpu.VMEM((D, half), bf16), pltpu.VMEM((D, half), bf16), dma((8,))]
        spaces = [VM, VM]
        if len(pairs) == 2:
            scratch += [
                pltpu.VMEM((D, rows), bf16),
                pltpu.VMEM((rows, D), bf16),
                pltpu.VMEM((D, rows), bf16),
                dma((3,)),
            ]
            spaces = [HBM, HBM, HBM, VM]
        return call(
            functools.partial(wgrad_kernel, len(pairs)),
            [shape(D, half, dtype=bf16)] * 2,
            scratch,
            20,
            [where, *[left for left, _ in pairs], *[right for _, right in pairs]],
            [SM, *spaces],
            after=after,
            out_specs=[HBM] * 2,
        )

    (mlp_flipped, attended_flipped, attn_flipped), flipped = call(
        flips_kernel,
        [shape(D, rows, dtype=bf16)] * 3,
        [pltpu.VMEM((rows, D), bf16)] * 2 + [pltpu.VMEM((2, D, rows), bf16), dma((4,))],
        16,
        [where, mlp_in, attended_kept, attn_in],
        [SM, VM, HBM, HBM],
        after=[hidden_ran],
        out_specs=[VM, HBM, HBM],
    )
    (probs,), probs_ran = call(
        probs_kernel,
        [shape(SLOTS * HEADS // 2 * LEN, 2 * LEN)],
        [
            pltpu.VMEM((rows, 2 * D), bf16),
            pltpu.VMEM((SLOTS * HEADS // 2 * LEN, 2 * LEN), f32),
            dma((2 * SLOTS,)),
        ],
        16,
        [qkv],
        [HBM],
        after=[flipped],
        out_specs=[HBM],
    )
    if cube:
        fc2_got = links.swap(fc2_send, 1)
        fc2_near, gathered = join([near_three, *over], [probs_ran], us=100)
        fc2_far = links.swap(fc2_near, 1)
        fc2_ones, fc2_first = links.first(fc2_keep, fc2_got, [gathered])
        before_fc2 = [fc2_first]
    else:
        before_fc2 = []
    (grad_hidden, fc1_bias_sum), _ = call(
        fc2_back_kernel,
        [shape(rows, F, dtype=bf16), shape(1, F)],
        [pltpu.VMEM((F, D), bf16), pltpu.VMEM((rows, F), bf16), dma((6,))],
        20,
        [where, grad_mlp_out, slope, fc2_near, fc2_far],
        [SM, VM, HBM, VM, VM],
        after=before_fc2,
    )
    (fc1_send, fc1_keep), fc1_ran = weight_grad((mlp_flipped, grad_hidden))
    (out_tail, gate_two_sum, result), out_ran = call(
        fc2_out_kernel,
        [shape(LEN, D, dtype=bf16), shape(SLOTS, D), shape(rows, D, dtype=bf16)],
        [
            pltpu.VMEM((rows, D), f32),
            pltpu.VMEM((rows, F), bf16),
            pltpu.VMEM((F, D), bf16),
            pltpu.VMEM((rows + LEN + 8, D), f32),
            pltpu.VMEM((rows, D), bf16),
            dma((3,)),
        ],
        20,
        [where, place, mod, grad_out, fc2_bias_all, middle_kept, activated, fc2_near, fc2_far],
        [SM] * 2 + [VM] * 3 + [HBM] * 2 + [VM] * 2,
        after=[fc1_ran],
        out_specs=[VM] * 2 + [HBM],
    )
    if cube:
        fc1_got = links.swap(fc1_send, 1)
        fc2_twos, fc2_second = links.second(fc2_keep, fc2_got, fc2_ones, [out_ran])
        fc1_ones, fc1_first = links.first(fc1_keep, fc1_got, [fc2_second])
        before_mid = [fc1_first]
    else:
        before_mid = [out_ran]
    (grad_attended, proj_bias_sum, grad_middle, grad_branch, early), mid_ran = call(
        mid_back_kernel,
        [
            shape(rows, D, dtype=bf16),
            shape(1, D),
            shape(rows, D),
            shape(rows, D, dtype=bf16),
            shape(devices, 16, D, dtype=bf16),
        ],
        [
            pltpu.VMEM((rows, D), f32),
            pltpu.VMEM((rows, D), bf16),
            pltpu.VMEM((devices, 16, D), bf16),
            pltpu.VMEM((D, D), bf16),
            pltpu.VMEM((D, F), bf16),
            pltpu.VMEM((rows, D), f32),
            pltpu.VMEM((16, D), f32),
            dma((3,)),
        ],
        20,
        [where, grad_hidden, middle, branch, mod, grad_out, gate_two_sum, *mid_halves],
        [SM] + [VM] * 10,
        out_specs=[VM] * 2 + [HBM] * 3,
        after=before_mid,
    )
    early = lax.all_to_all(early, "wide", 0, 0, tiled=True)
    if cube:
        fc2_near_sum, fc2_summed = links.near_sum(
            fc2_keep, fc2_got, fc2_ones, fc2_twos, False, [mid_ran]
        )
        before_back = [fc2_summed]
    else:
        before_back = []
    (grad_qkv, qkv_bias_sum), back_ran = call(
        attend_back_kernel,
        [shape(rows, 3 * D, dtype=bf16), shape(1, 3 * D)],
        [
            pltpu.VMEM((rows, 3 * D), bf16),
            pltpu.VMEM(probs.shape, f32),
            dma((2 * SLOTS,)),
        ],
        16,
        [qkv, probs, grad_attended],
        [HBM, HBM, VM],
        after=before_back,
    )
    before_qkv = []
    if cube:
        fc2_own, fc2_beyond, fc2_halved = links.halved_z(*fc2_near_sum, [back_ran])
        fc1_twos, fc1_second = links.second(fc1_keep, fc1_got, fc1_ones, [fc2_halved])
        before_qkv.append(fc1_second)
    (qkv_send, qkv_keep), qkv_grad_ran = weight_grad(
        (attended_flipped, grad_branch), (attn_flipped, grad_qkv), after=before_qkv
    )
    if cube:
        qkv_got = links.swap(qkv_send, 1)
    if cube:
        fc1_near_sum, fc1_summed = links.near_sum(
            fc1_keep, fc1_got, fc1_ones, fc1_twos, False, [qkv_grad_ran]
        )
        qkv_ones, qkv_first = links.first(qkv_keep, qkv_got, [fc1_summed])
        before_start = [qkv_first, early]
    else:
        before_start = [qkv_grad_ran]
    (tokens_back, tail, late), start_ran = call(
        start_back_kernel,
        [shape(rows, D), shape(3 * LEN, D, dtype=bf16), shape(devices, 2 * SLOTS, D, dtype=bf16)],
        [
            pltpu.VMEM((D, 3 * D), bf16),
            pltpu.VMEM((rows + LEN + 8, D), f32),
            pltpu.VMEM((rows, D), f32),
            pltpu.VMEM((rows, D), f32),
            pltpu.VMEM((2 * SLOTS, D), f32),
            pltpu.VMEM((3 * LEN, D), bf16),
            pltpu.VMEM((devices, 2 * SLOTS, D), bf16),
            dma((5,)),
            dma((SLOTS + 2,)),
        ],
        24,
        [place, grad_qkv, mod, out_tail, residual, grad_middle, qkv_laid],
        [SM] + [VM] * 3 + [HBM] * 3,
        after=before_start,
        out_specs=[HBM] * 3,
    )
    late = lax.all_to_all(late, "wide", 0, 0, tiled=True)

    if cube:
        fc1_own, fc1_beyond, fc1_halved = links.halved_z(*fc1_near_sum, [start_ran])
        qkv_twos, qkv_second = links.second(qkv_keep, qkv_got, qkv_ones, [fc1_halved], True)
        before_ada = [qkv_second]
    else:
        before_ada = [start_ran]

    onward = [(i, i + 1) for i in range(devices - 1)]
    tail = lax.ppermute(tail, "wide", onward)
    wide_images = -(-images // 128) * 128
    (ada_grad, ada_bias_sum, last), ada_ran = call(
        ada_kernel,
        [
            shape(own_dim, 6 * D),
            shape(1, 6 * D),
            shape(devices, own_dim + 8, wide_images, dtype=bf16),
        ],
        [pltpu.VMEM((devices * 16, images), f32), pltpu.VMEM((own_dim + 8, wide_images), f32)],
        24,
        [where, starts, early, late, ada_w, cond, qkv_bias_sum, proj_bias_sum, fc2_bias_sum, fc1_bias_sum],
        [SM] * 2 + [VM] * 8,
        after=before_ada,
        zeros=True,
    )
    last = lax.all_to_all(last, "wide", 0, 0, tiled=True)
    if cube:
        qkv_near_sum, qkv_summed = links.near_sum(
            qkv_keep, qkv_got, qkv_ones, qkv_twos, True, [ada_ran]
        )
        before_place = [qkv_summed]
    else:
        before_place = [ada_ran]
    (out, tokens_grad), placed = call(
        place_kernel,
        [shape(rows, D, dtype=bf16), shape(rows, D)],
        [
            pltpu.VMEM((rows + LEN + 8, D), f32),
            pltpu.VMEM((rows + LEN + 8, D), f32),
            pltpu.VMEM((rows, D), bf16),
            pltpu.VMEM((rows, D), bf16),
            pltpu.VMEM((rows, D), bf16),
            pltpu.VMEM((rows, D), bf16),
            pltpu.VMEM((rows, D), f32),
            dma((6,)),
        ],
        16,
        [place, tail, tokens, cotangent, result, tokens_back],
        [SM, VM] + [HBM] * 4,
        after=before_place,
        out_specs=[HBM] * 2,
    )


    (cond_grad, bias_grads), finished = call(
        finish_kernel,
        [shape(images, D), shape(8, wide_images)],
        [pltpu.VMEM((D, wide_images), f32)],
        16,
        [last],
        [VM],
        after=[placed],
        zeros=True,
    )
    fc1_widths, qkv_widths = [F // 2], [D // 2, 3 * D // 2]
    if cube:
        fc2_grad = tie(fc2_own, finished) + fc2_beyond.astype(f32)
        (fc1_grad,) = links.own_rows(
            tie(fc1_own, ada_ran) + fc1_beyond.astype(f32), fc1_widths
        )
        proj_grad, qkv_grad = links.own_rows(links.z_sum(finished, *qkv_near_sum), qkv_widths)
    else:
        fc2_grad = links.scattered_rows(fc2_send, fc2_keep)
        (fc1_grad,) = links.scattered(fc1_send, fc1_keep, fc1_widths)
        proj_grad, qkv_grad = links.scattered(qkv_send, qkv_keep, qkv_widths)
    bias_grads = bias_grads[:, :own_dim]
    ada_bias_grad = lax.dynamic_slice_in_dim(ada_bias_sum[0], me * span, span, 0)
    return (
        out,
        tokens_grad,
        cond_grad,
        ada_grad,
        ada_bias_grad,
        qkv_grad,
        bias_grads[0],
        bias_grads[1],
        proj_grad,
        bias_grads[2],
        fc1_grad,
        bias_grads[4:].reshape(-1),
        fc2_grad,
        bias_grads[3],
    )


def solution(mesh):
    row, flat = P("wide", None), P("wide")
    return jax.shard_map(
        on_device,
        mesh=mesh,
        in_specs=(row, row, P(), P(), P(), row, flat, row, flat, flat, row, flat, row, flat, row, flat),
        out_specs=(row, row, P(), row, flat, row, flat, flat, row, flat, row, flat, row, flat),
        check_vma=False,
    )
```

```python
import functools
import math

import jax
import jax.numpy as jnp
from jax import lax
from jax.experimental import pallas as pl
from jax.experimental.pallas import tpu as pltpu
from jax.sharding import PartitionSpec as P

D = 768
HEADS = 12
HD = 64
GRID = 16
LEN = 128
TOK_DEV = 512
SLOTS = TOK_DEV // LEN
F = 3072
BLOCKS = 16
NEAR_FIRST, FAR_FIRST = (0, 1, 2, 3), (0, 2, 1, 3)

NORM_EPS = 1e-06
GELU_COEF = 0.7978845608028654

f32 = jnp.float32
bf16 = jnp.bfloat16

VM = pl.BlockSpec(memory_space=pltpu.VMEM)
SM = pl.BlockSpec(memory_space=pltpu.SMEM)
ANY = pl.BlockSpec(memory_space=pl.ANY)
HBM = pl.BlockSpec(memory_space=pltpu.HBM)


def params(mib):
    return pltpu.CompilerParams(vmem_limit_bytes=mib * 1024 * 1024)


def cost(us):
    return pl.CostEstimate(flops=max(1, int(us * 1e9)), bytes_accessed=1, transcendentals=0)


def dot(left, right):
    return jnp.dot(left, right, preferred_element_type=f32)


def dot_nt(left, right):
    return lax.dot_general(left, right, (((1,), (1,)), ((), ())), preferred_element_type=f32)


def dot_tn(left, right):
    return lax.dot_general(left, right, (((0,), (0,)), ((), ())), preferred_element_type=f32)


def silu(values):
    return values / (1.0 + jnp.exp(-values))


def norm_parts(values):
    centred = values - jnp.mean(values, axis=-1, keepdims=True)
    spread = jnp.mean(centred * centred, axis=-1, keepdims=True)
    inverse = lax.rsqrt(spread + NORM_EPS)
    return centred * inverse, inverse


def norm_back(normed, inverse, scale_part, grad):
    t = grad * (1.0 + scale_part)
    mean_t = jnp.mean(t, axis=-1, keepdims=True)
    mean_tn = jnp.mean(t * normed, axis=-1, keepdims=True)
    return (t - mean_t - normed * mean_tn) * inverse


def rows_from(ref, start):
    base = pl.multiple_of(start // 8 * 8, 8)
    shift = start - base
    tall = LEN + 8
    turned = pltpu.roll(ref[pl.ds(base, tall), :], jnp.where(shift == 0, 0, tall - shift), 0)
    return turned[:LEN]


def slot_rows(slot):
    return slice(slot * LEN, (slot + 1) * LEN)


def mod_part(mod_ref, slot, part):
    return mod_ref[slot : slot + 1, part * D : (part + 1) * D]


def place_of(block, chip):
    rel = jnp.bitwise_xor(block, chip)
    return jnp.bitwise_and(rel, 3) * 4 + lax.shift_right_logical(rel, 2)


def lay_out(where_ref, halves, rows, targets, z_order, split_rows=False):
    chip, core = where_ref[0], where_ref[1]
    for side in range(2):
        half = core if side == 0 else 1 - core
        place = 0
        for ref in halves[side]:
            for spot in range(ref.shape[0] // rows):
                block = jnp.bitwise_xor(z_order[place % 4] * 4 + place // 4, chip)
                place += 1
                for target, first, width in targets:
                    if split_rows:
                        to_row, to_col = (2 * block + half) * rows, 0
                    else:
                        to_row, to_col = block * rows, pl.multiple_of(half * width, 128)
                    to_row = pl.multiple_of(to_row, 16)
                    target[pl.ds(to_row, rows), pl.ds(to_col, width)] = ref[
                        spot * rows : (spot + 1) * rows, first : first + width
                    ]


def start_all(copies):
    for copy in copies:
        copy.start()
    return copies


def fetch(pairs, sems, first=0):
    return start_all(
        [pltpu.make_async_copy(a, b, sems.at[first + i]) for i, (a, b) in enumerate(pairs)]
    )


def wait_all(copies):
    for copy in copies:
        copy.wait()


def begin_kernel(
    where_ref, counts_ref, cond_in, ada_in, tok_in, cot_in, qkv_in, proj_in, fc1_in,
    mine_ref, send_ref, edge_ref, place_ref, starts_ref, slots_ref, parts_ref,
    wide, cond, ada, sems,
):
    devices = counts_ref.shape[0]
    images = cond.shape[0]
    core, me = where_ref[1], where_ref[2]
    copies = []
    first = 0
    for ref in (qkv_in, proj_in, fc1_in):
        half = ref.shape[1] // 2
        for out, at in ((send_ref, 1 - core), (mine_ref, core)):
            copies.append(
                (
                    ref.at[:, pl.ds(pl.multiple_of(at * half, 128), half)],
                    out.at[:, pl.ds(first, half)],
                )
            )
        first += half
    copies.append((tok_in.at[pl.ds(0, LEN), :], edge_ref.at[pl.ds(0, LEN), :]))
    copies.append((cot_in.at[pl.ds(0, LEN), :], edge_ref.at[pl.ds(LEN, LEN), :]))
    copies = fetch([*copies, (cond_in, cond), (ada_in, ada)], sems)

    def step(d, first_row):
        count = counts_ref[d]
        begin = (first_row + LEN - 1) // LEN
        starts_ref[d] = begin

        @pl.when(d == me)
        def _():
            lead = begin * LEN - first_row
            place_ref[0] = lead
            place_ref[1] = count
            place_ref[2] = (first_row + count + LEN - 1) // LEN - begin
            place_ref[3] = count - lead
            place_ref[4] = begin

        return first_row + count

    lax.fori_loop(0, devices, step, jnp.int32(0))
    sub = lax.broadcasted_iota(jnp.int32, (8, images), 0)
    lane = lax.broadcasted_iota(jnp.int32, (8, images), 1)

    @pl.loop(0, devices)
    def _(d):
        hit = (lane == starts_ref[d] + sub) & (sub < SLOTS)
        wide[pl.ds(pl.multiple_of(d * 8, 8), 8), :] = jnp.where(hit, 1.0, 0.0)

    wait_all(copies)
    span = parts_ref.shape[2]
    for d in range(devices):
        parts_ref[d] = ada[:, d * span : (d + 1) * span]
    act = silu(cond[...].astype(f32)).astype(bf16)
    slots_ref[...] = dot(wide[...].astype(bf16), act).astype(bf16)


def ada_kernel(
    where_ref, starts_ref, early_ref, late_ref, ada_ref, cond_ref,
    qkv_sum_ref, proj_sum_ref, fc2_sum_ref, fc1_sum_ref,
    grad_ref, colsum_ref, last_ref, wide, packed,
):
    devices = early_ref.shape[0]
    images, own = cond_ref.shape[0], ada_ref.shape[0]
    me = where_ref[2]
    row = lax.broadcasted_iota(jnp.int32, (own, D), 0)
    lane = lax.broadcasted_iota(jnp.int32, (own, D), 1)
    chosen = jnp.where(lane == me * own + row, 1.0, 0.0).astype(bf16)
    act = silu(cond_ref[...].astype(f32)).astype(bf16)
    act_own = dot_nt(act, chosen).astype(bf16)
    cond_own = dot_nt(chosen, cond_ref[...])
    total = jnp.zeros((own, images), f32)
    for ref, parts in ((early_ref, (2, 3, 4, 5)), (late_ref, (0, 1))):
        many = len(parts)
        high = many * SLOTS
        tall = devices * high
        sub = lax.broadcasted_iota(jnp.int32, (high, images), 0)
        lane = lax.broadcasted_iota(jnp.int32, (high, images), 1)

        @pl.loop(0, devices)
        def _(d):
            hit = lane == starts_ref[d] + sub % SLOTS
            wide[pl.ds(pl.multiple_of(d * high, high), high), :] = jnp.where(hit, 1.0, 0.0)

        picker = wide[0:tall, :]
        act_rows = dot(picker.astype(bf16), act_own)
        part_down = lax.broadcasted_iota(jnp.int32, (tall, 1), 0) % high // SLOTS
        part_across = lax.broadcasted_iota(jnp.int32, (1, tall), 1) % high // SLOTS
        act_parts = jnp.concatenate(
            [jnp.where(part_down == i, act_rows, 0.0) for i in range(many)], axis=1
        ).astype(bf16)
        ours = lax.broadcasted_iota(jnp.int32, (8, tall), 0) == part_across
        ours = jnp.where(ours, 1.0, 0.0).astype(bf16)
        sums = ref[...].reshape(tall, D)
        grads = dot_tn(act_parts, sums)
        colsums = dot(ours, sums)
        back = jnp.zeros((own, tall), f32)
        for i, part in enumerate(parts):
            cols = slice(part * D, (part + 1) * D)
            grad_ref[:, cols] = grads[i * own : (i + 1) * own]
            colsum_ref[:, cols] = colsums[i : i + 1]
            back += jnp.where(part_across == i, dot_nt(ada_ref[:, cols], sums), 0.0)
        total += jnp.dot(back, picker, precision=lax.Precision.HIGHEST)
    gate = 1.0 / (1.0 + jnp.exp(-cond_own))
    total = total * (gate * (1.0 + cond_own * (1.0 - gate)))
    lanes = last_ref.shape[2]
    fc1_sum = fc1_sum_ref[...]
    both = qkv_sum_ref[...]
    vectors = [both[:, :D], both[:, 2 * D :], proj_sum_ref[...], fc2_sum_ref[...]]
    for d in range(devices):
        packed[...] = jnp.zeros(packed.shape, f32)
        packed[0:own, 0:images] = total
        for j in range(8):
            if j < 4:
                value = vectors[j][:, d * own : (d + 1) * own]
            else:
                at = (4 * d + j - 4) * own
                value = fc1_sum[:, at : at + own]
            packed[own + j : own + j + 1, 0:own] = value
        last_ref[d] = packed[...].astype(bf16)


def finish_kernel(got_ref, cond_ref, bias_ref, tall):
    devices, rows, _ = got_ref.shape
    own = rows - 8
    total = None
    for d in range(devices):
        got = got_ref[d].astype(f32)
        tall[d * own : (d + 1) * own, :] = got[0:own]
        total = got[own:rows] if total is None else total + got[own:rows]
    cond_ref[...] = tall[...].T[0 : cond_ref.shape[0], :]
    bias_ref[...] = total


def mod_kernel(slots_ref, cols_ref, addend_ref, out_ref):
    value = dot(slots_ref[...], cols_ref[...])
    for d in range(out_ref.shape[0]):
        out_ref[d] = value[d * 8 : (d + 1) * 8, :] + addend_ref[...]


def prep_kernel(
    place_ref, got_ref, tok_in, cot_in, halo_in, kept_in, table_in,
    res_ref, gc_ref, mod_ref, qkv_bias_ref, proj_bias_ref, fc2_bias_ref, fc1_bias_ref,
    tok, cot, halo, kept, table, sems,
):
    copies = fetch(
        [(table_in, table), (kept_in, kept), (halo_in, halo), (tok_in, tok), (cot_in, cot)], sems
    )
    devices, _, span = got_ref.shape
    width = D // devices
    qkv_bias_ref[:, D : 2 * D] = jnp.zeros((1, D), f32)
    for d in range(devices):
        got = got_ref[d]
        mod_ref[:, d * span : (d + 1) * span] = got[0:SLOTS]
        cols = slice(d * width, (d + 1) * width)
        qkv_bias_ref[:, cols] = got[4:5, 0:width]
        qkv_bias_ref[:, 2 * D + d * width : 2 * D + (d + 1) * width] = got[4:5, width : 2 * width]
        proj_bias_ref[:, cols] = got[4:5, 2 * width : 3 * width]
        fc2_bias_ref[:, cols] = got[4:5, 3 * width : 4 * width]
        fc1_bias_ref[:, d * 4 * width : (d + 1) * 4 * width] = got[5:6, 0 : 4 * width]
    lead, count, slots, begin = place_ref[0], place_ref[1], place_ref[2], place_ref[4]
    wait_all(copies)
    angles = table[...]
    high = angles.astype(bf16)
    rest = angles - high.astype(f32)
    middle = rest.astype(bf16)
    lowest = (rest - middle.astype(f32)).astype(bf16)
    images = kept.shape[0]
    sub = lax.broadcasted_iota(jnp.int32, (8, images), 0)
    lane = lax.broadcasted_iota(jnp.int32, (8, images), 1)
    picker = jnp.where(lane == begin + sub, 1.0, 0.0).astype(bf16)
    patches = dot(picker, kept[...].astype(f32).astype(bf16)).astype(jnp.int32)
    for slot in range(SLOTS):
        row = lax.broadcasted_iota(jnp.int32, (LEN, TOK_DEV), 0) + slot * LEN
        source = row + lead
        live = slot < slots
        column = lax.broadcasted_iota(jnp.int32, (LEN, TOK_DEV), 1)
        own = jnp.where((column == source) & (source < count) & live, 1.0, 0.0).astype(bf16)
        far = source[:, :LEN] - count
        spill = jnp.where((column[:, :LEN] == far) & live, 1.0, 0.0).astype(bf16)
        taken = dot(own, tok[...]) + dot(spill, halo[0:LEN, :])
        grad = dot(own, cot[...]) + dot(spill, halo[LEN : 2 * LEN, :])
        gc_ref[slot_rows(slot), :] = grad.astype(bf16)
        patch = patches[slot : slot + 1, :]
        index = lax.broadcasted_iota(jnp.int32, (GRID, LEN), 0)
        line = jnp.where((index == patch // GRID) & live, 1.0, 0.0).astype(bf16)
        across = jnp.where((index == patch % GRID) & live, 1.0, 0.0).astype(bf16)
        half = D // 2
        for start, picked in ((0, line), (half, across)):
            spot = dot_tn(picked, high) + (dot_tn(picked, middle) + dot_tn(picked, lowest))
            res_ref[slot_rows(slot), start : start + half] = taken[:, start : start + half] + spot


def head_masks():
    lane = lax.broadcasted_iota(jnp.int32, (1, 2 * HD), 1)
    first = jnp.where(lane < HD, 1.0, 0.0).astype(bf16)
    return first, (1.0 - first.astype(f32)).astype(bf16)


def both_heads(pair, masks):
    return jnp.concatenate([pair * masks[0], pair * masks[1]], axis=0)


def side_by_side(stacked):
    return jnp.concatenate([stacked[:LEN], stacked[LEN:]], axis=1)


def pair_probs(queries, keys):
    scores = dot_nt(queries, keys) * (1.0 / math.sqrt(HD))
    exp_terms = jnp.exp(scores - jnp.max(scores, axis=1, keepdims=True))
    return exp_terms * (1.0 / jnp.sum(exp_terms, axis=1, keepdims=True))


def qkv_kernel(
    where_ref, res_ref, mod_ref, bias_ref, near_ref, far_ref, ain_out, qkv_ref, weight_out, ain_ref, weight, sems
):
    for slot in range(SLOTS):
        normed, _ = norm_parts(res_ref[slot_rows(slot), :])
        ain_ref[slot_rows(slot), :] = (
            normed * (1.0 + mod_part(mod_ref, slot, 1)) + mod_part(mod_ref, slot, 0)
        ).astype(bf16)
    out = fetch([(ain_ref, ain_out)], sems)
    lay_out(where_ref, ([near_ref], [far_ref]), D // BLOCKS, [(weight, 0, 3 * D // 2)], NEAR_FIRST)
    out += fetch([(weight, weight_out)], sems, 1)

    @pl.loop(0, 3 * D // 256)
    def _(j):
        cols = pl.ds(pl.multiple_of(j * 256, 256), 256)
        qkv_ref[:, cols] = (dot(ain_ref[...], weight[:, cols]) + bias_ref[:, cols]).astype(bf16)

    wait_all(out)


def attend_kernel(qkv_ref, att_ref, att_out, sems):
    masks = head_masks()

    @pl.loop(0, SLOTS)
    def _(slot):
        rows = pl.ds(pl.multiple_of(slot * LEN, LEN), LEN)
        for pair in range(HEADS // 2):
            at = pair * 2 * HD
            probs = pair_probs(
                both_heads(qkv_ref[rows, at : at + 2 * HD], masks),
                qkv_ref[rows, D + at : D + at + 2 * HD],
            )
            values = both_heads(qkv_ref[rows, 2 * D + at : 2 * D + at + 2 * HD], masks)
            att_ref[rows, at : at + 2 * HD] = dot(
                side_by_side(probs.astype(bf16)), values
            ).astype(bf16)

    wait_all(fetch([(att_ref, att_out)], sems))


def join_kernel(*refs):
    *parts, both, sems = refs
    pairs, first = [], 0
    for ref in parts:
        rows = ref.shape[0]
        pairs.append((ref, both.at[pl.ds(first, rows), :]))
        first += rows
    wait_all(fetch(pairs, sems))


def cut_kernel(near_ref, x_ref, y_ref, most_ref, low_ref, high_ref, sems):
    rows = near_ref.shape[0]
    half = rows // 2
    pairs = [(y_ref.at[pl.ds(0, half), :], low_ref), (x_ref.at[pl.ds(half, half), :], high_ref)]
    for i, ref in enumerate((near_ref, x_ref, y_ref)):
        pairs.append((ref, most_ref.at[pl.ds(i * rows, rows), :]))
    wait_all(fetch(pairs, sems))


def flip(where_ref, lhs_ref, ordered, split_rows):
    chip, core = where_ref[0], where_ref[1]
    depth = ordered.shape[0]
    size = depth // BLOCKS
    if split_rows:
        size //= 2
    step = 384
    for m in range(depth // step):
        turned = lhs_ref[:, m * step : (m + 1) * step].T
        for i in range(step // size):
            block = m * (step // size) + i
            side = block % 2
            to = place_of(block // 2 if split_rows else block, chip) * size
            if split_rows:
                to = to + jnp.where(core == side, depth // 2, 0)
            ordered[pl.ds(pl.multiple_of(to, 16), size), :] = turned[i * size : (i + 1) * size, :]


def hidden_kernel(
    where_ref, res_ref, att_ref, mod_ref, gc_ref, proj_bias_ref, bias_ref, *rest
):
    mine, more, theirs, rest_far = rest[:4]
    branch_ref, mid_ref, min_ref, gmo_ref, colsum_ref, act_out, slope_out, send_out, keep_out, mid_out = rest[4:14]
    proj, weight, act, slope, ordered, made, out_sems = rest[14:]
    total = jnp.zeros((1, D), f32)
    for slot in range(SLOTS):
        rows = slot_rows(slot)
        grad = (mod_part(mod_ref, slot, 5) * gc_ref[rows, :].astype(f32)).astype(bf16)
        gmo_ref[rows, :] = grad
        total += jnp.sum(grad.astype(f32), axis=0, keepdims=True)
    colsum_ref[...] = total
    lay_out(
        where_ref,
        ([mine, more], [theirs, rest_far]),
        D // BLOCKS,
        [(proj, 0, D // 2), (weight, D // 2, F // 2)],
        NEAR_FIRST,
    )
    for j in range(D // 256):
        cols = slice(j * 256, (j + 1) * 256)
        branch_ref[:, cols] = dot(att_ref[...], proj[:, cols]) + proj_bias_ref[:, cols]
    for slot in range(SLOTS):
        rows = slot_rows(slot)
        mid = res_ref[rows, :] + mod_part(mod_ref, slot, 2) * branch_ref[rows, :]
        mid_ref[rows, :] = mid
        normed, _ = norm_parts(mid)
        min_ref[rows, :] = (
            normed * (1.0 + mod_part(mod_ref, slot, 4)) + mod_part(mod_ref, slot, 3)
        ).astype(bf16)

    @pl.loop(0, F // 256)
    def _(j):
        cols = pl.ds(pl.multiple_of(j * 256, 256), 256)
        u = dot(min_ref[...], weight[:, cols]) + bias_ref[:, cols]
        square = u * u
        bend = jnp.tanh(GELU_COEF * (u + 0.044715 * square * u))
        left = 0.5 * (1.0 + bend)
        act[:, cols] = (u * left).astype(bf16)
        slope[:, cols] = (
            left
            + 0.5 * u * (1.0 - bend * bend) * (GELU_COEF * (1.0 + 3.0 * 0.044715 * square))
        ).astype(bf16)

    out = fetch([(act, act_out), (slope, slope_out)], out_sems)
    out += fetch([(mid_ref, mid_out)], out_sems, 8)
    flip(where_ref, act, ordered, True)
    step = 512
    for j in range(F // step):
        made[j * step : (j + 1) * step, :] = dot(
            ordered[j * step : (j + 1) * step, :], gmo_ref[...]
        ).astype(bf16)
        to, at = (send_out, j) if j < F // step // 2 else (keep_out, j - F // step // 2)
        out += fetch(
            [(made.at[pl.ds(j * step, step), :], to.at[pl.ds(at * step, step), :])],
            out_sems,
            2 + j,
        )
    wait_all(out)


def flips_kernel(where_ref, first_ref, second_in, third_in, flipped_ref, second_out, third_out, second, third, turned, sems):
    copies = fetch([(second_in, second), (third_in, third)], sems)
    flip(where_ref, first_ref, flipped_ref, False)
    out = []
    for i, (ref, to) in enumerate(((second, second_out), (third, third_out))):
        wait_all([copies[i]])
        flip(where_ref, ref, turned.at[i], False)
        out += fetch([(turned.at[i], to)], sems, 2 + i)
    wait_all(out)


def wgrad_kernel(count, where_ref, *rest):
    lhs, rhs = rest[:count], rest[count : 2 * count]
    send_out, keep_out, send, keep, sems, *late = rest[2 * count :]
    core = where_ref[1]
    if late:
        *bufs, in_sems = late
        ins = fetch([(lhs[0], bufs[0]), (rhs[0], bufs[1]), (lhs[1], bufs[2])], in_sems)
        lhs, rhs = (bufs[0], bufs[2]), (bufs[1], rhs[1])
    step = 384
    first = 0
    out = []
    for ordered, rhs_ref in zip(lhs, rhs):
        if late:
            wait_all(ins[2:] if first else ins[:2])
        width = rhs_ref.shape[1] // 2
        for buf, to, half in ((send, send_out, 1 - core), (keep, keep_out, core)):
            cols = pl.ds(pl.multiple_of(half * width, 128), width)
            for j in range(D // step):
                rows = slice(j * step, (j + 1) * step)
                buf[rows, first : first + width] = dot(
                    ordered[rows, :], rhs_ref[:, cols]
                ).astype(bf16)
                here = (pl.ds(j * step, step), pl.ds(first, width))
                out += fetch([(buf.at[here], to.at[here])], sems, len(out))
        first += width
    wait_all(out)


def pair_sums(keep_in, got_ref, rows, spans, keep, sems, got=None):
    copies = []
    for i, first in enumerate(spans):
        here, there = pl.ds(i * rows, rows), pl.ds(first, rows)
        pairs = [(keep_in.at[there, :], keep.at[here, :])]
        if got is not None:
            pairs.append((got_ref.at[there, :], got.at[here, :]))
        copies.append(fetch(pairs, sems, 2 * i))

    def total(i):
        wait_all(copies[i])
        here = slice(i * rows, (i + 1) * rows)
        other = got_ref[spans[i] : spans[i] + rows, :] if got is None else got[here, :]
        return keep[here, :].astype(f32) + other.astype(f32)

    return total


def first_kernel(keep_in, got_ref, x_ref, y_ref, keep, sems, *got):
    rows = x_ref.shape[0] // 2
    total = pair_sums(keep_in, got_ref, rows, [2 * rows, 6 * rows, 5 * rows, 7 * rows], keep, sems, *got)
    for i in range(4):
        ref = (x_ref, y_ref)[i // 2]
        ref[i % 2 * rows : (i % 2 + 1) * rows, :] = total(i).astype(bf16)


def second_kernel(keep_in, got_ref, x_got_ref, y_got_ref, x_ref, y_ref, keep, sems, *got):
    rows = x_ref.shape[0]
    total = pair_sums(keep_in, got_ref, rows, [3 * rows, 4 * rows], keep, sems, *got)
    x_ref[...] = (total(0) + y_got_ref[rows:, :].astype(f32)).astype(bf16)
    y_ref[...] = (total(1) + x_got_ref[rows:, :].astype(f32)).astype(bf16)


def near_kernel(direct, keep_in, got_ref, x_one_ref, y_one_ref, x_two_ref, y_two_ref, *rest):
    if direct:
        outs, (keep, sems, *got) = rest[:4], rest[4:]
    else:
        send_ref, own_out, beyond_out, keep, sems, own, beyond, out_sems = rest
        got = ()
        outs = (send_ref, own, beyond)
    half = x_two_ref.shape[0]
    rows = half // 2
    total = pair_sums(keep_in, got_ref, half, [0, half], keep, sems, *got)
    for i, (one_ref, two_ref) in enumerate(((x_one_ref, y_two_ref), (y_one_ref, x_two_ref))):
        both = total(i) + one_ref[0:half, :].astype(f32) + two_ref[...].astype(f32)
        for j in range(2):
            z = 2 * i + j
            value = both[j * rows : (j + 1) * rows]
            if direct:
                outs[z][...] = value.astype(outs[z].dtype)
            elif j:
                outs[0][i * rows : (i + 1) * rows, :] = value.astype(bf16)
            else:
                outs[1 + i][...] = value
    if not direct:
        wait_all(fetch([(own, own_out), (beyond, beyond_out)], out_sems))


def beyond_kernel(got_ref, own_in, beyond_in, send_ref, total_out, own, beyond, sems):
    wait_all(fetch([(own_in, own), (beyond_in, beyond)], sems))
    rows = own.shape[0]
    send_ref[...] = (beyond[...] + got_ref[rows:, :].astype(f32)).astype(bf16)
    own[...] = own[...] + got_ref[0:rows, :].astype(f32)
    wait_all(fetch([(own, total_out)], sems, 2))


def lay_out_fc2(where_ref, near_ref, far_ref, fc2):
    lay_out(where_ref, ([near_ref], [far_ref]), F // (2 * BLOCKS), [(fc2, 0, D)], FAR_FIRST, True)


def fc2_back_kernel(
    where_ref, gmo_ref, slope_in, near_ref, far_ref, gh_ref, colsum_ref, fc2, slope, in_sems
):
    step = 512
    parts = [pl.ds(j * step, step) for j in range(F // step)]
    late = fetch([(slope_in.at[:, part], slope.at[:, part]) for part in parts], in_sems)
    lay_out_fc2(where_ref, near_ref, far_ref, fc2)
    for j in range(F // step):
        wait_all([late[j]])
        for half in range(2):
            cols = slice(j * step + half * 256, j * step + (half + 1) * 256)
            grad = dot_nt(gmo_ref[...], fc2[cols, :])
            value = (slope[:, cols].astype(f32) * grad).astype(bf16)
            gh_ref[:, cols] = value
            colsum_ref[:, cols] = jnp.sum(value.astype(f32), axis=0, keepdims=True)


def fc2_out_kernel(
    where_ref, place_ref, mod_ref, gc_ref, bias_ref, mid_in, act_in, near_ref, far_ref,
    tail_ref, gate_ref, out_out, mid_ref, act, fc2, mlp, made, in_sems,
):
    last = fetch([(act_in, act), (mid_in, mid_ref)], in_sems)
    lay_out_fc2(where_ref, near_ref, far_ref, fc2)
    wait_all(last)
    for j in range(D // 256):
        cols = slice(j * 256, (j + 1) * 256)
        mlp[0:TOK_DEV, cols] = dot(act[...], fc2[:, cols]) + bias_ref[:, cols]
    for slot in range(SLOTS):
        rows = slot_rows(slot)
        value = mlp[rows, :]
        gate_ref[slot : slot + 1, :] = jnp.sum(
            value * gc_ref[rows, :].astype(f32), axis=0, keepdims=True
        )
        value = mid_ref[rows, :] + mod_part(mod_ref, slot, 5) * value
        mlp[rows, :] = value
        made[rows, :] = value.astype(bf16)
    out = fetch([(made, out_out)], in_sems, 2)
    mlp[TOK_DEV:, :] = jnp.zeros((LEN + 8, D), f32)
    tail_ref[...] = rows_from(mlp, place_ref[3]).astype(bf16)
    wait_all(out)


def keep_sum(sums, part, slot, values):
    at = part * SLOTS + slot
    sums[at : at + 1, :] = jnp.sum(values, axis=0, keepdims=True)


def spread_sums(sums, spread_ref):
    value = sums[...].astype(bf16)
    for d in range(spread_ref.shape[0]):
        spread_ref[d] = value


def mid_back_kernel(
    where_ref, gh_ref, mid_ref, branch_ref, mod_ref, gc_ref, gate_ref, mine, more, theirs, rest_far,
    ga_ref, proj_sum_ref, gm_out, gb_out, spread_out,
    gm_ref, gb_ref, spread_ref, proj, weight, grads, sums, out_sems,
):
    lay_out(
        where_ref,
        ([mine, more], [theirs, rest_far]),
        D // BLOCKS,
        [(proj, 0, D // 2), (weight, D // 2, F // 2)],
        NEAR_FIRST,
    )
    for j in range(D // 256):
        cols = slice(j * 256, (j + 1) * 256)
        grads[:, cols] = dot_nt(gh_ref[...], weight[cols, :])
    total = jnp.zeros((1, D), f32)
    for slot in range(SLOTS):
        rows = slot_rows(slot)
        normed, inverse = norm_parts(mid_ref[rows, :])
        e = grads[rows, :]
        keep_sum(sums, 1, slot, e)
        keep_sum(sums, 2, slot, e * normed)
        grad_mid = gc_ref[rows, :].astype(f32) + norm_back(
            normed, inverse, mod_part(mod_ref, slot, 4), e
        )
        gm_ref[rows, :] = grad_mid
        keep_sum(sums, 0, slot, branch_ref[rows, :] * grad_mid)
        value = (mod_part(mod_ref, slot, 2) * grad_mid).astype(bf16)
        gb_ref[rows, :] = value
        total += jnp.sum(value.astype(f32), axis=0, keepdims=True)
    proj_sum_ref[...] = total
    sums[3 * SLOTS :, :] = gate_ref[...]
    spread_sums(sums, spread_ref)
    out = fetch([(gm_ref, gm_out), (gb_ref, gb_out), (spread_ref, spread_out)], out_sems)
    for j in range(D // 256):
        cols = slice(j * 256, (j + 1) * 256)
        ga_ref[:, cols] = dot_nt(gb_ref[...], proj[cols, :]).astype(bf16)
    wait_all(out)


def probs_kernel(qk_in, probs_out, qk, probs, sems):
    masks = head_masks()
    copies = fetch(
        [
            (qk_in.at[pl.ds(slot * LEN, LEN), pl.ds(0, 2 * D)], qk.at[pl.ds(slot * LEN, LEN), :])
            for slot in range(SLOTS)
        ],
        sems,
    )
    out = []
    for slot in range(SLOTS):
        wait_all([copies[slot]])
        rows = slot_rows(slot)
        tall = HEADS // 2 * LEN
        for pair in range(HEADS // 2):
            at = pair * 2 * HD
            queries = both_heads(qk[rows, at : at + 2 * HD], masks)
            scores = dot_nt(qk[rows, D + at : D + at + 2 * HD], queries) * (1.0 / math.sqrt(HD))
            exp_terms = jnp.exp(scores - jnp.max(scores, axis=0, keepdims=True))
            first = slot * tall + pair * LEN
            probs[first : first + LEN, :] = exp_terms * (
                1.0 / jnp.sum(exp_terms, axis=0, keepdims=True)
            )
        here = pl.ds(slot * tall, tall)
        out += fetch([(probs.at[here, :], probs_out.at[here, :])], sems, SLOTS + slot)
    wait_all(out)


def attend_back_kernel(qkv_in, probs_in, ga_ref, gqkv_ref, colsum_ref, qkv, probs, sems):
    masks = head_masks()
    first_head = lax.broadcasted_iota(jnp.int32, (1, 2 * HD), 1) < HD
    scale = 1.0 / math.sqrt(HD)
    tall = HEADS // 2 * LEN
    copies = []
    for slot in range(SLOTS):
        here, there = pl.ds(slot * LEN, LEN), pl.ds(slot * tall, tall)
        copies += fetch(
            [
                (qkv_in.at[here, :], qkv.at[here, :]),
                (probs_in.at[there, :], probs.at[there, :]),
            ],
            sems,
            2 * slot,
        )
    for first in range(0, SLOTS, 2):
        wait_all(copies[2 * first : 2 * first + 4])

        @pl.loop(first, first + 2)
        def _(slot):
            rows = pl.ds(pl.multiple_of(slot * LEN, LEN), LEN)
            for pair in range(HEADS // 2):
                at = pair * 2 * HD
                q_cols, k_cols, v_cols = (
                    slice(part * D + at, part * D + at + 2 * HD) for part in range(3)
                )
                chances = probs[pl.ds(pl.multiple_of(slot * tall + pair * LEN, LEN), LEN), :]
                grads = both_heads(ga_ref[rows, q_cols], masks)
                weighed = chances * dot_nt(qkv[rows, v_cols], grads)
                inner = jnp.sum(weighed, axis=0, keepdims=True)
                grad_scores = (weighed - chances * inner).astype(bf16)
                grad_queries = dot_tn(grad_scores, qkv[rows, k_cols]) * scale
                gqkv_ref[rows, q_cols] = jnp.where(
                    first_head, grad_queries[:LEN], grad_queries[LEN:]
                ).astype(bf16)
                queries = both_heads(qkv[rows, q_cols], masks)
                gqkv_ref[rows, k_cols] = (dot(grad_scores, queries) * scale).astype(bf16)
                gqkv_ref[rows, v_cols] = dot(chances.astype(bf16), grads).astype(bf16)

    for j in range(3 * D // 256):
        cols = slice(j * 256, (j + 1) * 256)
        colsum_ref[:, cols] = jnp.sum(gqkv_ref[:, cols].astype(f32), axis=0, keepdims=True)


def start_back_kernel(
    place_ref, gqkv_ref, mod_ref, out_tail_ref, res_in, gm_in, weight_in,
    tg_out, tail_out, spread_out, weight, grads, res, gm, sums, tail_ref, spread_ref, in_sems, out_sems,
):
    step = 256
    parts = [pl.ds(j * step, step) for j in range(D // step)]
    copies = fetch([(weight_in.at[part, :], weight.at[part, :]) for part in parts], in_sems)
    late = fetch([(res_in, res), (gm_in, gm)], in_sems, len(parts))
    for j in range(D // step):
        wait_all([copies[j]])
        cols = slice(j * step, (j + 1) * step)
        grads[0:TOK_DEV, cols] = dot_nt(gqkv_ref[...], weight[cols, :])
    wait_all(late)
    out = []
    for slot in range(SLOTS):
        rows = slot_rows(slot)
        normed, inverse = norm_parts(res[rows, :])
        e = grads[rows, :]
        keep_sum(sums, 0, slot, e)
        keep_sum(sums, 1, slot, e * normed)
        grads[rows, :] = gm[rows, :] + norm_back(normed, inverse, mod_part(mod_ref, slot, 1), e)
        here = pl.ds(slot * LEN, LEN)
        out += fetch([(grads.at[here, :], tg_out.at[here, :])], out_sems, slot)
    spread_sums(sums, spread_ref)
    out += fetch([(spread_ref, spread_out)], out_sems, SLOTS)
    grads[TOK_DEV:, :] = jnp.zeros((LEN + 8, D), f32)
    tail = rows_from(grads, place_ref[3])
    high = tail.astype(bf16)
    tail_ref[0:LEN, :] = out_tail_ref[...]
    tail_ref[LEN : 2 * LEN, :] = high
    tail_ref[2 * LEN :, :] = (tail - high.astype(f32)).astype(bf16)
    wait_all(out + fetch([(tail_ref, tail_out)], out_sems, SLOTS + 1))


def place_kernel(
    place_ref, tail_ref, tok_in, cot_in, out_in, tg_in,
    final_out, final_tg, out_rows, tg_rows, tok, cot, out, made_out, made_tg, sems,
):
    lead, count = place_ref[0], place_ref[1]
    copies = fetch(
        [(out_in, out), (tok_in, tok), (tg_in, tg_rows.at[pl.ds(LEN, TOK_DEV), :]), (cot_in, cot)],
        sems,
    )
    for rows in (out_rows, tg_rows):
        rows[0:LEN, :] = jnp.zeros((LEN, D), f32)
        rows[LEN + TOK_DEV :, :] = jnp.zeros((8, D), f32)
    wait_all(copies[:2])
    out_rows[LEN : LEN + TOK_DEV, :] = out[...].astype(f32)
    last = []
    out_tail = tail_ref[0:LEN, :].astype(f32)
    tg_tail = tail_ref[LEN : 2 * LEN, :].astype(f32) + tail_ref[2 * LEN :, :].astype(f32)
    for k, (rows, tail, pad, made, final) in enumerate(
        ((out_rows, out_tail, tok, made_out, final_out), (tg_rows, tg_tail, cot, made_tg, final_tg))
    ):
        if k:
            wait_all(copies[2:])
        for slot in range(SLOTS):
            here = slot_rows(slot)
            row = lax.broadcasted_iota(jnp.int32, (LEN, 1), 0) + slot * LEN
            value = rows_from(rows, LEN - lead + slot * LEN)
            if slot == 0:
                value = jnp.where(row < lead, tail, value)
            value = jnp.where(row < count, value, pad[here, :].astype(f32))
            made[here, :] = value.astype(made.dtype)
        last += fetch([(made, final)], sems, 4 + k)
    wait_all(last)


def shape(*dims, dtype=f32):
    return jax.ShapeDtypeStruct(dims, dtype)


def call(kernel, outs, scratch, mib, ins, spaces, after=(), out_specs=None, us=0, zeros=False):
    taken, held, made = len(ins), len(after), len(outs)
    out_specs = out_specs or [VM] * made

    def body(*refs):
        first = taken + held
        kernel(*refs[:taken], *refs[first : first + made], *refs[first + made + 1 :])
        if zeros:
            refs[first + made][...] = jnp.zeros((8, 128), f32)

    def settled(item):
        is_token = item.shape == (8, 128) and item.dtype == f32
        return pltpu.with_memory_space_constraint(item, pltpu.HBM) if is_token else item

    def placed(item, spec):
        return pltpu.with_memory_space_constraint(item, pltpu.HBM) if spec is HBM else item

    out_specs = [*out_specs, VM if zeros else HBM]
    out_shape = [
        pltpu.HBM(item.shape, item.dtype) if spec is HBM else item
        for item, spec in zip([*outs, shape(8, 128)], out_specs)
    ]
    *results, token = pl.pallas_call(
        body,
        out_shape=out_shape,
        in_specs=list(spaces) + [ANY] * held,
        out_specs=out_specs,
        scratch_shapes=scratch,
        compiler_params=params(mib),
        cost_estimate=cost(us),
        name=getattr(kernel, "func", kernel).__name__,
    )(*[placed(item, spec) for item, spec in zip(ins, spaces)], *[settled(item) for item in after])
    return results, token


def tie(value, token):
    return jnp.where(token[0, 0] == 0.0, value, jnp.zeros_like(value))


def join(parts, after=(), us=0, zeros=False):
    rows = sum(part.shape[0] for part in parts)
    (both,), token = call(
        join_kernel,
        [shape(rows, parts[0].shape[1], dtype=parts[0].dtype)],
        [pltpu.SemaphoreType.DMA((len(parts),))],
        8,
        parts,
        [ANY] * len(parts),
        after=after,
        out_specs=[ANY],
        us=us,
        zeros=zeros,
    )
    return both, token


def tie(value, token):
    return jnp.where(token[0, 0] == 0.0, value, jnp.zeros_like(value))


def low(value):
    return value.astype(bf16)


class Links:
    def __init__(self, devices):
        self.devices = devices
        self.cube = devices == 32
        self.me = lax.axis_index("wide").astype(jnp.int32)
        self.core = self.me % 2 if self.cube else jnp.int32(0)
        self.chip = self.me // 2 if self.cube else jnp.int32(0)
        self.where = jnp.stack([self.chip, self.core, self.me])

    def swap(self, array, bits):
        return lax.ppermute(array, "wide", [(i, i ^ bits) for i in range(self.devices)])

    def by_core(self, first, second):
        return jnp.where(self.core == 0, first, second)

    def pair(self, mine, got):
        return self.by_core(
            jnp.concatenate([mine, got], axis=0), jnp.concatenate([got, mine], axis=0)
        )

    def along_z(self, pair):
        return jnp.concatenate(
            [pair, self.swap(pair, 8), self.swap(pair, 16), self.swap(pair, 24)], axis=0
        )

    def doubled_z(self, pair):
        two = jnp.concatenate([pair, self.swap(pair, 8)], axis=0)
        return jnp.concatenate([two, self.swap(two, 16)], axis=0)

    def gathered(self, shards):
        halves = [[], []]
        for shard in shards:
            whole = lax.all_gather(shard, "wide", axis=0, tiled=True)
            rows, width = whole.shape[0], whole.shape[1] // 2
            whole = whole.reshape(4, 4, rows // BLOCKS, -1).transpose(1, 0, 2, 3)
            whole = whole.reshape(rows, -1)
            halves[0].append(whole[:, :width])
            halves[1].append(whole[:, width:])
        return [jnp.concatenate(half, axis=1) for half in halves]

    def scattered(self, send, keep, widths):
        outs, first = [], 0
        rows = keep.shape[0]
        for width in widths:
            cols = slice(first, first + width)
            whole = jnp.concatenate([keep[:, cols], send[:, cols]], axis=1)
            whole = whole.reshape(4, 4, rows // BLOCKS, -1).transpose(1, 0, 2, 3)
            whole = whole.reshape(rows, -1).astype(f32)
            outs.append(lax.psum_scatter(whole, "wide", scatter_dimension=0, tiled=True))
            first += width
        return outs

    def scattered_rows(self, send, keep):
        whole = jnp.stack([keep, send]).reshape(2, 4, 4, -1, D)
        whole = whole.transpose(2, 1, 0, 3, 4).reshape(-1, D)
        return lax.psum_scatter(whole.astype(f32), "wide", scatter_dimension=0, tiled=True)

    def gathered_rows(self, shard):
        whole = lax.all_gather(shard, "wide", axis=0, tiled=True).reshape(4, 4, 2, -1, D)
        whole = jnp.stack([whole[z] for z in FAR_FIRST], axis=1)
        return [whole[:, :, half].reshape(-1, D) for half in range(2)]

    def first(self, keep, got, after, copied=False):
        rows, width = keep.shape[0] // 4, keep.shape[1]
        (x, y), token = call(
            first_kernel,
            [shape(rows, width, dtype=bf16)] * 2,
            [pltpu.VMEM((2 * rows, width), bf16), pltpu.SemaphoreType.DMA((8,))]
            + [pltpu.VMEM((2 * rows, width), bf16)] * copied,
            16,
            [keep, got],
            [HBM, HBM if copied else VM],
            after=after,
        )
        return [self.swap(x, 2), self.swap(y, 4)], token

    def second(self, keep, got, ones, after, copied=False):
        rows, width = keep.shape[0] // 8, keep.shape[1]
        (x, y), token = call(
            second_kernel,
            [shape(rows, width, dtype=bf16)] * 2,
            [pltpu.VMEM((2 * rows, width), bf16), pltpu.SemaphoreType.DMA((4,))]
            + [pltpu.VMEM((2 * rows, width), bf16)] * copied,
            16,
            [keep, got, *ones],
            [HBM, HBM if copied else VM, VM, VM],
            after=after,
            us=100,
        )
        return [self.swap(x, 2), self.swap(y, 4)], token

    def near_sum(self, keep, got, ones, twos, direct, after):
        tall, width = keep.shape[0] // 4, keep.shape[1]
        rows = tall // 4
        if direct:
            outs = [shape(rows, width)] + [shape(rows, width, dtype=bf16)] * 3
        else:
            outs = [shape(2 * rows, width, dtype=bf16)] + [shape(rows, width)] * 2
        scratch = [pltpu.VMEM((tall, width), bf16), pltpu.SemaphoreType.DMA((4,))]
        scratch += [pltpu.VMEM((tall, width), bf16)] * direct
        if not direct:
            scratch += [pltpu.VMEM((rows, width), f32)] * 2 + [pltpu.SemaphoreType.DMA((2,))]
        return call(
            functools.partial(near_kernel, direct),
            outs,
            scratch,
            16,
            [keep, got, *ones, *twos],
            [HBM, HBM if direct else VM] + [VM] * 4,
            after=after,
            out_specs=[VM] * 4 if direct else [VM, HBM, HBM],
            us=100,
        )

    def z_sum(self, token, own, *parts):
        own = tie(own, token)
        for part, bits in zip(parts, (8, 16, 24)):
            own = own + self.swap(part, bits).astype(f32)
        return own

    def halved_z(self, send, own, beyond, after):
        (send, total), token = call(
            beyond_kernel,
            [shape(*own.shape, dtype=bf16), shape(*own.shape)],
            [pltpu.VMEM(own.shape, f32)] * 2 + [pltpu.SemaphoreType.DMA((3,))],
            8,
            [self.swap(send, 8), own, beyond],
            [VM, HBM, HBM],
            after=after,
            out_specs=[VM, HBM],
        )
        return total, self.swap(send, 16), token

    def own_rows(self, own, widths):
        rows = own.shape[0] // 2
        mine = self.by_core(own[:rows], own[rows:])
        got = self.swap(self.by_core(own[rows:], own[:rows]), 1)
        outs, first = [], 0
        for width in widths:
            a, b = mine[:, first : first + width], got[:, first : first + width]
            outs.append(
                self.by_core(jnp.concatenate([a, b], axis=1), jnp.concatenate([b, a], axis=1))
            )
            first += width
        return outs


def on_device(
    tokens,
    cotangent,
    cond,
    kept,
    counts,
    ada_w,
    ada_bias,
    qkv_w,
    q_bias,
    v_bias,
    proj_w,
    proj_bias,
    fc1_w,
    fc1_bias,
    fc2_w,
    fc2_bias,
):
    devices = lax.axis_size("wide")
    images = cond.shape[0]
    span = ada_bias.shape[0]
    own_dim = ada_w.shape[0]
    links = Links(devices)
    me, where, cube = links.me, links.where, links.cube
    rows = TOK_DEV
    dma = pltpu.SemaphoreType.DMA
    half_sum = (qkv_w.shape[1] + proj_w.shape[1] + fc1_w.shape[1]) // 2

    (mine, send, edge, place, starts, cond_slots, ada_parts), _ = call(
        begin_kernel,
        [
            shape(own_dim, half_sum, dtype=bf16),
            shape(own_dim, half_sum, dtype=bf16),
            shape(2 * LEN, D, dtype=bf16),
            shape(8, dtype=jnp.int32),
            shape(devices, dtype=jnp.int32),
            shape(devices * 8, D, dtype=bf16),
            shape(devices, own_dim, span, dtype=bf16),
        ],
        [
            pltpu.VMEM((devices * 8, images), f32),
            pltpu.VMEM(cond.shape, bf16),
            pltpu.VMEM(ada_w.shape, bf16),
            dma((10,)),
        ],
        16,
        [where, counts, cond, ada_w, tokens, cotangent, qkv_w, proj_w, fc1_w],
        [SM, SM] + [HBM] * 7,
        out_specs=[VM, VM, VM, SM, SM, VM, VM],
    )
    if cube:
        pair = links.pair(mine, links.swap(send, 1))
        near_one = links.along_z(pair[:, : 3 * D // 2])
        before_mod = [pair]
    else:
        before_mod = []
    halo = lax.ppermute(edge, "wide", [(i + 1, i) for i in range(devices - 1)])

    ada_cols = lax.all_to_all(ada_parts, "wide", 0, 0, tiled=True)
    ada_cols = ada_cols.reshape(D, span)
    lanes = lambda items: jnp.pad(
        jnp.concatenate(items), (0, span - sum(i.shape[0] for i in items))
    ).reshape(1, span)
    addend = jnp.concatenate(
        [
            jnp.broadcast_to(ada_bias.reshape(1, span), (SLOTS, span)),
            lanes([q_bias, v_bias, proj_bias, fc2_bias]),
            lanes([fc1_bias]),
            jnp.zeros((2, span), bf16),
        ],
        axis=0,
    ).astype(f32)
    (mod_cols,), mod_ran = call(
        mod_kernel,
        [shape(devices, 8, span)],
        [],
        16,
        [cond_slots, ada_cols, addend],
        [VM] * 3,
        after=before_mod,
        zeros=True,
    )
    mixed = lax.all_to_all(mod_cols, "wide", 0, 0, tiled=True)

    quarter = D // 4
    frequency = jnp.exp(-math.log(10000.0) * jnp.arange(quarter).astype(f32) / quarter)
    angle = jnp.arange(GRID).astype(f32)[:, None] * frequency[None, :]
    table = jnp.concatenate([jnp.sin(angle), jnp.cos(angle)], axis=1)
    if cube:
        near_one = tie(near_one, mod_ran)
        over = [links.swap(near_one, bits) for bits in (2, 4, 6)]
        pair_two = tie(pair[:, 3 * D // 2 :], mod_ran)
        two = jnp.concatenate([pair_two, links.swap(pair_two, 8)], axis=0)
        before_prep = [near_one, two]
    else:
        before_prep = []
    (residual, grad_out, mod, qkv_bias, proj_bias_all, fc2_bias_all, fc1_bias_all), prepared = call(
        prep_kernel,
        [
            shape(rows, D),
            shape(rows, D, dtype=bf16),
            shape(SLOTS, 6 * D),
            shape(1, 3 * D),
            shape(1, D),
            shape(1, D),
            shape(1, F),
        ],
        [
            pltpu.VMEM((rows, D), bf16),
            pltpu.VMEM((rows, D), bf16),
            pltpu.VMEM((2 * LEN, D), bf16),
            pltpu.VMEM(kept.shape, jnp.int32),
            pltpu.VMEM(table.shape, f32),
            dma((5,)),
        ],
        16,
        [place, mixed, tokens, cotangent, halo, kept, table],
        [SM, VM, HBM, HBM, ANY, HBM, ANY],
        after=before_prep,
        us=10,
    )

    if cube:
        near_two = jnp.concatenate([two, links.swap(two, 16)], axis=0)
        qkv_near, joined = join([near_one, *over], [prepared, near_two])
        qkv_far = links.swap(qkv_near, 1)
        over_x, over_y = links.swap(near_two, 2), links.swap(near_two, 4)
        before_qkv = []
    else:
        qkv_near, qkv_far = links.gathered([qkv_w])
        before_qkv = []

    (attn_in, qkv, qkv_laid), qkv_ran = call(
        qkv_kernel,
        [
            shape(rows, D, dtype=bf16),
            shape(rows, 3 * D, dtype=bf16),
            shape(D, 3 * D, dtype=bf16),
        ],
        [pltpu.VMEM((rows, D), bf16), pltpu.VMEM((D, 3 * D), bf16), dma((2,))],
        16,
        [where, residual, mod, qkv_bias, qkv_near, qkv_far],
        [SM] + [VM] * 5,
        after=before_qkv,
        out_specs=[HBM, VM, HBM],
        zeros=True,
    )
    before_attend = [qkv_ran]
    if cube:
        two, _ = join([fc2_w, links.swap(fc2_w, 16)], [qkv_ran])
        before_attend.append(two)
        near_three = jnp.concatenate([two, links.swap(two, 8)], axis=0)
    (attended, attended_kept), attend_ran = call(
        attend_kernel,
        [shape(rows, D, dtype=bf16)] * 2,
        [dma((1,))],
        16,
        [qkv],
        [VM],
        after=before_attend,
        out_specs=[VM, HBM],
        zeros=True,
    )
    if cube:
        half = near_two.shape[0] // 2
        width = near_two.shape[1]
        (most, low_half, high_half), _ = call(
            cut_kernel,
            [
                shape(6 * half, width, dtype=bf16),
                shape(half, width, dtype=bf16),
                shape(half, width, dtype=bf16),
            ],
            [dma((5,))],
            8,
            [near_two, over_x, over_y],
            [ANY] * 3,
            after=[attend_ran],
            out_specs=[ANY] * 3,
        )
        most_far = links.swap(most, 1)
        diag = [links.swap(low_half, 2), links.swap(high_half, 4)]
        diag, _ = join(diag)
        mid_halves = [most, diag, most_far, links.swap(diag, 1)]
        over = [links.swap(near_three, bits) for bits in (2, 4, 6)]
    else:
        mid_near, mid_far = links.gathered([proj_w, fc1_w])
        cut = 3 * D // 4
        mid_halves = [mid_near[:cut], mid_near[cut:], mid_far[:cut], mid_far[cut:]]
        fc2_near, fc2_far = links.gathered_rows(fc2_w)

    (
        branch, middle, mlp_in, grad_mlp_out, fc2_bias_sum, activated, slope, fc2_send, fc2_keep,
        middle_kept,
    ), hidden_ran = call(
        hidden_kernel,
        [
            shape(rows, D),
            shape(rows, D),
            shape(rows, D, dtype=bf16),
            shape(rows, D, dtype=bf16),
            shape(1, D),
            shape(rows, F, dtype=bf16),
            shape(rows, F, dtype=bf16),
            shape(F // 2, D, dtype=bf16),
            shape(F // 2, D, dtype=bf16),
            shape(rows, D),
        ],
        [
            pltpu.VMEM((D, D), bf16),
            pltpu.VMEM((D, F), bf16),
            pltpu.VMEM((rows, F), bf16),
            pltpu.VMEM((rows, F), bf16),
            pltpu.VMEM((F, rows), bf16),
            pltpu.VMEM((F, D), bf16),
            dma((9,)),
        ],
        32,
        [where, residual, attended, mod, grad_out, proj_bias_all, fc1_bias_all, *mid_halves],
        [SM] + [VM] * 10,
        out_specs=[VM] * 5 + [HBM] * 5,
    )
    def weight_grad(*pairs, after=()):
        half = sum(right.shape[1] for _, right in pairs) // 2
        scratch = [pltpu.VMEM((D, half), bf16), pltpu.VMEM((D, half), bf16), dma((8,))]
        spaces = [VM, VM]
        if len(pairs) == 2:
            scratch += [
                pltpu.VMEM((D, rows), bf16),
                pltpu.VMEM((rows, D), bf16),
                pltpu.VMEM((D, rows), bf16),
                dma((3,)),
            ]
            spaces = [HBM, HBM, HBM, VM]
        return call(
            functools.partial(wgrad_kernel, len(pairs)),
            [shape(D, half, dtype=bf16)] * 2,
            scratch,
            20,
            [where, *[left for left, _ in pairs], *[right for _, right in pairs]],
            [SM, *spaces],
            after=after,
            out_specs=[HBM] * 2,
        )

    (mlp_flipped, attended_flipped, attn_flipped), flipped = call(
        flips_kernel,
        [shape(D, rows, dtype=bf16)] * 3,
        [pltpu.VMEM((rows, D), bf16)] * 2 + [pltpu.VMEM((2, D, rows), bf16), dma((4,))],
        16,
        [where, mlp_in, attended_kept, attn_in],
        [SM, VM, HBM, HBM],
        after=[hidden_ran],
        out_specs=[VM, HBM, HBM],
    )
    (probs,), probs_ran = call(
        probs_kernel,
        [shape(SLOTS * HEADS // 2 * LEN, 2 * LEN)],
        [
            pltpu.VMEM((rows, 2 * D), bf16),
            pltpu.VMEM((SLOTS * HEADS // 2 * LEN, 2 * LEN), f32),
            dma((2 * SLOTS,)),
        ],
        16,
        [qkv],
        [HBM],
        after=[flipped],
        out_specs=[HBM],
    )
    if cube:
        fc2_got = links.swap(fc2_send, 1)
        fc2_near, gathered = join([near_three, *over], [probs_ran], us=100)
        fc2_far = links.swap(fc2_near, 1)
        fc2_ones, fc2_first = links.first(fc2_keep, fc2_got, [gathered])
        before_fc2 = [fc2_first]
    else:
        before_fc2 = []
    (grad_hidden, fc1_bias_sum), _ = call(
        fc2_back_kernel,
        [shape(rows, F, dtype=bf16), shape(1, F)],
        [pltpu.VMEM((F, D), bf16), pltpu.VMEM((rows, F), bf16), dma((6,))],
        20,
        [where, grad_mlp_out, slope, fc2_near, fc2_far],
        [SM, VM, HBM, VM, VM],
        after=before_fc2,
    )
    (fc1_send, fc1_keep), fc1_ran = weight_grad((mlp_flipped, grad_hidden))
    (out_tail, gate_two_sum, result), out_ran = call(
        fc2_out_kernel,
        [shape(LEN, D, dtype=bf16), shape(SLOTS, D), shape(rows, D, dtype=bf16)],
        [
            pltpu.VMEM((rows, D), f32),
            pltpu.VMEM((rows, F), bf16),
            pltpu.VMEM((F, D), bf16),
            pltpu.VMEM((rows + LEN + 8, D), f32),
            pltpu.VMEM((rows, D), bf16),
            dma((3,)),
        ],
        20,
        [where, place, mod, grad_out, fc2_bias_all, middle_kept, activated, fc2_near, fc2_far],
        [SM] * 2 + [VM] * 3 + [HBM] * 2 + [VM] * 2,
        after=[fc1_ran],
        out_specs=[VM] * 2 + [HBM],
    )
    if cube:
        fc1_got = links.swap(fc1_send, 1)
        fc2_twos, fc2_second = links.second(fc2_keep, fc2_got, fc2_ones, [out_ran])
        fc1_ones, fc1_first = links.first(fc1_keep, fc1_got, [fc2_second])
        before_mid = [fc1_first]
    else:
        before_mid = [out_ran]
    (grad_attended, proj_bias_sum, grad_middle, grad_branch, early), mid_ran = call(
        mid_back_kernel,
        [
            shape(rows, D, dtype=bf16),
            shape(1, D),
            shape(rows, D),
            shape(rows, D, dtype=bf16),
            shape(devices, 16, D, dtype=bf16),
        ],
        [
            pltpu.VMEM((rows, D), f32),
            pltpu.VMEM((rows, D), bf16),
            pltpu.VMEM((devices, 16, D), bf16),
            pltpu.VMEM((D, D), bf16),
            pltpu.VMEM((D, F), bf16),
            pltpu.VMEM((rows, D), f32),
            pltpu.VMEM((16, D), f32),
            dma((3,)),
        ],
        20,
        [where, grad_hidden, middle, branch, mod, grad_out, gate_two_sum, *mid_halves],
        [SM] + [VM] * 10,
        out_specs=[VM] * 2 + [HBM] * 3,
        after=before_mid,
    )
    early = lax.all_to_all(early, "wide", 0, 0, tiled=True)
    if cube:
        fc2_near_sum, fc2_summed = links.near_sum(
            fc2_keep, fc2_got, fc2_ones, fc2_twos, False, [mid_ran]
        )
        before_back = [fc2_summed]
    else:
        before_back = []
    (grad_qkv, qkv_bias_sum), back_ran = call(
        attend_back_kernel,
        [shape(rows, 3 * D, dtype=bf16), shape(1, 3 * D)],
        [
            pltpu.VMEM((rows, 3 * D), bf16),
            pltpu.VMEM(probs.shape, f32),
            dma((2 * SLOTS,)),
        ],
        16,
        [qkv, probs, grad_attended],
        [HBM, HBM, VM],
        after=before_back,
    )
    before_qkv = []
    if cube:
        fc2_own, fc2_beyond, fc2_halved = links.halved_z(*fc2_near_sum, [back_ran])
        fc1_twos, fc1_second = links.second(fc1_keep, fc1_got, fc1_ones, [fc2_halved])
        before_qkv.append(fc1_second)
    (qkv_send, qkv_keep), qkv_grad_ran = weight_grad(
        (attended_flipped, grad_branch), (attn_flipped, grad_qkv), after=before_qkv
    )
    if cube:
        qkv_got = links.swap(qkv_send, 1)
    if cube:
        fc1_near_sum, fc1_summed = links.near_sum(
            fc1_keep, fc1_got, fc1_ones, fc1_twos, False, [qkv_grad_ran]
        )
        qkv_ones, qkv_first = links.first(qkv_keep, qkv_got, [fc1_summed])
        before_start = [qkv_first, early]
    else:
        before_start = [qkv_grad_ran]
    (tokens_back, tail, late), start_ran = call(
        start_back_kernel,
        [shape(rows, D), shape(3 * LEN, D, dtype=bf16), shape(devices, 2 * SLOTS, D, dtype=bf16)],
        [
            pltpu.VMEM((D, 3 * D), bf16),
            pltpu.VMEM((rows + LEN + 8, D), f32),
            pltpu.VMEM((rows, D), f32),
            pltpu.VMEM((rows, D), f32),
            pltpu.VMEM((2 * SLOTS, D), f32),
            pltpu.VMEM((3 * LEN, D), bf16),
            pltpu.VMEM((devices, 2 * SLOTS, D), bf16),
            dma((5,)),
            dma((SLOTS + 2,)),
        ],
        24,
        [place, grad_qkv, mod, out_tail, residual, grad_middle, qkv_laid],
        [SM] + [VM] * 3 + [HBM] * 3,
        after=before_start,
        out_specs=[HBM] * 3,
    )
    late = lax.all_to_all(late, "wide", 0, 0, tiled=True)

    if cube:
        qkv_twos, qkv_second = links.second(qkv_keep, qkv_got, qkv_ones, [start_ran], True)
        fc1_own, fc1_beyond, fc1_halved = links.halved_z(*fc1_near_sum, [qkv_second])
        before_ada = [fc1_halved]
    else:
        before_ada = [start_ran]

    onward = [(i, i + 1) for i in range(devices - 1)]
    tail = lax.ppermute(tail, "wide", onward)
    wide_images = -(-images // 128) * 128
    (ada_grad, ada_bias_sum, last), ada_ran = call(
        ada_kernel,
        [
            shape(own_dim, 6 * D),
            shape(1, 6 * D),
            shape(devices, own_dim + 8, wide_images, dtype=bf16),
        ],
        [pltpu.VMEM((devices * 16, images), f32), pltpu.VMEM((own_dim + 8, wide_images), f32)],
        24,
        [where, starts, early, late, ada_w, cond, qkv_bias_sum, proj_bias_sum, fc2_bias_sum, fc1_bias_sum],
        [SM] * 2 + [VM] * 8,
        after=before_ada,
        zeros=True,
    )
    last = lax.all_to_all(last, "wide", 0, 0, tiled=True)
    if cube:
        qkv_near_sum, qkv_summed = links.near_sum(
            qkv_keep, qkv_got, qkv_ones, qkv_twos, True, [ada_ran]
        )
        before_place = [qkv_summed]
    else:
        before_place = [ada_ran]
    (out, tokens_grad), placed = call(
        place_kernel,
        [shape(rows, D, dtype=bf16), shape(rows, D)],
        [
            pltpu.VMEM((rows + LEN + 8, D), f32),
            pltpu.VMEM((rows + LEN + 8, D), f32),
            pltpu.VMEM((rows, D), bf16),
            pltpu.VMEM((rows, D), bf16),
            pltpu.VMEM((rows, D), bf16),
            pltpu.VMEM((rows, D), bf16),
            pltpu.VMEM((rows, D), f32),
            dma((6,)),
        ],
        16,
        [place, tail, tokens, cotangent, result, tokens_back],
        [SM, VM] + [HBM] * 4,
        after=before_place,
        out_specs=[HBM] * 2,
    )


    (cond_grad, bias_grads), finished = call(
        finish_kernel,
        [shape(images, D), shape(8, wide_images)],
        [pltpu.VMEM((D, wide_images), f32)],
        16,
        [last],
        [VM],
        after=[placed],
        zeros=True,
    )
    fc1_widths, qkv_widths = [F // 2], [D // 2, 3 * D // 2]
    if cube:
        fc2_grad = tie(fc2_own, ada_ran) + fc2_beyond.astype(f32)
        (fc1_grad,) = links.own_rows(
            tie(fc1_own, ada_ran) + fc1_beyond.astype(f32), fc1_widths
        )
        proj_grad, qkv_grad = links.own_rows(links.z_sum(finished, *qkv_near_sum), qkv_widths)
    else:
        fc2_grad = links.scattered_rows(fc2_send, fc2_keep)
        (fc1_grad,) = links.scattered(fc1_send, fc1_keep, fc1_widths)
        proj_grad, qkv_grad = links.scattered(qkv_send, qkv_keep, qkv_widths)
    bias_grads = bias_grads[:, :own_dim]
    ada_bias_grad = lax.dynamic_slice_in_dim(ada_bias_sum[0], me * span, span, 0)
    return (
        out,
        tokens_grad,
        cond_grad,
        ada_grad,
        ada_bias_grad,
        qkv_grad,
        bias_grads[0],
        bias_grads[1],
        proj_grad,
        bias_grads[2],
        fc1_grad,
        bias_grads[4:].reshape(-1),
        fc2_grad,
        bias_grads[3],
    )


def solution(mesh):
    row, flat = P("wide", None), P("wide")
    return jax.shard_map(
        on_device,
        mesh=mesh,
        in_specs=(row, row, P(), P(), P(), row, flat, row, flat, flat, row, flat, row, flat, row, flat),
        out_specs=(row, row, P(), row, flat, row, flat, flat, row, flat, row, flat, row, flat),
        check_vma=False,
    )
```

```python
import functools
import math

import jax
import jax.numpy as jnp
from jax import lax
from jax.experimental import pallas as pl
from jax.experimental.pallas import tpu as pltpu
from jax.sharding import PartitionSpec as P

D = 768
HEADS = 12
HD = 64
GRID = 16
LEN = 128
TOK_DEV = 512
SLOTS = TOK_DEV // LEN
F = 3072
BLOCKS = 16
NEAR_FIRST, FAR_FIRST = (0, 1, 2, 3), (0, 2, 1, 3)

NORM_EPS = 1e-06
GELU_COEF = 0.7978845608028654

f32 = jnp.float32
bf16 = jnp.bfloat16

VM = pl.BlockSpec(memory_space=pltpu.VMEM)
SM = pl.BlockSpec(memory_space=pltpu.SMEM)
ANY = pl.BlockSpec(memory_space=pl.ANY)
HBM = pl.BlockSpec(memory_space=pltpu.HBM)


def params(mib):
    return pltpu.CompilerParams(vmem_limit_bytes=mib * 1024 * 1024)


def cost(us):
    return pl.CostEstimate(flops=max(1, int(us * 1e9)), bytes_accessed=1, transcendentals=0)


def dot(left, right):
    return jnp.dot(left, right, preferred_element_type=f32)


def dot_nt(left, right):
    return lax.dot_general(left, right, (((1,), (1,)), ((), ())), preferred_element_type=f32)


def dot_tn(left, right):
    return lax.dot_general(left, right, (((0,), (0,)), ((), ())), preferred_element_type=f32)


def silu(values):
    return values / (1.0 + jnp.exp(-values))


def norm_parts(values):
    centred = values - jnp.mean(values, axis=-1, keepdims=True)
    spread = jnp.mean(centred * centred, axis=-1, keepdims=True)
    inverse = lax.rsqrt(spread + NORM_EPS)
    return centred * inverse, inverse


def norm_back(normed, inverse, scale_part, grad):
    t = grad * (1.0 + scale_part)
    mean_t = jnp.mean(t, axis=-1, keepdims=True)
    mean_tn = jnp.mean(t * normed, axis=-1, keepdims=True)
    return (t - mean_t - normed * mean_tn) * inverse


def rows_from(ref, start):
    base = pl.multiple_of(start // 8 * 8, 8)
    shift = start - base
    tall = LEN + 8
    turned = pltpu.roll(ref[pl.ds(base, tall), :], jnp.where(shift == 0, 0, tall - shift), 0)
    return turned[:LEN]


def slot_rows(slot):
    return slice(slot * LEN, (slot + 1) * LEN)


def mod_part(mod_ref, slot, part):
    return mod_ref[slot : slot + 1, part * D : (part + 1) * D]


def place_of(block, chip):
    rel = jnp.bitwise_xor(block, chip)
    return jnp.bitwise_and(rel, 3) * 4 + lax.shift_right_logical(rel, 2)


def lay_out(where_ref, halves, rows, targets, z_order, split_rows=False):
    chip, core = where_ref[0], where_ref[1]
    for side in range(2):
        half = core if side == 0 else 1 - core
        place = 0
        for ref in halves[side]:
            for spot in range(ref.shape[0] // rows):
                block = jnp.bitwise_xor(z_order[place % 4] * 4 + place // 4, chip)
                place += 1
                for target, first, width in targets:
                    if split_rows:
                        to_row, to_col = (2 * block + half) * rows, 0
                    else:
                        to_row, to_col = block * rows, pl.multiple_of(half * width, 128)
                    to_row = pl.multiple_of(to_row, 16)
                    target[pl.ds(to_row, rows), pl.ds(to_col, width)] = ref[
                        spot * rows : (spot + 1) * rows, first : first + width
                    ]


def start_all(copies):
    for copy in copies:
        copy.start()
    return copies


def fetch(pairs, sems, first=0):
    return start_all(
        [pltpu.make_async_copy(a, b, sems.at[first + i]) for i, (a, b) in enumerate(pairs)]
    )


def wait_all(copies):
    for copy in copies:
        copy.wait()


def begin_kernel(
    where_ref, counts_ref, cond_in, ada_in, tok_in, cot_in, qkv_in, proj_in, fc1_in,
    mine_ref, send_ref, edge_ref, place_ref, starts_ref, slots_ref, parts_ref,
    wide, cond, ada, sems,
):
    devices = counts_ref.shape[0]
    images = cond.shape[0]
    core, me = where_ref[1], where_ref[2]
    copies = []
    first = 0
    for ref in (qkv_in, proj_in, fc1_in):
        half = ref.shape[1] // 2
        for out, at in ((send_ref, 1 - core), (mine_ref, core)):
            copies.append(
                (
                    ref.at[:, pl.ds(pl.multiple_of(at * half, 128), half)],
                    out.at[:, pl.ds(first, half)],
                )
            )
        first += half
    copies.append((tok_in.at[pl.ds(0, LEN), :], edge_ref.at[pl.ds(0, LEN), :]))
    copies.append((cot_in.at[pl.ds(0, LEN), :], edge_ref.at[pl.ds(LEN, LEN), :]))
    copies = fetch([*copies, (cond_in, cond), (ada_in, ada)], sems)

    def step(d, first_row):
        count = counts_ref[d]
        begin = (first_row + LEN - 1) // LEN
        starts_ref[d] = begin

        @pl.when(d == me)
        def _():
            lead = begin * LEN - first_row
            place_ref[0] = lead
            place_ref[1] = count
            place_ref[2] = (first_row + count + LEN - 1) // LEN - begin
            place_ref[3] = count - lead
            place_ref[4] = begin

        return first_row + count

    lax.fori_loop(0, devices, step, jnp.int32(0))
    sub = lax.broadcasted_iota(jnp.int32, (8, images), 0)
    lane = lax.broadcasted_iota(jnp.int32, (8, images), 1)

    @pl.loop(0, devices)
    def _(d):
        hit = (lane == starts_ref[d] + sub) & (sub < SLOTS)
        wide[pl.ds(pl.multiple_of(d * 8, 8), 8), :] = jnp.where(hit, 1.0, 0.0)

    wait_all(copies)
    span = parts_ref.shape[2]
    for d in range(devices):
        parts_ref[d] = ada[:, d * span : (d + 1) * span]
    act = silu(cond[...].astype(f32)).astype(bf16)
    slots_ref[...] = dot(wide[...].astype(bf16), act).astype(bf16)


def ada_kernel(
    where_ref, starts_ref, early_ref, late_ref, ada_ref, cond_ref,
    qkv_sum_ref, proj_sum_ref, fc2_sum_ref, fc1_sum_ref,
    grad_ref, colsum_ref, last_ref, wide, packed,
):
    devices = early_ref.shape[0]
    images, own = cond_ref.shape[0], ada_ref.shape[0]
    me = where_ref[2]
    row = lax.broadcasted_iota(jnp.int32, (own, D), 0)
    lane = lax.broadcasted_iota(jnp.int32, (own, D), 1)
    chosen = jnp.where(lane == me * own + row, 1.0, 0.0).astype(bf16)
    act = silu(cond_ref[...].astype(f32)).astype(bf16)
    act_own = dot_nt(act, chosen).astype(bf16)
    cond_own = dot_nt(chosen, cond_ref[...])
    total = jnp.zeros((own, images), f32)
    for ref, parts in ((early_ref, (2, 3, 4, 5)), (late_ref, (0, 1))):
        many = len(parts)
        high = many * SLOTS
        tall = devices * high
        sub = lax.broadcasted_iota(jnp.int32, (high, images), 0)
        lane = lax.broadcasted_iota(jnp.int32, (high, images), 1)

        @pl.loop(0, devices)
        def _(d):
            hit = lane == starts_ref[d] + sub % SLOTS
            wide[pl.ds(pl.multiple_of(d * high, high), high), :] = jnp.where(hit, 1.0, 0.0)

        picker = wide[0:tall, :]
        act_rows = dot(picker.astype(bf16), act_own)
        part_down = lax.broadcasted_iota(jnp.int32, (tall, 1), 0) % high // SLOTS
        part_across = lax.broadcasted_iota(jnp.int32, (1, tall), 1) % high // SLOTS
        act_parts = jnp.concatenate(
            [jnp.where(part_down == i, act_rows, 0.0) for i in range(many)], axis=1
        ).astype(bf16)
        ours = lax.broadcasted_iota(jnp.int32, (8, tall), 0) == part_across
        ours = jnp.where(ours, 1.0, 0.0).astype(bf16)
        sums = ref[...].reshape(tall, D)
        grads = dot_tn(act_parts, sums)
        colsums = dot(ours, sums)
        back = jnp.zeros((own, tall), f32)
        for i, part in enumerate(parts):
            cols = slice(part * D, (part + 1) * D)
            grad_ref[:, cols] = grads[i * own : (i + 1) * own]
            colsum_ref[:, cols] = colsums[i : i + 1]
            back += jnp.where(part_across == i, dot_nt(ada_ref[:, cols], sums), 0.0)
        total += jnp.dot(back, picker, precision=lax.Precision.HIGHEST)
    gate = 1.0 / (1.0 + jnp.exp(-cond_own))
    total = total * (gate * (1.0 + cond_own * (1.0 - gate)))
    lanes = last_ref.shape[2]
    fc1_sum = fc1_sum_ref[...]
    both = qkv_sum_ref[...]
    vectors = [both[:, :D], both[:, 2 * D :], proj_sum_ref[...], fc2_sum_ref[...]]
    for d in range(devices):
        packed[...] = jnp.zeros(packed.shape, f32)
        packed[0:own, 0:images] = total
        for j in range(8):
            if j < 4:
                value = vectors[j][:, d * own : (d + 1) * own]
            else:
                at = (4 * d + j - 4) * own
                value = fc1_sum[:, at : at + own]
            packed[own + j : own + j + 1, 0:own] = value
        last_ref[d] = packed[...].astype(bf16)


def finish_kernel(got_ref, cond_ref, bias_ref, tall):
    devices, rows, _ = got_ref.shape
    own = rows - 8
    total = None
    for d in range(devices):
        got = got_ref[d].astype(f32)
        tall[d * own : (d + 1) * own, :] = got[0:own]
        total = got[own:rows] if total is None else total + got[own:rows]
    cond_ref[...] = tall[...].T[0 : cond_ref.shape[0], :]
    bias_ref[...] = total


def mod_kernel(slots_ref, cols_ref, addend_ref, out_ref):
    value = dot(slots_ref[...], cols_ref[...])
    for d in range(out_ref.shape[0]):
        out_ref[d] = value[d * 8 : (d + 1) * 8, :] + addend_ref[...]


def prep_kernel(
    place_ref, got_ref, tok_in, cot_in, halo_in, kept_in, table_in,
    res_ref, gc_ref, mod_ref, qkv_bias_ref, proj_bias_ref, fc2_bias_ref, fc1_bias_ref,
    tok, cot, halo, kept, table, sems,
):
    copies = fetch(
        [(table_in, table), (kept_in, kept), (halo_in, halo), (tok_in, tok), (cot_in, cot)], sems
    )
    devices, _, span = got_ref.shape
    width = D // devices
    qkv_bias_ref[:, D : 2 * D] = jnp.zeros((1, D), f32)
    for d in range(devices):
        got = got_ref[d]
        mod_ref[:, d * span : (d + 1) * span] = got[0:SLOTS]
        cols = slice(d * width, (d + 1) * width)
        qkv_bias_ref[:, cols] = got[4:5, 0:width]
        qkv_bias_ref[:, 2 * D + d * width : 2 * D + (d + 1) * width] = got[4:5, width : 2 * width]
        proj_bias_ref[:, cols] = got[4:5, 2 * width : 3 * width]
        fc2_bias_ref[:, cols] = got[4:5, 3 * width : 4 * width]
        fc1_bias_ref[:, d * 4 * width : (d + 1) * 4 * width] = got[5:6, 0 : 4 * width]
    lead, count, slots, begin = place_ref[0], place_ref[1], place_ref[2], place_ref[4]
    wait_all(copies)
    angles = table[...]
    high = angles.astype(bf16)
    rest = angles - high.astype(f32)
    middle = rest.astype(bf16)
    lowest = (rest - middle.astype(f32)).astype(bf16)
    images = kept.shape[0]
    sub = lax.broadcasted_iota(jnp.int32, (8, images), 0)
    lane = lax.broadcasted_iota(jnp.int32, (8, images), 1)
    picker = jnp.where(lane == begin + sub, 1.0, 0.0).astype(bf16)
    patches = dot(picker, kept[...].astype(f32).astype(bf16)).astype(jnp.int32)
    for slot in range(SLOTS):
        row = lax.broadcasted_iota(jnp.int32, (LEN, TOK_DEV), 0) + slot * LEN
        source = row + lead
        live = slot < slots
        column = lax.broadcasted_iota(jnp.int32, (LEN, TOK_DEV), 1)
        own = jnp.where((column == source) & (source < count) & live, 1.0, 0.0).astype(bf16)
        far = source[:, :LEN] - count
        spill = jnp.where((column[:, :LEN] == far) & live, 1.0, 0.0).astype(bf16)
        taken = dot(own, tok[...]) + dot(spill, halo[0:LEN, :])
        grad = dot(own, cot[...]) + dot(spill, halo[LEN : 2 * LEN, :])
        gc_ref[slot_rows(slot), :] = grad.astype(bf16)
        patch = patches[slot : slot + 1, :]
        index = lax.broadcasted_iota(jnp.int32, (GRID, LEN), 0)
        line = jnp.where((index == patch // GRID) & live, 1.0, 0.0).astype(bf16)
        across = jnp.where((index == patch % GRID) & live, 1.0, 0.0).astype(bf16)
        half = D // 2
        for start, picked in ((0, line), (half, across)):
            spot = dot_tn(picked, high) + (dot_tn(picked, middle) + dot_tn(picked, lowest))
            res_ref[slot_rows(slot), start : start + half] = taken[:, start : start + half] + spot


def head_masks():
    lane = lax.broadcasted_iota(jnp.int32, (1, 2 * HD), 1)
    first = jnp.where(lane < HD, 1.0, 0.0).astype(bf16)
    return first, (1.0 - first.astype(f32)).astype(bf16)


def both_heads(pair, masks):
    return jnp.concatenate([pair * masks[0], pair * masks[1]], axis=0)


def side_by_side(stacked):
    return jnp.concatenate([stacked[:LEN], stacked[LEN:]], axis=1)


def pair_probs(queries, keys):
    scores = dot_nt(queries, keys) * (1.0 / math.sqrt(HD))
    exp_terms = jnp.exp(scores - jnp.max(scores, axis=1, keepdims=True))
    return exp_terms * (1.0 / jnp.sum(exp_terms, axis=1, keepdims=True))


def qkv_kernel(
    where_ref, res_ref, mod_ref, bias_ref, near_ref, far_ref, ain_out, qkv_ref, weight_out, ain_ref, weight, sems
):
    for slot in range(SLOTS):
        normed, _ = norm_parts(res_ref[slot_rows(slot), :])
        ain_ref[slot_rows(slot), :] = (
            normed * (1.0 + mod_part(mod_ref, slot, 1)) + mod_part(mod_ref, slot, 0)
        ).astype(bf16)
    out = fetch([(ain_ref, ain_out)], sems)
    lay_out(where_ref, ([near_ref], [far_ref]), D // BLOCKS, [(weight, 0, 3 * D // 2)], NEAR_FIRST)
    out += fetch([(weight, weight_out)], sems, 1)

    @pl.loop(0, 3 * D // 256)
    def _(j):
        cols = pl.ds(pl.multiple_of(j * 256, 256), 256)
        qkv_ref[:, cols] = (dot(ain_ref[...], weight[:, cols]) + bias_ref[:, cols]).astype(bf16)

    wait_all(out)


def attend_kernel(qkv_ref, att_ref, att_out, sems):
    masks = head_masks()

    @pl.loop(0, SLOTS)
    def _(slot):
        rows = pl.ds(pl.multiple_of(slot * LEN, LEN), LEN)
        for pair in range(HEADS // 2):
            at = pair * 2 * HD
            probs = pair_probs(
                both_heads(qkv_ref[rows, at : at + 2 * HD], masks),
                qkv_ref[rows, D + at : D + at + 2 * HD],
            )
            values = both_heads(qkv_ref[rows, 2 * D + at : 2 * D + at + 2 * HD], masks)
            att_ref[rows, at : at + 2 * HD] = dot(
                side_by_side(probs.astype(bf16)), values
            ).astype(bf16)

    wait_all(fetch([(att_ref, att_out)], sems))


def join_kernel(*refs):
    *parts, both, sems = refs
    pairs, first = [], 0
    for ref in parts:
        rows = ref.shape[0]
        pairs.append((ref, both.at[pl.ds(first, rows), :]))
        first += rows
    wait_all(fetch(pairs, sems))


def cut_kernel(near_ref, x_ref, y_ref, most_ref, low_ref, high_ref, sems):
    rows = near_ref.shape[0]
    half = rows // 2
    pairs = [(y_ref.at[pl.ds(0, half), :], low_ref), (x_ref.at[pl.ds(half, half), :], high_ref)]
    for i, ref in enumerate((near_ref, x_ref, y_ref)):
        pairs.append((ref, most_ref.at[pl.ds(i * rows, rows), :]))
    wait_all(fetch(pairs, sems))


def flip(where_ref, lhs_ref, ordered, split_rows):
    chip, core = where_ref[0], where_ref[1]
    depth = ordered.shape[0]
    size = depth // BLOCKS
    if split_rows:
        size //= 2
    step = 384
    for m in range(depth // step):
        turned = lhs_ref[:, m * step : (m + 1) * step].T
        for i in range(step // size):
            block = m * (step // size) + i
            side = block % 2
            to = place_of(block // 2 if split_rows else block, chip) * size
            if split_rows:
                to = to + jnp.where(core == side, depth // 2, 0)
            ordered[pl.ds(pl.multiple_of(to, 16), size), :] = turned[i * size : (i + 1) * size, :]


def hidden_kernel(
    where_ref, res_ref, att_ref, mod_ref, gc_ref, proj_bias_ref, bias_ref, *rest
):
    mine, more, theirs, rest_far = rest[:4]
    branch_ref, mid_ref, min_ref, gmo_ref, colsum_ref, act_out, slope_out, send_out, keep_out, mid_out = rest[4:14]
    proj, weight, act, slope, ordered, made, out_sems = rest[14:]
    total = jnp.zeros((1, D), f32)
    for slot in range(SLOTS):
        rows = slot_rows(slot)
        grad = (mod_part(mod_ref, slot, 5) * gc_ref[rows, :].astype(f32)).astype(bf16)
        gmo_ref[rows, :] = grad
        total += jnp.sum(grad.astype(f32), axis=0, keepdims=True)
    colsum_ref[...] = total
    lay_out(
        where_ref,
        ([mine, more], [theirs, rest_far]),
        D // BLOCKS,
        [(proj, 0, D // 2), (weight, D // 2, F // 2)],
        NEAR_FIRST,
    )
    for j in range(D // 256):
        cols = slice(j * 256, (j + 1) * 256)
        branch_ref[:, cols] = dot(att_ref[...], proj[:, cols]) + proj_bias_ref[:, cols]
    for slot in range(SLOTS):
        rows = slot_rows(slot)
        mid = res_ref[rows, :] + mod_part(mod_ref, slot, 2) * branch_ref[rows, :]
        mid_ref[rows, :] = mid
        normed, _ = norm_parts(mid)
        min_ref[rows, :] = (
            normed * (1.0 + mod_part(mod_ref, slot, 4)) + mod_part(mod_ref, slot, 3)
        ).astype(bf16)

    @pl.loop(0, F // 256)
    def _(j):
        cols = pl.ds(pl.multiple_of(j * 256, 256), 256)
        u = dot(min_ref[...], weight[:, cols]) + bias_ref[:, cols]
        square = u * u
        bend = jnp.tanh(GELU_COEF * (u + 0.044715 * square * u))
        left = 0.5 * (1.0 + bend)
        act[:, cols] = (u * left).astype(bf16)
        slope[:, cols] = (
            left
            + 0.5 * u * (1.0 - bend * bend) * (GELU_COEF * (1.0 + 3.0 * 0.044715 * square))
        ).astype(bf16)

    out = fetch([(act, act_out), (slope, slope_out)], out_sems)
    out += fetch([(mid_ref, mid_out)], out_sems, 8)
    flip(where_ref, act, ordered, True)
    step = 512
    for j in range(F // step):
        made[j * step : (j + 1) * step, :] = dot(
            ordered[j * step : (j + 1) * step, :], gmo_ref[...]
        ).astype(bf16)
        to, at = (send_out, j) if j < F // step // 2 else (keep_out, j - F // step // 2)
        out += fetch(
            [(made.at[pl.ds(j * step, step), :], to.at[pl.ds(at * step, step), :])],
            out_sems,
            2 + j,
        )
    wait_all(out)


def flips_kernel(where_ref, first_ref, second_in, third_in, flipped_ref, second_out, third_out, second, third, turned, sems):
    copies = fetch([(second_in, second), (third_in, third)], sems)
    flip(where_ref, first_ref, flipped_ref, False)
    out = []
    for i, (ref, to) in enumerate(((second, second_out), (third, third_out))):
        wait_all([copies[i]])
        flip(where_ref, ref, turned.at[i], False)
        out += fetch([(turned.at[i], to)], sems, 2 + i)
    wait_all(out)


def wgrad_kernel(count, where_ref, *rest):
    lhs, rhs = rest[:count], rest[count : 2 * count]
    send_out, keep_out, send, keep, sems, *late = rest[2 * count :]
    core = where_ref[1]
    if late:
        *bufs, in_sems = late
        ins = fetch([(lhs[0], bufs[0]), (rhs[0], bufs[1]), (lhs[1], bufs[2])], in_sems)
        lhs, rhs = (bufs[0], bufs[2]), (bufs[1], rhs[1])
    step = 384
    first = 0
    out = []
    for ordered, rhs_ref in zip(lhs, rhs):
        if late:
            wait_all(ins[2:] if first else ins[:2])
        width = rhs_ref.shape[1] // 2
        for buf, to, half in ((send, send_out, 1 - core), (keep, keep_out, core)):
            cols = pl.ds(pl.multiple_of(half * width, 128), width)
            for j in range(D // step):
                rows = slice(j * step, (j + 1) * step)
                buf[rows, first : first + width] = dot(
                    ordered[rows, :], rhs_ref[:, cols]
                ).astype(bf16)
                here = (pl.ds(j * step, step), pl.ds(first, width))
                out += fetch([(buf.at[here], to.at[here])], sems, len(out))
        first += width
    wait_all(out)


def pair_sums(keep_in, got_ref, rows, spans, keep, sems, got=None):
    copies = []
    for i, first in enumerate(spans):
        here, there = pl.ds(i * rows, rows), pl.ds(first, rows)
        pairs = [(keep_in.at[there, :], keep.at[here, :])]
        if got is not None:
            pairs.append((got_ref.at[there, :], got.at[here, :]))
        copies.append(fetch(pairs, sems, 2 * i))

    def total(i):
        wait_all(copies[i])
        here = slice(i * rows, (i + 1) * rows)
        other = got_ref[spans[i] : spans[i] + rows, :] if got is None else got[here, :]
        return keep[here, :].astype(f32) + other.astype(f32)

    return total


def first_kernel(keep_in, got_ref, x_ref, y_ref, keep, sems, *got):
    rows = x_ref.shape[0] // 2
    total = pair_sums(keep_in, got_ref, rows, [2 * rows, 6 * rows, 5 * rows, 7 * rows], keep, sems, *got)
    for i in range(4):
        ref = (x_ref, y_ref)[i // 2]
        ref[i % 2 * rows : (i % 2 + 1) * rows, :] = total(i).astype(bf16)


def second_kernel(keep_in, got_ref, x_got_ref, y_got_ref, x_ref, y_ref, keep, sems, *got):
    rows = x_ref.shape[0]
    total = pair_sums(keep_in, got_ref, rows, [3 * rows, 4 * rows], keep, sems, *got)
    x_ref[...] = (total(0) + y_got_ref[rows:, :].astype(f32)).astype(bf16)
    y_ref[...] = (total(1) + x_got_ref[rows:, :].astype(f32)).astype(bf16)


def near_kernel(direct, keep_in, got_ref, x_one_ref, y_one_ref, x_two_ref, y_two_ref, *rest):
    if direct:
        outs, (keep, sems, *got) = rest[:4], rest[4:]
    else:
        send_ref, own_out, beyond_out, keep, sems, own, beyond, out_sems = rest
        got = ()
        outs = (send_ref, own, beyond)
    half = x_two_ref.shape[0]
    rows = half // 2
    total = pair_sums(keep_in, got_ref, half, [0, half], keep, sems, *got)
    for i, (one_ref, two_ref) in enumerate(((x_one_ref, y_two_ref), (y_one_ref, x_two_ref))):
        both = total(i) + one_ref[0:half, :].astype(f32) + two_ref[...].astype(f32)
        for j in range(2):
            z = 2 * i + j
            value = both[j * rows : (j + 1) * rows]
            if direct:
                outs[z][...] = value.astype(outs[z].dtype)
            elif j:
                outs[0][i * rows : (i + 1) * rows, :] = value.astype(bf16)
            else:
                outs[1 + i][...] = value
    if not direct:
        wait_all(fetch([(own, own_out), (beyond, beyond_out)], out_sems))


def beyond_kernel(got_ref, own_in, beyond_in, send_ref, total_out, own, beyond, sems):
    wait_all(fetch([(own_in, own), (beyond_in, beyond)], sems))
    rows = own.shape[0]
    send_ref[...] = (beyond[...] + got_ref[rows:, :].astype(f32)).astype(bf16)
    own[...] = own[...] + got_ref[0:rows, :].astype(f32)
    wait_all(fetch([(own, total_out)], sems, 2))


def lay_out_fc2(where_ref, near_ref, far_ref, fc2):
    lay_out(where_ref, ([near_ref], [far_ref]), F // (2 * BLOCKS), [(fc2, 0, D)], FAR_FIRST, True)


def fc2_back_kernel(
    where_ref, gmo_ref, slope_in, near_ref, far_ref, gh_ref, colsum_ref, fc2, slope, in_sems
):
    step = 512
    parts = [pl.ds(j * step, step) for j in range(F // step)]
    late = fetch([(slope_in.at[:, part], slope.at[:, part]) for part in parts], in_sems)
    lay_out_fc2(where_ref, near_ref, far_ref, fc2)
    for j in range(F // step):
        wait_all([late[j]])
        for half in range(2):
            cols = slice(j * step + half * 256, j * step + (half + 1) * 256)
            grad = dot_nt(gmo_ref[...], fc2[cols, :])
            value = (slope[:, cols].astype(f32) * grad).astype(bf16)
            gh_ref[:, cols] = value
            colsum_ref[:, cols] = jnp.sum(value.astype(f32), axis=0, keepdims=True)


def fc2_out_kernel(
    where_ref, place_ref, mod_ref, gc_ref, bias_ref, mid_in, act_in, near_ref, far_ref,
    tail_ref, gate_ref, out_out, mid_ref, act, fc2, mlp, made, in_sems,
):
    last = fetch([(act_in, act), (mid_in, mid_ref)], in_sems)
    lay_out_fc2(where_ref, near_ref, far_ref, fc2)
    wait_all(last)
    for j in range(D // 256):
        cols = slice(j * 256, (j + 1) * 256)
        mlp[0:TOK_DEV, cols] = dot(act[...], fc2[:, cols]) + bias_ref[:, cols]
    for slot in range(SLOTS):
        rows = slot_rows(slot)
        value = mlp[rows, :]
        gate_ref[slot : slot + 1, :] = jnp.sum(
            value * gc_ref[rows, :].astype(f32), axis=0, keepdims=True
        )
        value = mid_ref[rows, :] + mod_part(mod_ref, slot, 5) * value
        mlp[rows, :] = value
        made[rows, :] = value.astype(bf16)
    out = fetch([(made, out_out)], in_sems, 2)
    mlp[TOK_DEV:, :] = jnp.zeros((LEN + 8, D), f32)
    tail_ref[...] = rows_from(mlp, place_ref[3]).astype(bf16)
    wait_all(out)


def keep_sum(sums, part, slot, values):
    at = part * SLOTS + slot
    sums[at : at + 1, :] = jnp.sum(values, axis=0, keepdims=True)


def spread_sums(sums, spread_ref):
    value = sums[...].astype(bf16)
    for d in range(spread_ref.shape[0]):
        spread_ref[d] = value


def mid_back_kernel(
    where_ref, gh_ref, mid_ref, branch_ref, mod_ref, gc_ref, gate_ref, mine, more, theirs, rest_far,
    ga_ref, proj_sum_ref, gm_out, gb_out, spread_out,
    gm_ref, gb_ref, spread_ref, proj, weight, grads, sums, out_sems,
):
    lay_out(
        where_ref,
        ([mine, more], [theirs, rest_far]),
        D // BLOCKS,
        [(proj, 0, D // 2), (weight, D // 2, F // 2)],
        NEAR_FIRST,
    )
    for j in range(D // 256):
        cols = slice(j * 256, (j + 1) * 256)
        grads[:, cols] = dot_nt(gh_ref[...], weight[cols, :])
    total = jnp.zeros((1, D), f32)
    for slot in range(SLOTS):
        rows = slot_rows(slot)
        normed, inverse = norm_parts(mid_ref[rows, :])
        e = grads[rows, :]
        keep_sum(sums, 1, slot, e)
        keep_sum(sums, 2, slot, e * normed)
        grad_mid = gc_ref[rows, :].astype(f32) + norm_back(
            normed, inverse, mod_part(mod_ref, slot, 4), e
        )
        gm_ref[rows, :] = grad_mid
        keep_sum(sums, 0, slot, branch_ref[rows, :] * grad_mid)
        value = (mod_part(mod_ref, slot, 2) * grad_mid).astype(bf16)
        gb_ref[rows, :] = value
        total += jnp.sum(value.astype(f32), axis=0, keepdims=True)
    proj_sum_ref[...] = total
    sums[3 * SLOTS :, :] = gate_ref[...]
    spread_sums(sums, spread_ref)
    out = fetch([(gm_ref, gm_out), (gb_ref, gb_out), (spread_ref, spread_out)], out_sems)
    for j in range(D // 256):
        cols = slice(j * 256, (j + 1) * 256)
        ga_ref[:, cols] = dot_nt(gb_ref[...], proj[cols, :]).astype(bf16)
    wait_all(out)


def probs_kernel(qk_in, probs_out, qk, probs, sems):
    masks = head_masks()
    copies = fetch(
        [
            (qk_in.at[pl.ds(slot * LEN, LEN), pl.ds(0, 2 * D)], qk.at[pl.ds(slot * LEN, LEN), :])
            for slot in range(SLOTS)
        ],
        sems,
    )
    out = []
    for slot in range(SLOTS):
        wait_all([copies[slot]])
        rows = slot_rows(slot)
        tall = HEADS // 2 * LEN
        for pair in range(HEADS // 2):
            at = pair * 2 * HD
            queries = both_heads(qk[rows, at : at + 2 * HD], masks)
            scores = dot_nt(qk[rows, D + at : D + at + 2 * HD], queries) * (1.0 / math.sqrt(HD))
            exp_terms = jnp.exp(scores - jnp.max(scores, axis=0, keepdims=True))
            first = slot * tall + pair * LEN
            probs[first : first + LEN, :] = exp_terms * (
                1.0 / jnp.sum(exp_terms, axis=0, keepdims=True)
            )
        here = pl.ds(slot * tall, tall)
        out += fetch([(probs.at[here, :], probs_out.at[here, :])], sems, SLOTS + slot)
    wait_all(out)


def attend_back_kernel(qkv_in, probs_in, ga_ref, gqkv_ref, colsum_ref, qkv, probs, sems):
    masks = head_masks()
    first_head = lax.broadcasted_iota(jnp.int32, (1, 2 * HD), 1) < HD
    scale = 1.0 / math.sqrt(HD)
    tall = HEADS // 2 * LEN
    copies = []
    for slot in range(SLOTS):
        here, there = pl.ds(slot * LEN, LEN), pl.ds(slot * tall, tall)
        copies += fetch(
            [
                (qkv_in.at[here, :], qkv.at[here, :]),
                (probs_in.at[there, :], probs.at[there, :]),
            ],
            sems,
            2 * slot,
        )
    for first in range(0, SLOTS, 2):
        wait_all(copies[2 * first : 2 * first + 4])

        @pl.loop(first, first + 2)
        def _(slot):
            rows = pl.ds(pl.multiple_of(slot * LEN, LEN), LEN)
            for pair in range(HEADS // 2):
                at = pair * 2 * HD
                q_cols, k_cols, v_cols = (
                    slice(part * D + at, part * D + at + 2 * HD) for part in range(3)
                )
                chances = probs[pl.ds(pl.multiple_of(slot * tall + pair * LEN, LEN), LEN), :]
                grads = both_heads(ga_ref[rows, q_cols], masks)
                weighed = chances * dot_nt(qkv[rows, v_cols], grads)
                inner = jnp.sum(weighed, axis=0, keepdims=True)
                grad_scores = (weighed - chances * inner).astype(bf16)
                grad_queries = dot_tn(grad_scores, qkv[rows, k_cols]) * scale
                gqkv_ref[rows, q_cols] = jnp.where(
                    first_head, grad_queries[:LEN], grad_queries[LEN:]
                ).astype(bf16)
                queries = both_heads(qkv[rows, q_cols], masks)
                gqkv_ref[rows, k_cols] = (dot(grad_scores, queries) * scale).astype(bf16)
                gqkv_ref[rows, v_cols] = dot(chances.astype(bf16), grads).astype(bf16)

    for j in range(3 * D // 256):
        cols = slice(j * 256, (j + 1) * 256)
        colsum_ref[:, cols] = jnp.sum(gqkv_ref[:, cols].astype(f32), axis=0, keepdims=True)


def start_back_kernel(
    place_ref, gqkv_ref, mod_ref, out_tail_ref, res_in, gm_in, weight_in,
    tg_out, tail_out, spread_out, weight, grads, res, gm, sums, tail_ref, spread_ref, in_sems, out_sems,
):
    step = 256
    parts = [pl.ds(j * step, step) for j in range(D // step)]
    copies = fetch([(weight_in.at[part, :], weight.at[part, :]) for part in parts], in_sems)
    late = fetch([(res_in, res), (gm_in, gm)], in_sems, len(parts))
    for j in range(D // step):
        wait_all([copies[j]])
        cols = slice(j * step, (j + 1) * step)
        grads[0:TOK_DEV, cols] = dot_nt(gqkv_ref[...], weight[cols, :])
    wait_all(late)
    out = []
    for slot in range(SLOTS):
        rows = slot_rows(slot)
        normed, inverse = norm_parts(res[rows, :])
        e = grads[rows, :]
        keep_sum(sums, 0, slot, e)
        keep_sum(sums, 1, slot, e * normed)
        grads[rows, :] = gm[rows, :] + norm_back(normed, inverse, mod_part(mod_ref, slot, 1), e)
        here = pl.ds(slot * LEN, LEN)
        out += fetch([(grads.at[here, :], tg_out.at[here, :])], out_sems, slot)
    spread_sums(sums, spread_ref)
    out += fetch([(spread_ref, spread_out)], out_sems, SLOTS)
    grads[TOK_DEV:, :] = jnp.zeros((LEN + 8, D), f32)
    tail = rows_from(grads, place_ref[3])
    high = tail.astype(bf16)
    tail_ref[0:LEN, :] = out_tail_ref[...]
    tail_ref[LEN : 2 * LEN, :] = high
    tail_ref[2 * LEN :, :] = (tail - high.astype(f32)).astype(bf16)
    wait_all(out + fetch([(tail_ref, tail_out)], out_sems, SLOTS + 1))


def place_kernel(
    place_ref, tail_ref, tok_in, cot_in, out_in, tg_in,
    final_out, final_tg, out_rows, tg_rows, tok, cot, out, made_out, made_tg, sems,
):
    lead, count = place_ref[0], place_ref[1]
    copies = fetch(
        [(out_in, out), (tok_in, tok), (tg_in, tg_rows.at[pl.ds(LEN, TOK_DEV), :]), (cot_in, cot)],
        sems,
    )
    for rows in (out_rows, tg_rows):
        rows[0:LEN, :] = jnp.zeros((LEN, D), f32)
        rows[LEN + TOK_DEV :, :] = jnp.zeros((8, D), f32)
    wait_all(copies[:2])
    out_rows[LEN : LEN + TOK_DEV, :] = out[...].astype(f32)
    last = []
    out_tail = tail_ref[0:LEN, :].astype(f32)
    tg_tail = tail_ref[LEN : 2 * LEN, :].astype(f32) + tail_ref[2 * LEN :, :].astype(f32)
    for k, (rows, tail, pad, made, final) in enumerate(
        ((out_rows, out_tail, tok, made_out, final_out), (tg_rows, tg_tail, cot, made_tg, final_tg))
    ):
        if k:
            wait_all(copies[2:])
        for slot in range(SLOTS):
            here = slot_rows(slot)
            row = lax.broadcasted_iota(jnp.int32, (LEN, 1), 0) + slot * LEN
            value = rows_from(rows, LEN - lead + slot * LEN)
            if slot == 0:
                value = jnp.where(row < lead, tail, value)
            value = jnp.where(row < count, value, pad[here, :].astype(f32))
            made[here, :] = value.astype(made.dtype)
        last += fetch([(made, final)], sems, 4 + k)
    wait_all(last)


def shape(*dims, dtype=f32):
    return jax.ShapeDtypeStruct(dims, dtype)


def call(kernel, outs, scratch, mib, ins, spaces, after=(), out_specs=None, us=0, zeros=False):
    taken, held, made = len(ins), len(after), len(outs)
    out_specs = out_specs or [VM] * made

    def body(*refs):
        first = taken + held
        kernel(*refs[:taken], *refs[first : first + made], *refs[first + made + 1 :])
        if zeros:
            refs[first + made][...] = jnp.zeros((8, 128), f32)

    def settled(item):
        is_token = item.shape == (8, 128) and item.dtype == f32
        return pltpu.with_memory_space_constraint(item, pltpu.HBM) if is_token else item

    def placed(item, spec):
        return pltpu.with_memory_space_constraint(item, pltpu.HBM) if spec is HBM else item

    out_specs = [*out_specs, VM if zeros else HBM]
    out_shape = [
        pltpu.HBM(item.shape, item.dtype) if spec is HBM else item
        for item, spec in zip([*outs, shape(8, 128)], out_specs)
    ]
    *results, token = pl.pallas_call(
        body,
        out_shape=out_shape,
        in_specs=list(spaces) + [ANY] * held,
        out_specs=out_specs,
        scratch_shapes=scratch,
        compiler_params=params(mib),
        cost_estimate=cost(us),
        name=getattr(kernel, "func", kernel).__name__,
    )(*[placed(item, spec) for item, spec in zip(ins, spaces)], *[settled(item) for item in after])
    return results, token


def tie(value, token):
    return jnp.where(token[0, 0] == 0.0, value, jnp.zeros_like(value))


def join(parts, after=(), us=0, zeros=False):
    rows = sum(part.shape[0] for part in parts)
    (both,), token = call(
        join_kernel,
        [shape(rows, parts[0].shape[1], dtype=parts[0].dtype)],
        [pltpu.SemaphoreType.DMA((len(parts),))],
        8,
        parts,
        [ANY] * len(parts),
        after=after,
        out_specs=[ANY],
        us=us,
        zeros=zeros,
    )
    return both, token


def tie(value, token):
    return jnp.where(token[0, 0] == 0.0, value, jnp.zeros_like(value))


def low(value):
    return value.astype(bf16)


class Links:
    def __init__(self, devices):
        self.devices = devices
        self.cube = devices == 32
        self.me = lax.axis_index("wide").astype(jnp.int32)
        self.core = self.me % 2 if self.cube else jnp.int32(0)
        self.chip = self.me // 2 if self.cube else jnp.int32(0)
        self.where = jnp.stack([self.chip, self.core, self.me])

    def swap(self, array, bits):
        return lax.ppermute(array, "wide", [(i, i ^ bits) for i in range(self.devices)])

    def by_core(self, first, second):
        return jnp.where(self.core == 0, first, second)

    def pair(self, mine, got):
        return self.by_core(
            jnp.concatenate([mine, got], axis=0), jnp.concatenate([got, mine], axis=0)
        )

    def along_z(self, pair):
        return jnp.concatenate(
            [pair, self.swap(pair, 8), self.swap(pair, 16), self.swap(pair, 24)], axis=0
        )

    def doubled_z(self, pair):
        two = jnp.concatenate([pair, self.swap(pair, 8)], axis=0)
        return jnp.concatenate([two, self.swap(two, 16)], axis=0)

    def gathered(self, shards):
        halves = [[], []]
        for shard in shards:
            whole = lax.all_gather(shard, "wide", axis=0, tiled=True)
            rows, width = whole.shape[0], whole.shape[1] // 2
            whole = whole.reshape(4, 4, rows // BLOCKS, -1).transpose(1, 0, 2, 3)
            whole = whole.reshape(rows, -1)
            halves[0].append(whole[:, :width])
            halves[1].append(whole[:, width:])
        return [jnp.concatenate(half, axis=1) for half in halves]

    def scattered(self, send, keep, widths):
        outs, first = [], 0
        rows = keep.shape[0]
        for width in widths:
            cols = slice(first, first + width)
            whole = jnp.concatenate([keep[:, cols], send[:, cols]], axis=1)
            whole = whole.reshape(4, 4, rows // BLOCKS, -1).transpose(1, 0, 2, 3)
            whole = whole.reshape(rows, -1).astype(f32)
            outs.append(lax.psum_scatter(whole, "wide", scatter_dimension=0, tiled=True))
            first += width
        return outs

    def scattered_rows(self, send, keep):
        whole = jnp.stack([keep, send]).reshape(2, 4, 4, -1, D)
        whole = whole.transpose(2, 1, 0, 3, 4).reshape(-1, D)
        return lax.psum_scatter(whole.astype(f32), "wide", scatter_dimension=0, tiled=True)

    def gathered_rows(self, shard):
        whole = lax.all_gather(shard, "wide", axis=0, tiled=True).reshape(4, 4, 2, -1, D)
        whole = jnp.stack([whole[z] for z in FAR_FIRST], axis=1)
        return [whole[:, :, half].reshape(-1, D) for half in range(2)]

    def first(self, keep, got, after, copied=False):
        rows, width = keep.shape[0] // 4, keep.shape[1]
        (x, y), token = call(
            first_kernel,
            [shape(rows, width, dtype=bf16)] * 2,
            [pltpu.VMEM((2 * rows, width), bf16), pltpu.SemaphoreType.DMA((8,))]
            + [pltpu.VMEM((2 * rows, width), bf16)] * copied,
            16,
            [keep, got],
            [HBM, HBM if copied else VM],
            after=after,
        )
        return [self.swap(x, 2), self.swap(y, 4)], token

    def second(self, keep, got, ones, after, copied=False):
        rows, width = keep.shape[0] // 8, keep.shape[1]
        (x, y), token = call(
            second_kernel,
            [shape(rows, width, dtype=bf16)] * 2,
            [pltpu.VMEM((2 * rows, width), bf16), pltpu.SemaphoreType.DMA((4,))]
            + [pltpu.VMEM((2 * rows, width), bf16)] * copied,
            16,
            [keep, got, *ones],
            [HBM, HBM if copied else VM, VM, VM],
            after=after,
            us=100,
        )
        return [self.swap(x, 2), self.swap(y, 4)], token

    def near_sum(self, keep, got, ones, twos, direct, after):
        tall, width = keep.shape[0] // 4, keep.shape[1]
        rows = tall // 4
        if direct:
            outs = [shape(rows, width)] + [shape(rows, width, dtype=bf16)] * 3
        else:
            outs = [shape(2 * rows, width, dtype=bf16)] + [shape(rows, width)] * 2
        scratch = [pltpu.VMEM((tall, width), bf16), pltpu.SemaphoreType.DMA((4,))]
        scratch += [pltpu.VMEM((tall, width), bf16)] * direct
        if not direct:
            scratch += [pltpu.VMEM((rows, width), f32)] * 2 + [pltpu.SemaphoreType.DMA((2,))]
        return call(
            functools.partial(near_kernel, direct),
            outs,
            scratch,
            16,
            [keep, got, *ones, *twos],
            [HBM, HBM if direct else VM] + [VM] * 4,
            after=after,
            out_specs=[VM] * 4 if direct else [VM, HBM, HBM],
            us=100,
        )

    def z_sum(self, token, own, *parts):
        own = tie(own, token)
        for part, bits in zip(parts, (8, 16, 24)):
            own = own + self.swap(part, bits).astype(f32)
        return own

    def halved_z(self, send, own, beyond, after):
        (send, total), token = call(
            beyond_kernel,
            [shape(*own.shape, dtype=bf16), shape(*own.shape)],
            [pltpu.VMEM(own.shape, f32)] * 2 + [pltpu.SemaphoreType.DMA((3,))],
            8,
            [self.swap(send, 8), own, beyond],
            [VM, HBM, HBM],
            after=after,
            out_specs=[VM, HBM],
        )
        return total, self.swap(send, 16), token

    def own_rows(self, own, widths):
        rows = own.shape[0] // 2
        mine = self.by_core(own[:rows], own[rows:])
        got = self.swap(self.by_core(own[rows:], own[:rows]), 1)
        outs, first = [], 0
        for width in widths:
            a, b = mine[:, first : first + width], got[:, first : first + width]
            outs.append(
                self.by_core(jnp.concatenate([a, b], axis=1), jnp.concatenate([b, a], axis=1))
            )
            first += width
        return outs


def on_device(
    tokens,
    cotangent,
    cond,
    kept,
    counts,
    ada_w,
    ada_bias,
    qkv_w,
    q_bias,
    v_bias,
    proj_w,
    proj_bias,
    fc1_w,
    fc1_bias,
    fc2_w,
    fc2_bias,
):
    devices = lax.axis_size("wide")
    images = cond.shape[0]
    span = ada_bias.shape[0]
    own_dim = ada_w.shape[0]
    links = Links(devices)
    me, where, cube = links.me, links.where, links.cube
    rows = TOK_DEV
    dma = pltpu.SemaphoreType.DMA
    half_sum = (qkv_w.shape[1] + proj_w.shape[1] + fc1_w.shape[1]) // 2

    (mine, send, edge, place, starts, cond_slots, ada_parts), _ = call(
        begin_kernel,
        [
            shape(own_dim, half_sum, dtype=bf16),
            shape(own_dim, half_sum, dtype=bf16),
            shape(2 * LEN, D, dtype=bf16),
            shape(8, dtype=jnp.int32),
            shape(devices, dtype=jnp.int32),
            shape(devices * 8, D, dtype=bf16),
            shape(devices, own_dim, span, dtype=bf16),
        ],
        [
            pltpu.VMEM((devices * 8, images), f32),
            pltpu.VMEM(cond.shape, bf16),
            pltpu.VMEM(ada_w.shape, bf16),
            dma((10,)),
        ],
        16,
        [where, counts, cond, ada_w, tokens, cotangent, qkv_w, proj_w, fc1_w],
        [SM, SM] + [HBM] * 7,
        out_specs=[VM, VM, VM, SM, SM, VM, VM],
    )
    if cube:
        pair = links.pair(mine, links.swap(send, 1))
        near_one = links.along_z(pair[:, : 3 * D // 2])
        before_mod = [pair]
    else:
        before_mod = []
    halo = lax.ppermute(edge, "wide", [(i + 1, i) for i in range(devices - 1)])

    ada_cols = lax.all_to_all(ada_parts, "wide", 0, 0, tiled=True)
    ada_cols = ada_cols.reshape(D, span)
    lanes = lambda items: jnp.pad(
        jnp.concatenate(items), (0, span - sum(i.shape[0] for i in items))
    ).reshape(1, span)
    addend = jnp.concatenate(
        [
            jnp.broadcast_to(ada_bias.reshape(1, span), (SLOTS, span)),
            lanes([q_bias, v_bias, proj_bias, fc2_bias]),
            lanes([fc1_bias]),
            jnp.zeros((2, span), bf16),
        ],
        axis=0,
    ).astype(f32)
    (mod_cols,), mod_ran = call(
        mod_kernel,
        [shape(devices, 8, span)],
        [],
        16,
        [cond_slots, ada_cols, addend],
        [VM] * 3,
        after=before_mod,
        zeros=True,
    )
    mixed = lax.all_to_all(mod_cols, "wide", 0, 0, tiled=True)

    quarter = D // 4
    frequency = jnp.exp(-math.log(10000.0) * jnp.arange(quarter).astype(f32) / quarter)
    angle = jnp.arange(GRID).astype(f32)[:, None] * frequency[None, :]
    table = jnp.concatenate([jnp.sin(angle), jnp.cos(angle)], axis=1)
    if cube:
        near_one = tie(near_one, mod_ran)
        over = [links.swap(near_one, bits) for bits in (2, 4, 6)]
        pair_two = tie(pair[:, 3 * D // 2 :], mod_ran)
        two = jnp.concatenate([pair_two, links.swap(pair_two, 8)], axis=0)
        before_prep = [near_one, two]
    else:
        before_prep = []
    (residual, grad_out, mod, qkv_bias, proj_bias_all, fc2_bias_all, fc1_bias_all), prepared = call(
        prep_kernel,
        [
            shape(rows, D),
            shape(rows, D, dtype=bf16),
            shape(SLOTS, 6 * D),
            shape(1, 3 * D),
            shape(1, D),
            shape(1, D),
            shape(1, F),
        ],
        [
            pltpu.VMEM((rows, D), bf16),
            pltpu.VMEM((rows, D), bf16),
            pltpu.VMEM((2 * LEN, D), bf16),
            pltpu.VMEM(kept.shape, jnp.int32),
            pltpu.VMEM(table.shape, f32),
            dma((5,)),
        ],
        16,
        [place, mixed, tokens, cotangent, halo, kept, table],
        [SM, VM, HBM, HBM, ANY, HBM, ANY],
        after=before_prep,
        us=10,
    )

    if cube:
        near_two = jnp.concatenate([two, links.swap(two, 16)], axis=0)
        qkv_near, joined = join([near_one, *over], [prepared, near_two])
        qkv_far = links.swap(qkv_near, 1)
        over_x, over_y = links.swap(near_two, 2), links.swap(near_two, 4)
        before_qkv = []
    else:
        qkv_near, qkv_far = links.gathered([qkv_w])
        before_qkv = []

    (attn_in, qkv, qkv_laid), qkv_ran = call(
        qkv_kernel,
        [
            shape(rows, D, dtype=bf16),
            shape(rows, 3 * D, dtype=bf16),
            shape(D, 3 * D, dtype=bf16),
        ],
        [pltpu.VMEM((rows, D), bf16), pltpu.VMEM((D, 3 * D), bf16), dma((2,))],
        16,
        [where, residual, mod, qkv_bias, qkv_near, qkv_far],
        [SM] + [VM] * 5,
        after=before_qkv,
        out_specs=[HBM, VM, HBM],
        zeros=True,
    )
    before_attend = [qkv_ran]
    if cube:
        two, _ = join([fc2_w, links.swap(fc2_w, 16)], [qkv_ran])
        before_attend.append(two)
        near_three = jnp.concatenate([two, links.swap(two, 8)], axis=0)
    (attended, attended_kept), attend_ran = call(
        attend_kernel,
        [shape(rows, D, dtype=bf16)] * 2,
        [dma((1,))],
        16,
        [qkv],
        [VM],
        after=before_attend,
        out_specs=[VM, HBM],
        zeros=True,
    )
    if cube:
        half = near_two.shape[0] // 2
        width = near_two.shape[1]
        (most, low_half, high_half), _ = call(
            cut_kernel,
            [
                shape(6 * half, width, dtype=bf16),
                shape(half, width, dtype=bf16),
                shape(half, width, dtype=bf16),
            ],
            [dma((5,))],
            8,
            [near_two, over_x, over_y],
            [ANY] * 3,
            after=[attend_ran],
            out_specs=[ANY] * 3,
        )
        most_far = links.swap(most, 1)
        diag = [links.swap(low_half, 2), links.swap(high_half, 4)]
        diag, _ = join(diag)
        mid_halves = [most, diag, most_far, links.swap(diag, 1)]
        over = [links.swap(near_three, bits) for bits in (2, 4, 6)]
    else:
        mid_near, mid_far = links.gathered([proj_w, fc1_w])
        cut = 3 * D // 4
        mid_halves = [mid_near[:cut], mid_near[cut:], mid_far[:cut], mid_far[cut:]]
        fc2_near, fc2_far = links.gathered_rows(fc2_w)

    (
        branch, middle, mlp_in, grad_mlp_out, fc2_bias_sum, activated, slope, fc2_send, fc2_keep,
        middle_kept,
    ), hidden_ran = call(
        hidden_kernel,
        [
            shape(rows, D),
            shape(rows, D),
            shape(rows, D, dtype=bf16),
            shape(rows, D, dtype=bf16),
            shape(1, D),
            shape(rows, F, dtype=bf16),
            shape(rows, F, dtype=bf16),
            shape(F // 2, D, dtype=bf16),
            shape(F // 2, D, dtype=bf16),
            shape(rows, D),
        ],
        [
            pltpu.VMEM((D, D), bf16),
            pltpu.VMEM((D, F), bf16),
            pltpu.VMEM((rows, F), bf16),
            pltpu.VMEM((rows, F), bf16),
            pltpu.VMEM((F, rows), bf16),
            pltpu.VMEM((F, D), bf16),
            dma((9,)),
        ],
        32,
        [where, residual, attended, mod, grad_out, proj_bias_all, fc1_bias_all, *mid_halves],
        [SM] + [VM] * 10,
        out_specs=[VM] * 5 + [HBM] * 5,
    )
    def weight_grad(*pairs, after=()):
        half = sum(right.shape[1] for _, right in pairs) // 2
        scratch = [pltpu.VMEM((D, half), bf16), pltpu.VMEM((D, half), bf16), dma((8,))]
        spaces = [VM, VM]
        if len(pairs) == 2:
            scratch += [
                pltpu.VMEM((D, rows), bf16),
                pltpu.VMEM((rows, D), bf16),
                pltpu.VMEM((D, rows), bf16),
                dma((3,)),
            ]
            spaces = [HBM, HBM, HBM, VM]
        return call(
            functools.partial(wgrad_kernel, len(pairs)),
            [shape(D, half, dtype=bf16)] * 2,
            scratch,
            20,
            [where, *[left for left, _ in pairs], *[right for _, right in pairs]],
            [SM, *spaces],
            after=after,
            out_specs=[HBM] * 2,
        )

    (mlp_flipped, attended_flipped, attn_flipped), flipped = call(
        flips_kernel,
        [shape(D, rows, dtype=bf16)] * 3,
        [pltpu.VMEM((rows, D), bf16)] * 2 + [pltpu.VMEM((2, D, rows), bf16), dma((4,))],
        16,
        [where, mlp_in, attended_kept, attn_in],
        [SM, VM, HBM, HBM],
        after=[hidden_ran],
        out_specs=[VM, HBM, HBM],
    )
    (probs,), probs_ran = call(
        probs_kernel,
        [shape(SLOTS * HEADS // 2 * LEN, 2 * LEN)],
        [
            pltpu.VMEM((rows, 2 * D), bf16),
            pltpu.VMEM((SLOTS * HEADS // 2 * LEN, 2 * LEN), f32),
            dma((2 * SLOTS,)),
        ],
        16,
        [qkv],
        [HBM],
        after=[flipped],
        out_specs=[HBM],
    )
    if cube:
        fc2_got = links.swap(fc2_send, 1)
        fc2_near, gathered = join([near_three, *over], [probs_ran], us=100)
        fc2_far = links.swap(fc2_near, 1)
        fc2_ones, fc2_first = links.first(fc2_keep, fc2_got, [gathered])
        before_fc2 = [fc2_first]
    else:
        before_fc2 = []
    (grad_hidden, fc1_bias_sum), _ = call(
        fc2_back_kernel,
        [shape(rows, F, dtype=bf16), shape(1, F)],
        [pltpu.VMEM((F, D), bf16), pltpu.VMEM((rows, F), bf16), dma((6,))],
        20,
        [where, grad_mlp_out, slope, fc2_near, fc2_far],
        [SM, VM, HBM, VM, VM],
        after=before_fc2,
    )
    (fc1_send, fc1_keep), fc1_ran = weight_grad((mlp_flipped, grad_hidden))
    (out_tail, gate_two_sum, result), out_ran = call(
        fc2_out_kernel,
        [shape(LEN, D, dtype=bf16), shape(SLOTS, D), shape(rows, D, dtype=bf16)],
        [
            pltpu.VMEM((rows, D), f32),
            pltpu.VMEM((rows, F), bf16),
            pltpu.VMEM((F, D), bf16),
            pltpu.VMEM((rows + LEN + 8, D), f32),
            pltpu.VMEM((rows, D), bf16),
            dma((3,)),
        ],
        20,
        [where, place, mod, grad_out, fc2_bias_all, middle_kept, activated, fc2_near, fc2_far],
        [SM] * 2 + [VM] * 3 + [HBM] * 2 + [VM] * 2,
        after=[fc1_ran],
        out_specs=[VM] * 2 + [HBM],
    )
    if cube:
        fc1_got = links.swap(fc1_send, 1)
        fc2_twos, fc2_second = links.second(fc2_keep, fc2_got, fc2_ones, [out_ran])
        fc1_ones, fc1_first = links.first(fc1_keep, fc1_got, [fc2_second])
        before_mid = [fc1_first]
    else:
        before_mid = [out_ran]
    (grad_attended, proj_bias_sum, grad_middle, grad_branch, early), mid_ran = call(
        mid_back_kernel,
        [
            shape(rows, D, dtype=bf16),
            shape(1, D),
            shape(rows, D),
            shape(rows, D, dtype=bf16),
            shape(devices, 16, D, dtype=bf16),
        ],
        [
            pltpu.VMEM((rows, D), f32),
            pltpu.VMEM((rows, D), bf16),
            pltpu.VMEM((devices, 16, D), bf16),
            pltpu.VMEM((D, D), bf16),
            pltpu.VMEM((D, F), bf16),
            pltpu.VMEM((rows, D), f32),
            pltpu.VMEM((16, D), f32),
            dma((3,)),
        ],
        20,
        [where, grad_hidden, middle, branch, mod, grad_out, gate_two_sum, *mid_halves],
        [SM] + [VM] * 10,
        out_specs=[VM] * 2 + [HBM] * 3,
        after=before_mid,
    )
    early = lax.all_to_all(early, "wide", 0, 0, tiled=True)
    if cube:
        fc2_near_sum, fc2_summed = links.near_sum(
            fc2_keep, fc2_got, fc2_ones, fc2_twos, False, [mid_ran]
        )
        before_back = [fc2_summed]
    else:
        before_back = []
    (grad_qkv, qkv_bias_sum), back_ran = call(
        attend_back_kernel,
        [shape(rows, 3 * D, dtype=bf16), shape(1, 3 * D)],
        [
            pltpu.VMEM((rows, 3 * D), bf16),
            pltpu.VMEM(probs.shape, f32),
            dma((2 * SLOTS,)),
        ],
        16,
        [qkv, probs, grad_attended],
        [HBM, HBM, VM],
        after=before_back,
    )
    before_qkv = []
    if cube:
        fc2_own, fc2_beyond, fc2_halved = links.halved_z(*fc2_near_sum, [back_ran])
        fc1_twos, fc1_second = links.second(fc1_keep, fc1_got, fc1_ones, [fc2_halved])
        before_qkv.append(fc1_second)
    (qkv_send, qkv_keep), qkv_grad_ran = weight_grad(
        (attended_flipped, grad_branch), (attn_flipped, grad_qkv), after=before_qkv
    )
    if cube:
        qkv_got = links.swap(qkv_send, 1)
    if cube:
        fc1_near_sum, fc1_summed = links.near_sum(
            fc1_keep, fc1_got, fc1_ones, fc1_twos, False, [qkv_grad_ran]
        )
        qkv_ones, qkv_first = links.first(qkv_keep, qkv_got, [fc1_summed])
        before_start = [qkv_first, early]
    else:
        before_start = [qkv_grad_ran]
    (tokens_back, tail, late), start_ran = call(
        start_back_kernel,
        [shape(rows, D), shape(3 * LEN, D, dtype=bf16), shape(devices, 2 * SLOTS, D, dtype=bf16)],
        [
            pltpu.VMEM((D, 3 * D), bf16),
            pltpu.VMEM((rows + LEN + 8, D), f32),
            pltpu.VMEM((rows, D), f32),
            pltpu.VMEM((rows, D), f32),
            pltpu.VMEM((2 * SLOTS, D), f32),
            pltpu.VMEM((3 * LEN, D), bf16),
            pltpu.VMEM((devices, 2 * SLOTS, D), bf16),
            dma((5,)),
            dma((SLOTS + 2,)),
        ],
        24,
        [place, grad_qkv, mod, out_tail, residual, grad_middle, qkv_laid],
        [SM] + [VM] * 3 + [HBM] * 3,
        after=before_start,
        out_specs=[HBM] * 3,
    )
    late = lax.all_to_all(late, "wide", 0, 0, tiled=True)

    if cube:
        fc1_own, fc1_beyond, fc1_halved = links.halved_z(*fc1_near_sum, [start_ran])
        qkv_twos, qkv_second = links.second(qkv_keep, qkv_got, qkv_ones, [fc1_halved], True)
        before_ada = [qkv_second]
    else:
        before_ada = [start_ran]

    onward = [(i, i + 1) for i in range(devices - 1)]
    tail = lax.ppermute(tail, "wide", onward)
    wide_images = -(-images // 128) * 128
    (ada_grad, ada_bias_sum, last), ada_ran = call(
        ada_kernel,
        [
            shape(own_dim, 6 * D),
            shape(1, 6 * D),
            shape(devices, own_dim + 8, wide_images, dtype=bf16),
        ],
        [pltpu.VMEM((devices * 16, images), f32), pltpu.VMEM((own_dim + 8, wide_images), f32)],
        24,
        [where, starts, early, late, ada_w, cond, qkv_bias_sum, proj_bias_sum, fc2_bias_sum, fc1_bias_sum],
        [SM] * 2 + [VM] * 8,
        after=before_ada,
        zeros=True,
    )
    last = lax.all_to_all(last, "wide", 0, 0, tiled=True)
    if cube:
        qkv_near_sum, qkv_summed = links.near_sum(
            qkv_keep, qkv_got, qkv_ones, qkv_twos, True, [ada_ran]
        )
        before_place = [qkv_summed]
    else:
        before_place = [ada_ran]
    (out, tokens_grad), placed = call(
        place_kernel,
        [shape(rows, D, dtype=bf16), shape(rows, D)],
        [
            pltpu.VMEM((rows + LEN + 8, D), f32),
            pltpu.VMEM((rows + LEN + 8, D), f32),
            pltpu.VMEM((rows, D), bf16),
            pltpu.VMEM((rows, D), bf16),
            pltpu.VMEM((rows, D), bf16),
            pltpu.VMEM((rows, D), bf16),
            pltpu.VMEM((rows, D), f32),
            dma((6,)),
        ],
        16,
        [place, tail, tokens, cotangent, result, tokens_back],
        [SM, VM] + [HBM] * 4,
        after=before_place,
        out_specs=[HBM] * 2,
    )


    (cond_grad, bias_grads), finished = call(
        finish_kernel,
        [shape(images, D), shape(8, wide_images)],
        [pltpu.VMEM((D, wide_images), f32)],
        16,
        [last],
        [VM],
        after=[placed],
        zeros=True,
    )
    fc1_widths, qkv_widths = [F // 2], [D // 2, 3 * D // 2]
    if cube:
        fc2_grad = tie(fc2_own, ada_ran) + fc2_beyond.astype(f32)
        (fc1_grad,) = links.own_rows(
            tie(fc1_own, ada_ran) + fc1_beyond.astype(f32), fc1_widths
        )
        proj_grad, qkv_grad = links.own_rows(links.z_sum(finished, *qkv_near_sum), qkv_widths)
    else:
        fc2_grad = links.scattered_rows(fc2_send, fc2_keep)
        (fc1_grad,) = links.scattered(fc1_send, fc1_keep, fc1_widths)
        proj_grad, qkv_grad = links.scattered(qkv_send, qkv_keep, qkv_widths)
    bias_grads = bias_grads[:, :own_dim]
    ada_bias_grad = lax.dynamic_slice_in_dim(ada_bias_sum[0], me * span, span, 0)
    return (
        out,
        tokens_grad,
        cond_grad,
        ada_grad,
        ada_bias_grad,
        qkv_grad,
        bias_grads[0],
        bias_grads[1],
        proj_grad,
        bias_grads[2],
        fc1_grad,
        bias_grads[4:].reshape(-1),
        fc2_grad,
        bias_grads[3],
    )


def solution(mesh):
    row, flat = P("wide", None), P("wide")
    return jax.shard_map(
        on_device,
        mesh=mesh,
        in_specs=(row, row, P(), P(), P(), row, flat, row, flat, flat, row, flat, row, flat, row, flat),
        out_specs=(row, row, P(), row, flat, row, flat, flat, row, flat, row, flat, row, flat),
        check_vma=False,
    )
```
